32 devices in a mesh: seq: 8 (over z, y), head: 4 (over x, core).
Axes of the slice: x: 2, y: 2, z: 4, core: 2. Of those that a mesh axis runs over, the one named last changes fastest.
Arguments:
- queries: float32 [1024, 32, 128], P('seq', 'head'), may hold values from -0.6 to 0.6
- keys: float32 [1024, 32, 128], P('seq', 'head'), may hold values from -0.6 to 0.6
- values: float32 [1024, 32, 128], P('seq', 'head'), may hold values from -6 to 6
- level_weights: float32 [5, 32, 1024], P(None, 'head', 'seq'), may hold values from 0.02 to 0.2
- out_proj: bfloat16 [4096, 4096], P('head'), may hold values from -0.125 to 0.125
- out_grad: bfloat16 [1024, 4096], P('seq', 'head'), may hold values from -6 to 6
Outputs:
- mixed: bfloat16 [1024, 4096], P('seq', 'head')
- query_grad: float32 [1024, 32, 128], P('seq', 'head')
- key_grad: float32 [1024, 32, 128], P('seq', 'head')
- value_grad: float32 [1024, 32, 128], P('seq', 'head')
- proj_grad: float32 [4096, 4096], P('head', 'seq')
The draws below stay inside these ranges and needn't reach their ends.
All inputs are finite; a program needn't handle non-finite values.
Results may differ from the reference program's by a relative error of at most 0.015.
Values may be sent and summed in bfloat16 or wider, within the bound.
No kernel may reach another device: no remote copies, remote signals or barrier semaphores. Data moves between devices by JAX's collectives and lax.ppermute only.
A program may use at most 128 MiB of HBM per device.

```python
import math
import jax
import jax.numpy as jnp
from jax import lax

D = 4096
HEADS = 32
HD = 128
CH = 64
TOKENS = 1024
LOCAL_BITS = 1
SEQ_BITS = 3
LEVELS = 5


def with_spikes(entries, stream_key, source, target, parts, factor):
    def block_of(axis_at):
        return (jnp.arange(entries.shape[axis_at]) // (entries.shape[axis_at] // parts)).reshape((-1,) + (1,) * (entries.ndim - 1 - axis_at))

    one_side = jax.random.permutation(stream_key, parts)[block_of(target)]
    second = (block_of(target) + parts // 2) % parts
    return jnp.where((block_of(source) == one_side) | (block_of(source) == second), factor * entries, entries)


def steps_of(key, dims, shards, least, top_value):
    def one(axis_at, blocks):
        steps = jax.random.uniform(jax.random.fold_in(jax.random.fold_in(key, 6), axis_at), (blocks,), jnp.float32, least / len(shards), top_value / len(shards))
        return jnp.repeat(jnp.exp(steps), dims[axis_at] // blocks).reshape((-1,) + (1,) * (len(dims) - axis_at - 1))

    factor_of = one(*shards[0])
    for cut in shards[1:]:
        factor_of = factor_of * one(*cut)
    return factor_of


def gaussian(key, shape, deviation, limit, pieces=(), held_as=jnp.bfloat16):
    loudness = steps_of(key, shape, pieces, -0.22, 0.18) if pieces else 1.0
    entries = jax.random.normal(key, shape, jnp.float32) * deviation * loudness
    return jnp.minimum(jnp.maximum(entries, -limit), limit).astype(held_as)


def heavy_noise(rng, dims, spread, bound, split, heavy, kind=jnp.bfloat16):
    array = spread * jax.random.normal(rng, dims, jnp.float32)
    if split:
        array = array * steps_of(rng, dims, split, -0.22, 0.18)
    return jnp.clip(with_spikes(array, jax.random.fold_in(rng, 3), *heavy), -bound, bound).astype(kind)


def setup_inputs(seed: int = 0) -> dict:
    streams_of = jax.random.split(jax.random.key(seed), 7)
    return {
        "queries": gaussian(streams_of[0], (TOKENS, HEADS, HD), 0.1, 0.6, ((0, 8), (1, 4)), jnp.float32),
        "keys": gaussian(streams_of[1], (TOKENS, HEADS, HD), 0.1, 0.6, ((0, 8), (1, 4)), jnp.float32),
        "values": gaussian(streams_of[2], (TOKENS, HEADS, HD), 1.0, 6.0, ((0, 8), (1, 4)), jnp.float32),
        "level_weights": jnp.clip(jnp.exp(math.log(0.2) - 2.3025851 * jax.random.uniform(streams_of[3], (LEVELS, HEADS, TOKENS), jnp.float32) ** steps_of(streams_of[3], (LEVELS, HEADS, TOKENS), ((1, 4), (2, 8)), -0.2, 0.2)), 0.02, 0.2),
        "out_proj": heavy_noise(streams_of[4], (D, D), D ** -0.5, 0.125, ((0, 4),), (0, 1, 4, 2.0)),
        "out_grad": heavy_noise(streams_of[5], (TOKENS, D), 1.0, 6.0, ((0, 8), (1, 4)), (0, 1, 8, 2.0)),
    }


def head_pass(qh, kh, vh, lamh, gh):
    hp = lax.Precision.HIGHEST
    total, hdim = qh.shape
    nchunk = total // CH
    qc = qh.reshape(nchunk, CH, hdim)
    kc = kh.reshape(nchunk, CH, hdim)
    vc = vh.reshape(nchunk, CH, hdim)
    gc = gh.reshape(nchunk, CH, hdim)
    causal = (jnp.arange(CH)[:, None] >= jnp.arange(CH)[None, :]).astype(jnp.float32)
    weight = lamh[0].reshape(nchunk, CH)[:, :, None] * causal
    scores = jnp.einsum('csd,crd->csr', qc, kc, precision=hp)
    probs = scores * weight
    out = jnp.einsum('csr,crd->csd', probs, vc, precision=hp).reshape(total, hdim)
    dprobs = jnp.einsum('csd,crd->csr', gc, vc, precision=hp) * weight
    dq = jnp.einsum('csr,crd->csd', dprobs, kc, precision=hp).reshape(total, hdim)
    dk = jnp.einsum('csr,csd->crd', dprobs, qc, precision=hp).reshape(total, hdim)
    dv = jnp.einsum('csr,csd->crd', probs, gc, precision=hp).reshape(total, hdim)
    for bit in range(LOCAL_BITS + SEQ_BITS):
        span = CH * 2 ** bit
        groups = total // (2 * span)
        q2 = qh.reshape(groups, 2, span, hdim)
        k2 = kh.reshape(groups, 2, span, hdim)
        v2 = vh.reshape(groups, 2, span, hdim)
        g2 = gh.reshape(groups, 2, span, hdim)
        lam2 = lamh[1 + bit].reshape(groups, 2, span)[:, 1, :, None]
        state = jnp.einsum('nrd,nre->nde', k2[:, 0], v2[:, 0], precision=hp)
        grads = jnp.einsum('nrd,nre->nde', lam2 * q2[:, 1], g2[:, 1], precision=hp)
        zero = jnp.zeros((groups, span, hdim), jnp.float32)
        out_inc = lam2 * jnp.einsum('nrd,nde->nre', q2[:, 1], state, precision=hp)
        dq_inc = lam2 * jnp.einsum('nre,nde->nrd', g2[:, 1], state, precision=hp)
        dk_inc = jnp.einsum('nre,nde->nrd', v2[:, 0], grads, precision=hp)
        dv_inc = jnp.einsum('nrd,nde->nre', k2[:, 0], grads, precision=hp)
        out = out + jnp.stack([zero, out_inc], axis=1).reshape(total, hdim)
        dq = dq + jnp.stack([zero, dq_inc], axis=1).reshape(total, hdim)
        dk = dk + jnp.stack([dk_inc, zero], axis=1).reshape(total, hdim)
        dv = dv + jnp.stack([dv_inc, zero], axis=1).reshape(total, hdim)
    return out, dq, dk, dv


def reference(queries, keys, values, level_weights, out_proj, out_grad):
    total, heads, hdim = queries.shape
    grad_heads = jnp.dot(out_grad, out_proj.T, preferred_element_type=jnp.float32).reshape(total, heads, hdim)

    def one_head(index):
        return head_pass(queries[:, index], keys[:, index], values[:, index], level_weights[:, index], grad_heads[:, index])

    out, dq, dk, dv = lax.map(one_head, jnp.arange(heads, dtype=jnp.int32))
    attended = jnp.transpose(out, (1, 0, 2)).reshape(total, heads * hdim).astype(jnp.bfloat16)
    mixed = jnp.dot(attended, out_proj, preferred_element_type=jnp.float32).astype(jnp.bfloat16)
    proj_grad = jnp.dot(attended.T, out_grad, preferred_element_type=jnp.float32)
    return (mixed, jnp.transpose(dq, (1, 0, 2)), jnp.transpose(dk, (1, 0, 2)), jnp.transpose(dv, (1, 0, 2)), proj_grad)
```

```python
import jax
import jax.numpy as jnp
from jax import lax
from jax.sharding import PartitionSpec as P

CH = 64
BF = jnp.bfloat16
F32 = jnp.float32


def across(block, axis, stride, up_only=False, down_only=False):
    count = lax.axis_size(axis)
    route = []
    for low in range(count):
        high = low | 1 << stride
        if high != low and high < count:
            if not down_only:
                route.append((low, high))
            if not up_only:
                route.append((high, low))
    return lax.ppermute(block, axis, route)


def dot(spec, a, b):
    return jnp.einsum(spec, a, b, preferred_element_type=F32)


def body(queries, keys, values, level_weights, out_proj, out_grad):
    rows, heads_dev, head_dim = queries.shape
    local_bits = (rows // CH).bit_length() - 1
    seq_bits = lax.axis_size("seq").bit_length() - 1
    heads = lax.axis_size("head")
    seq_place = lax.axis_index("seq")
    head_place = lax.axis_index("head")
    q, k, v = queries.astype(BF), keys.astype(BF), values.astype(BF)

    grad_full = lax.all_gather(out_grad, "head", axis=1, tiled=True)
    grad_columns = lax.all_to_all(grad_full, "seq", split_axis=1, concat_axis=0, tiled=True)

    running = dot("shd,she->hde", k, v)
    partner_keys = []
    for digit in range(seq_bits):
        arrived = across(running.astype(BF), "seq", digit, up_only=digit == seq_bits - 1)
        partner_keys.append(arrived)
        running = running + arrived.astype(F32)

    position = jnp.arange(rows, dtype=jnp.int32)
    stretch = position // CH
    differ = stretch[:, None] ^ stretch[None, :]
    level = jnp.zeros_like(differ)
    for digit in range(local_bits):
        level = level + (differ >= 1 << digit).astype(jnp.int32)
    causal = position[:, None] >= position[None, :]
    pair_weight = jnp.zeros((heads_dev, rows, rows), F32)
    for depth in range(local_bits + 1):
        pair_weight = jnp.where(
            (level == depth) & causal, level_weights[depth][:, :, None], pair_weight
        )
    uppers = [(seq_place >> digit & 1).astype(F32) for digit in range(seq_bits)]
    scales = [
        jnp.transpose(level_weights[1 + local_bits + digit])[:, :, None] for digit in range(seq_bits)
    ]

    probs = (dot("thd,shd->hts", q, k) * pair_weight).astype(BF)
    attended_f = dot("hts,shd->thd", probs, v)

    grad_heads = lax.dot_general(
        grad_full, out_proj, (((1,), (1,)), ((), ())), preferred_element_type=F32
    )
    g = grad_heads.astype(BF).reshape(rows, heads_dev, head_dim)

    pending = None
    for digit in reversed(range(seq_bits)):
        own = dot("thd,the->hde", (queries * scales[digit]).astype(BF), g) * uppers[digit]
        outgoing = own if pending is None else pending + own
        landed = across(outgoing.astype(BF), "seq", digit, down_only=digit == seq_bits - 1)
        pending = landed.astype(F32) if pending is None else pending + landed.astype(F32)
    later = pending.astype(BF)

    dprobs = (dot("thd,shd->hts", g, v) * pair_weight).astype(BF)
    query_grad = dot("hts,shd->thd", dprobs, k)
    key_grad = dot("hts,thd->shd", dprobs, q)
    value_grad = dot("hts,thd->shd", probs, g)

    for digit in range(seq_bits):
        scale = scales[digit] * uppers[digit]
        attended_f = attended_f + scale * dot("thd,hde->the", q, partner_keys[digit])
        query_grad = query_grad + scale * dot("the,hde->thd", g, partner_keys[digit])
    attended = attended_f.reshape(rows, heads_dev * head_dim).astype(BF)

    every_token = lax.all_gather(attended, "seq", axis=0, tiled=True)
    share = jnp.dot(attended, out_proj, preferred_element_type=F32)
    share = share.reshape(rows, heads, -1)
    mixed = lax.dynamic_index_in_dim(share, head_place, 1, keepdims=False)
    for shift in range(1, heads):
        target = (head_place + shift) % heads
        block = lax.dynamic_index_in_dim(share, target, 1, keepdims=False).astype(BF)
        route = [(place, (place + shift) % heads) for place in range(heads)]
        mixed = mixed + lax.ppermute(block, "head", route).astype(F32)
    mixed = mixed.astype(BF)

    key_grad = key_grad + dot("the,hde->thd", v, later)
    value_grad = value_grad + dot("thd,hde->the", k, later)

    proj_grad = lax.dot_general(
        every_token, grad_columns, (((0,), (0,)), ((), ())), preferred_element_type=F32
    )
    return (mixed, query_grad, key_grad, value_grad, proj_grad)


def solution(mesh):
    placed = (
        P("seq", "head", None),
        P("seq", "head", None),
        P("seq", "head", None),
        P(None, "head", "seq"),
        P("head", None),
        P("seq", "head"),
    )
    return jax.shard_map(
        body,
        mesh=mesh,
        in_specs=placed,
        out_specs=(
            P("seq", "head"),
            P("seq", "head", None),
            P("seq", "head", None),
            P("seq", "head", None),
            P("head", "seq"),
        ),
        check_vma=False,
    )
```

```python
import functools

import jax
import jax.numpy as jnp
from jax import lax
from jax.experimental import pallas as pl
from jax.experimental.pallas import tpu as pltpu
from jax.sharding import PartitionSpec as P

CH = 64
BF = jnp.bfloat16
F32 = jnp.float32
NN = (((1,), (0,)), ((), ()))
NT = (((1,), (1,)), ((), ()))
TN = (((0,), (0,)), ((), ()))
VMEM = pl.BlockSpec(memory_space=pltpu.VMEM)
SMEM = pl.BlockSpec(memory_space=pltpu.SMEM)
PARAMS = pltpu.CompilerParams(vmem_limit_bytes=40 * 2**20)


def mm(a, b, dims):
    return lax.dot_general(a, b, dims, preferred_element_type=F32)


def cost(flops, moved):
    return pl.CostEstimate(flops=flops, bytes_accessed=moved, transcendentals=0)


def like(shape, dtype):
    return jax.ShapeDtypeStruct(shape, dtype)


def across(block, axis, stride, up_only=False, down_only=False):
    count = lax.axis_size(axis)
    route = []
    for low in range(count):
        high = low | 1 << stride
        if high != low and high < count:
            if not down_only:
                route.append((low, high))
            if not up_only:
                route.append((high, low))
    return lax.ppermute(block, axis, route)


def state_kernel(k_ref, v_ref, s_ref, kh_ref, vh_ref):
    for h in range(k_ref.shape[1]):
        k = k_ref[:, h, :].astype(BF)
        v = v_ref[:, h, :].astype(BF)
        kh_ref[h] = k
        vh_ref[h] = v
        s_ref[h] = mm(k, v, TN).astype(BF)


def weight_of(lam_ref, h, rows):
    local_bits = (rows // CH).bit_length() - 1
    s = lax.broadcasted_iota(jnp.int32, (rows, rows), 0)
    t = lax.broadcasted_iota(jnp.int32, (rows, rows), 1)
    differ = (s // CH) ^ (t // CH)
    weight = jnp.broadcast_to(lam_ref[0, h : h + 1, :], (rows, rows))
    for digit in range(local_bits):
        weight = jnp.where(differ >= 1 << digit, lam_ref[1 + digit, h : h + 1, :], weight)
    return jnp.where(s <= t, weight, 0.0)


def local_kernel(q_ref, kh_ref, vh_ref, lam_ref, lamu_ref, pt_ref, att_ref, qh_ref, qw_ref):
    rows, heads_dev, _ = q_ref.shape
    for h in range(heads_dev):
        q32 = q_ref[:, h, :]
        q = q32.astype(BF)
        qh_ref[h] = q
        for b in range(qw_ref.shape[0]):
            column = b * heads_dev + h
            qw_ref[b, h] = (q32 * lamu_ref[:, column : column + 1]).astype(BF)
        pt = (mm(kh_ref[h], q, NT) * weight_of(lam_ref, h, rows)).astype(BF)
        pt_ref[h] = pt
        att_ref[h] = mm(pt, vh_ref[h], TN)


def attended_kernel(bits, att_ref, qw_ref, *refs):
    states, out_ref = refs[:bits], refs[bits]
    heads_dev, _, head_dim = att_ref.shape
    for h in range(heads_dev):
        total = att_ref[h]
        for b in range(bits):
            total = total + mm(qw_ref[b, h], states[b][h], NN)
        out_ref[:, h * head_dim : (h + 1) * head_dim] = total.astype(BF)


def cotangent_kernel(blocks, order_ref, *refs):
    parts, (w_ref, qw_ref, g_ref), sums, acc = (
        refs[:blocks],
        refs[blocks : blocks + 3],
        refs[blocks + 3 : -1],
        refs[-1],
    )
    del order_ref
    step = pl.program_id(0)
    for i in range(blocks):

        @pl.when(step == i)
        def _(i=i):
            part = mm(parts[i][...], w_ref[...], NT)
            acc[...] = part if i == 0 else acc[...] + part

    @pl.when(step == blocks - 1)
    def _():
        g_ref[...] = acc[...].astype(BF)
        heads_dev, _, head_dim = qw_ref.shape[1:]
        for b in range(len(sums)):
            for h in range(heads_dev):
                g = g_ref[:, h * head_dim : (h + 1) * head_dim]
                sums[b][h] = mm(qw_ref[b, h], g, TN).astype(BF)


def local_grad_kernel(
    bits, g_ref, qh_ref, kh_ref, vh_ref, pt_ref, lam_ref, lamu_ref, *refs
):
    states, (dq_ref, dk_ref, dv_ref) = refs[:bits], refs[bits:]
    heads_dev, rows, head_dim = qh_ref.shape
    for h in range(heads_dev):
        g = g_ref[:, h * head_dim : (h + 1) * head_dim]
        g32 = g.astype(F32)
        dpt = (mm(vh_ref[h], g, NT) * weight_of(lam_ref, h, rows)).astype(BF)
        dk_ref[h] = mm(dpt, qh_ref[h], NN)
        dv_ref[h] = mm(pt_ref[h], g, NN)
        dq = mm(dpt, kh_ref[h], TN)
        for b in range(bits):
            column = b * heads_dev + h
            gw = (g32 * lamu_ref[:, column : column + 1]).astype(BF)
            dq = dq + mm(gw, states[b][h], NT)
        dq_ref[:, h, :] = dq


def later_grad_kernel(late_ref, kh_ref, vh_ref, dkl_ref, dvl_ref, dk_ref, dv_ref):
    for h in range(kh_ref.shape[0]):
        late = late_ref[h]
        dk_ref[:, h, :] = dkl_ref[h] + mm(vh_ref[h], late, NT)
        dv_ref[:, h, :] = dvl_ref[h] + mm(kh_ref[h], late, NN)


def share_kernel(blocks, order_ref, att_ref, w_ref, *outs):
    del order_ref
    step = pl.program_id(0)
    for i in range(blocks):

        @pl.when(step == i)
        def _(i=i):
            outs[i][...] = mm(att_ref[...], w_ref[...], NN).astype(outs[i].dtype)


def proj_kernel(count, first, owner_ref, cols_ref, *refs):
    if first:
        out_ref = refs[count]
    else:
        out_ref = refs[count + 1]
    total = None if first else refs[count][...]
    for i in range(count):
        cols = cols_ref[:, owner_ref[i]]
        cols = cols.reshape(cols.shape[0] * cols.shape[1], cols.shape[2])
        part = mm(refs[i][...], cols, TN)
        total = part if total is None else total + part
    out_ref[...] = total


def body(queries, keys, values, level_weights, out_proj, out_grad):
    rows, heads_dev, head_dim = queries.shape
    width = heads_dev * head_dim
    local_bits = (rows // CH).bit_length() - 1
    devices = lax.axis_size("seq")
    seq_bits = devices.bit_length() - 1
    heads = lax.axis_size("head")
    head_bits = heads.bit_length() - 1
    seq_place = lax.axis_index("seq")
    head_place = lax.axis_index("head")
    columns_dev = out_proj.shape[1] // devices

    head_state = like((heads_dev, head_dim, head_dim), BF)
    per_head = like((heads_dev, rows, head_dim), BF)
    per_head_f32 = like((heads_dev, rows, head_dim), F32)
    flops_head = 2 * heads_dev * rows * rows * head_dim
    moved_head = 2 * rows * width

    own_state, kh, vh = pl.pallas_call(
        state_kernel,
        out_shape=(head_state, per_head, per_head),
        in_specs=[VMEM] * 2,
        out_specs=(VMEM,) * 3,
        compiler_params=PARAMS,
        cost_estimate=cost(flops_head, 7 * moved_head),
    )(keys, values)

    grad_blocks = {0: out_grad}
    for digit in reversed(range(head_bits)):
        held = sorted(grad_blocks)
        sent = jnp.stack([grad_blocks[i] for i in held]) if len(held) > 1 else grad_blocks[0][None]
        landed = across(sent, "head", digit)
        for n, i in enumerate(held):
            grad_blocks[i ^ 1 << digit] = landed[n]
    xor_order = list(range(heads))
    order = jnp.stack([head_place ^ i for i in xor_order]).astype(jnp.int32)

    uppers = jnp.stack([(seq_place >> b & 1).astype(F32) for b in range(seq_bits)])
    lamu = (level_weights[1 + local_bits :] * uppers[:, None, None]).reshape(-1, rows).T
    lam = level_weights[: 1 + local_bits]

    probs_t, att_local, qh, qw = pl.pallas_call(
        local_kernel,
        out_shape=(
            like((heads_dev, rows, rows), BF),
            per_head_f32,
            per_head,
            like((seq_bits, heads_dev, rows, head_dim), BF),
        ),
        in_specs=[VMEM] * 5,
        out_specs=(VMEM,) * 4,
        compiler_params=PARAMS,
        cost_estimate=cost(2 * flops_head, 12 * moved_head),
    )(queries, kh, vh, lam, lamu)

    partner_states = []
    running = own_state
    for digit in range(seq_bits):
        arrived = across(running, "seq", digit, up_only=digit == seq_bits - 1)
        partner_states.append(arrived)
        running = (running.astype(F32) + arrived.astype(F32)).astype(BF)

    g, *grad_sums = pl.pallas_call(
        functools.partial(cotangent_kernel, heads),
        out_shape=(like((rows, width), BF),) + (head_state,) * seq_bits,
        grid_spec=pltpu.PrefetchScalarGridSpec(
            num_scalar_prefetch=1,
            grid=(heads,),
            in_specs=[VMEM] * heads
            + [pl.BlockSpec((width, out_grad.shape[1]), lambda i, o: (0, o[i])), VMEM],
            out_specs=(VMEM,) * (1 + seq_bits),
            scratch_shapes=[pltpu.VMEM((rows, width), F32)],
        ),
        compiler_params=PARAMS,
        cost_estimate=cost(2 * rows * width * out_proj.shape[1], 2 * width * out_proj.shape[1]),
    )(order, *[grad_blocks[i] for i in xor_order], out_proj, qw)

    pending = None
    for digit in reversed(range(seq_bits)):
        outgoing = grad_sums[digit]
        if pending is not None:
            outgoing = (outgoing.astype(F32) + pending).astype(BF)
        landed = across(outgoing, "seq", digit, down_only=digit == seq_bits - 1).astype(F32)
        pending = landed if pending is None else pending + landed
    later = pending.astype(BF)

    part = rows // heads
    quarter = jnp.stack(
        [lax.dynamic_slice_in_dim(grad_blocks[i], head_place * part, part, 0) for i in xor_order]
    )
    quarter = quarter.reshape((2,) * head_bits + quarter.shape[1:])
    for digit in range(head_bits):
        axis = head_bits - 1 - digit
        quarter = jnp.where((head_place >> digit & 1) == 1, jnp.flip(quarter, axis), quarter)
    quarter = quarter.reshape(heads, part, devices // heads, columns_dev)
    quarter = quarter.transpose(0, 2, 1, 3).reshape((2,) * seq_bits + (part, columns_dev))
    for digit in reversed(range(seq_bits)):
        axis = seq_bits - 1 - digit
        mine = (seq_place >> digit & 1) == 1
        low = lax.index_in_dim(quarter, 0, axis, keepdims=False)
        high = lax.index_in_dim(quarter, 1, axis, keepdims=False)
        landed = across(jnp.where(mine, low, high), "seq", digit)
        kept = jnp.where(mine, high, low)
        quarter = jnp.stack(
            [jnp.where(mine, landed, kept), jnp.where(mine, kept, landed)], axis
        )
    quarter = quarter.reshape(devices, part, columns_dev)
    grad_columns = lax.all_gather(quarter, "head", axis=0, tiled=False)

    attended = pl.pallas_call(
        functools.partial(attended_kernel, seq_bits),
        out_shape=like((rows, width), BF),
        in_specs=[VMEM] * (2 + seq_bits),
        out_specs=VMEM,
        compiler_params=PARAMS,
        cost_estimate=cost(seq_bits * flops_head, 8 * moved_head),
    )(att_local, qw, *partner_states)

    share_order = list(reversed(xor_order))
    shares = pl.pallas_call(
        functools.partial(share_kernel, heads),
        out_shape=tuple(like((rows, width), BF if i else F32) for i in share_order),
        grid_spec=pltpu.PrefetchScalarGridSpec(
            num_scalar_prefetch=1,
            grid=(heads,),
            in_specs=[VMEM, pl.BlockSpec((width, width), lambda i, o: (0, o[i]))],
            out_specs=(VMEM,) * heads,
        ),
        compiler_params=PARAMS,
        cost_estimate=cost(2 * rows * width * out_proj.shape[1], 2 * width * out_proj.shape[1]),
    )(order[::-1], attended, out_proj)
    mixed = shares[-1]
    for i, block in zip(share_order[:-1], shares[:-1]):
        route = [(place, place ^ i) for place in range(heads)]
        mixed = mixed + lax.ppermute(block, "head", route).astype(F32)
    mixed = mixed.astype(BF)

    query_grad, key_local, value_local = pl.pallas_call(
        functools.partial(local_grad_kernel, seq_bits),
        out_shape=(like((rows, heads_dev, head_dim), F32), per_head_f32, per_head_f32),
        in_specs=[VMEM] * (7 + seq_bits),
        out_specs=(VMEM,) * 3,
        compiler_params=PARAMS,
        cost_estimate=cost((4 + seq_bits) * flops_head, 14 * moved_head),
    )(g, qh, kh, vh, probs_t, lam, lamu, *partner_states)
    key_grad, value_grad = pl.pallas_call(
        later_grad_kernel,
        out_shape=(like((rows, heads_dev, head_dim), F32),) * 2,
        in_specs=[VMEM] * 5,
        out_specs=(VMEM,) * 2,
        compiler_params=PARAMS,
        cost_estimate=cost(2 * flops_head, 11 * moved_head),
    )(later, kh, vh, key_local, value_local)

    ring = list(range(0, devices, 2)) + list(range(devices - 1, 0, -2))
    where_in_ring = jnp.array([ring.index(d) for d in range(devices)], jnp.int32)
    place = where_in_ring[seq_place]
    ring_order = jnp.array(ring, jnp.int32)

    def owner(offset):
        return ring_order[(place + offset) % devices]

    forward = [(ring[i], ring[(i + 1) % devices]) for i in range(devices)]
    backward = [(b, a) for a, b in forward]

    def accumulate(total, blocks, owners):
        count = len(blocks)
        operands = blocks if total is None else blocks + [total]
        return pl.pallas_call(
            functools.partial(proj_kernel, count, total is None),
            out_shape=like((width, columns_dev), F32),
            in_specs=[SMEM] + [VMEM] * (1 + len(operands)),
            out_specs=VMEM,
            compiler_params=PARAMS,
            cost_estimate=cost(
                2 * count * rows * width * columns_dev, 4 * width * columns_dev
            ),
        )(jnp.stack(owners).astype(jnp.int32), grad_columns, *operands)

    blocks, owners, total = [attended], [seq_place], None
    ahead = behind = attended
    half = rows // 2
    for step in range(1, devices // 2):
        ahead = lax.ppermute(ahead, "seq", forward)
        behind = lax.ppermute(behind, "seq", backward)
        if step == devices // 2 - 1:
            last = [
                lax.ppermute(ahead[:half], "seq", forward),
                lax.ppermute(behind[half:], "seq", backward),
            ]
        blocks += [ahead, behind]
        owners += [owner(-step), owner(step)]
    total = accumulate(None, blocks, owners)
    proj_grad = accumulate(total, [jnp.concatenate(last)], [owner(devices // 2)])
    return (mixed, query_grad, key_grad, value_grad, proj_grad)


def solution(mesh):
    placed = (
        P("seq", "head", None),
        P("seq", "head", None),
        P("seq", "head", None),
        P(None, "head", "seq"),
        P("head", None),
        P("seq", "head"),
    )
    return jax.shard_map(
        body,
        mesh=mesh,
        in_specs=placed,
        out_specs=(
            P("seq", "head"),
            P("seq", "head", None),
            P("seq", "head", None),
            P("seq", "head", None),
            P("head", "seq"),
        ),
        check_vma=False,
    )
```

```python
import functools

import jax
import jax.numpy as jnp
from jax import lax
from jax.experimental import pallas as pl
from jax.experimental.pallas import tpu as pltpu
from jax.sharding import PartitionSpec as P

CH = 64
BF = jnp.bfloat16
F32 = jnp.float32
NN = (((1,), (0,)), ((), ()))
NT = (((1,), (1,)), ((), ()))
TN = (((0,), (0,)), ((), ()))
TT = (((0,), (1,)), ((), ()))
VMEM = pl.BlockSpec(memory_space=pltpu.VMEM)
ANY = pl.BlockSpec(memory_space=pl.ANY)
SMEM = pl.BlockSpec(memory_space=pltpu.SMEM)
PARAMS = pltpu.CompilerParams(vmem_limit_bytes=14 * 2**20)


def mm(a, b, dims):
    return lax.dot_general(a, b, dims, preferred_element_type=F32)


def cost(flops, moved):
    return pl.CostEstimate(flops=flops, bytes_accessed=moved, transcendentals=0)


def like(shape, dtype):
    return jax.ShapeDtypeStruct(shape, dtype)


def across(block, axis, stride, up_only=False, down_only=False):
    count = lax.axis_size(axis)
    route = []
    for low in range(count):
        high = low | 1 << stride
        if high != low and high < count:
            if not down_only:
                route.append((low, high))
            if not up_only:
                route.append((high, low))
    return lax.ppermute(block, axis, route)


def state_kernel(k_ref, v_ref, s_ref, kh_ref, vh_ref):
    for h in range(k_ref.shape[1]):
        k = k_ref[:, h, :].astype(BF)
        v = v_ref[:, h, :].astype(BF)
        kh_ref[h] = k
        vh_ref[h] = v
        s_ref[h] = mm(k, v, TN).astype(BF)


def weight_of(lam_ref, h, rows):
    local_bits = (rows // CH).bit_length() - 1
    s = lax.broadcasted_iota(jnp.int32, (rows, rows), 0)
    t = lax.broadcasted_iota(jnp.int32, (rows, rows), 1)
    differ = (s // CH) ^ (t // CH)
    weight = jnp.broadcast_to(lam_ref[0, h : h + 1, :], (rows, rows))
    for digit in range(local_bits):
        weight = jnp.where(differ >= 1 << digit, lam_ref[1 + digit, h : h + 1, :], weight)
    return jnp.where(s <= t, weight, 0.0)


def local_kernel(q_ref, kh_ref, vh_ref, lam_ref, lamu_ref, pt_ref, att_ref, qh_ref, qw_ref):
    rows, heads_dev, _ = q_ref.shape
    for h in range(heads_dev):
        q32 = q_ref[:, h, :]
        q = q32.astype(BF)
        qh_ref[h] = q
        for b in range(qw_ref.shape[0]):
            column = b * heads_dev + h
            qw_ref[b, h] = (q32 * lamu_ref[:, column : column + 1]).astype(BF)
        pt = (mm(kh_ref[h], q, NT) * weight_of(lam_ref, h, rows)).astype(BF)
        pt_ref[h] = pt
        att_ref[h] = mm(pt, vh_ref[h], TN)


def attended_kernel(bits, att_ref, qw_ref, after_ref, *refs):
    del after_ref
    states, out_ref = refs[:bits], refs[bits]
    heads_dev, _, head_dim = att_ref.shape
    for h in range(heads_dev):
        total = att_ref[h]
        for b in range(bits):
            total = total + mm(qw_ref[b, h], states[b][h], NN)
        out_ref[:, h * head_dim : (h + 1) * head_dim] = total.astype(BF)


def cotangent_kernel(bits, full_ref, w_ref, qw_ref, after_ref, gt_ref, *sums):
    del after_ref
    groups, _, deep = full_ref.shape
    total = None
    for j in range(groups):
        part = mm(w_ref[:, j * deep : (j + 1) * deep], full_ref[j], NT)
        total = part if total is None else total + part
    gt = total.astype(BF)
    gt_ref[...] = gt
    head_dim = qw_ref.shape[3]
    for b in range(bits):
        for h in range(qw_ref.shape[1]):
            sums[b][h] = mm(gt[h * head_dim : (h + 1) * head_dim], qw_ref[b, h], NN).astype(BF)


def local_grad_kernel(
    bits, gt_ref, qh_ref, kh_ref, vh_ref, pt_ref, lam_ref, lamu_ref, after_ref, *refs
):
    del after_ref
    states, (dq_ref, dk_ref, dv_ref) = refs[:bits], refs[bits:]
    heads_dev, rows, head_dim = qh_ref.shape
    for h in range(heads_dev):
        gt = gt_ref[h * head_dim : (h + 1) * head_dim, :]
        g32 = gt.astype(F32)
        dpt = (mm(vh_ref[h], gt, NN) * weight_of(lam_ref, h, rows)).astype(BF)
        dk_ref[h] = mm(dpt, qh_ref[h], NN)
        dv_ref[h] = mm(pt_ref[h], gt, NT)
        dq = mm(dpt, kh_ref[h], TN)
        for b in range(bits):
            gw = (g32 * lamu_ref[b, h : h + 1, :]).astype(BF)
            dq = dq + mm(gw, states[b][h], TT)
        dq_ref[:, h, :] = dq


def later_grad_kernel(late_ref, kh_ref, vh_ref, dkl_ref, dvl_ref, dk_ref, dv_ref):
    for h in range(kh_ref.shape[0]):
        late = late_ref[h]
        dk_ref[:, h, :] = dkl_ref[h] + mm(vh_ref[h], late, NN)
        dv_ref[:, h, :] = dvl_ref[h] + mm(kh_ref[h], late, NT)


def share_kernel(blocks, order_ref, att_ref, w_ref, *outs):
    del order_ref
    step = pl.program_id(0)
    for i in range(blocks):

        @pl.when(step == i)
        def _(i=i):
            outs[i][...] = mm(att_ref[...], w_ref[...], NN).astype(outs[i].dtype)


def ring_owner(place, offset, devices):
    at = jnp.where(place % 2 == 0, place // 2, devices - 1 - place // 2)
    at = (at + offset + devices) % devices
    return jnp.where(at < devices // 2, 2 * at, 2 * (devices - 1 - at) + 1)


def proj_kernel(offsets, devices, first, place_ref, cols_ref, *refs):
    count = len(offsets)
    total = None if first else refs[count][...]
    for i, offset in enumerate(offsets):
        cols = cols_ref[:, ring_owner(place_ref[0], offset, devices)]
        cols = cols.reshape(cols.shape[0] * cols.shape[1], cols.shape[2])
        part = mm(refs[i][...], cols, TN)
        total = part if total is None else total + part
    refs[-1][...] = total


def body(queries, keys, values, level_weights, out_proj, out_grad):
    rows, heads_dev, head_dim = queries.shape
    width = heads_dev * head_dim
    local_bits = (rows // CH).bit_length() - 1
    devices = lax.axis_size("seq")
    seq_bits = devices.bit_length() - 1
    heads = lax.axis_size("head")
    head_bits = heads.bit_length() - 1
    seq_place = lax.axis_index("seq")
    head_place = lax.axis_index("head")
    columns_dev = out_proj.shape[1] // devices

    head_state = like((heads_dev, head_dim, head_dim), BF)
    per_head = like((heads_dev, rows, head_dim), BF)
    per_head_f32 = like((heads_dev, rows, head_dim), F32)
    flops_head = 2 * heads_dev * rows * rows * head_dim
    moved_head = 2 * rows * width

    own_state, kh, vh = pl.pallas_call(
        state_kernel,
        out_shape=(head_state, per_head, per_head),
        in_specs=[VMEM] * 2,
        out_specs=(VMEM,) * 3,
        compiler_params=PARAMS,
        cost_estimate=cost(flops_head, 7 * moved_head),
    )(keys, values)

    grad_full = lax.all_gather(out_grad, "head", axis=0, tiled=False)

    uppers = jnp.stack([(seq_place >> b & 1).astype(F32) for b in range(seq_bits)])
    lamu = level_weights[1 + local_bits :] * uppers[:, None, None]
    lamu_columns = lamu.reshape(-1, rows).T
    lam = level_weights[: 1 + local_bits]

    probs_t, att_local, qh, qw = pl.pallas_call(
        local_kernel,
        out_shape=(
            like((heads_dev, rows, rows), BF),
            per_head_f32,
            per_head,
            like((seq_bits, heads_dev, rows, head_dim), BF),
        ),
        in_specs=[VMEM] * 5,
        out_specs=(VMEM,) * 4,
        compiler_params=PARAMS,
        cost_estimate=cost(2 * flops_head, 12 * moved_head),
    )(queries, kh, vh, lam, lamu_columns)

    partner_states = []
    running = own_state
    for digit in range(seq_bits):
        arrived = across(running, "seq", digit, up_only=digit == seq_bits - 1)
        partner_states.append(arrived)
        if digit == seq_bits - 1:
            break
        running = (running.astype(F32) + arrived.astype(F32)).astype(BF)

    at_once = 2
    gt, *grad_sums = pl.pallas_call(
        functools.partial(cotangent_kernel, seq_bits),
        out_shape=(like((width, rows), BF),) + (head_state,) * seq_bits,
        grid=(heads_dev // at_once,),
        in_specs=[
            VMEM,
            pl.BlockSpec((at_once * head_dim, out_proj.shape[1]), lambda i: (i, 0)),
            pl.BlockSpec((seq_bits, at_once, rows, head_dim), lambda i: (0, i, 0, 0)),
            ANY,
        ],
        out_specs=(pl.BlockSpec((at_once * head_dim, rows), lambda i: (i, 0)),)
        + (pl.BlockSpec((at_once, head_dim, head_dim), lambda i: (i, 0, 0)),) * seq_bits,
        compiler_params=PARAMS,
        cost_estimate=cost(2 * rows * width * out_proj.shape[1], 2 * width * out_proj.shape[1]),
    )(grad_full, out_proj, qw, running)

    pending = None
    for digit in reversed(range(seq_bits)):
        outgoing = grad_sums[digit]
        if pending is not None:
            outgoing = (outgoing.astype(F32) + pending).astype(BF)
        landed = across(outgoing, "seq", digit, down_only=digit == seq_bits - 1).astype(F32)
        pending = landed if pending is None else pending + landed
    later = pending.astype(BF)

    part = rows // heads
    quarter = lax.dynamic_slice_in_dim(grad_full, head_place * part, part, 1)
    quarter = quarter.reshape(heads, part, devices // heads, columns_dev).transpose(0, 2, 1, 3)
    quarter = quarter.reshape(devices, part, columns_dev)
    quarter = lax.all_to_all(quarter, "seq", split_axis=0, concat_axis=0, tiled=True)
    grad_columns = lax.all_gather(quarter, "head", axis=0, tiled=False)

    attended = pl.pallas_call(
        functools.partial(attended_kernel, seq_bits),
        out_shape=like((rows, width), BF),
        in_specs=[VMEM] * 2 + [ANY] + [VMEM] * seq_bits,
        out_specs=VMEM,
        compiler_params=PARAMS,
        cost_estimate=cost(seq_bits * flops_head, 8 * moved_head),
    )(att_local, qw, gt, *partner_states)

    share_order = list(reversed(range(heads)))
    shares = pl.pallas_call(
        functools.partial(share_kernel, heads),
        out_shape=tuple(like((rows, width), BF if i else F32) for i in share_order),
        grid_spec=pltpu.PrefetchScalarGridSpec(
            num_scalar_prefetch=1,
            grid=(heads,),
            in_specs=[VMEM, pl.BlockSpec((width, width), lambda i, o: (0, o[0] ^ (heads - 1 - i)))],
            out_specs=(VMEM,) * heads,
        ),
        compiler_params=PARAMS,
        cost_estimate=cost(2 * rows * width * out_proj.shape[1], 2 * width * out_proj.shape[1]),
    )(head_place.reshape(1).astype(jnp.int32), attended, out_proj)
    mixed = shares[-1]
    for i, block in zip(share_order[:-1], shares[:-1]):
        route = [(place, place ^ i) for place in range(heads)]
        mixed = mixed + lax.ppermute(block, "head", route).astype(F32)
    mixed = mixed.astype(BF)

    query_grad, key_local, value_local = pl.pallas_call(
        functools.partial(local_grad_kernel, seq_bits),
        out_shape=(like((rows, heads_dev, head_dim), F32), per_head_f32, per_head_f32),
        in_specs=[VMEM] * 7 + [ANY] + [VMEM] * seq_bits,
        out_specs=(VMEM,) * 3,
        compiler_params=PARAMS,
        cost_estimate=cost((4 + seq_bits) * flops_head, 14 * moved_head),
    )(gt, qh, kh, vh, probs_t, lam, lamu, shares[0], *partner_states)
    key_grad, value_grad = pl.pallas_call(
        later_grad_kernel,
        out_shape=(like((rows, heads_dev, head_dim), F32),) * 2,
        in_specs=[VMEM] * 5,
        out_specs=(VMEM,) * 2,
        compiler_params=PARAMS,
        cost_estimate=cost(2 * flops_head, 11 * moved_head),
    )(later, kh, vh, key_local, value_local)

    ring = list(range(0, devices, 2)) + list(range(devices - 1, 0, -2))
    forward = [(ring[i], ring[(i + 1) % devices]) for i in range(devices)]
    backward = [(b, a) for a, b in forward]

    def accumulate(total, blocks, offsets):
        operands = blocks if total is None else blocks + [total]
        return pl.pallas_call(
            functools.partial(proj_kernel, offsets, devices, total is None),
            out_shape=like((width, columns_dev), F32),
            in_specs=[SMEM] + [VMEM] * (1 + len(operands)),
            out_specs=VMEM,
            compiler_params=PARAMS,
            cost_estimate=cost(
                2 * len(blocks) * rows * width * columns_dev, 4 * width * columns_dev
            ),
        )(seq_place.reshape(1).astype(jnp.int32), grad_columns, *operands)

    blocks, offsets = [attended], [0]
    ahead = behind = attended
    half = rows // 2
    for step in range(1, devices // 2):
        ahead = lax.ppermute(ahead, "seq", forward)
        behind = lax.ppermute(behind, "seq", backward)
        if step == devices // 2 - 1:
            last = [
                lax.ppermute(ahead[:half], "seq", forward),
                lax.ppermute(behind[half:], "seq", backward),
            ]
        blocks += [ahead, behind]
        offsets += [-step, step]
    total = accumulate(None, blocks, offsets)
    proj_grad = accumulate(total, [jnp.concatenate(last)], [devices // 2])
    return (mixed, query_grad, key_grad, value_grad, proj_grad)


def solution(mesh):
    placed = (
        P("seq", "head", None),
        P("seq", "head", None),
        P("seq", "head", None),
        P(None, "head", "seq"),
        P("head", None),
        P("seq", "head"),
    )
    return jax.shard_map(
        body,
        mesh=mesh,
        in_specs=placed,
        out_specs=(
            P("seq", "head"),
            P("seq", "head", None),
            P("seq", "head", None),
            P("seq", "head", None),
            P("head", "seq"),
        ),
        check_vma=False,
    )
```

```python
import functools

import jax
import jax.numpy as jnp
from jax import lax
from jax.experimental import pallas as pl
from jax.experimental.pallas import tpu as pltpu
from jax.sharding import PartitionSpec as P

CH = 64
BF = jnp.bfloat16
F32 = jnp.float32
NN = (((1,), (0,)), ((), ()))
NT = (((1,), (1,)), ((), ()))
TN = (((0,), (0,)), ((), ()))
TT = (((0,), (1,)), ((), ()))
VMEM = pl.BlockSpec(memory_space=pltpu.VMEM)
ANY = pl.BlockSpec(memory_space=pl.ANY)
SMEM = pl.BlockSpec(memory_space=pltpu.SMEM)
PARAMS = pltpu.CompilerParams(vmem_limit_bytes=14 * 2**20)


def mm(a, b, dims):
    return lax.dot_general(a, b, dims, preferred_element_type=F32)


def cost(flops, moved):
    return pl.CostEstimate(flops=flops, bytes_accessed=moved, transcendentals=0)


def like(shape, dtype):
    return jax.ShapeDtypeStruct(shape, dtype)


def across(block, axis, stride, up_only=False, down_only=False):
    count = lax.axis_size(axis)
    route = []
    for low in range(count):
        high = low | 1 << stride
        if high != low and high < count:
            if not down_only:
                route.append((low, high))
            if not up_only:
                route.append((high, low))
    return lax.ppermute(block, axis, route)


def hbm(array):
    return pltpu.with_memory_space_constraint(array, pltpu.HBM)


def state_kernel(k_hbm, v_hbm, s_ref, kh_ref, vh_ref, k_ref, v_ref, sems):
    copies = [
        pltpu.make_async_copy(k_hbm, k_ref, sems.at[0]),
        pltpu.make_async_copy(v_hbm, v_ref, sems.at[1]),
    ]
    for copy in copies:
        copy.start()
    for copy in copies:
        copy.wait()
    for h in range(k_ref.shape[1]):
        k = k_ref[:, h, :].astype(BF)
        v = v_ref[:, h, :].astype(BF)
        kh_ref[h] = k
        vh_ref[h] = v
        s_ref[h] = mm(k, v, TN).astype(BF)


def weight_of(lam_ref, h, rows):
    local_bits = (rows // CH).bit_length() - 1
    s = lax.broadcasted_iota(jnp.int32, (rows, rows), 0)
    t = lax.broadcasted_iota(jnp.int32, (rows, rows), 1)
    differ = (s // CH) ^ (t // CH)
    weight = jnp.broadcast_to(lam_ref[0, h : h + 1, :], (rows, rows))
    for digit in range(local_bits):
        weight = jnp.where(differ >= 1 << digit, lam_ref[1 + digit, h : h + 1, :], weight)
    return jnp.where(s <= t, weight, 0.0)


def local_kernel(
    q_ref, kh_ref, vh_ref, lam_ref, lamu_ref, w_hbm, pt_ref, att_ref, qh_ref, qw_ref, w_ref, sems
):
    rows, heads_dev, _ = q_ref.shape
    pieces = sems.shape[0]
    share = w_hbm.shape[0] // pieces
    copies = [
        pltpu.make_async_copy(
            w_hbm.at[pl.ds(i * share, share)], w_ref.at[pl.ds(i * share, share)], sems.at[i]
        )
        for i in range(pieces)
    ]
    for copy in copies:
        copy.start()
    for h in range(heads_dev):
        q32 = q_ref[:, h, :]
        q = q32.astype(BF)
        qh_ref[h] = q
        for b in range(qw_ref.shape[0]):
            column = b * heads_dev + h
            qw_ref[b, h] = (q32 * lamu_ref[:, column : column + 1]).astype(BF)
        pt = (mm(kh_ref[h], q, NT) * weight_of(lam_ref, h, rows)).astype(BF)
        pt_ref[h] = pt
        att_ref[h] = mm(pt, vh_ref[h], TN)
    for copy in copies:
        copy.wait()


def attended_kernel(bits, att_ref, qw_ref, after_ref, *refs):
    del after_ref
    states, out_ref = refs[:bits], refs[bits]
    heads_dev, _, head_dim = att_ref.shape
    for h in range(heads_dev):
        total = att_ref[h]
        for b in range(bits):
            total = total + mm(qw_ref[b, h], states[b][h], NN)
        out_ref[:, h * head_dim : (h + 1) * head_dim] = total.astype(BF)


def cotangent_kernel(blocks, bits, head_ref, *refs):
    parts, (w_ref, qw_ref, _, gt_ref), sums = (
        refs[:blocks],
        refs[blocks : blocks + 4],
        refs[blocks + 4 :],
    )
    deep = parts[0].shape[1]
    _, heads_dev, _, head_dim = qw_ref.shape
    step = 2 * head_dim
    for at in range(0, heads_dev * head_dim, step):
        total = None
        for i in range(blocks):
            column = pl.multiple_of((head_ref[0] ^ i) * deep, deep)
            part = mm(w_ref[at : at + step, pl.ds(column, deep)], parts[i][...], NT)
            total = part if total is None else total + part
        gt = total.astype(BF)
        gt_ref[at : at + step] = gt
        for h in range(2):
            for b in range(bits):
                head = at // head_dim + h
                own = gt[h * head_dim : (h + 1) * head_dim]
                sums[b][head] = mm(own, qw_ref[b, head], NN).astype(BF)


def meet_kernel(top, place_ref, grad_ref, running_ref, arrived_ref, out_ref):
    upper = (place_ref[0] >> top & 1) == 1
    running = running_ref[...].astype(F32)
    if arrived_ref is not None:
        running = running + arrived_ref[...].astype(F32)
    out_ref[...] = jnp.where(upper, grad_ref[...], running.astype(BF))


def landed_sum(top, place_ref, landed):
    upper = (place_ref[0] >> top & 1) == 1
    total = jnp.where(upper, 0.0, landed[0].astype(F32))
    for block in landed[1:]:
        total = total + block.astype(F32)
    return total


def pending_kernel(top, place_ref, own_ref, after_ref, *refs):
    del after_ref
    landed, out_ref = [ref[...] for ref in refs[:-1]], refs[-1]
    out_ref[...] = (own_ref[...].astype(F32) + landed_sum(top, place_ref, landed)).astype(BF)


def quarter_kernel(blocks, head_ref, after_ref, *refs):
    del after_ref
    parts, out_ref = refs[:blocks], refs[blocks]
    _, part, columns = out_ref.shape
    per = parts[0].shape[1] // columns
    rows = pl.ds(pl.multiple_of(head_ref[0] * part, part), part)
    for i in range(blocks):
        for c in range(per):
            target = (head_ref[0] ^ i) * per + c
            out_ref[target] = parts[i][rows, c * columns : (c + 1) * columns]


def local_grad_kernel(
    bits, gt_ref, qh_ref, kh_ref, vh_ref, pt_ref, lam_ref, lamu_ref, after_ref, *refs
):
    del after_ref
    states, (dq_ref, dk_ref, dv_ref) = refs[:bits], refs[bits:]
    heads_dev, rows, head_dim = qh_ref.shape
    for h in range(heads_dev):
        gt = gt_ref[h * head_dim : (h + 1) * head_dim, :]
        g32 = gt.astype(F32)
        dpt = (mm(vh_ref[h], gt, NN) * weight_of(lam_ref, h, rows)).astype(BF)
        dk_ref[h] = mm(dpt, qh_ref[h], NN)
        dv_ref[h] = mm(pt_ref[h], gt, NT)
        dq = mm(dpt, kh_ref[h], TN)
        for b in range(bits):
            gw = (g32 * lamu_ref[b, h : h + 1, :]).astype(BF)
            dq = dq + mm(gw, states[b][h], TT)
        dq_ref[:, h, :] = dq


def later_grad_kernel(top, place_ref, kh_ref, vh_ref, dkl_ref, dvl_ref, after_ref, *refs):
    del after_ref
    landed, (dk_ref, dv_ref) = refs[:-2], refs[-2:]
    for h in range(kh_ref.shape[0]):
        late = landed_sum(top, place_ref, [ref[h] for ref in landed]).astype(BF)
        dk_ref[:, h, :] = dkl_ref[h] + mm(vh_ref[h], late, NN)
        dv_ref[:, h, :] = dvl_ref[h] + mm(kh_ref[h], late, NT)


def share_kernel(blocks, head_ref, att_ref, w_ref, *outs):
    width = outs[0].shape[1]
    for i in range(blocks):
        column = pl.multiple_of((head_ref[0] ^ (blocks - 1 - i)) * width, width)
        outs[i][...] = mm(att_ref[...], w_ref[:, pl.ds(column, width)], NN).astype(outs[i].dtype)


def ring_owner(place, offset, devices):
    at = jnp.where(place % 2 == 0, place // 2, devices - 1 - place // 2)
    at = (at + offset + devices) % devices
    return jnp.where(at < devices // 2, 2 * at, 2 * (devices - 1 - at) + 1)


def proj_kernel(offsets, devices, first, place_ref, cols_ref, *refs):
    total = None if first else refs[-2][...]
    part, at = cols_ref.shape[2], 0
    for i, (offset, low, high) in enumerate(offsets):
        owner = ring_owner(place_ref[0], offset, devices)
        cols = cols_ref[low // part : high // part, owner]
        cols = cols.reshape(high - low, cols.shape[2])
        product = mm(refs[i][...], cols, TN)
        total = product if total is None else total + product
    refs[-1][...] = total


def body(queries, keys, values, level_weights, out_proj, out_grad):
    rows, heads_dev, head_dim = queries.shape
    width = heads_dev * head_dim
    local_bits = (rows // CH).bit_length() - 1
    devices = lax.axis_size("seq")
    seq_bits = devices.bit_length() - 1
    heads = lax.axis_size("head")
    head_bits = heads.bit_length() - 1
    seq_place = lax.axis_index("seq")
    head_place = lax.axis_index("head")
    columns_dev = out_proj.shape[1] // devices

    head_state = like((heads_dev, head_dim, head_dim), BF)
    pinned_state = pltpu.VMEM((heads_dev, head_dim, head_dim), BF)
    per_head = pltpu.VMEM((heads_dev, rows, head_dim), BF)
    per_head_f32 = pltpu.VMEM((heads_dev, rows, head_dim), F32)
    flops_head = 2 * heads_dev * rows * rows * head_dim
    moved_head = 2 * rows * width
    top = seq_bits - 1
    place = seq_place.reshape(1).astype(jnp.int32)
    group = head_place.reshape(1).astype(jnp.int32)

    grad_blocks = [out_grad]
    for i in range(1, heads):
        route = [(at, at ^ i) for at in range(heads)]
        grad_blocks.append(lax.ppermute(out_grad, "head", route))

    own_state, kh, vh = pl.pallas_call(
        state_kernel,
        out_shape=(head_state, per_head, per_head),
        in_specs=[ANY] * 2,
        out_specs=(VMEM,) * 3,
        scratch_shapes=[
            pltpu.VMEM(keys.shape, F32),
            pltpu.VMEM(keys.shape, F32),
            pltpu.SemaphoreType.DMA((2,)),
        ],
        compiler_params=PARAMS,
        cost_estimate=cost(flops_head, 7 * moved_head),
    )(hbm(keys), hbm(values))

    uppers = jnp.stack([(seq_place >> b & 1).astype(F32) for b in range(seq_bits)])
    lamu = level_weights[1 + local_bits :] * uppers[:, None, None]
    lamu_columns = lamu.reshape(-1, rows).T
    lam = level_weights[: 1 + local_bits]

    probs_t, att_local, qh, qw, w = pl.pallas_call(
        local_kernel,
        out_shape=(
            pltpu.VMEM((heads_dev, rows, rows), BF),
            per_head_f32,
            per_head,
            pltpu.VMEM((seq_bits, heads_dev, rows, head_dim), BF),
            pltpu.VMEM(out_proj.shape, BF),
        ),
        in_specs=[VMEM] * 5 + [ANY],
        out_specs=(VMEM,) * 5,
        scratch_shapes=[pltpu.SemaphoreType.DMA((8,))],
        compiler_params=PARAMS,
        cost_estimate=cost(2 * flops_head, 12 * moved_head),
    )(queries, kh, vh, lam, lamu_columns, hbm(out_proj))

    partner_states = []
    running, arrived = own_state, None
    for digit in range(top):
        if arrived is not None:
            running = (running.astype(F32) + arrived.astype(F32)).astype(BF)
        arrived = across(running, "seq", digit)
        partner_states.append(arrived)

    gt, *grad_sums = pl.pallas_call(
        functools.partial(cotangent_kernel, heads, seq_bits),
        out_shape=(pltpu.VMEM((width, rows), BF),) + (pinned_state,) * seq_bits,
        in_specs=[SMEM] + [VMEM] * (heads + 2) + [ANY],
        out_specs=(VMEM,) * (1 + seq_bits),
        compiler_params=PARAMS,
        cost_estimate=cost(2 * rows * width * out_proj.shape[1], 2 * width * out_proj.shape[1]),
    )(group, *grad_blocks, w, qw, running)

    meeting = pl.pallas_call(
        functools.partial(meet_kernel, top)
        if arrived is not None
        else lambda place_ref, grad_ref, running_ref, out_ref: meet_kernel(
            top, place_ref, grad_ref, running_ref, None, out_ref
        ),
        out_shape=head_state,
        in_specs=[SMEM] + [VMEM] * (2 if arrived is None else 3),
        out_specs=VMEM,
        compiler_params=PARAMS,
        cost_estimate=cost(0, 4 * moved_head),
    )(place, grad_sums[top], running, *([] if arrived is None else [arrived]))
    landed = [across(meeting, "seq", top)]
    partner_states.append(landed[0])

    part = rows // heads
    quarter = pl.pallas_call(
        functools.partial(quarter_kernel, heads),
        out_shape=like((devices, part, columns_dev), BF),
        in_specs=[SMEM, ANY] + [VMEM] * heads,
        out_specs=VMEM,
        compiler_params=PARAMS,
        cost_estimate=cost(0, 2 * moved_head),
    )(group, meeting, *grad_blocks)
    quarter = lax.all_to_all(quarter, "seq", split_axis=0, concat_axis=0, tiled=True)
    grad_columns = lax.all_gather(quarter, "head", axis=0, tiled=False)

    attended = pl.pallas_call(
        functools.partial(attended_kernel, seq_bits),
        out_shape=like((rows, width), BF),
        in_specs=[VMEM] * 2 + [ANY] + [VMEM] * seq_bits,
        out_specs=VMEM,
        compiler_params=PARAMS,
        cost_estimate=cost(seq_bits * flops_head, 8 * moved_head),
    )(att_local, qw, gt, *partner_states)

    for digit in reversed(range(top)):
        outgoing = pl.pallas_call(
            functools.partial(pending_kernel, top),
            out_shape=head_state,
            in_specs=[SMEM, VMEM, ANY] + [VMEM] * len(landed),
            out_specs=VMEM,
            compiler_params=PARAMS,
            cost_estimate=cost(0, 4 * moved_head),
        )(place, grad_sums[digit], attended, *landed)
        landed.append(across(outgoing, "seq", digit))

    share_order = list(reversed(range(heads)))
    shares = pl.pallas_call(
        functools.partial(share_kernel, heads),
        out_shape=tuple(like((rows, width), BF if i else F32) for i in share_order),
        in_specs=[SMEM, VMEM, VMEM],
        out_specs=(VMEM,) * heads,
        compiler_params=PARAMS,
        cost_estimate=cost(2 * rows * width * out_proj.shape[1], 2 * width * out_proj.shape[1]),
    )(group, attended, w)
    mixed = shares[-1]
    for i, block in zip(share_order[:-1], shares[:-1]):
        route = [(place, place ^ i) for place in range(heads)]
        mixed = mixed + lax.ppermute(block, "head", route).astype(F32)
    mixed = mixed.astype(BF)

    query_grad, key_local, value_local = pl.pallas_call(
        functools.partial(local_grad_kernel, seq_bits),
        out_shape=(like((rows, heads_dev, head_dim), F32), per_head_f32, per_head_f32),
        in_specs=[VMEM] * 7 + [ANY] + [VMEM] * seq_bits,
        out_specs=(VMEM,) * 3,
        compiler_params=PARAMS,
        cost_estimate=cost((4 + seq_bits) * flops_head, 14 * moved_head),
    )(gt, qh, kh, vh, probs_t, lam, lamu, shares[0], *partner_states)

    ring = list(range(0, devices, 2)) + list(range(devices - 1, 0, -2))
    forward = [(ring[i], ring[(i + 1) % devices]) for i in range(devices)]
    backward = [(b, a) for a, b in forward]

    def accumulate(total, blocks, offsets):
        operands = blocks if total is None else blocks + [total]
        return pl.pallas_call(
            functools.partial(proj_kernel, offsets, devices, total is None),
            out_shape=like((width, columns_dev), F32),
            in_specs=[SMEM] + [VMEM] * (1 + len(operands)),
            out_specs=VMEM,
            compiler_params=PARAMS,
            cost_estimate=cost(
                2 * len(blocks) * rows * width * columns_dev, 4 * width * columns_dev
            ),
        )(place, grad_columns, *operands)

    blocks, offsets = [attended], [(0, 0, rows)]
    ahead = behind = attended
    half, steps, total = rows // 2, devices // 2, None
    for step in range(1, steps):
        ahead = lax.ppermute(ahead, "seq", forward)
        behind = lax.ppermute(behind, "seq", backward)
        blocks += [ahead, behind]
        offsets += [(-step, 0, rows), (step, 0, rows)]
        if step == steps - 2:
            total = accumulate(None, blocks, offsets)
            blocks, offsets = [], []
    if blocks:
        total = accumulate(total, blocks, offsets)
    last = [
        lax.ppermute(ahead[:half], "seq", forward),
        lax.ppermute(behind[half:], "seq", backward),
    ]
    proj_grad = accumulate(total, last, [(steps, 0, half), (steps, half, rows)])

    key_grad, value_grad = pl.pallas_call(
        functools.partial(later_grad_kernel, top),
        out_shape=(like((rows, heads_dev, head_dim), F32),) * 2,
        in_specs=[SMEM] + [VMEM] * 4 + [ANY] + [VMEM] * seq_bits,
        out_specs=(VMEM,) * 2,
        compiler_params=PARAMS,
        cost_estimate=cost(2 * flops_head, 11 * moved_head),
    )(place, kh, vh, key_local, value_local, total, *landed)
    return (mixed, query_grad, key_grad, value_grad, proj_grad)


def solution(mesh):
    placed = (
        P("seq", "head", None),
        P("seq", "head", None),
        P("seq", "head", None),
        P(None, "head", "seq"),
        P("head", None),
        P("seq", "head"),
    )
    return jax.shard_map(
        body,
        mesh=mesh,
        in_specs=placed,
        out_specs=(
            P("seq", "head"),
            P("seq", "head", None),
            P("seq", "head", None),
            P("seq", "head", None),
            P("head", "seq"),
        ),
        check_vma=False,
    )
```

```python
import functools

import jax
import jax.numpy as jnp
from jax import lax
from jax.experimental import pallas as pl
from jax.experimental.pallas import tpu as pltpu
from jax.sharding import PartitionSpec as P

CH = 64
BF = jnp.bfloat16
F32 = jnp.float32
NN = (((1,), (0,)), ((), ()))
NT = (((1,), (1,)), ((), ()))
TN = (((0,), (0,)), ((), ()))
TT = (((0,), (1,)), ((), ()))
VMEM = pl.BlockSpec(memory_space=pltpu.VMEM)
ANY = pl.BlockSpec(memory_space=pl.ANY)
SMEM = pl.BlockSpec(memory_space=pltpu.SMEM)
PARAMS = pltpu.CompilerParams(vmem_limit_bytes=14 * 2**20)


def mm(a, b, dims):
    return lax.dot_general(a, b, dims, preferred_element_type=F32)


def cost(flops, moved):
    return pl.CostEstimate(flops=flops, bytes_accessed=moved, transcendentals=0)


def like(shape, dtype):
    return jax.ShapeDtypeStruct(shape, dtype)


def across(block, axis, stride, up_only=False, down_only=False):
    count = lax.axis_size(axis)
    route = []
    for low in range(count):
        high = low | 1 << stride
        if high != low and high < count:
            if not down_only:
                route.append((low, high))
            if not up_only:
                route.append((high, low))
    return lax.ppermute(block, axis, route)


def hbm(array):
    return pltpu.with_memory_space_constraint(array, pltpu.HBM)


def state_kernel(k_hbm, v_hbm, s_ref, kh_ref, vh_ref, k_ref, v_ref, sems):
    copies = [
        pltpu.make_async_copy(k_hbm, k_ref, sems.at[0]),
        pltpu.make_async_copy(v_hbm, v_ref, sems.at[1]),
    ]
    for copy in copies:
        copy.start()
    for copy in copies:
        copy.wait()
    for h in range(k_ref.shape[1]):
        k = k_ref[:, h, :].astype(BF)
        v = v_ref[:, h, :].astype(BF)
        kh_ref[h] = k
        vh_ref[h] = v
        s_ref[h] = mm(k, v, TN).astype(BF)


def weight_of(lam_ref, h, rows):
    local_bits = (rows // CH).bit_length() - 1
    s = lax.broadcasted_iota(jnp.int32, (rows, rows), 0)
    t = lax.broadcasted_iota(jnp.int32, (rows, rows), 1)
    differ = (s // CH) ^ (t // CH)
    weight = jnp.broadcast_to(lam_ref[0, h : h + 1, :], (rows, rows))
    for digit in range(local_bits):
        weight = jnp.where(differ >= 1 << digit, lam_ref[1 + digit, h : h + 1, :], weight)
    return jnp.where(s <= t, weight, 0.0)


def upper_weight(place_ref, lam_ref, b, h, rows):
    local_bits = (rows // CH).bit_length() - 1
    upper = (place_ref[0] >> b & 1).astype(F32)
    return lam_ref[1 + local_bits + b, h : h + 1, :] * upper


def local_kernel(place_ref, q_hbm, kh_ref, vh_ref, lam_hbm, *refs):
    pt_ref, att_ref, qh_ref, qw_ref, lam_ref, q_ref, lam_rows, sems = refs
    copies = [
        pltpu.make_async_copy(q_hbm, q_ref, sems.at[0]),
        pltpu.make_async_copy(lam_hbm, lam_ref, sems.at[1]),
    ]
    for copy in copies:
        copy.start()
    for copy in copies:
        copy.wait()
    rows, heads_dev, _ = q_ref.shape
    bits = qw_ref.shape[0]
    lam_rows[...] = jnp.zeros_like(lam_rows)
    for b in range(bits):
        for h in range(heads_dev):
            at = b * heads_dev + h
            lam_rows[at : at + 1, :] = upper_weight(place_ref, lam_ref, b, h, rows)
    lam_columns = lam_rows[...].T
    for h in range(heads_dev):
        q32 = q_ref[:, h, :]
        q = q32.astype(BF)
        qh_ref[h] = q
        for b in range(bits):
            at = b * heads_dev + h
            qw_ref[b, h] = (q32 * lam_columns[:, at : at + 1]).astype(BF)
        pt = (mm(kh_ref[h], q, NT) * weight_of(lam_ref, h, rows)).astype(BF)
        pt_ref[h] = pt
        att_ref[h] = mm(pt, vh_ref[h], TN)


def attended_kernel(bits, att_ref, qw_ref, after_ref, *refs):
    del after_ref
    states, out_ref = refs[:bits], refs[bits]
    heads_dev, _, head_dim = att_ref.shape
    for h in range(heads_dev):
        total = att_ref[h]
        for b in range(bits):
            total = total + mm(qw_ref[b, h], states[b][h], NN)
        out_ref[:, h * head_dim : (h + 1) * head_dim] = total.astype(BF)


def cotangent_kernel(blocks, bits, head_ref, *refs):
    del head_ref
    parts, (w_ref, qw_ref, _, gt_ref), sums, acc = (
        refs[:blocks],
        refs[blocks : blocks + 4],
        refs[blocks + 4 : -1],
        refs[-1],
    )
    _, heads_dev, _, head_dim = qw_ref.shape
    step = pl.program_id(0)
    for i in range(blocks):

        @pl.when(step == i)
        def _(i=i):
            product = mm(w_ref[...], parts[i][...], NT)
            acc[...] = product if i == 0 else acc[...] + product

    @pl.when(step == blocks - 1)
    def _():
        for h in range(heads_dev):
            gt = acc[h * head_dim : (h + 1) * head_dim, :].astype(BF)
            gt_ref[h * head_dim : (h + 1) * head_dim, :] = gt
            for b in range(bits):
                sums[b][h] = mm(gt, qw_ref[b, h], NN).astype(BF)


def meet_kernel(top, place_ref, after_ref, grad_ref, running_ref, arrived_ref, out_ref):
    del after_ref
    upper = (place_ref[0] >> top & 1) == 1
    running = running_ref[...].astype(F32)
    if arrived_ref is not None:
        running = running + arrived_ref[...].astype(F32)
    out_ref[...] = jnp.where(upper, grad_ref[...], running.astype(BF))


def landed_sum(top, place_ref, landed):
    upper = (place_ref[0] >> top & 1) == 1
    total = jnp.where(upper, 0.0, landed[0].astype(F32))
    for block in landed[1:]:
        total = total + block.astype(F32)
    return total


def pending_kernel(top, place_ref, own_ref, after_ref, *refs):
    del after_ref
    landed, out_ref = [ref[...] for ref in refs[:-1]], refs[-1]
    out_ref[...] = (own_ref[...].astype(F32) + landed_sum(top, place_ref, landed)).astype(BF)


def chunk_kernel(place_ref, block_ref, *outs):
    columns = outs[0].shape[1]
    low = place_ref[0] % len(outs)
    for r, out in enumerate(outs):
        out[...] = block_ref[:, pl.ds(pl.multiple_of((low ^ r) * columns, columns), columns)]


def columns_kernel(blocks, place_ref, head_ref, *refs):
    parts, out_ref = refs[:blocks], refs[blocks]
    per = parts[0].shape[0]
    low = place_ref[0] % per
    for i in range(blocks):
        for r in range(per):
            out_ref[(head_ref[0] ^ i) * per + (low ^ r)] = parts[i][r]


def local_grad_kernel(
    bits, place_ref, gt_ref, qh_ref, kh_ref, vh_ref, pt_ref, lam_ref, after_ref, *refs
):
    del after_ref
    states, (dq_ref, dk_ref, dv_ref) = refs[:bits], refs[bits:]
    heads_dev, rows, head_dim = qh_ref.shape
    for h in range(heads_dev):
        gt = gt_ref[h * head_dim : (h + 1) * head_dim, :]
        g32 = gt.astype(F32)
        dpt = (mm(vh_ref[h], gt, NN) * weight_of(lam_ref, h, rows)).astype(BF)
        dk_ref[h] = mm(dpt, qh_ref[h], NN)
        dv_ref[h] = mm(pt_ref[h], gt, NT)
        dq = mm(dpt, kh_ref[h], TN)
        for b in range(bits):
            gw = (g32 * upper_weight(place_ref, lam_ref, b, h, rows)).astype(BF)
            dq = dq + mm(gw, states[b][h], TT)
        dq_ref[:, h, :] = dq


def later_grad_kernel(top, place_ref, kh_ref, vh_ref, dkl_ref, dvl_ref, after_ref, *refs):
    del after_ref
    landed, (dk_ref, dv_ref) = refs[:-2], refs[-2:]
    for h in range(kh_ref.shape[0]):
        late = landed_sum(top, place_ref, [ref[h] for ref in landed]).astype(BF)
        dk_ref[:, h, :] = dkl_ref[h] + mm(vh_ref[h], late, NN)
        dv_ref[:, h, :] = dvl_ref[h] + mm(kh_ref[h], late, NT)


def share_kernel(blocks, head_ref, att_ref, w_ref, send_ref, kept_ref):
    del head_ref
    step = pl.program_id(0)
    half = blocks // 2
    for i in range(blocks):

        @pl.when(step == i)
        def _(i=i):
            out = send_ref if i < half else kept_ref
            out[i % half] = mm(att_ref[...], w_ref[...], NN).astype(out.dtype)


def ring_owner(place, offset, devices):
    at = jnp.where(place % 2 == 0, place // 2, devices - 1 - place // 2)
    at = (at + offset + devices) % devices
    return jnp.where(at < devices // 2, 2 * at, 2 * (devices - 1 - at) + 1)


def proj_kernel(offsets, devices, first, place_ref, cols_ref, *refs):
    total = None if first else refs[len(offsets)][...]
    for i, (offset, low, high) in enumerate(offsets):
        owner = ring_owner(place_ref[0], offset, devices)
        product = mm(refs[i][...], cols_ref[owner, low:high, :], TN)
        total = product if total is None else total + product
    refs[-1][...] = total


def last_kernel(
    offset, devices, place_ref, cols_ref, low_ref, high_ref, total_ref, after_ref, out_ref, held
):
    del after_ref
    half = low_ref.shape[0]
    held[:half] = low_ref[...]
    held[half:] = high_ref[...]
    owner = ring_owner(place_ref[0], offset, devices)
    out_ref[...] = total_ref[...] + mm(held[...], cols_ref[owner], TN)


def body(queries, keys, values, level_weights, out_proj, out_grad):
    rows, heads_dev, head_dim = queries.shape
    width = heads_dev * head_dim
    devices = lax.axis_size("seq")
    seq_bits = devices.bit_length() - 1
    heads = lax.axis_size("head")
    head_bits = heads.bit_length() - 1
    seq_place = lax.axis_index("seq")
    head_place = lax.axis_index("head")
    columns_dev = out_proj.shape[1] // devices

    head_state = like((heads_dev, head_dim, head_dim), BF)
    pinned_state = pltpu.VMEM((heads_dev, head_dim, head_dim), BF)
    per_head = pltpu.VMEM((heads_dev, rows, head_dim), BF)
    per_head_f32 = pltpu.VMEM((heads_dev, rows, head_dim), F32)
    flops_head = 2 * heads_dev * rows * rows * head_dim
    moved_head = 2 * rows * width
    top = seq_bits - 1
    place = seq_place.reshape(1).astype(jnp.int32)
    group = head_place.reshape(1).astype(jnp.int32)

    own_state, kh, vh = pl.pallas_call(
        state_kernel,
        out_shape=(head_state, per_head, per_head),
        in_specs=[ANY] * 2,
        out_specs=(VMEM,) * 3,
        scratch_shapes=[
            pltpu.VMEM(keys.shape, F32),
            pltpu.VMEM(keys.shape, F32),
            pltpu.SemaphoreType.DMA((2,)),
        ],
        compiler_params=PARAMS,
        cost_estimate=cost(flops_head, 7 * moved_head),
    )(hbm(keys), hbm(values))

    def to_group(block, i):
        return lax.ppermute(block, "head", [(at, at ^ i) for at in range(heads)])

    def every_group(block):
        blocks = {0: block}
        for digit in reversed(range(head_bits)):
            for i in sorted(blocks):
                blocks[i ^ 1 << digit] = to_group(blocks[i], 1 << digit)
        return [blocks[i] for i in range(heads)]

    grad_blocks = every_group(out_grad)

    per = devices // heads
    route = [
        ((high * per + low) * heads + group_at, (group_at * per + low) * heads + high)
        for high in range(heads)
        for low in range(per)
        for group_at in range(heads)
    ]
    turned = lax.ppermute(out_grad, ("seq", "head"), route)
    chunks = pl.pallas_call(
        chunk_kernel,
        out_shape=(like((rows, columns_dev), BF),) * per,
        in_specs=[SMEM, VMEM],
        out_specs=(VMEM,) * per,
        compiler_params=PARAMS,
        cost_estimate=cost(0, 2 * moved_head),
    )(place, turned)
    chunks = [chunks[0]] + [
        lax.ppermute(chunks[r], "seq", [(at, at ^ r) for at in range(devices)])
        for r in range(1, per)
    ]
    grad_columns = pl.pallas_call(
        functools.partial(columns_kernel, heads),
        out_shape=pltpu.VMEM((devices, rows, columns_dev), BF),
        in_specs=[SMEM] * 2 + [VMEM] * heads,
        out_specs=VMEM,
        compiler_params=PARAMS,
        cost_estimate=cost(0, 8 * moved_head),
    )(place, group, *every_group(jnp.stack(chunks)))

    probs_t, att_local, qh, qw, lam = pl.pallas_call(
        local_kernel,
        out_shape=(
            pltpu.VMEM((heads_dev, rows, rows), BF),
            per_head_f32,
            per_head,
            pltpu.VMEM((seq_bits, heads_dev, rows, head_dim), BF),
            pltpu.VMEM(level_weights.shape, F32),
        ),
        in_specs=[SMEM, ANY, VMEM, VMEM, ANY],
        out_specs=(VMEM,) * 5,
        scratch_shapes=[
            pltpu.VMEM(queries.shape, F32),
            pltpu.VMEM((rows, rows), F32),
            pltpu.SemaphoreType.DMA((2,)),
        ],
        compiler_params=PARAMS,
        cost_estimate=cost(2 * flops_head, 12 * moved_head),
    )(place, hbm(queries), kh, vh, hbm(level_weights))

    partner_states = []
    running, arrived = own_state, None
    for digit in range(top):
        if arrived is not None:
            running = (running.astype(F32) + arrived.astype(F32)).astype(BF)
        arrived = across(running, "seq", digit)
        partner_states.append(arrived)

    gt, *grad_sums = pl.pallas_call(
        functools.partial(cotangent_kernel, heads, seq_bits),
        out_shape=(pltpu.VMEM((width, rows), BF),) + (pinned_state,) * seq_bits,
        grid_spec=pltpu.PrefetchScalarGridSpec(
            num_scalar_prefetch=1,
            grid=(heads,),
            in_specs=[VMEM] * heads
            + [pl.BlockSpec((width, width), lambda i, o: (0, o[0] ^ i)), VMEM, ANY],
            out_specs=(VMEM,) * (1 + seq_bits),
            scratch_shapes=[pltpu.VMEM((width, rows), F32)],
        ),
        compiler_params=PARAMS,
        cost_estimate=cost(2 * rows * width * out_proj.shape[1], 2 * width * out_proj.shape[1]),
    )(group, *grad_blocks, hbm(out_proj), qw, running)

    meeting = pl.pallas_call(
        functools.partial(meet_kernel, top)
        if arrived is not None
        else lambda place_ref, after_ref, grad_ref, running_ref, out_ref: meet_kernel(
            top, place_ref, after_ref, grad_ref, running_ref, None, out_ref
        ),
        out_shape=head_state,
        in_specs=[SMEM, ANY] + [VMEM] * (2 if arrived is None else 3),
        out_specs=VMEM,
        compiler_params=PARAMS,
        cost_estimate=cost(0, 4 * moved_head),
    )(place, turned, grad_sums[top], running, *([] if arrived is None else [arrived]))
    landed = [across(meeting, "seq", top)]
    partner_states.append(landed[0])

    attended = pl.pallas_call(
        functools.partial(attended_kernel, seq_bits),
        out_shape=like((rows, width), BF),
        in_specs=[VMEM] * 2 + [ANY] + [VMEM] * seq_bits,
        out_specs=VMEM,
        compiler_params=PARAMS,
        cost_estimate=cost(seq_bits * flops_head, 8 * moved_head),
    )(att_local, qw, gt, *partner_states)

    for digit in reversed(range(top)):
        outgoing = pl.pallas_call(
            functools.partial(pending_kernel, top),
            out_shape=head_state,
            in_specs=[SMEM, VMEM, ANY] + [VMEM] * len(landed),
            out_specs=VMEM,
            compiler_params=PARAMS,
            cost_estimate=cost(0, 4 * moved_head),
        )(place, grad_sums[digit], attended, *landed)
        landed.append(across(outgoing, "seq", digit))

    send, kept = pl.pallas_call(
        functools.partial(share_kernel, heads),
        out_shape=(like((heads // 2, rows, width), BF), like((heads // 2, rows, width), F32)),
        grid_spec=pltpu.PrefetchScalarGridSpec(
            num_scalar_prefetch=1,
            grid=(heads,),
            in_specs=[
                VMEM,
                pl.BlockSpec(
                    (width, width),
                    lambda i, o: (0, o[0] ^ (2 * (i % (heads // 2)) + 1 - i // (heads // 2))),
                ),
            ],
            out_specs=(VMEM,) * 2,
        ),
        compiler_params=PARAMS,
        cost_estimate=cost(2 * rows * width * out_proj.shape[1], 2 * width * out_proj.shape[1]),
    )(group, attended, hbm(out_proj))
    for digit in range(head_bits):
        kept = kept + to_group(send, 1 << digit).astype(F32)
        if digit < head_bits - 1:
            send, kept = kept[1::2].astype(BF), kept[0::2]
    mixed = kept[0].astype(BF)

    query_grad, key_local, value_local = pl.pallas_call(
        functools.partial(local_grad_kernel, seq_bits),
        out_shape=(like((rows, heads_dev, head_dim), F32), per_head_f32, per_head_f32),
        in_specs=[SMEM] + [VMEM] * 6 + [ANY] + [VMEM] * seq_bits,
        out_specs=(VMEM,) * 3,
        compiler_params=PARAMS,
        cost_estimate=cost((4 + seq_bits) * flops_head, 14 * moved_head),
    )(place, gt, qh, kh, vh, probs_t, lam, send, *partner_states)

    ring = list(range(0, devices, 2)) + list(range(devices - 1, 0, -2))
    forward = [(ring[i], ring[(i + 1) % devices]) for i in range(devices)]
    backward = [(b, a) for a, b in forward]

    def accumulate(total, blocks, offsets):
        operands = blocks if total is None else blocks + [total]
        return pl.pallas_call(
            functools.partial(proj_kernel, offsets, devices, total is None),
            out_shape=like((width, columns_dev), F32),
            in_specs=[SMEM] + [VMEM] * (1 + len(operands)),
            out_specs=VMEM,
            compiler_params=PARAMS,
            cost_estimate=cost(
                2 * len(blocks) * rows * width * columns_dev, 4 * width * columns_dev
            ),
        )(place, grad_columns, *operands)

    blocks, offsets = [attended], [(0, 0, rows)]
    ahead = behind = attended
    half, steps, total = rows // 2, devices // 2, None
    for step in range(1, steps):
        ahead = lax.ppermute(ahead, "seq", forward)
        behind = lax.ppermute(behind, "seq", backward)
        blocks += [ahead, behind]
        offsets += [(-step, 0, rows), (step, 0, rows)]
        if step == steps - 2:
            total = accumulate(None, blocks, offsets)
            blocks, offsets = [], []
    if blocks:
        total = accumulate(total, blocks, offsets)
    last = [
        lax.ppermute(ahead[:half], "seq", forward),
        lax.ppermute(behind[half:], "seq", backward),
    ]
    key_grad, value_grad = pl.pallas_call(
        functools.partial(later_grad_kernel, top),
        out_shape=(like((rows, heads_dev, head_dim), F32),) * 2,
        in_specs=[SMEM] + [VMEM] * 4 + [ANY] + [VMEM] * seq_bits,
        out_specs=(VMEM,) * 2,
        compiler_params=PARAMS,
        cost_estimate=cost(2 * flops_head, 11 * moved_head),
    )(place, kh, vh, key_local, value_local, total, *landed)
    quarter_rows = width // 4
    proj_grad = pl.pallas_call(
        functools.partial(last_kernel, steps, devices),
        out_shape=like((width, columns_dev), F32),
        grid=(4,),
        in_specs=[
            SMEM,
            VMEM,
            pl.BlockSpec((half, quarter_rows), lambda i: (0, i)),
            pl.BlockSpec((half, quarter_rows), lambda i: (0, i)),
            pl.BlockSpec((quarter_rows, columns_dev), lambda i: (i, 0)),
            ANY,
        ],
        out_specs=pl.BlockSpec((quarter_rows, columns_dev), lambda i: (i, 0)),
        scratch_shapes=[pltpu.VMEM((rows, quarter_rows), BF)],
        compiler_params=PARAMS,
        cost_estimate=cost(2 * rows * width * columns_dev, 8 * width * columns_dev),
    )(place, grad_columns, *last, total, hbm(key_grad))
    return (mixed, query_grad, key_grad, value_grad, proj_grad)


def solution(mesh):
    placed = (
        P("seq", "head", None),
        P("seq", "head", None),
        P("seq", "head", None),
        P(None, "head", "seq"),
        P("head", None),
        P("seq", "head"),
    )
    return jax.shard_map(
        body,
        mesh=mesh,
        in_specs=placed,
        out_specs=(
            P("seq", "head"),
            P("seq", "head", None),
            P("seq", "head", None),
            P("seq", "head", None),
            P("head", "seq"),
        ),
        check_vma=False,
    )
```

```python
import functools

import jax
import jax.numpy as jnp
from jax import lax
from jax.experimental import pallas as pl
from jax.experimental.pallas import tpu as pltpu
from jax.sharding import PartitionSpec as P

CH = 64
BF = jnp.bfloat16
F32 = jnp.float32
NN = (((1,), (0,)), ((), ()))
NT = (((1,), (1,)), ((), ()))
TN = (((0,), (0,)), ((), ()))
TT = (((0,), (1,)), ((), ()))
VMEM = pl.BlockSpec(memory_space=pltpu.VMEM)
ANY = pl.BlockSpec(memory_space=pl.ANY)
SMEM = pl.BlockSpec(memory_space=pltpu.SMEM)
PARAMS = pltpu.CompilerParams(vmem_limit_bytes=14 * 2**20)


def mm(a, b, dims):
    return lax.dot_general(a, b, dims, preferred_element_type=F32)


def cost(flops, moved):
    return pl.CostEstimate(flops=flops, bytes_accessed=moved, transcendentals=0)


def like(shape, dtype):
    return jax.ShapeDtypeStruct(shape, dtype)


def across(block, axis, stride, up_only=False, down_only=False):
    count = lax.axis_size(axis)
    route = []
    for low in range(count):
        high = low | 1 << stride
        if high != low and high < count:
            if not down_only:
                route.append((low, high))
            if not up_only:
                route.append((high, low))
    return lax.ppermute(block, axis, route)


def hbm(array):
    return pltpu.with_memory_space_constraint(array, pltpu.HBM)


def state_kernel(k_hbm, v_hbm, s_ref, kh_ref, vh_ref, k_ref, v_ref, sems):
    copies = [
        pltpu.make_async_copy(k_hbm, k_ref, sems.at[0]),
        pltpu.make_async_copy(v_hbm, v_ref, sems.at[1]),
    ]
    for copy in copies:
        copy.start()
    for copy in copies:
        copy.wait()
    for h in range(k_ref.shape[1]):
        k = k_ref[:, h, :].astype(BF)
        v = v_ref[:, h, :].astype(BF)
        kh_ref[h] = k
        vh_ref[h] = v
        s_ref[h] = mm(k, v, TN).astype(BF)


def weight_of(lam_ref, h, rows):
    local_bits = (rows // CH).bit_length() - 1
    s = lax.broadcasted_iota(jnp.int32, (rows, rows), 0)
    t = lax.broadcasted_iota(jnp.int32, (rows, rows), 1)
    differ = (s // CH) ^ (t // CH)
    weight = jnp.broadcast_to(lam_ref[0, h : h + 1, :], (rows, rows))
    for digit in range(local_bits):
        weight = jnp.where(differ >= 1 << digit, lam_ref[1 + digit, h : h + 1, :], weight)
    return jnp.where(s <= t, weight, 0.0)


def upper_weight(place_ref, lam_ref, b, h, rows):
    local_bits = (rows // CH).bit_length() - 1
    upper = (place_ref[0] >> b & 1).astype(F32)
    return lam_ref[1 + local_bits + b, h : h + 1, :] * upper


def local_kernel(place_ref, q_hbm, kh_ref, vh_ref, lam_hbm, w_hbm, *refs):
    pt_ref, att_ref, qh_ref, qw_ref, lam_ref, w_ref, q_ref, lam_rows, sems = refs
    pieces = sems.shape[0] - 2
    share = w_hbm.shape[0] // pieces
    copies = [
        pltpu.make_async_copy(q_hbm, q_ref, sems.at[0]),
        pltpu.make_async_copy(lam_hbm, lam_ref, sems.at[1]),
    ]
    for i in range(pieces):
        piece = pl.ds(i * share, share)
        copies.append(pltpu.make_async_copy(w_hbm.at[piece], w_ref.at[piece], sems.at[2 + i]))
    for copy in copies:
        copy.start()
    for copy in copies[:2]:
        copy.wait()
    rows, heads_dev, _ = q_ref.shape
    bits = qw_ref.shape[0]
    lam_rows[...] = jnp.zeros_like(lam_rows)
    for b in range(bits):
        for h in range(heads_dev):
            at = b * heads_dev + h
            lam_rows[at : at + 1, :] = upper_weight(place_ref, lam_ref, b, h, rows)
    lam_columns = lam_rows[...].T
    for h in range(heads_dev):
        q32 = q_ref[:, h, :]
        q = q32.astype(BF)
        qh_ref[h] = q
        for b in range(bits):
            at = b * heads_dev + h
            qw_ref[b, h] = (q32 * lam_columns[:, at : at + 1]).astype(BF)
        pt = (mm(kh_ref[h], q, NT) * weight_of(lam_ref, h, rows)).astype(BF)
        pt_ref[h] = pt
        att_ref[h] = mm(pt, vh_ref[h], TN)
    for copy in copies[2:]:
        copy.wait()


def attended_kernel(bits, att_ref, qw_ref, after_ref, *refs):
    del after_ref
    states, out_ref = refs[:bits], refs[bits]
    heads_dev, _, head_dim = att_ref.shape
    for h in range(heads_dev):
        total = att_ref[h]
        for b in range(bits):
            total = total + mm(qw_ref[b, h], states[b][h], NN)
        out_ref[:, h * head_dim : (h + 1) * head_dim] = total.astype(BF)


def cotangent_kernel(blocks, bits, head_ref, *refs):
    parts, (w_ref, qw_ref, _, gt_ref), sums = (
        refs[:blocks],
        refs[blocks : blocks + 4],
        refs[blocks + 4 :],
    )
    deep = parts[0].shape[1]
    _, heads_dev, _, head_dim = qw_ref.shape
    total = None
    for i in range(blocks):
        column = pl.multiple_of((head_ref[0] ^ i) * deep, deep)
        product = mm(w_ref[:, pl.ds(column, deep)], parts[i][...], NT)
        total = product if total is None else total + product
    for h in range(heads_dev):
        gt = total[h * head_dim : (h + 1) * head_dim].astype(BF)
        gt_ref[h * head_dim : (h + 1) * head_dim, :] = gt
        for b in range(bits):
            sums[b][h] = mm(gt, qw_ref[b, h], NN).astype(BF)


def running_kernel(running_ref, arrived_ref, *refs):
    refs[-1][...] = (running_ref[...].astype(F32) + arrived_ref[...].astype(F32)).astype(BF)


def meet_kernel(top, place_ref, after_ref, grad_ref, running_ref, arrived_ref, out_ref):
    del after_ref
    upper = (place_ref[0] >> top & 1) == 1
    running = running_ref[...].astype(F32)
    if arrived_ref is not None:
        running = running + arrived_ref[...].astype(F32)
    out_ref[...] = jnp.where(upper, grad_ref[...], running.astype(BF))


def landed_sum(top, place_ref, landed):
    upper = (place_ref[0] >> top & 1) == 1
    total = jnp.where(upper, 0.0, landed[0].astype(F32))
    for block in landed[1:]:
        total = total + block.astype(F32)
    return total


def pending_kernel(top, place_ref, own_ref, after_ref, *refs):
    del after_ref
    landed, out_ref = [ref[...] for ref in refs[:-1]], refs[-1]
    out_ref[...] = (own_ref[...].astype(F32) + landed_sum(top, place_ref, landed)).astype(BF)


def chunk_kernel(place_ref, block_ref, after_ref, *outs):
    del after_ref
    columns = outs[0].shape[1]
    low = place_ref[0] % len(outs)
    for r, out in enumerate(outs):
        out[...] = block_ref[:, pl.ds(pl.multiple_of((low ^ r) * columns, columns), columns)]


def stack_kernel(after_ref, *refs):
    del after_ref
    for r, ref in enumerate(refs[:-1]):
        refs[-1][r] = ref[...]


def columns_kernel(blocks, place_ref, head_ref, *refs):
    parts, out_ref = refs[:blocks], refs[blocks]
    per = parts[0].shape[0]
    low = place_ref[0] % per
    for i in range(blocks):
        for r in range(per):
            out_ref[(head_ref[0] ^ i) * per + (low ^ r)] = parts[i][r]


def local_grad_kernel(
    bits, place_ref, gt_ref, qh_ref, kh_ref, vh_ref, pt_ref, lam_ref, after_ref, *refs
):
    del after_ref
    states, (dq_ref, dk_ref, dv_ref) = refs[:bits], refs[bits:]
    heads_dev, rows, head_dim = qh_ref.shape
    for h in range(heads_dev):
        gt = gt_ref[h * head_dim : (h + 1) * head_dim, :]
        g32 = gt.astype(F32)
        dpt = (mm(vh_ref[h], gt, NN) * weight_of(lam_ref, h, rows)).astype(BF)
        dk_ref[h] = mm(dpt, qh_ref[h], NN)
        dv_ref[h] = mm(pt_ref[h], gt, NT)
        dq = mm(dpt, kh_ref[h], TN)
        for b in range(bits):
            gw = (g32 * upper_weight(place_ref, lam_ref, b, h, rows)).astype(BF)
            dq = dq + mm(gw, states[b][h], TT)
        dq_ref[:, h, :] = dq


def later_grad_kernel(top, place_ref, kh_ref, vh_ref, dkl_ref, dvl_ref, after_ref, *refs):
    del after_ref
    landed, (dk_ref, dv_ref) = refs[:-2], refs[-2:]
    for h in range(kh_ref.shape[0]):
        late = landed_sum(top, place_ref, [ref[h] for ref in landed]).astype(BF)
        dk_ref[:, h, :] = dkl_ref[h] + mm(vh_ref[h], late, NN)
        dv_ref[:, h, :] = dvl_ref[h] + mm(kh_ref[h], late, NT)


def share_kernel(blocks, head_ref, att_ref, w_ref, send_ref, kept_ref):
    width = send_ref.shape[2]
    for i in range(blocks):
        out = send_ref if i % 2 else kept_ref
        column = pl.multiple_of((head_ref[0] ^ i) * width, width)
        out[i // 2] = mm(att_ref[...], w_ref[:, pl.ds(column, width)], NN).astype(out.dtype)


def ring_owner(place, offset, devices):
    at = jnp.where(place % 2 == 0, place // 2, devices - 1 - place // 2)
    at = (at + offset + devices) % devices
    return jnp.where(at < devices // 2, 2 * at, 2 * (devices - 1 - at) + 1)


def proj_kernel(offsets, devices, first, place_ref, cols_ref, *refs):
    total = None if first else refs[len(offsets)][...]
    for i, (offset, low, high) in enumerate(offsets):
        owner = ring_owner(place_ref[0], offset, devices)
        product = mm(refs[i][...], cols_ref[owner, low:high, :], TN)
        total = product if total is None else total + product
    refs[-1][...] = total


def last_kernel(
    offset, devices, place_ref, cols_ref, low_ref, high_ref, total_ref, after_ref, out_ref, held
):
    del after_ref
    half = low_ref.shape[0]
    held[:half] = low_ref[...]
    held[half:] = high_ref[...]
    owner = ring_owner(place_ref[0], offset, devices)
    out_ref[...] = total_ref[...] + mm(held[...], cols_ref[owner], TN)


def body(queries, keys, values, level_weights, out_proj, out_grad):
    rows, heads_dev, head_dim = queries.shape
    width = heads_dev * head_dim
    devices = lax.axis_size("seq")
    seq_bits = devices.bit_length() - 1
    heads = lax.axis_size("head")
    head_bits = heads.bit_length() - 1
    seq_place = lax.axis_index("seq")
    head_place = lax.axis_index("head")
    columns_dev = out_proj.shape[1] // devices

    head_state = like((heads_dev, head_dim, head_dim), BF)
    pinned_state = pltpu.VMEM((heads_dev, head_dim, head_dim), BF)
    per_head = pltpu.VMEM((heads_dev, rows, head_dim), BF)
    per_head_f32 = pltpu.VMEM((heads_dev, rows, head_dim), F32)
    flops_head = 2 * heads_dev * rows * rows * head_dim
    moved_head = 2 * rows * width
    top = seq_bits - 1
    place = seq_place.reshape(1).astype(jnp.int32)
    group = head_place.reshape(1).astype(jnp.int32)

    own_state, kh, vh = pl.pallas_call(
        state_kernel,
        out_shape=(head_state, per_head, per_head),
        in_specs=[ANY] * 2,
        out_specs=(VMEM,) * 3,
        scratch_shapes=[
            pltpu.VMEM(keys.shape, F32),
            pltpu.VMEM(keys.shape, F32),
            pltpu.SemaphoreType.DMA((2,)),
        ],
        compiler_params=PARAMS,
        cost_estimate=cost(flops_head, 7 * moved_head),
    )(hbm(keys), hbm(values))

    def to_group(block, i):
        return lax.ppermute(block, "head", [(at, at ^ i) for at in range(heads)])

    def every_group(block):
        blocks = {0: block}
        for digit in reversed(range(head_bits)):
            for i in sorted(blocks):
                blocks[i ^ 1 << digit] = to_group(blocks[i], 1 << digit)
        return [blocks[i] for i in range(heads)]

    grad_blocks = every_group(out_grad)

    per = devices // heads
    route = [
        ((high * per + low) * heads + group_at, (group_at * per + low) * heads + high)
        for high in range(heads)
        for low in range(per)
        for group_at in range(heads)
    ]
    turned = lax.ppermute(out_grad, ("seq", "head"), route)
    probs_t, att_local, qh, qw, lam, w = pl.pallas_call(
        local_kernel,
        out_shape=(
            pltpu.VMEM((heads_dev, rows, rows), BF),
            per_head_f32,
            per_head,
            pltpu.VMEM((seq_bits, heads_dev, rows, head_dim), BF),
            pltpu.VMEM(level_weights.shape, F32),
            pltpu.VMEM(out_proj.shape, BF),
        ),
        in_specs=[SMEM, ANY, VMEM, VMEM, ANY, ANY],
        out_specs=(VMEM,) * 6,
        scratch_shapes=[
            pltpu.VMEM(queries.shape, F32),
            pltpu.VMEM((rows, rows), F32),
            pltpu.SemaphoreType.DMA((10,)),
        ],
        compiler_params=PARAMS,
        cost_estimate=cost(2 * flops_head, 12 * moved_head),
    )(place, hbm(queries), kh, vh, hbm(level_weights), hbm(out_proj))

    partner_states = []
    running, arrived = own_state, None
    for digit in range(top):
        if arrived is not None:
            running = pl.pallas_call(
                running_kernel,
                out_shape=head_state,
                in_specs=[VMEM] * 2 + [ANY] * 2,
                out_specs=VMEM,
                compiler_params=PARAMS,
                cost_estimate=cost(0, 3 * moved_head),
            )(running, arrived, turned, qw)
        arrived = across(running, "seq", digit)
        partner_states.append(arrived)

    chunks = pl.pallas_call(
        chunk_kernel,
        out_shape=(like((rows, columns_dev), BF),) * per,
        in_specs=[SMEM, VMEM, ANY],
        out_specs=(VMEM,) * per,
        compiler_params=PARAMS,
        cost_estimate=cost(0, 2 * moved_head),
    )(place, turned, running)
    own_chunks = chunks
    chunks = [chunks[0]] + [
        lax.ppermute(chunks[r], "seq", [(at, at ^ r) for at in range(devices)])
        for r in range(1, per)
    ]
    gt, *grad_sums = pl.pallas_call(
        functools.partial(cotangent_kernel, heads, seq_bits),
        out_shape=(pltpu.VMEM((width, rows), BF),) + (pinned_state,) * seq_bits,
        in_specs=[SMEM] + [VMEM] * (heads + 2) + [ANY],
        out_specs=(VMEM,) * (1 + seq_bits),
        compiler_params=PARAMS,
        cost_estimate=cost(2 * rows * width * out_proj.shape[1], 2 * width * out_proj.shape[1]),
    )(group, *grad_blocks, w, qw, own_chunks[-1])

    stacked = pl.pallas_call(
        stack_kernel,
        out_shape=like((per, rows, columns_dev), BF),
        in_specs=[ANY] + [VMEM] * per,
        out_specs=VMEM,
        compiler_params=PARAMS,
        cost_estimate=cost(0, 2 * moved_head),
    )(gt, *chunks)
    column_blocks = every_group(stacked)

    meeting = pl.pallas_call(
        functools.partial(meet_kernel, top)
        if arrived is not None
        else lambda place_ref, after_ref, grad_ref, running_ref, out_ref: meet_kernel(
            top, place_ref, after_ref, grad_ref, running_ref, None, out_ref
        ),
        out_shape=head_state,
        in_specs=[SMEM, ANY] + [VMEM] * (2 if arrived is None else 3),
        out_specs=VMEM,
        compiler_params=PARAMS,
        cost_estimate=cost(0, 4 * moved_head),
    )(place, stacked, grad_sums[top], running, *([] if arrived is None else [arrived]))
    landed = [across(meeting, "seq", top)]
    partner_states.append(landed[0])

    grad_columns = pl.pallas_call(
        functools.partial(columns_kernel, heads),
        out_shape=pltpu.VMEM((devices, rows, columns_dev), BF),
        in_specs=[SMEM] * 2 + [VMEM] * heads,
        out_specs=VMEM,
        compiler_params=PARAMS,
        cost_estimate=cost(0, 8 * moved_head),
    )(place, group, *column_blocks)

    attended = pl.pallas_call(
        functools.partial(attended_kernel, seq_bits),
        out_shape=like((rows, width), BF),
        in_specs=[VMEM] * 2 + [ANY] + [VMEM] * seq_bits,
        out_specs=VMEM,
        compiler_params=PARAMS,
        cost_estimate=cost(seq_bits * flops_head, 8 * moved_head),
    )(att_local, qw, column_blocks[-1], *partner_states)

    for digit in reversed(range(top)):
        outgoing = pl.pallas_call(
            functools.partial(pending_kernel, top),
            out_shape=head_state,
            in_specs=[SMEM, VMEM, ANY] + [VMEM] * len(landed),
            out_specs=VMEM,
            compiler_params=PARAMS,
            cost_estimate=cost(0, 4 * moved_head),
        )(place, grad_sums[digit], attended, *landed)
        landed.append(across(outgoing, "seq", digit))

    send, kept = pl.pallas_call(
        functools.partial(share_kernel, heads),
        out_shape=(like((heads // 2, rows, width), BF), like((heads // 2, rows, width), F32)),
        in_specs=[SMEM, VMEM, VMEM],
        out_specs=(VMEM,) * 2,
        compiler_params=PARAMS,
        cost_estimate=cost(2 * rows * width * out_proj.shape[1], 2 * width * out_proj.shape[1]),
    )(group, attended, w)
    for digit in range(head_bits):
        kept = kept + to_group(send, 1 << digit).astype(F32)
        if digit < head_bits - 1:
            send, kept = kept[1::2].astype(BF), kept[0::2]
    mixed = kept[0].astype(BF)

    query_grad, key_local, value_local = pl.pallas_call(
        functools.partial(local_grad_kernel, seq_bits),
        out_shape=(like((rows, heads_dev, head_dim), F32), per_head_f32, per_head_f32),
        in_specs=[SMEM] + [VMEM] * 6 + [ANY] + [VMEM] * seq_bits,
        out_specs=(VMEM,) * 3,
        compiler_params=PARAMS,
        cost_estimate=cost((4 + seq_bits) * flops_head, 14 * moved_head),
    )(place, gt, qh, kh, vh, probs_t, lam, send, *partner_states)

    ring = list(range(0, devices, 2)) + list(range(devices - 1, 0, -2))
    forward = [(ring[i], ring[(i + 1) % devices]) for i in range(devices)]
    backward = [(b, a) for a, b in forward]

    def accumulate(total, blocks, offsets):
        operands = blocks if total is None else blocks + [total]
        return pl.pallas_call(
            functools.partial(proj_kernel, offsets, devices, total is None),
            out_shape=like((width, columns_dev), F32),
            in_specs=[SMEM] + [VMEM] * (1 + len(operands)),
            out_specs=VMEM,
            compiler_params=PARAMS,
            cost_estimate=cost(
                2 * len(blocks) * rows * width * columns_dev, 4 * width * columns_dev
            ),
        )(place, grad_columns, *operands)

    blocks, offsets = [attended], [(0, 0, rows)]
    ahead = behind = attended
    half, steps, total = rows // 2, devices // 2, None
    for step in range(1, steps):
        ahead = lax.ppermute(ahead, "seq", forward)
        behind = lax.ppermute(behind, "seq", backward)
        blocks += [ahead, behind]
        offsets += [(-step, 0, rows), (step, 0, rows)]
        if step == steps - 2:
            total = accumulate(None, blocks, offsets)
            blocks, offsets = [], []
    if blocks:
        total = accumulate(total, blocks, offsets)
    last = [
        lax.ppermute(ahead[:half], "seq", forward),
        lax.ppermute(behind[half:], "seq", backward),
    ]
    key_grad, value_grad = pl.pallas_call(
        functools.partial(later_grad_kernel, top),
        out_shape=(like((rows, heads_dev, head_dim), F32),) * 2,
        in_specs=[SMEM] + [VMEM] * 4 + [ANY] + [VMEM] * seq_bits,
        out_specs=(VMEM,) * 2,
        compiler_params=PARAMS,
        cost_estimate=cost(2 * flops_head, 11 * moved_head),
    )(place, kh, vh, key_local, value_local, total, *landed)
    quarter_rows = width // 4
    proj_grad = pl.pallas_call(
        functools.partial(last_kernel, steps, devices),
        out_shape=like((width, columns_dev), F32),
        grid=(4,),
        in_specs=[
            SMEM,
            VMEM,
            pl.BlockSpec((half, quarter_rows), lambda i: (0, i)),
            pl.BlockSpec((half, quarter_rows), lambda i: (0, i)),
            pl.BlockSpec((quarter_rows, columns_dev), lambda i: (i, 0)),
            ANY,
        ],
        out_specs=pl.BlockSpec((quarter_rows, columns_dev), lambda i: (i, 0)),
        scratch_shapes=[pltpu.VMEM((rows, quarter_rows), BF)],
        compiler_params=PARAMS,
        cost_estimate=cost(2 * rows * width * columns_dev, 8 * width * columns_dev),
    )(place, grad_columns, *last, total, hbm(key_grad))
    return (mixed, query_grad, key_grad, value_grad, proj_grad)


def solution(mesh):
    placed = (
        P("seq", "head", None),
        P("seq", "head", None),
        P("seq", "head", None),
        P(None, "head", "seq"),
        P("head", None),
        P("seq", "head"),
    )
    return jax.shard_map(
        body,
        mesh=mesh,
        in_specs=placed,
        out_specs=(
            P("seq", "head"),
            P("seq", "head", None),
            P("seq", "head", None),
            P("seq", "head", None),
            P("head", "seq"),
        ),
        check_vma=False,
    )
```

```python
import functools

import jax
import jax.numpy as jnp
from jax import lax
from jax.experimental import pallas as pl
from jax.experimental.pallas import tpu as pltpu
from jax.sharding import PartitionSpec as P

CH = 64
BF = jnp.bfloat16
F32 = jnp.float32
NN = (((1,), (0,)), ((), ()))
NT = (((1,), (1,)), ((), ()))
TN = (((0,), (0,)), ((), ()))
TT = (((0,), (1,)), ((), ()))
VMEM = pl.BlockSpec(memory_space=pltpu.VMEM)
ANY = pl.BlockSpec(memory_space=pl.ANY)
SMEM = pl.BlockSpec(memory_space=pltpu.SMEM)
PARAMS = pltpu.CompilerParams(vmem_limit_bytes=14 * 2**20)


def mm(a, b, dims):
    return lax.dot_general(a, b, dims, preferred_element_type=F32)


def cost(flops, moved):
    return pl.CostEstimate(flops=flops, bytes_accessed=moved, transcendentals=0)


def like(shape, dtype):
    return jax.ShapeDtypeStruct(shape, dtype)


def across(block, axis, stride, up_only=False, down_only=False):
    count = lax.axis_size(axis)
    route = []
    for low in range(count):
        high = low | 1 << stride
        if high != low and high < count:
            if not down_only:
                route.append((low, high))
            if not up_only:
                route.append((high, low))
    return lax.ppermute(block, axis, route)


def hbm(array):
    return pltpu.with_memory_space_constraint(array, pltpu.HBM)


def state_kernel(place_ref, k_hbm, v_hbm, s_ref, kh_ref, vh_ref, k_ref, v_ref, sems):
    del place_ref
    copies = [
        pltpu.make_async_copy(k_hbm, k_ref, sems.at[0]),
        pltpu.make_async_copy(v_hbm, v_ref, sems.at[1]),
    ]
    for copy in copies:
        copy.start()
    for copy in copies:
        copy.wait()
    for h in range(k_ref.shape[1]):
        k = k_ref[:, h, :].astype(BF)
        v = v_ref[:, h, :].astype(BF)
        kh_ref[h] = k
        vh_ref[h] = v
        s_ref[h] = mm(k, v, TN).astype(BF)


def weight_of(lam_ref, h, rows):
    local_bits = (rows // CH).bit_length() - 1
    s = lax.broadcasted_iota(jnp.int32, (rows, rows), 0)
    t = lax.broadcasted_iota(jnp.int32, (rows, rows), 1)
    differ = (s // CH) ^ (t // CH)
    weight = jnp.broadcast_to(lam_ref[0, h : h + 1, :], (rows, rows))
    for digit in range(local_bits):
        weight = jnp.where(differ >= 1 << digit, lam_ref[1 + digit, h : h + 1, :], weight)
    return jnp.where(s <= t, weight, 0.0)


def upper_weight(place_ref, lam_ref, b, h, rows):
    local_bits = (rows // CH).bit_length() - 1
    upper = (place_ref[0] >> b & 1).astype(F32)
    return lam_ref[1 + local_bits + b, h : h + 1, :] * upper


def local_kernel(place_ref, q_hbm, kh_ref, vh_ref, lam_hbm, w_hbm, grad_hbm, *refs):
    pt_ref, att_ref, qh_ref, qw_ref, lam_ref, w_ref, grad_ref, q_ref, lam_rows, sems = refs
    pieces = sems.shape[0] - 3
    share = w_hbm.shape[0] // pieces
    copies = [
        pltpu.make_async_copy(q_hbm, q_ref, sems.at[0]),
        pltpu.make_async_copy(lam_hbm, lam_ref, sems.at[1]),
    ]
    for i in range(pieces):
        piece = pl.ds(i * share, share)
        copies.append(pltpu.make_async_copy(w_hbm.at[piece], w_ref.at[piece], sems.at[3 + i]))
    copies.append(pltpu.make_async_copy(grad_hbm, grad_ref, sems.at[2]))
    for copy in copies:
        copy.start()
    for copy in copies[:2]:
        copy.wait()
    rows, heads_dev, _ = q_ref.shape
    bits = qw_ref.shape[0]
    lam_rows[...] = jnp.zeros_like(lam_rows)
    for b in range(bits):
        for h in range(heads_dev):
            at = b * heads_dev + h
            lam_rows[at : at + 1, :] = upper_weight(place_ref, lam_ref, b, h, rows)
    lam_columns = lam_rows[...].T
    for h in range(heads_dev):
        q32 = q_ref[:, h, :]
        q = q32.astype(BF)
        qh_ref[h] = q
        for b in range(bits):
            at = b * heads_dev + h
            qw_ref[b, h] = (q32 * lam_columns[:, at : at + 1]).astype(BF)
        pt = (mm(kh_ref[h], q, NT) * weight_of(lam_ref, h, rows)).astype(BF)
        pt_ref[h] = pt
        att_ref[h] = mm(pt, vh_ref[h], TN)
    for copy in copies[2:]:
        copy.wait()


def attended_kernel(bits, att_ref, qw_ref, *refs):
    states, out_ref = refs[:bits], refs[-1]
    heads_dev, _, head_dim = att_ref.shape
    for h in range(heads_dev):
        total = att_ref[h]
        for b in range(bits):
            total = total + mm(qw_ref[b, h], states[b][h], NN)
        out_ref[:, h * head_dim : (h + 1) * head_dim] = total.astype(BF)


def cotangent_kernel(blocks, bits, place_ref, *refs):
    parts, (w_ref, qw_ref, _, gt_ref), sums = (
        refs[:blocks],
        refs[blocks : blocks + 4],
        refs[blocks + 4 :],
    )
    deep = parts[0].shape[1]
    _, heads_dev, _, head_dim = qw_ref.shape
    total = None
    for i in range(blocks):
        column = pl.multiple_of((place_ref[1] ^ i) * deep, deep)
        product = mm(w_ref[:, pl.ds(column, deep)], parts[i][...], NT)
        total = product if total is None else total + product
    for h in range(heads_dev):
        gt = total[h * head_dim : (h + 1) * head_dim].astype(BF)
        gt_ref[h * head_dim : (h + 1) * head_dim, :] = gt
        for b in range(bits):
            sums[b][h] = mm(gt, qw_ref[b, h], NN).astype(BF)


def running_kernel(running_ref, arrived_ref, *refs):
    refs[-1][...] = (running_ref[...].astype(F32) + arrived_ref[...].astype(F32)).astype(BF)


def meet_kernel(top, place_ref, after_ref, grad_ref, running_ref, arrived_ref, out_ref):
    del after_ref
    upper = (place_ref[0] >> top & 1) == 1
    running = running_ref[...].astype(F32)
    if arrived_ref is not None:
        running = running + arrived_ref[...].astype(F32)
    out_ref[...] = jnp.where(upper, grad_ref[...], running.astype(BF))


def landed_sum(top, place_ref, landed):
    upper = (place_ref[0] >> top & 1) == 1
    total = jnp.where(upper, 0.0, landed[0].astype(F32))
    for block in landed[1:]:
        total = total + block.astype(F32)
    return total


def pending_kernel(top, place_ref, own_ref, after_ref, *refs):
    del after_ref
    landed, out_ref = [ref[...] for ref in refs[:-1]], refs[-1]
    out_ref[...] = (own_ref[...].astype(F32) + landed_sum(top, place_ref, landed)).astype(BF)


def chunk_kernel(place_ref, block_ref, after_ref, *outs):
    del after_ref
    columns = outs[0].shape[1]
    low = place_ref[0] % len(outs)
    for r, out in enumerate(outs):
        out[...] = block_ref[:, pl.ds(pl.multiple_of((low ^ r) * columns, columns), columns)]


def stack_kernel(after_ref, *refs):
    del after_ref
    for r, ref in enumerate(refs[:-1]):
        refs[-1][r] = ref[...]


def columns_kernel(blocks, place_ref, *refs):
    parts, out_ref = refs[:blocks], refs[blocks]
    per = parts[0].shape[0]
    low = place_ref[0] % per
    for i in range(blocks):
        for r in range(per):
            out_ref[(place_ref[1] ^ i) * per + (low ^ r)] = parts[i][r]


def local_grad_kernel(
    bits, place_ref, gt_ref, qh_ref, kh_ref, vh_ref, pt_ref, lam_ref, after_ref, *refs
):
    del after_ref
    states, (dq_ref, dk_ref, dv_ref) = refs[:bits], refs[bits:]
    heads_dev, rows, head_dim = qh_ref.shape
    for h in range(heads_dev):
        gt = gt_ref[h * head_dim : (h + 1) * head_dim, :]
        g32 = gt.astype(F32)
        dpt = (mm(vh_ref[h], gt, NN) * weight_of(lam_ref, h, rows)).astype(BF)
        dk_ref[h] = mm(dpt, qh_ref[h], NN)
        dv_ref[h] = mm(pt_ref[h], gt, NT)
        dq = mm(dpt, kh_ref[h], TN)
        for b in range(bits):
            gw = (g32 * upper_weight(place_ref, lam_ref, b, h, rows)).astype(BF)
            dq = dq + mm(gw, states[b][h], TT)
        dq_ref[h] = dq


def query_grad_kernel(top, place_ref, gt_ref, lam_ref, dql_ref, state_ref, dq_ref):
    heads_dev, rows, head_dim = dql_ref.shape
    for h in range(heads_dev):
        g32 = gt_ref[h * head_dim : (h + 1) * head_dim, :].astype(F32)
        gw = (g32 * upper_weight(place_ref, lam_ref, top, h, rows)).astype(BF)
        dq_ref[:, h, :] = dql_ref[h] + mm(gw, state_ref[h], TT)


def later_grad_kernel(top, place_ref, kh_ref, vh_ref, dkl_ref, dvl_ref, after_ref, *refs):
    del after_ref
    landed, (dk_ref, dv_ref) = refs[:-2], refs[-2:]
    for h in range(kh_ref.shape[0]):
        late = landed_sum(top, place_ref, [ref[h] for ref in landed]).astype(BF)
        dk_ref[:, h, :] = dkl_ref[h] + mm(vh_ref[h], late, NN)
        dv_ref[:, h, :] = dvl_ref[h] + mm(kh_ref[h], late, NT)


def share_kernel(blocks, place_ref, att_ref, w_ref, after_ref, send_ref, kept_ref):
    del after_ref
    width = send_ref.shape[2]
    for i in range(blocks):
        out = send_ref if i % 2 else kept_ref
        column = pl.multiple_of((place_ref[1] ^ i) * width, width)
        out[i // 2] = mm(att_ref[...], w_ref[:, pl.ds(column, width)], NN).astype(out.dtype)


def ring_owner(place, offset, devices):
    at = jnp.where(place % 2 == 0, place // 2, devices - 1 - place // 2)
    at = (at + offset + devices) % devices
    return jnp.where(at < devices // 2, 2 * at, 2 * (devices - 1 - at) + 1)


def proj_kernel(offsets, devices, first, place_ref, cols_ref, *refs):
    total = None if first else refs[len(offsets)][...]
    for i, (offset, low, high) in enumerate(offsets):
        owner = ring_owner(place_ref[0], offset, devices)
        product = mm(refs[i][...], cols_ref[owner, low:high, :], TN)
        total = product if total is None else total + product
    refs[-1][...] = total


def last_kernel(
    offset, devices, place_ref, cols_ref, low_ref, high_ref, total_ref, after_ref, out_ref, held
):
    del after_ref
    half, block = low_ref.shape[0], out_ref.shape[0]
    at = pl.ds(pl.multiple_of(pl.program_id(0) * block, block), block)
    held[:half] = low_ref[:, at]
    held[half:] = high_ref[:, at]
    owner = ring_owner(place_ref[0], offset, devices)
    out_ref[...] = total_ref[at, :] + mm(held[...], cols_ref[owner], TN)


def body(queries, keys, values, level_weights, out_proj, out_grad):
    rows, heads_dev, head_dim = queries.shape
    width = heads_dev * head_dim
    devices = lax.axis_size("seq")
    seq_bits = devices.bit_length() - 1
    heads = lax.axis_size("head")
    head_bits = heads.bit_length() - 1
    seq_place = lax.axis_index("seq")
    head_place = lax.axis_index("head")
    columns_dev = out_proj.shape[1] // devices

    head_state = like((heads_dev, head_dim, head_dim), BF)
    pinned_state = pltpu.VMEM((heads_dev, head_dim, head_dim), BF)
    per_head = pltpu.VMEM((heads_dev, rows, head_dim), BF)
    per_head_f32 = pltpu.VMEM((heads_dev, rows, head_dim), F32)
    flops_head = 2 * heads_dev * rows * rows * head_dim
    moved_head = 2 * rows * width
    top = seq_bits - 1
    place = jnp.stack([seq_place, head_place]).astype(jnp.int32)

    own_state, kh, vh = pl.pallas_call(
        state_kernel,
        out_shape=(head_state, per_head, per_head),
        in_specs=[SMEM] + [ANY] * 2,
        out_specs=(VMEM,) * 3,
        scratch_shapes=[
            pltpu.VMEM(keys.shape, F32),
            pltpu.VMEM(keys.shape, F32),
            pltpu.SemaphoreType.DMA((2,)),
        ],
        compiler_params=PARAMS,
        cost_estimate=cost(flops_head, 7 * moved_head),
    )(place, hbm(keys), hbm(values))

    def to_group(block, i):
        return lax.ppermute(block, "head", [(at, at ^ i) for at in range(heads)])

    def every_group(block):
        blocks = {0: block}
        for digit in reversed(range(head_bits)):
            for i in sorted(blocks):
                blocks[i ^ 1 << digit] = to_group(blocks[i], 1 << digit)
        return [blocks[i] for i in range(heads)]

    grad_blocks = every_group(out_grad)

    per = devices // heads
    route = [
        ((high * per + low) * heads + group_at, (group_at * per + low) * heads + high)
        for high in range(heads)
        for low in range(per)
        for group_at in range(heads)
    ]
    turned = lax.ppermute(out_grad, ("seq", "head"), route)
    probs_t, att_local, qh, qw, lam, w, own_grad = pl.pallas_call(
        local_kernel,
        out_shape=(
            pltpu.VMEM((heads_dev, rows, rows), BF),
            per_head_f32,
            per_head,
            pltpu.VMEM((seq_bits, heads_dev, rows, head_dim), BF),
            pltpu.VMEM(level_weights.shape, F32),
            pltpu.VMEM(out_proj.shape, BF),
            pltpu.VMEM(out_grad.shape, BF),
        ),
        in_specs=[SMEM, ANY, VMEM, VMEM, ANY, ANY, ANY],
        out_specs=(VMEM,) * 7,
        scratch_shapes=[
            pltpu.VMEM(queries.shape, F32),
            pltpu.VMEM((rows, rows), F32),
            pltpu.SemaphoreType.DMA((11,)),
        ],
        compiler_params=PARAMS,
        cost_estimate=cost(2 * flops_head, 12 * moved_head),
    )(place, hbm(queries), kh, vh, hbm(level_weights), hbm(out_proj), hbm(out_grad))

    chunks = pl.pallas_call(
        chunk_kernel,
        out_shape=(like((rows, columns_dev), BF),) * per,
        in_specs=[SMEM, VMEM, ANY],
        out_specs=(VMEM,) * per,
        compiler_params=PARAMS,
        cost_estimate=cost(0, 2 * moved_head),
    )(place, turned, qw)
    own_chunks = chunks
    chunks = [chunks[0]] + [
        lax.ppermute(chunks[r], "seq", [(at, at ^ r) for at in range(devices)])
        for r in range(1, per)
    ]
    partner_states = []
    running, arrived = own_state, None
    for digit in range(top):
        if arrived is not None:
            running = pl.pallas_call(
                running_kernel,
                out_shape=head_state,
                in_specs=[VMEM] * 2 + [ANY],
                out_specs=VMEM,
                compiler_params=PARAMS,
                cost_estimate=cost(0, 3 * moved_head),
            )(running, arrived, own_chunks[-1])
        arrived = across(running, "seq", digit)
        partner_states.append(arrived)

    gt, *grad_sums = pl.pallas_call(
        functools.partial(cotangent_kernel, heads, seq_bits),
        out_shape=(pltpu.VMEM((width, rows), BF),) + (pinned_state,) * seq_bits,
        in_specs=[SMEM] + [VMEM] * (heads + 2) + [ANY],
        out_specs=(VMEM,) * (1 + seq_bits),
        compiler_params=PARAMS,
        cost_estimate=cost(2 * rows * width * out_proj.shape[1], 2 * width * out_proj.shape[1]),
    )(place, own_grad, *grad_blocks[1:], w, qw, own_chunks[-1])

    stacked = pl.pallas_call(
        stack_kernel,
        out_shape=like((per, rows, columns_dev), BF),
        in_specs=[ANY] + [VMEM] * per,
        out_specs=VMEM,
        compiler_params=PARAMS,
        cost_estimate=cost(0, 2 * moved_head),
    )(gt, *chunks)
    column_blocks = every_group(stacked)

    meeting = pl.pallas_call(
        functools.partial(meet_kernel, top)
        if arrived is not None
        else lambda place_ref, after_ref, grad_ref, running_ref, out_ref: meet_kernel(
            top, place_ref, after_ref, grad_ref, running_ref, None, out_ref
        ),
        out_shape=head_state,
        in_specs=[SMEM, ANY] + [VMEM] * (2 if arrived is None else 3),
        out_specs=VMEM,
        compiler_params=PARAMS,
        cost_estimate=cost(0, 4 * moved_head),
    )(place, stacked, grad_sums[top], running, *([] if arrived is None else [arrived]))
    landed = [across(meeting, "seq", top)]
    partner_states.append(landed[0])

    grad_columns = pl.pallas_call(
        functools.partial(columns_kernel, heads),
        out_shape=pltpu.VMEM((devices, rows, columns_dev), BF),
        in_specs=[SMEM] + [VMEM] * heads,
        out_specs=VMEM,
        compiler_params=PARAMS,
        cost_estimate=cost(0, 8 * moved_head),
    )(place, *column_blocks)

    query_local, key_local, value_local = pl.pallas_call(
        functools.partial(local_grad_kernel, top),
        out_shape=(per_head_f32,) * 3,
        in_specs=[SMEM] + [VMEM] * 6 + [ANY] + [VMEM] * top,
        out_specs=(VMEM,) * 3,
        compiler_params=PARAMS,
        cost_estimate=cost((4 + top) * flops_head, 14 * moved_head),
    )(place, gt, qh, kh, vh, probs_t, lam, meeting, *partner_states[:top])

    attended = pl.pallas_call(
        functools.partial(attended_kernel, seq_bits),
        out_shape=like((rows, width), BF),
        in_specs=[VMEM] * (2 + seq_bits) + [ANY] * heads,
        out_specs=VMEM,
        compiler_params=PARAMS,
        cost_estimate=cost(seq_bits * flops_head, 8 * moved_head),
    )(att_local, qw, *partner_states, key_local, *column_blocks[1:])

    first_pending = attended
    for digit in reversed(range(top)):
        outgoing = pl.pallas_call(
            functools.partial(pending_kernel, top),
            out_shape=head_state,
            in_specs=[SMEM, VMEM, ANY] + [VMEM] * len(landed),
            out_specs=VMEM,
            compiler_params=PARAMS,
            cost_estimate=cost(0, 4 * moved_head),
        )(place, grad_sums[digit], attended, *landed)
        if len(landed) == 1:
            first_pending = outgoing
        landed.append(across(outgoing, "seq", digit))

    send, kept = pl.pallas_call(
        functools.partial(share_kernel, heads),
        out_shape=(like((heads // 2, rows, width), BF), like((heads // 2, rows, width), F32)),
        in_specs=[SMEM, VMEM, VMEM, ANY],
        out_specs=(VMEM,) * 2,
        compiler_params=PARAMS,
        cost_estimate=cost(2 * rows * width * out_proj.shape[1], 2 * width * out_proj.shape[1]),
    )(place, attended, w, first_pending)
    for digit in range(head_bits):
        kept = kept + to_group(send, 1 << digit).astype(F32)
        if digit < head_bits - 1:
            send, kept = kept[1::2].astype(BF), kept[0::2]
    mixed = kept[0].astype(BF)

    query_grad = pl.pallas_call(
        functools.partial(query_grad_kernel, top),
        out_shape=like((rows, heads_dev, head_dim), F32),
        in_specs=[SMEM] + [VMEM] * 4,
        out_specs=VMEM,
        compiler_params=PARAMS,
        cost_estimate=cost(flops_head, 6 * moved_head),
    )(place, gt, lam, query_local, partner_states[top])

    ring = list(range(0, devices, 2)) + list(range(devices - 1, 0, -2))
    forward = [(ring[i], ring[(i + 1) % devices]) for i in range(devices)]
    backward = [(b, a) for a, b in forward]

    def accumulate(total, blocks, offsets):
        operands = blocks if total is None else blocks + [total]
        return pl.pallas_call(
            functools.partial(proj_kernel, offsets, devices, total is None),
            out_shape=like((width, columns_dev), F32),
            in_specs=[SMEM] + [VMEM] * (1 + len(operands)),
            out_specs=VMEM,
            compiler_params=PARAMS,
            cost_estimate=cost(
                2 * len(blocks) * rows * width * columns_dev, 4 * width * columns_dev
            ),
        )(place, grad_columns, *operands)

    blocks, offsets = [attended], [(0, 0, rows)]
    ahead = behind = attended
    half, steps, total = rows // 2, devices // 2, None
    for step in range(1, steps):
        ahead = lax.ppermute(ahead, "seq", forward)
        behind = lax.ppermute(behind, "seq", backward)
        blocks += [ahead, behind]
        offsets += [(-step, 0, rows), (step, 0, rows)]
        if step == steps - 2:
            total = accumulate(None, blocks, offsets)
            blocks, offsets = [], []
    if blocks:
        total = accumulate(total, blocks, offsets)
    last = [
        lax.ppermute(ahead[:half], "seq", forward),
        lax.ppermute(behind[half:], "seq", backward),
    ]
    key_grad, value_grad = pl.pallas_call(
        functools.partial(later_grad_kernel, top),
        out_shape=(like((rows, heads_dev, head_dim), F32),) * 2,
        in_specs=[SMEM] + [VMEM] * 4 + [ANY] + [VMEM] * seq_bits,
        out_specs=(VMEM,) * 2,
        compiler_params=PARAMS,
        cost_estimate=cost(2 * flops_head, 11 * moved_head),
    )(place, kh, vh, key_local, value_local, total, *landed)
    quarter_rows = width // 4
    proj_grad = pl.pallas_call(
        functools.partial(last_kernel, steps, devices),
        out_shape=like((width, columns_dev), F32),
        grid=(4,),
        in_specs=[
            SMEM,
            VMEM,
            VMEM,
            VMEM,
            VMEM,
            ANY,
        ],
        out_specs=pl.BlockSpec((quarter_rows, columns_dev), lambda i: (i, 0)),
        scratch_shapes=[pltpu.VMEM((rows, quarter_rows), BF)],
        compiler_params=PARAMS,
        cost_estimate=cost(2 * rows * width * columns_dev, 8 * width * columns_dev),
    )(place, grad_columns, *last, total, hbm(key_grad))
    return (mixed, query_grad, key_grad, value_grad, proj_grad)


def solution(mesh):
    placed = (
        P("seq", "head", None),
        P("seq", "head", None),
        P("seq", "head", None),
        P(None, "head", "seq"),
        P("head", None),
        P("seq", "head"),
    )
    return jax.shard_map(
        body,
        mesh=mesh,
        in_specs=placed,
        out_specs=(
            P("seq", "head"),
            P("seq", "head", None),
            P("seq", "head", None),
            P("seq", "head", None),
            P("head", "seq"),
        ),
        check_vma=False,
    )
```

```python
import functools

import jax
import jax.numpy as jnp
from jax import lax
from jax.experimental import pallas as pl
from jax.experimental.pallas import tpu as pltpu
from jax.sharding import PartitionSpec as P

CH = 64
BF = jnp.bfloat16
F32 = jnp.float32
NN = (((1,), (0,)), ((), ()))
NT = (((1,), (1,)), ((), ()))
TN = (((0,), (0,)), ((), ()))
TT = (((0,), (1,)), ((), ()))
VMEM = pl.BlockSpec(memory_space=pltpu.VMEM)
ANY = pl.BlockSpec(memory_space=pl.ANY)
PARAMS = pltpu.CompilerParams(vmem_limit_bytes=14 * 2**20)


def mm(a, b, dims):
    return lax.dot_general(a, b, dims, preferred_element_type=F32)


def cost(flops, moved):
    return pl.CostEstimate(flops=flops, bytes_accessed=moved, transcendentals=0)


def like(shape, dtype):
    return jax.ShapeDtypeStruct(shape, dtype)


def across(block, axis, stride, up_only=False, down_only=False):
    count = lax.axis_size(axis)
    route = []
    for low in range(count):
        high = low | 1 << stride
        if high != low and high < count:
            if not down_only:
                route.append((low, high))
            if not up_only:
                route.append((high, low))
    return lax.ppermute(block, axis, route)


def hbm(array):
    return pltpu.with_memory_space_constraint(array, pltpu.HBM)


def state_kernel(k_hbm, v_hbm, grad_hbm, s_ref, kh_ref, vh_ref, grad_ref, k_ref, v_ref, sems):
    copies = [
        pltpu.make_async_copy(k_hbm, k_ref, sems.at[0]),
        pltpu.make_async_copy(v_hbm, v_ref, sems.at[1]),
        pltpu.make_async_copy(grad_hbm, grad_ref, sems.at[2]),
    ]
    for copy in copies:
        copy.start()
    for copy in copies[:2]:
        copy.wait()
    for h in range(k_ref.shape[1]):
        k = k_ref[:, h, :].astype(BF)
        v = v_ref[:, h, :].astype(BF)
        kh_ref[h] = k
        vh_ref[h] = v
        s_ref[h] = mm(k, v, TN).astype(BF)
    copies[2].wait()


def weight_of(lam_ref, h, rows):
    local_bits = (rows // CH).bit_length() - 1
    s = lax.broadcasted_iota(jnp.int32, (rows, rows), 0)
    t = lax.broadcasted_iota(jnp.int32, (rows, rows), 1)
    differ = (s // CH) ^ (t // CH)
    weight = jnp.broadcast_to(lam_ref[0, h : h + 1, :], (rows, rows))
    for digit in range(local_bits):
        weight = jnp.where(differ >= 1 << digit, lam_ref[1 + digit, h : h + 1, :], weight)
    return jnp.where(s <= t, weight, 0.0)


def upper_weight(lam_ref, b, h, rows):
    local_bits = (rows // CH).bit_length() - 1
    upper = (lax.axis_index("seq") >> b & 1).astype(F32)
    return lam_ref[1 + local_bits + b, h : h + 1, :] * upper


def local_kernel(q_hbm, kh_ref, vh_ref, lam_hbm, w_hbm, *refs):
    pt_ref, att_ref, qh_ref, qw_ref, lam_ref, w_ref, q_ref, lam_rows, sems = refs
    pieces = sems.shape[0] - 2
    share = w_hbm.shape[0] // pieces
    copies = [
        pltpu.make_async_copy(q_hbm, q_ref, sems.at[0]),
        pltpu.make_async_copy(lam_hbm, lam_ref, sems.at[1]),
    ]
    for i in range(pieces):
        piece = pl.ds(i * share, share)
        copies.append(pltpu.make_async_copy(w_hbm.at[piece], w_ref.at[piece], sems.at[2 + i]))
    for copy in copies:
        copy.start()
    for copy in copies[:2]:
        copy.wait()
    rows, heads_dev, _ = q_ref.shape
    bits = qw_ref.shape[0]
    lam_rows[...] = jnp.zeros_like(lam_rows)
    for b in range(bits):
        for h in range(heads_dev):
            at = b * heads_dev + h
            lam_rows[at : at + 1, :] = upper_weight(lam_ref, b, h, rows)
    lam_columns = lam_rows[...].T
    for h in range(heads_dev):
        q32 = q_ref[:, h, :]
        q = q32.astype(BF)
        qh_ref[h] = q
        for b in range(bits):
            at = b * heads_dev + h
            qw_ref[b, h] = (q32 * lam_columns[:, at : at + 1]).astype(BF)
        pt = (mm(kh_ref[h], q, NT) * weight_of(lam_ref, h, rows)).astype(BF)
        pt_ref[h] = pt
        att_ref[h] = mm(pt, vh_ref[h], TN)
    for copy in copies[2:]:
        copy.wait()


def attended_kernel(bits, att_ref, qw_ref, *refs):
    states, out_ref = refs[:bits], refs[-1]
    heads_dev, _, head_dim = att_ref.shape
    for h in range(heads_dev):
        total = att_ref[h]
        for b in range(bits):
            total = total + mm(qw_ref[b, h], states[b][h], NN)
        out_ref[:, h * head_dim : (h + 1) * head_dim] = total.astype(BF)


def cotangent_kernel(blocks, bits, *refs):
    parts, (w_ref, qw_ref, _, gt_ref), sums = (
        refs[:blocks],
        refs[blocks : blocks + 4],
        refs[blocks + 4 :],
    )
    deep = parts[0].shape[1]
    _, heads_dev, _, head_dim = qw_ref.shape
    total = None
    for i in range(blocks):
        column = pl.multiple_of((lax.axis_index("head") ^ i) * deep, deep)
        product = mm(w_ref[:, pl.ds(column, deep)], parts[i][...], NT)
        total = product if total is None else total + product
    for h in range(heads_dev):
        gt = total[h * head_dim : (h + 1) * head_dim].astype(BF)
        gt_ref[h * head_dim : (h + 1) * head_dim, :] = gt
        for b in range(bits):
            sums[b][h] = mm(gt, qw_ref[b, h], NN).astype(BF)


def running_kernel(running_ref, arrived_ref, *refs):
    refs[-1][...] = (running_ref[...].astype(F32) + arrived_ref[...].astype(F32)).astype(BF)


def meet_kernel(top, after_ref, grad_ref, running_ref, arrived_ref, out_ref):
    del after_ref
    upper = (lax.axis_index("seq") >> top & 1) == 1
    running = running_ref[...].astype(F32)
    if arrived_ref is not None:
        running = running + arrived_ref[...].astype(F32)
    out_ref[...] = jnp.where(upper, grad_ref[...], running.astype(BF))


def landed_sum(top, landed):
    upper = (lax.axis_index("seq") >> top & 1) == 1
    total = jnp.where(upper, 0.0, landed[0].astype(F32))
    for block in landed[1:]:
        total = total + block.astype(F32)
    return total


def pending_kernel(top, own_ref, after_ref, *refs):
    del after_ref
    landed, out_ref = [ref[...] for ref in refs[:-1]], refs[-1]
    out_ref[...] = (own_ref[...].astype(F32) + landed_sum(top, landed)).astype(BF)


def chunk_kernel(block_ref, after_ref, *outs):
    del after_ref
    columns = outs[0].shape[1]
    low = lax.axis_index("seq") % len(outs)
    for r, out in enumerate(outs):
        out[...] = block_ref[:, pl.ds(pl.multiple_of((low ^ r) * columns, columns), columns)]


def stack_kernel(after_ref, *refs):
    del after_ref
    for r, ref in enumerate(refs[:-1]):
        refs[-1][r] = ref[...]


def columns_kernel(blocks, *refs):
    parts, out_ref = refs[:blocks], refs[blocks]
    per = parts[0].shape[0]
    low = lax.axis_index("seq") % per
    for i in range(blocks):
        for r in range(per):
            out_ref[(lax.axis_index("head") ^ i) * per + (low ^ r)] = parts[i][r]


def local_grad_kernel(
    bits, gt_ref, qh_ref, kh_ref, vh_ref, pt_ref, lam_ref, after_ref, *refs
):
    del after_ref
    states, (dq_ref, dk_ref, dv_ref) = refs[:bits], refs[bits:]
    heads_dev, rows, head_dim = qh_ref.shape
    for h in range(heads_dev):
        gt = gt_ref[h * head_dim : (h + 1) * head_dim, :]
        g32 = gt.astype(F32)
        dpt = (mm(vh_ref[h], gt, NN) * weight_of(lam_ref, h, rows)).astype(BF)
        dk_ref[h] = mm(dpt, qh_ref[h], NN)
        dv_ref[h] = mm(pt_ref[h], gt, NT)
        dq = mm(dpt, kh_ref[h], TN)
        for b in range(bits):
            gw = (g32 * upper_weight(lam_ref, b, h, rows)).astype(BF)
            dq = dq + mm(gw, states[b][h], TT)
        dq_ref[h] = dq


def query_grad_kernel(top, gt_ref, lam_ref, dql_ref, state_ref, after_ref, dq_ref):
    del after_ref
    heads_dev, rows, head_dim = dql_ref.shape
    for h in range(heads_dev):
        g32 = gt_ref[h * head_dim : (h + 1) * head_dim, :].astype(F32)
        gw = (g32 * upper_weight(lam_ref, top, h, rows)).astype(BF)
        dq_ref[:, h, :] = dql_ref[h] + mm(gw, state_ref[h], TT)


def later_grad_kernel(top, kh_ref, vh_ref, dkl_ref, dvl_ref, after_ref, *refs):
    del after_ref
    landed, (dk_ref, dv_ref) = refs[:-2], refs[-2:]
    for h in range(kh_ref.shape[0]):
        late = landed_sum(top, [ref[h] for ref in landed]).astype(BF)
        dk_ref[:, h, :] = dkl_ref[h] + mm(vh_ref[h], late, NN)
        dv_ref[:, h, :] = dvl_ref[h] + mm(kh_ref[h], late, NT)


def share_kernel(blocks, att_ref, w_ref, *refs):
    send_ref, kept_ref = refs[-2:]
    width = send_ref.shape[2]
    for i in range(blocks):
        out = send_ref if i % 2 else kept_ref
        column = pl.multiple_of((lax.axis_index("head") ^ i) * width, width)
        out[i // 2] = mm(att_ref[...], w_ref[:, pl.ds(column, width)], NN).astype(out.dtype)


def ring_owner(place, offset, devices):
    at = jnp.where(place % 2 == 0, place // 2, devices - 1 - place // 2)
    at = (at + offset + devices) % devices
    return jnp.where(at < devices // 2, 2 * at, 2 * (devices - 1 - at) + 1)


def proj_kernel(offsets, devices, first, cols_ref, *refs):
    total = None if first else refs[len(offsets)][...]
    for i, (offset, low, high) in enumerate(offsets):
        owner = ring_owner(lax.axis_index("seq"), offset, devices)
        product = mm(refs[i][...], cols_ref[owner, low:high, :], TN)
        total = product if total is None else total + product
    refs[-1][...] = total


def last_kernel(
    offset, devices, cols_ref, low_ref, high_ref, total_ref, after_ref, out_ref, held
):
    del after_ref
    half, block = low_ref.shape[0], out_ref.shape[0]
    at = pl.ds(pl.multiple_of(pl.program_id(0) * block, block), block)
    held[:half] = low_ref[:, at]
    held[half:] = high_ref[:, at]
    owner = ring_owner(lax.axis_index("seq"), offset, devices)
    out_ref[...] = total_ref[at, :] + mm(held[...], cols_ref[owner], TN)


def body(queries, keys, values, level_weights, out_proj, out_grad):
    rows, heads_dev, head_dim = queries.shape
    width = heads_dev * head_dim
    devices = lax.axis_size("seq")
    seq_bits = devices.bit_length() - 1
    heads = lax.axis_size("head")
    head_bits = heads.bit_length() - 1
    columns_dev = out_proj.shape[1] // devices

    head_state = like((heads_dev, head_dim, head_dim), BF)
    pinned_state = pltpu.VMEM((heads_dev, head_dim, head_dim), BF)
    per_head = pltpu.VMEM((heads_dev, rows, head_dim), BF)
    per_head_f32 = pltpu.VMEM((heads_dev, rows, head_dim), F32)
    flops_head = 2 * heads_dev * rows * rows * head_dim
    moved_head = 2 * rows * width
    top = seq_bits - 1

    own_state, kh, vh, own_grad = pl.pallas_call(
        state_kernel,
        out_shape=(head_state, per_head, per_head, like(out_grad.shape, BF)),
        in_specs=[ANY] * 3,
        out_specs=(VMEM,) * 4,
        scratch_shapes=[
            pltpu.VMEM(keys.shape, F32),
            pltpu.VMEM(keys.shape, F32),
            pltpu.SemaphoreType.DMA((3,)),
        ],
        compiler_params=PARAMS,
        cost_estimate=cost(flops_head, 7 * moved_head),
    )(hbm(keys), hbm(values), hbm(out_grad))

    def to_group(block, i):
        return lax.ppermute(block, "head", [(at, at ^ i) for at in range(heads)])

    def every_group(block):
        blocks = {0: block}
        for digit in reversed(range(head_bits)):
            for i in sorted(blocks):
                blocks[i ^ 1 << digit] = to_group(blocks[i], 1 << digit)
        return [blocks[i] for i in range(heads)]

    grad_blocks = [own_grad] + [to_group(own_grad, i) for i in range(1, heads)]

    per = devices // heads
    route = [
        ((high * per + low) * heads + group_at, (group_at * per + low) * heads + high)
        for high in range(heads)
        for low in range(per)
        for group_at in range(heads)
    ]
    turned = lax.ppermute(out_grad, ("seq", "head"), route)
    probs_t, att_local, qh, qw, lam, w = pl.pallas_call(
        local_kernel,
        out_shape=(
            pltpu.VMEM((heads_dev, rows, rows), BF),
            per_head_f32,
            per_head,
            pltpu.VMEM((seq_bits, heads_dev, rows, head_dim), BF),
            pltpu.VMEM(level_weights.shape, F32),
            pltpu.VMEM(out_proj.shape, BF),
        ),
        in_specs=[ANY, VMEM, VMEM, ANY, ANY],
        out_specs=(VMEM,) * 6,
        scratch_shapes=[
            pltpu.VMEM(queries.shape, F32),
            pltpu.VMEM((rows, rows), F32),
            pltpu.SemaphoreType.DMA((10,)),
        ],
        compiler_params=PARAMS,
        cost_estimate=cost(2 * flops_head, 12 * moved_head),
    )(hbm(queries), kh, vh, hbm(level_weights), hbm(out_proj))

    chunks = pl.pallas_call(
        chunk_kernel,
        out_shape=(like((rows, columns_dev), BF),) * per,
        in_specs=[VMEM, ANY],
        out_specs=(VMEM,) * per,
        compiler_params=PARAMS,
        cost_estimate=cost(0, 2 * moved_head),
    )(turned, qw)
    own_chunks = chunks
    chunks = [chunks[0]] + [
        lax.ppermute(chunks[r], "seq", [(at, at ^ r) for at in range(devices)])
        for r in range(1, per)
    ]
    partner_states = []
    running, arrived = own_state, None
    for digit in range(top):
        if arrived is not None:
            running = pl.pallas_call(
                running_kernel,
                out_shape=head_state,
                in_specs=[VMEM] * 2 + [ANY],
                out_specs=VMEM,
                compiler_params=PARAMS,
                cost_estimate=cost(0, 3 * moved_head),
            )(running, arrived, own_chunks[-1])
        arrived = across(running, "seq", digit)
        partner_states.append(arrived)

    gt, *grad_sums = pl.pallas_call(
        functools.partial(cotangent_kernel, heads, seq_bits),
        out_shape=(pltpu.VMEM((width, rows), BF),) + (pinned_state,) * seq_bits,
        in_specs=[VMEM] * (heads + 2) + [ANY],
        out_specs=(VMEM,) * (1 + seq_bits),
        compiler_params=PARAMS,
        cost_estimate=cost(2 * rows * width * out_proj.shape[1], 2 * width * out_proj.shape[1]),
    )(*grad_blocks, w, qw, own_chunks[-1])

    stacked = pl.pallas_call(
        stack_kernel,
        out_shape=like((per, rows, columns_dev), BF),
        in_specs=[ANY] + [VMEM] * per,
        out_specs=VMEM,
        compiler_params=PARAMS,
        cost_estimate=cost(0, 2 * moved_head),
    )(gt, *chunks)
    column_blocks = every_group(stacked)

    meeting = pl.pallas_call(
        functools.partial(meet_kernel, top)
        if arrived is not None
        else lambda after_ref, grad_ref, running_ref, out_ref: meet_kernel(
            top, after_ref, grad_ref, running_ref, None, out_ref
        ),
        out_shape=head_state,
        in_specs=[ANY] + [VMEM] * (2 if arrived is None else 3),
        out_specs=VMEM,
        compiler_params=PARAMS,
        cost_estimate=cost(0, 4 * moved_head),
    )(stacked, grad_sums[top], running, *([] if arrived is None else [arrived]))
    landed = [across(meeting, "seq", top)]
    partner_states.append(landed[0])

    grad_columns = pl.pallas_call(
        functools.partial(columns_kernel, heads),
        out_shape=pltpu.VMEM((devices, rows, columns_dev), BF),
        in_specs=[VMEM] * heads,
        out_specs=VMEM,
        compiler_params=PARAMS,
        cost_estimate=cost(0, 8 * moved_head),
    )(*column_blocks)

    query_local, key_local, value_local = pl.pallas_call(
        functools.partial(local_grad_kernel, top),
        out_shape=(per_head_f32,) * 3,
        in_specs=[VMEM] * 6 + [ANY] + [VMEM] * top,
        out_specs=(VMEM,) * 3,
        compiler_params=PARAMS,
        cost_estimate=cost((4 + top) * flops_head, 14 * moved_head),
    )(gt, qh, kh, vh, probs_t, lam, meeting, *partner_states[:top])

    attended = pl.pallas_call(
        functools.partial(attended_kernel, seq_bits),
        out_shape=like((rows, width), BF),
        in_specs=[VMEM] * (2 + seq_bits) + [ANY] * heads,
        out_specs=VMEM,
        compiler_params=PARAMS,
        cost_estimate=cost(seq_bits * flops_head, 8 * moved_head),
    )(att_local, qw, *partner_states, key_local, *column_blocks[1:])

    first_pending = attended
    for digit in reversed(range(top)):
        outgoing = pl.pallas_call(
            functools.partial(pending_kernel, top),
            out_shape=head_state,
            in_specs=[VMEM, ANY] + [VMEM] * len(landed),
            out_specs=VMEM,
            compiler_params=PARAMS,
            cost_estimate=cost(0, 4 * moved_head),
        )(grad_sums[digit], attended, *landed)
        if len(landed) == 1:
            first_pending = outgoing
        landed.append(across(outgoing, "seq", digit))

    query_grad = pl.pallas_call(
        functools.partial(query_grad_kernel, top),
        out_shape=like((rows, heads_dev, head_dim), F32),
        in_specs=[VMEM] * 4 + [ANY],
        out_specs=VMEM,
        compiler_params=PARAMS,
        cost_estimate=cost(flops_head, 6 * moved_head),
    )(gt, lam, query_local, partner_states[top], attended)

    send, kept = pl.pallas_call(
        functools.partial(share_kernel, heads),
        out_shape=(like((heads // 2, rows, width), BF), like((heads // 2, rows, width), F32)),
        in_specs=[VMEM, VMEM, ANY, ANY, ANY],
        out_specs=(VMEM,) * 2,
        compiler_params=PARAMS,
        cost_estimate=cost(2 * rows * width * out_proj.shape[1], 2 * width * out_proj.shape[1]),
    )(attended, w, first_pending, hbm(query_grad), grad_columns)
    for digit in range(head_bits):
        kept = kept + to_group(send, 1 << digit).astype(F32)
        if digit < head_bits - 1:
            send, kept = kept[1::2].astype(BF), kept[0::2]
    mixed = kept[0].astype(BF)

    ring = list(range(0, devices, 2)) + list(range(devices - 1, 0, -2))
    forward = [(ring[i], ring[(i + 1) % devices]) for i in range(devices)]
    backward = [(b, a) for a, b in forward]

    def accumulate(total, blocks, offsets):
        operands = blocks if total is None else blocks + [total]
        return pl.pallas_call(
            functools.partial(proj_kernel, offsets, devices, total is None),
            out_shape=pltpu.VMEM((width, columns_dev), F32),
            in_specs=[VMEM] * (1 + len(operands)),
            out_specs=VMEM,
            compiler_params=PARAMS,
            cost_estimate=cost(
                2 * len(blocks) * rows * width * columns_dev, 4 * width * columns_dev
            ),
        )(grad_columns, *operands)

    blocks, offsets = [attended], [(0, 0, rows)]
    ahead = behind = attended
    half, steps, total = rows // 2, devices // 2, None
    for step in range(1, steps):
        ahead = lax.ppermute(ahead, "seq", forward)
        behind = lax.ppermute(behind, "seq", backward)
        blocks += [ahead, behind]
        offsets += [(-step, 0, rows), (step, 0, rows)]
        if step == steps - 2:
            total = accumulate(None, blocks, offsets)
            blocks, offsets = [], []
    if blocks:
        total = accumulate(total, blocks, offsets)
    last = [
        lax.ppermute(ahead[:half], "seq", forward),
        lax.ppermute(behind[half:], "seq", backward),
    ]
    key_grad, value_grad = pl.pallas_call(
        functools.partial(later_grad_kernel, top),
        out_shape=(like((rows, heads_dev, head_dim), F32),) * 2,
        in_specs=[VMEM] * 4 + [ANY] + [VMEM] * seq_bits,
        out_specs=(VMEM,) * 2,
        compiler_params=PARAMS,
        cost_estimate=cost(2 * flops_head, 11 * moved_head),
    )(kh, vh, key_local, value_local, total, *landed)
    quarter_rows = width // 4
    proj_grad = pl.pallas_call(
        functools.partial(last_kernel, steps, devices),
        out_shape=like((width, columns_dev), F32),
        grid=(4,),
        in_specs=[
            VMEM,
            VMEM,
            VMEM,
            VMEM,
            ANY,
        ],
        out_specs=pl.BlockSpec((quarter_rows, columns_dev), lambda i: (i, 0)),
        scratch_shapes=[pltpu.VMEM((rows, quarter_rows), BF)],
        compiler_params=PARAMS,
        cost_estimate=cost(2 * rows * width * columns_dev, 8 * width * columns_dev),
    )(grad_columns, *last, total, hbm(key_grad))
    return (mixed, query_grad, key_grad, value_grad, proj_grad)


def solution(mesh):
    placed = (
        P("seq", "head", None),
        P("seq", "head", None),
        P("seq", "head", None),
        P(None, "head", "seq"),
        P("head", None),
        P("seq", "head"),
    )
    return jax.shard_map(
        body,
        mesh=mesh,
        in_specs=placed,
        out_specs=(
            P("seq", "head"),
            P("seq", "head", None),
            P("seq", "head", None),
            P("seq", "head", None),
            P("head", "seq"),
        ),
        check_vma=False,
    )
```

```python
import functools

import jax
import jax.numpy as jnp
from jax import lax
from jax.experimental import pallas as pl
from jax.experimental.pallas import tpu as pltpu
from jax.sharding import PartitionSpec as P

CH = 64
BF = jnp.bfloat16
F32 = jnp.float32
NN = (((1,), (0,)), ((), ()))
NT = (((1,), (1,)), ((), ()))
TN = (((0,), (0,)), ((), ()))
TT = (((0,), (1,)), ((), ()))
VMEM = pl.BlockSpec(memory_space=pltpu.VMEM)
ANY = pl.BlockSpec(memory_space=pl.ANY)
PARAMS = pltpu.CompilerParams(vmem_limit_bytes=14 * 2**20)


def mm(a, b, dims):
    return lax.dot_general(a, b, dims, preferred_element_type=F32)


def cost(flops, moved):
    return pl.CostEstimate(flops=flops, bytes_accessed=moved, transcendentals=0)


def like(shape, dtype):
    return jax.ShapeDtypeStruct(shape, dtype)


def across(block, axis, stride, up_only=False, down_only=False):
    count = lax.axis_size(axis)
    route = []
    for low in range(count):
        high = low | 1 << stride
        if high != low and high < count:
            if not down_only:
                route.append((low, high))
            if not up_only:
                route.append((high, low))
    return lax.ppermute(block, axis, route)


def hbm(array):
    return pltpu.with_memory_space_constraint(array, pltpu.HBM)


def state_kernel(k_hbm, v_hbm, grad_hbm, s_ref, kh_ref, vh_ref, grad_ref, k_ref, v_ref, sems):
    copies = [
        pltpu.make_async_copy(k_hbm, k_ref, sems.at[0]),
        pltpu.make_async_copy(v_hbm, v_ref, sems.at[1]),
        pltpu.make_async_copy(grad_hbm, grad_ref, sems.at[2]),
    ]
    for copy in copies:
        copy.start()
    for copy in copies[:2]:
        copy.wait()
    for h in range(k_ref.shape[1]):
        k = k_ref[:, h, :].astype(BF)
        v = v_ref[:, h, :].astype(BF)
        kh_ref[h] = k
        vh_ref[h] = v
        s_ref[h] = mm(k, v, TN).astype(BF)
    copies[2].wait()


def weight_of(lam_ref, h, rows):
    local_bits = (rows // CH).bit_length() - 1
    s = lax.broadcasted_iota(jnp.int32, (rows, rows), 0)
    t = lax.broadcasted_iota(jnp.int32, (rows, rows), 1)
    differ = (s // CH) ^ (t // CH)
    weight = jnp.broadcast_to(lam_ref[0, h : h + 1, :], (rows, rows))
    for digit in range(local_bits):
        weight = jnp.where(differ >= 1 << digit, lam_ref[1 + digit, h : h + 1, :], weight)
    return jnp.where(s <= t, weight, 0.0)


def upper_weight(lam_ref, b, h, rows):
    local_bits = (rows // CH).bit_length() - 1
    upper = (lax.axis_index("seq") >> b & 1).astype(F32)
    return lam_ref[1 + local_bits + b, h : h + 1, :] * upper


def local_kernel(q_hbm, kh_ref, vh_ref, lam_hbm, w_hbm, *refs):
    pt_ref, att_ref, qh_ref, qw_ref, lam_ref, w_ref, q_ref, lam_rows, sems = refs
    pieces = sems.shape[0] - 2
    share = w_hbm.shape[0] // pieces
    copies = [
        pltpu.make_async_copy(q_hbm, q_ref, sems.at[0]),
        pltpu.make_async_copy(lam_hbm, lam_ref, sems.at[1]),
    ]
    for i in range(pieces):
        piece = pl.ds(i * share, share)
        copies.append(pltpu.make_async_copy(w_hbm.at[piece], w_ref.at[piece], sems.at[2 + i]))
    for copy in copies:
        copy.start()
    for copy in copies[:2]:
        copy.wait()
    rows, heads_dev, _ = q_ref.shape
    bits = qw_ref.shape[0]
    lam_rows[...] = jnp.zeros_like(lam_rows)
    for b in range(bits):
        for h in range(heads_dev):
            at = b * heads_dev + h
            lam_rows[at : at + 1, :] = upper_weight(lam_ref, b, h, rows)
    lam_columns = lam_rows[...].T
    for h in range(heads_dev):
        q32 = q_ref[:, h, :]
        q = q32.astype(BF)
        qh_ref[h] = q
        for b in range(bits):
            at = b * heads_dev + h
            qw_ref[b, h] = (q32 * lam_columns[:, at : at + 1]).astype(BF)
        pt = (mm(kh_ref[h], q, NT) * weight_of(lam_ref, h, rows)).astype(BF)
        pt_ref[h] = pt
        att_ref[h] = mm(pt, vh_ref[h], TN)
    for copy in copies[2:]:
        copy.wait()


def attended_kernel(bits, att_ref, qw_ref, *refs):
    states, out_ref = refs[:bits], refs[-1]
    heads_dev, _, head_dim = att_ref.shape
    for h in range(heads_dev):
        total = att_ref[h]
        for b in range(bits):
            total = total + mm(qw_ref[b, h], states[b][h], NN)
        out_ref[:, h * head_dim : (h + 1) * head_dim] = total.astype(BF)


def cotangent_kernel(blocks, bits, *refs):
    parts, (w_ref, qw_ref, _, gt_ref), sums = (
        refs[:blocks],
        refs[blocks : blocks + 4],
        refs[blocks + 4 :],
    )
    deep = parts[0].shape[1]
    _, heads_dev, _, head_dim = qw_ref.shape
    total = None
    for i in range(blocks):
        column = pl.multiple_of((lax.axis_index("head") ^ i) * deep, deep)
        product = mm(w_ref[:, pl.ds(column, deep)], parts[i][...], NT)
        total = product if total is None else total + product
    for h in range(heads_dev):
        gt = total[h * head_dim : (h + 1) * head_dim].astype(BF)
        gt_ref[h * head_dim : (h + 1) * head_dim, :] = gt
        for b in range(bits):
            sums[b][h] = mm(gt, qw_ref[b, h], NN).astype(BF)


def running_kernel(running_ref, arrived_ref, *refs):
    refs[-1][...] = (running_ref[...].astype(F32) + arrived_ref[...].astype(F32)).astype(BF)


def meet_kernel(top, grad_ref, running_ref, arrived_ref, out_ref):
    upper = (lax.axis_index("seq") >> top & 1) == 1
    running = running_ref[...].astype(F32)
    if arrived_ref is not None:
        running = running + arrived_ref[...].astype(F32)
    out_ref[...] = jnp.where(upper, grad_ref[...], running.astype(BF))


def landed_sum(top, landed):
    upper = (lax.axis_index("seq") >> top & 1) == 1
    total = jnp.where(upper, 0.0, landed[0].astype(F32))
    for block in landed[1:]:
        total = total + block.astype(F32)
    return total


def pending_kernel(top, own_ref, after_ref, *refs):
    del after_ref
    landed, out_ref = [ref[...] for ref in refs[:-1]], refs[-1]
    out_ref[...] = (own_ref[...].astype(F32) + landed_sum(top, landed)).astype(BF)


def turned_group(high, group, bits):
    turned = high >> 1 | (high & 1) << bits - 1
    return turned ^ ((group >> bits - 1 ^ group) & 1) << bits - 1


def turned_high(turned, group, bits):
    turned = turned ^ ((group >> bits - 1 ^ group) & 1) << bits - 1
    return (turned << 1 & (1 << bits) - 1) | turned >> bits - 1


def chunk_kernel(block_ref, after_ref, *outs):
    del after_ref
    columns = outs[0].shape[1]
    low = lax.axis_index("seq") % len(outs)
    for r, out in enumerate(outs):
        out[...] = block_ref[:, pl.ds(pl.multiple_of((low ^ r) * columns, columns), columns)]


def stack_kernel(after_ref, *refs):
    del after_ref
    for r, ref in enumerate(refs[:-1]):
        refs[-1][r] = ref[...]


def columns_kernel(blocks, *refs):
    parts, out_ref = refs[:blocks], refs[blocks]
    per = parts[0].shape[0]
    bits = blocks.bit_length() - 1
    low = lax.axis_index("seq") % per
    for i in range(blocks):
        high = turned_high(lax.axis_index("head") ^ i, lax.axis_index("seq") // per, bits)
        for r in range(per):
            out_ref[high * per + (low ^ r)] = parts[i][r]


def local_grad_kernel(
    bits, gt_ref, qh_ref, kh_ref, vh_ref, pt_ref, lam_ref, after_ref, *refs
):
    del after_ref
    states, (dq_ref, dk_ref, dv_ref) = refs[:bits], refs[bits:]
    heads_dev, rows, head_dim = qh_ref.shape
    for h in range(heads_dev):
        gt = gt_ref[h * head_dim : (h + 1) * head_dim, :]
        g32 = gt.astype(F32)
        dpt = (mm(vh_ref[h], gt, NN) * weight_of(lam_ref, h, rows)).astype(BF)
        dk_ref[h] = mm(dpt, qh_ref[h], NN)
        dv_ref[h] = mm(pt_ref[h], gt, NT)
        dq = mm(dpt, kh_ref[h], TN)
        for b in range(bits):
            gw = (g32 * upper_weight(lam_ref, b, h, rows)).astype(BF)
            dq = dq + mm(gw, states[b][h], TT)
        dq_ref[h] = dq


def query_grad_kernel(top, gt_ref, lam_ref, dql_ref, state_ref, after_ref, dq_ref):
    del after_ref
    heads_dev, rows, head_dim = dql_ref.shape
    for h in range(heads_dev):
        g32 = gt_ref[h * head_dim : (h + 1) * head_dim, :].astype(F32)
        gw = (g32 * upper_weight(lam_ref, top, h, rows)).astype(BF)
        dq_ref[:, h, :] = dql_ref[h] + mm(gw, state_ref[h], TT)


def later_grad_kernel(top, kh_ref, vh_ref, dkl_ref, dvl_ref, after_ref, *refs):
    del after_ref
    landed, (dk_ref, dv_ref) = refs[:-2], refs[-2:]
    for h in range(kh_ref.shape[0]):
        late = landed_sum(top, [ref[h] for ref in landed]).astype(BF)
        dk_ref[:, h, :] = dkl_ref[h] + mm(vh_ref[h], late, NN)
        dv_ref[:, h, :] = dvl_ref[h] + mm(kh_ref[h], late, NT)


def share_kernel(blocks, att_ref, w_ref, *refs):
    send_ref, kept_ref = refs[-2:]
    width = send_ref.shape[2]
    for i in range(blocks):
        out = send_ref if i % 2 else kept_ref
        column = pl.multiple_of((lax.axis_index("head") ^ i) * width, width)
        out[i // 2] = mm(att_ref[...], w_ref[:, pl.ds(column, width)], NN).astype(out.dtype)


def ring_owner(place, offset, devices):
    at = jnp.where(place % 2 == 0, place // 2, devices - 1 - place // 2)
    at = (at + offset + devices) % devices
    return jnp.where(at < devices // 2, 2 * at, 2 * (devices - 1 - at) + 1)


def proj_kernel(offsets, devices, first, cols_ref, *refs):
    total = None if first else refs[len(offsets)][...]
    for i, (offset, low, high) in enumerate(offsets):
        owner = ring_owner(lax.axis_index("seq"), offset, devices)
        product = mm(refs[i][...], cols_ref[owner, low:high, :], TN)
        total = product if total is None else total + product
    refs[-1][...] = total


def last_kernel(
    offset, devices, cols_ref, low_ref, high_ref, total_ref, after_ref, out_ref, held
):
    del after_ref
    half, block = low_ref.shape[0], out_ref.shape[0]
    at = pl.ds(pl.multiple_of(pl.program_id(0) * block, block), block)
    held[:half] = low_ref[:, at]
    held[half:] = high_ref[:, at]
    owner = ring_owner(lax.axis_index("seq"), offset, devices)
    out_ref[...] = total_ref[at, :] + mm(held[...], cols_ref[owner], TN)


def body(queries, keys, values, level_weights, out_proj, out_grad):
    rows, heads_dev, head_dim = queries.shape
    width = heads_dev * head_dim
    devices = lax.axis_size("seq")
    seq_bits = devices.bit_length() - 1
    heads = lax.axis_size("head")
    head_bits = heads.bit_length() - 1
    columns_dev = out_proj.shape[1] // devices

    head_state = like((heads_dev, head_dim, head_dim), BF)
    pinned_state = pltpu.VMEM((heads_dev, head_dim, head_dim), BF)
    per_head = pltpu.VMEM((heads_dev, rows, head_dim), BF)
    per_head_f32 = pltpu.VMEM((heads_dev, rows, head_dim), F32)
    flops_head = 2 * heads_dev * rows * rows * head_dim
    moved_head = 2 * rows * width
    top = seq_bits - 1

    own_state, kh, vh, own_grad = pl.pallas_call(
        state_kernel,
        out_shape=(head_state, per_head, per_head, like(out_grad.shape, BF)),
        in_specs=[ANY] * 3,
        out_specs=(VMEM,) * 4,
        scratch_shapes=[
            pltpu.VMEM(keys.shape, F32),
            pltpu.VMEM(keys.shape, F32),
            pltpu.SemaphoreType.DMA((3,)),
        ],
        compiler_params=PARAMS,
        cost_estimate=cost(flops_head, 7 * moved_head),
    )(hbm(keys), hbm(values), hbm(out_grad))

    def to_group(block, i):
        return lax.ppermute(block, "head", [(at, at ^ i) for at in range(heads)])

    def every_group(block):
        blocks = {0: block}
        for digit in reversed(range(head_bits)):
            for i in sorted(blocks):
                blocks[i ^ 1 << digit] = to_group(blocks[i], 1 << digit)
        return [blocks[i] for i in range(heads)]

    grad_blocks = [own_grad] + [to_group(own_grad, i) for i in range(1, heads)]

    per = devices // heads
    route = [
        (
            (high * per + low) * heads + group_at,
            (group_at * per + low) * heads + turned_group(high, group_at, head_bits),
        )
        for high in range(heads)
        for low in range(per)
        for group_at in range(heads)
    ]
    turned = lax.ppermute(out_grad, ("seq", "head"), route)
    probs_t, att_local, qh, qw, lam, w = pl.pallas_call(
        local_kernel,
        out_shape=(
            pltpu.VMEM((heads_dev, rows, rows), BF),
            per_head_f32,
            per_head,
            pltpu.VMEM((seq_bits, heads_dev, rows, head_dim), BF),
            pltpu.VMEM(level_weights.shape, F32),
            pltpu.VMEM(out_proj.shape, BF),
        ),
        in_specs=[ANY, VMEM, VMEM, ANY, ANY],
        out_specs=(VMEM,) * 6,
        scratch_shapes=[
            pltpu.VMEM(queries.shape, F32),
            pltpu.VMEM((rows, rows), F32),
            pltpu.SemaphoreType.DMA((10,)),
        ],
        compiler_params=PARAMS,
        cost_estimate=cost(2 * flops_head, 12 * moved_head),
    )(hbm(queries), kh, vh, hbm(level_weights), hbm(out_proj))

    chunks = pl.pallas_call(
        chunk_kernel,
        out_shape=(like((rows, columns_dev), BF),) * per,
        in_specs=[VMEM, ANY],
        out_specs=(VMEM,) * per,
        compiler_params=PARAMS,
        cost_estimate=cost(0, 2 * moved_head),
    )(turned, qw)
    own_chunks = chunks
    chunks = [chunks[0]] + [
        lax.ppermute(chunks[r], "seq", [(at, at ^ r) for at in range(devices)])
        for r in range(1, per)
    ]
    partner_states = []
    running, arrived = own_state, None
    for digit in range(top):
        if arrived is not None:
            running = pl.pallas_call(
                running_kernel,
                out_shape=head_state,
                in_specs=[VMEM] * 2 + [ANY],
                out_specs=VMEM,
                compiler_params=PARAMS,
                cost_estimate=cost(0, 3 * moved_head),
            )(running, arrived, own_chunks[-1])
        arrived = across(running, "seq", digit)
        partner_states.append(arrived)

    gt, *grad_sums = pl.pallas_call(
        functools.partial(cotangent_kernel, heads, seq_bits),
        out_shape=(pltpu.VMEM((width, rows), BF),) + (pinned_state,) * seq_bits,
        in_specs=[VMEM] * (heads + 2) + [ANY],
        out_specs=(VMEM,) * (1 + seq_bits),
        compiler_params=PARAMS,
        cost_estimate=cost(2 * rows * width * out_proj.shape[1], 2 * width * out_proj.shape[1]),
    )(*grad_blocks, w, qw, own_chunks[-1])

    meeting = pl.pallas_call(
        functools.partial(meet_kernel, top)
        if arrived is not None
        else lambda grad_ref, running_ref, out_ref: meet_kernel(
            top, grad_ref, running_ref, None, out_ref
        ),
        out_shape=head_state,
        in_specs=[VMEM] * (2 if arrived is None else 3),
        out_specs=VMEM,
        compiler_params=PARAMS,
        cost_estimate=cost(0, 4 * moved_head),
    )(grad_sums[top], running, *([] if arrived is None else [arrived]))
    landed = [across(meeting, "seq", top)]
    partner_states.append(landed[0])

    stacked = pl.pallas_call(
        stack_kernel,
        out_shape=like((per, rows, columns_dev), BF),
        in_specs=[ANY] + [VMEM] * per,
        out_specs=VMEM,
        compiler_params=PARAMS,
        cost_estimate=cost(0, 2 * moved_head),
    )(meeting, *chunks)
    column_blocks = [stacked] + [to_group(stacked, i) for i in range(1, heads)]

    grad_columns = pl.pallas_call(
        functools.partial(columns_kernel, heads),
        out_shape=pltpu.VMEM((devices, rows, columns_dev), BF),
        in_specs=[VMEM] * heads,
        out_specs=VMEM,
        compiler_params=PARAMS,
        cost_estimate=cost(0, 8 * moved_head),
    )(*column_blocks)

    query_local, key_local, value_local = pl.pallas_call(
        functools.partial(local_grad_kernel, top),
        out_shape=(per_head_f32,) * 3,
        in_specs=[VMEM] * 6 + [ANY] + [VMEM] * top,
        out_specs=(VMEM,) * 3,
        compiler_params=PARAMS,
        cost_estimate=cost((4 + top) * flops_head, 14 * moved_head),
    )(gt, qh, kh, vh, probs_t, lam, meeting, *partner_states[:top])

    attended = pl.pallas_call(
        functools.partial(attended_kernel, seq_bits),
        out_shape=like((rows, width), BF),
        in_specs=[VMEM] * (2 + seq_bits) + [ANY] * 2,
        out_specs=VMEM,
        compiler_params=PARAMS,
        cost_estimate=cost(seq_bits * flops_head, 8 * moved_head),
    )(att_local, qw, *partner_states, key_local, stacked)

    first_pending = attended
    for digit in reversed(range(top)):
        outgoing = pl.pallas_call(
            functools.partial(pending_kernel, top),
            out_shape=head_state,
            in_specs=[VMEM, ANY] + [VMEM] * len(landed),
            out_specs=VMEM,
            compiler_params=PARAMS,
            cost_estimate=cost(0, 4 * moved_head),
        )(grad_sums[digit], attended, *landed)
        if len(landed) == 1:
            first_pending = outgoing
        landed.append(across(outgoing, "seq", digit))

    query_grad = pl.pallas_call(
        functools.partial(query_grad_kernel, top),
        out_shape=like((rows, heads_dev, head_dim), F32),
        in_specs=[VMEM] * 4 + [ANY],
        out_specs=VMEM,
        compiler_params=PARAMS,
        cost_estimate=cost(flops_head, 6 * moved_head),
    )(gt, lam, query_local, partner_states[top], attended)

    send, kept = pl.pallas_call(
        functools.partial(share_kernel, heads),
        out_shape=(like((heads // 2, rows, width), BF), like((heads // 2, rows, width), F32)),
        in_specs=[VMEM, VMEM, ANY, ANY, ANY],
        out_specs=(VMEM,) * 2,
        compiler_params=PARAMS,
        cost_estimate=cost(2 * rows * width * out_proj.shape[1], 2 * width * out_proj.shape[1]),
    )(attended, w, first_pending, hbm(query_grad), grad_columns)
    for digit in range(head_bits):
        kept = kept + to_group(send, 1 << digit).astype(F32)
        if digit < head_bits - 1:
            send, kept = kept[1::2].astype(BF), kept[0::2]
    mixed = kept[0].astype(BF)

    ring = list(range(0, devices, 2)) + list(range(devices - 1, 0, -2))
    forward = [(ring[i], ring[(i + 1) % devices]) for i in range(devices)]
    backward = [(b, a) for a, b in forward]

    def accumulate(total, blocks, offsets):
        operands = blocks if total is None else blocks + [total]
        return pl.pallas_call(
            functools.partial(proj_kernel, offsets, devices, total is None),
            out_shape=pltpu.VMEM((width, columns_dev), F32),
            in_specs=[VMEM] * (1 + len(operands)),
            out_specs=VMEM,
            compiler_params=PARAMS,
            cost_estimate=cost(
                2 * len(blocks) * rows * width * columns_dev, 4 * width * columns_dev
            ),
        )(grad_columns, *operands)

    blocks, offsets = [attended], [(0, 0, rows)]
    ahead = behind = attended
    half, steps, total = rows // 2, devices // 2, None
    for step in range(1, steps):
        ahead = lax.ppermute(ahead, "seq", forward)
        behind = lax.ppermute(behind, "seq", backward)
        blocks += [ahead, behind]
        offsets += [(-step, 0, rows), (step, 0, rows)]
        if step == steps - 2:
            total = accumulate(None, blocks, offsets)
            blocks, offsets = [], []
    if blocks:
        total = accumulate(total, blocks, offsets)
    last = [
        lax.ppermute(ahead[:half], "seq", forward),
        lax.ppermute(behind[half:], "seq", backward),
    ]
    key_grad, value_grad = pl.pallas_call(
        functools.partial(later_grad_kernel, top),
        out_shape=(like((rows, heads_dev, head_dim), F32),) * 2,
        in_specs=[VMEM] * 4 + [ANY] + [VMEM] * seq_bits,
        out_specs=(VMEM,) * 2,
        compiler_params=PARAMS,
        cost_estimate=cost(2 * flops_head, 11 * moved_head),
    )(kh, vh, key_local, value_local, total, *landed)
    quarter_rows = width // 4
    proj_grad = pl.pallas_call(
        functools.partial(last_kernel, steps, devices),
        out_shape=like((width, columns_dev), F32),
        grid=(4,),
        in_specs=[
            VMEM,
            VMEM,
            VMEM,
            VMEM,
            ANY,
        ],
        out_specs=pl.BlockSpec((quarter_rows, columns_dev), lambda i: (i, 0)),
        scratch_shapes=[pltpu.VMEM((rows, quarter_rows), BF)],
        compiler_params=PARAMS,
        cost_estimate=cost(2 * rows * width * columns_dev, 8 * width * columns_dev),
    )(grad_columns, *last, total, hbm(key_grad))
    return (mixed, query_grad, key_grad, value_grad, proj_grad)


def solution(mesh):
    placed = (
        P("seq", "head", None),
        P("seq", "head", None),
        P("seq", "head", None),
        P(None, "head", "seq"),
        P("head", None),
        P("seq", "head"),
    )
    return jax.shard_map(
        body,
        mesh=mesh,
        in_specs=placed,
        out_specs=(
            P("seq", "head"),
            P("seq", "head", None),
            P("seq", "head", None),
            P("seq", "head", None),
            P("head", "seq"),
        ),
        check_vma=False,
    )
```

```python
import functools

import jax
import jax.numpy as jnp
from jax import lax
from jax.experimental import pallas as pl
from jax.experimental.pallas import tpu as pltpu
from jax.sharding import PartitionSpec as P

CH = 64
BF = jnp.bfloat16
F32 = jnp.float32
NN = (((1,), (0,)), ((), ()))
NT = (((1,), (1,)), ((), ()))
TN = (((0,), (0,)), ((), ()))
TT = (((0,), (1,)), ((), ()))
VMEM = pl.BlockSpec(memory_space=pltpu.VMEM)
ANY = pl.BlockSpec(memory_space=pl.ANY)
PARAMS = pltpu.CompilerParams(vmem_limit_bytes=14 * 2**20)


def mm(a, b, dims):
    return lax.dot_general(a, b, dims, preferred_element_type=F32)


def cost(flops, moved):
    return pl.CostEstimate(flops=flops, bytes_accessed=moved, transcendentals=0)


def like(shape, dtype):
    return jax.ShapeDtypeStruct(shape, dtype)


def across(block, axis, stride, up_only=False, down_only=False):
    count = lax.axis_size(axis)
    route = []
    for low in range(count):
        high = low | 1 << stride
        if high != low and high < count:
            if not down_only:
                route.append((low, high))
            if not up_only:
                route.append((high, low))
    return lax.ppermute(block, axis, route)


def hbm(array):
    return pltpu.with_memory_space_constraint(array, pltpu.HBM)


def state_kernel(k_hbm, v_hbm, grad_hbm, s_ref, kh_ref, vh_ref, grad_ref, k_ref, v_ref, sems):
    copies = [
        pltpu.make_async_copy(k_hbm, k_ref, sems.at[0]),
        pltpu.make_async_copy(v_hbm, v_ref, sems.at[1]),
        pltpu.make_async_copy(grad_hbm, grad_ref, sems.at[2]),
    ]
    for copy in copies:
        copy.start()
    for copy in copies[:2]:
        copy.wait()
    for h in range(k_ref.shape[1]):
        k = k_ref[:, h, :].astype(BF)
        v = v_ref[:, h, :].astype(BF)
        kh_ref[h] = k
        vh_ref[h] = v
        s_ref[h] = mm(k, v, TN).astype(BF)
    copies[2].wait()


def weight_of(lam_ref, h, rows):
    local_bits = (rows // CH).bit_length() - 1
    s = lax.broadcasted_iota(jnp.int32, (rows, rows), 0)
    t = lax.broadcasted_iota(jnp.int32, (rows, rows), 1)
    differ = (s // CH) ^ (t // CH)
    weight = jnp.broadcast_to(lam_ref[0, h : h + 1, :], (rows, rows))
    for digit in range(local_bits):
        weight = jnp.where(differ >= 1 << digit, lam_ref[1 + digit, h : h + 1, :], weight)
    return jnp.where(s <= t, weight, 0.0)


def upper_weight(lam_ref, b, h, rows):
    local_bits = (rows // CH).bit_length() - 1
    upper = (lax.axis_index("seq") >> b & 1).astype(F32)
    return lam_ref[1 + local_bits + b, h : h + 1, :] * upper


def local_kernel(q_hbm, kh_ref, vh_ref, lam_hbm, w_hbm, after_ref, *refs):
    del after_ref
    pt_ref, att_ref, qh_ref, qw_ref, lam_ref, w_ref, q_ref, lam_rows, sems = refs
    pieces = sems.shape[0] - 2
    share = w_hbm.shape[0] // pieces
    copies = [
        pltpu.make_async_copy(q_hbm, q_ref, sems.at[0]),
        pltpu.make_async_copy(lam_hbm, lam_ref, sems.at[1]),
    ]
    for i in range(pieces):
        piece = pl.ds(i * share, share)
        copies.append(pltpu.make_async_copy(w_hbm.at[piece], w_ref.at[piece], sems.at[2 + i]))
    for copy in copies:
        copy.start()
    for copy in copies[:2]:
        copy.wait()
    rows, heads_dev, _ = q_ref.shape
    bits = qw_ref.shape[0]
    lam_rows[...] = jnp.zeros_like(lam_rows)
    for b in range(bits):
        for h in range(heads_dev):
            at = b * heads_dev + h
            lam_rows[at : at + 1, :] = upper_weight(lam_ref, b, h, rows)
    lam_columns = lam_rows[...].T
    for h in range(heads_dev):
        q32 = q_ref[:, h, :]
        q = q32.astype(BF)
        qh_ref[h] = q
        for b in range(bits):
            at = b * heads_dev + h
            qw_ref[b, h] = (q32 * lam_columns[:, at : at + 1]).astype(BF)
        pt = (mm(kh_ref[h], q, NT) * weight_of(lam_ref, h, rows)).astype(BF)
        pt_ref[h] = pt
        att_ref[h] = mm(pt, vh_ref[h], TN)
    for copy in copies[2:]:
        copy.wait()


def attended_kernel(bits, att_ref, qw_ref, *refs):
    states, out_ref = refs[:bits], refs[-1]
    heads_dev, _, head_dim = att_ref.shape
    for h in range(heads_dev):
        total = att_ref[h]
        for b in range(bits):
            total = total + mm(qw_ref[b, h], states[b][h], NN)
        out_ref[:, h * head_dim : (h + 1) * head_dim] = total.astype(BF)


def cotangent_kernel(blocks, bits, *refs):
    parts, (w_ref, qw_ref, _, gt_ref), sums = (
        refs[:blocks],
        refs[blocks : blocks + 4],
        refs[blocks + 4 :],
    )
    deep = parts[0].shape[1]
    _, heads_dev, _, head_dim = qw_ref.shape
    total = None
    for i in range(blocks):
        column = pl.multiple_of((lax.axis_index("head") ^ i) * deep, deep)
        product = mm(w_ref[:, pl.ds(column, deep)], parts[i][...], NT)
        total = product if total is None else total + product
    for h in range(heads_dev):
        gt = total[h * head_dim : (h + 1) * head_dim].astype(BF)
        gt_ref[h * head_dim : (h + 1) * head_dim, :] = gt
        for b in range(bits):
            sums[b][h] = mm(gt, qw_ref[b, h], NN).astype(BF)


def running_kernel(running_ref, arrived_ref, *refs):
    refs[-1][...] = (running_ref[...].astype(F32) + arrived_ref[...].astype(F32)).astype(BF)


def meet_kernel(top, grad_ref, running_ref, arrived_ref, out_ref):
    upper = (lax.axis_index("seq") >> top & 1) == 1
    running = running_ref[...].astype(F32)
    if arrived_ref is not None:
        running = running + arrived_ref[...].astype(F32)
    out_ref[...] = jnp.where(upper, grad_ref[...], running.astype(BF))


def landed_sum(top, landed):
    upper = (lax.axis_index("seq") >> top & 1) == 1
    total = jnp.where(upper, 0.0, landed[0].astype(F32))
    for block in landed[1:]:
        total = total + block.astype(F32)
    return total


def pending_kernel(top, own_ref, after_ref, *refs):
    del after_ref
    landed, out_ref = [ref[...] for ref in refs[:-1]], refs[-1]
    out_ref[...] = (own_ref[...].astype(F32) + landed_sum(top, landed)).astype(BF)


def turned_group(high, group, bits):
    turned = high >> 1 | (high & 1) << bits - 1
    return turned ^ ((group >> bits - 1 ^ group) & 1) << bits - 1


def turned_high(turned, group, bits):
    turned = turned ^ ((group >> bits - 1 ^ group) & 1) << bits - 1
    return (turned << 1 & (1 << bits) - 1) | turned >> bits - 1


def chunk_kernel(block_ref, after_ref, *outs):
    del after_ref
    columns = outs[0].shape[1]
    low = lax.axis_index("seq") % len(outs)
    for r, out in enumerate(outs):
        out[...] = block_ref[:, pl.ds(pl.multiple_of((low ^ r) * columns, columns), columns)]


def stack_kernel(after_ref, *refs):
    del after_ref
    for r, ref in enumerate(refs[:-1]):
        refs[-1][r] = ref[...]


def columns_kernel(blocks, *refs):
    parts, out_ref = refs[:blocks], refs[blocks]
    per = parts[0].shape[0]
    bits = blocks.bit_length() - 1
    low = lax.axis_index("seq") % per
    for i in range(blocks):
        high = turned_high(lax.axis_index("head") ^ i, lax.axis_index("seq") // per, bits)
        for r in range(per):
            out_ref[high * per + (low ^ r)] = parts[i][r]


def local_grad_kernel(
    bits, gt_ref, qh_ref, kh_ref, vh_ref, pt_ref, lam_ref, after_ref, *refs
):
    del after_ref
    states, (dq_ref, dk_ref, dv_ref) = refs[:bits], refs[bits:]
    heads_dev, rows, head_dim = qh_ref.shape
    for h in range(heads_dev):
        gt = gt_ref[h * head_dim : (h + 1) * head_dim, :]
        g32 = gt.astype(F32)
        dpt = (mm(vh_ref[h], gt, NN) * weight_of(lam_ref, h, rows)).astype(BF)
        dk_ref[h] = mm(dpt, qh_ref[h], NN)
        dv_ref[h] = mm(pt_ref[h], gt, NT)
        dq = mm(dpt, kh_ref[h], TN)
        for b in range(bits):
            gw = (g32 * upper_weight(lam_ref, b, h, rows)).astype(BF)
            dq = dq + mm(gw, states[b][h], TT)
        dq_ref[h] = dq


def query_grad_kernel(top, gt_ref, lam_ref, dql_ref, state_ref, after_ref, dq_ref):
    del after_ref
    heads_dev, rows, head_dim = dql_ref.shape
    for h in range(heads_dev):
        g32 = gt_ref[h * head_dim : (h + 1) * head_dim, :].astype(F32)
        gw = (g32 * upper_weight(lam_ref, top, h, rows)).astype(BF)
        dq_ref[:, h, :] = dql_ref[h] + mm(gw, state_ref[h], TT)


def later_grad_kernel(top, kh_ref, vh_ref, dkl_ref, dvl_ref, after_ref, *refs):
    del after_ref
    landed, (dk_ref, dv_ref) = refs[:-2], refs[-2:]
    for h in range(kh_ref.shape[0]):
        late = landed_sum(top, [ref[h] for ref in landed]).astype(BF)
        dk_ref[:, h, :] = dkl_ref[h] + mm(vh_ref[h], late, NN)
        dv_ref[:, h, :] = dvl_ref[h] + mm(kh_ref[h], late, NT)


def share_kernel(blocks, att_ref, w_ref, *refs):
    send_ref, kept_ref = refs[-2:]
    width = send_ref.shape[2]
    for i in range(blocks):
        out = send_ref if i % 2 else kept_ref
        column = pl.multiple_of((lax.axis_index("head") ^ i) * width, width)
        out[i // 2] = mm(att_ref[...], w_ref[:, pl.ds(column, width)], NN).astype(out.dtype)


def ring_owner(place, offset, devices):
    at = jnp.where(place % 2 == 0, place // 2, devices - 1 - place // 2)
    at = (at + offset + devices) % devices
    return jnp.where(at < devices // 2, 2 * at, 2 * (devices - 1 - at) + 1)


def proj_kernel(offsets, devices, first, cols_ref, *refs):
    total = None if first else refs[len(offsets)][...]
    for i, (offset, low, high) in enumerate(offsets):
        owner = ring_owner(lax.axis_index("seq"), offset, devices)
        product = mm(refs[i][...], cols_ref[owner, low:high, :], TN)
        total = product if total is None else total + product
    refs[-1][...] = total


def last_kernel(
    offset, devices, cols_ref, low_ref, high_ref, total_ref, after_ref, out_ref, held
):
    del after_ref
    half, block = low_ref.shape[0], out_ref.shape[0]
    at = pl.ds(pl.multiple_of(pl.program_id(0) * block, block), block)
    held[:half] = low_ref[:, at]
    held[half:] = high_ref[:, at]
    owner = ring_owner(lax.axis_index("seq"), offset, devices)
    out_ref[...] = total_ref[at, :] + mm(held[...], cols_ref[owner], TN)


def body(queries, keys, values, level_weights, out_proj, out_grad):
    rows, heads_dev, head_dim = queries.shape
    width = heads_dev * head_dim
    devices = lax.axis_size("seq")
    seq_bits = devices.bit_length() - 1
    heads = lax.axis_size("head")
    head_bits = heads.bit_length() - 1
    columns_dev = out_proj.shape[1] // devices

    head_state = like((heads_dev, head_dim, head_dim), BF)
    pinned_state = pltpu.VMEM((heads_dev, head_dim, head_dim), BF)
    per_head = pltpu.VMEM((heads_dev, rows, head_dim), BF)
    per_head_f32 = pltpu.VMEM((heads_dev, rows, head_dim), F32)
    flops_head = 2 * heads_dev * rows * rows * head_dim
    moved_head = 2 * rows * width
    top = seq_bits - 1

    own_state, kh, vh, own_grad = pl.pallas_call(
        state_kernel,
        out_shape=(head_state, per_head, per_head, like(out_grad.shape, BF)),
        in_specs=[ANY] * 3,
        out_specs=(VMEM,) * 4,
        scratch_shapes=[
            pltpu.VMEM(keys.shape, F32),
            pltpu.VMEM(keys.shape, F32),
            pltpu.SemaphoreType.DMA((3,)),
        ],
        compiler_params=PARAMS,
        cost_estimate=cost(flops_head, 7 * moved_head),
    )(hbm(keys), hbm(values), hbm(out_grad))

    def to_group(block, i):
        return lax.ppermute(block, "head", [(at, at ^ i) for at in range(heads)])

    def every_group(block):
        blocks = {0: block}
        for digit in reversed(range(head_bits)):
            for i in sorted(blocks):
                blocks[i ^ 1 << digit] = to_group(blocks[i], 1 << digit)
        return [blocks[i] for i in range(heads)]

    grad_blocks = every_group(own_grad)

    per = devices // heads
    route = [
        (
            (high * per + low) * heads + group_at,
            (group_at * per + low) * heads + turned_group(high, group_at, head_bits),
        )
        for high in range(heads)
        for low in range(per)
        for group_at in range(heads)
    ]
    turned = lax.ppermute(own_grad, ("seq", "head"), route)
    partner_states = []
    running, arrived = own_state, None
    for digit in range(top):
        if arrived is not None:
            running = pl.pallas_call(
                running_kernel,
                out_shape=head_state,
                in_specs=[VMEM] * 2,
                out_specs=VMEM,
                compiler_params=PARAMS,
                cost_estimate=cost(0, 3 * moved_head),
            )(running, arrived)
        arrived = across(running, "seq", digit)
        partner_states.append(arrived)

    probs_t, att_local, qh, qw, lam, w = pl.pallas_call(
        local_kernel,
        out_shape=(
            pltpu.VMEM((heads_dev, rows, rows), BF),
            per_head_f32,
            per_head,
            pltpu.VMEM((seq_bits, heads_dev, rows, head_dim), BF),
            pltpu.VMEM(level_weights.shape, F32),
            pltpu.VMEM(out_proj.shape, BF),
        ),
        in_specs=[ANY, VMEM, VMEM, ANY, ANY, ANY],
        out_specs=(VMEM,) * 6,
        scratch_shapes=[
            pltpu.VMEM(queries.shape, F32),
            pltpu.VMEM((rows, rows), F32),
            pltpu.SemaphoreType.DMA((10,)),
        ],
        compiler_params=PARAMS,
        cost_estimate=cost(2 * flops_head, 12 * moved_head),
    )(hbm(queries), kh, vh, hbm(level_weights), hbm(out_proj), running)

    chunks = pl.pallas_call(
        chunk_kernel,
        out_shape=(like((rows, columns_dev), BF),) * per,
        in_specs=[VMEM, ANY],
        out_specs=(VMEM,) * per,
        compiler_params=PARAMS,
        cost_estimate=cost(0, 2 * moved_head),
    )(turned, qw)
    own_chunks = chunks
    chunks = [chunks[0]] + [
        lax.ppermute(chunks[r], "seq", [(at, at ^ r) for at in range(devices)])
        for r in range(1, per)
    ]
    gt, *grad_sums = pl.pallas_call(
        functools.partial(cotangent_kernel, heads, seq_bits),
        out_shape=(pltpu.VMEM((width, rows), BF),) + (pinned_state,) * seq_bits,
        in_specs=[VMEM] * (heads + 2) + [ANY],
        out_specs=(VMEM,) * (1 + seq_bits),
        compiler_params=PARAMS,
        cost_estimate=cost(2 * rows * width * out_proj.shape[1], 2 * width * out_proj.shape[1]),
    )(*grad_blocks, w, qw, own_chunks[-1])

    meeting = pl.pallas_call(
        functools.partial(meet_kernel, top)
        if arrived is not None
        else lambda grad_ref, running_ref, out_ref: meet_kernel(
            top, grad_ref, running_ref, None, out_ref
        ),
        out_shape=head_state,
        in_specs=[VMEM] * (2 if arrived is None else 3),
        out_specs=VMEM,
        compiler_params=PARAMS,
        cost_estimate=cost(0, 4 * moved_head),
    )(grad_sums[top], running, *([] if arrived is None else [arrived]))
    landed = [across(meeting, "seq", top)]
    partner_states.append(landed[0])

    stacked = pl.pallas_call(
        stack_kernel,
        out_shape=like((per, rows, columns_dev), BF),
        in_specs=[ANY] + [VMEM] * per,
        out_specs=VMEM,
        compiler_params=PARAMS,
        cost_estimate=cost(0, 2 * moved_head),
    )(meeting, *chunks)
    column_blocks = [stacked] + [to_group(stacked, i) for i in range(1, heads)]

    grad_columns = pl.pallas_call(
        functools.partial(columns_kernel, heads),
        out_shape=pltpu.VMEM((devices, rows, columns_dev), BF),
        in_specs=[VMEM] * heads,
        out_specs=VMEM,
        compiler_params=PARAMS,
        cost_estimate=cost(0, 8 * moved_head),
    )(*column_blocks)

    query_local, key_local, value_local = pl.pallas_call(
        functools.partial(local_grad_kernel, top),
        out_shape=(per_head_f32,) * 3,
        in_specs=[VMEM] * 6 + [ANY] + [VMEM] * top,
        out_specs=(VMEM,) * 3,
        compiler_params=PARAMS,
        cost_estimate=cost((4 + top) * flops_head, 14 * moved_head),
    )(gt, qh, kh, vh, probs_t, lam, meeting, *partner_states[:top])

    attended = pl.pallas_call(
        functools.partial(attended_kernel, seq_bits),
        out_shape=like((rows, width), BF),
        in_specs=[VMEM] * (2 + seq_bits) + [ANY] * 2,
        out_specs=VMEM,
        compiler_params=PARAMS,
        cost_estimate=cost(seq_bits * flops_head, 8 * moved_head),
    )(att_local, qw, *partner_states, key_local, stacked)

    first_pending = attended
    for digit in reversed(range(top)):
        outgoing = pl.pallas_call(
            functools.partial(pending_kernel, top),
            out_shape=head_state,
            in_specs=[VMEM, ANY] + [VMEM] * len(landed),
            out_specs=VMEM,
            compiler_params=PARAMS,
            cost_estimate=cost(0, 4 * moved_head),
        )(grad_sums[digit], attended, *landed)
        if len(landed) == 1:
            first_pending = outgoing
        landed.append(across(outgoing, "seq", digit))

    query_grad = pl.pallas_call(
        functools.partial(query_grad_kernel, top),
        out_shape=like((rows, heads_dev, head_dim), F32),
        in_specs=[VMEM] * 4 + [ANY],
        out_specs=VMEM,
        compiler_params=PARAMS,
        cost_estimate=cost(flops_head, 6 * moved_head),
    )(gt, lam, query_local, partner_states[top], attended)

    send, kept = pl.pallas_call(
        functools.partial(share_kernel, heads),
        out_shape=(like((heads // 2, rows, width), BF), like((heads // 2, rows, width), F32)),
        in_specs=[VMEM, VMEM, ANY, ANY, ANY],
        out_specs=(VMEM,) * 2,
        compiler_params=PARAMS,
        cost_estimate=cost(2 * rows * width * out_proj.shape[1], 2 * width * out_proj.shape[1]),
    )(attended, w, first_pending, hbm(query_grad), grad_columns)
    for digit in range(head_bits):
        kept = kept + to_group(send, 1 << digit).astype(F32)
        if digit < head_bits - 1:
            send, kept = kept[1::2].astype(BF), kept[0::2]
    mixed = kept[0].astype(BF)

    ring = list(range(0, devices, 2)) + list(range(devices - 1, 0, -2))
    forward = [(ring[i], ring[(i + 1) % devices]) for i in range(devices)]
    backward = [(b, a) for a, b in forward]

    def accumulate(total, blocks, offsets):
        operands = blocks if total is None else blocks + [total]
        return pl.pallas_call(
            functools.partial(proj_kernel, offsets, devices, total is None),
            out_shape=pltpu.VMEM((width, columns_dev), F32),
            in_specs=[VMEM] * (1 + len(operands)),
            out_specs=VMEM,
            compiler_params=PARAMS,
            cost_estimate=cost(
                2 * len(blocks) * rows * width * columns_dev, 4 * width * columns_dev
            ),
        )(grad_columns, *operands)

    blocks, offsets = [attended], [(0, 0, rows)]
    ahead = behind = attended
    half, steps, total = rows // 2, devices // 2, None
    for step in range(1, steps):
        ahead = lax.ppermute(ahead, "seq", forward)
        behind = lax.ppermute(behind, "seq", backward)
        blocks += [ahead, behind]
        offsets += [(-step, 0, rows), (step, 0, rows)]
        if step == steps - 2:
            total = accumulate(None, blocks, offsets)
            blocks, offsets = [], []
    if blocks:
        total = accumulate(total, blocks, offsets)
    last = [
        lax.ppermute(ahead[:half], "seq", forward),
        lax.ppermute(behind[half:], "seq", backward),
    ]
    key_grad, value_grad = pl.pallas_call(
        functools.partial(later_grad_kernel, top),
        out_shape=(like((rows, heads_dev, head_dim), F32),) * 2,
        in_specs=[VMEM] * 4 + [ANY] + [VMEM] * seq_bits,
        out_specs=(VMEM,) * 2,
        compiler_params=PARAMS,
        cost_estimate=cost(2 * flops_head, 11 * moved_head),
    )(kh, vh, key_local, value_local, total, *landed)
    quarter_rows = width // 4
    proj_grad = pl.pallas_call(
        functools.partial(last_kernel, steps, devices),
        out_shape=like((width, columns_dev), F32),
        grid=(4,),
        in_specs=[
            VMEM,
            VMEM,
            VMEM,
            VMEM,
            ANY,
        ],
        out_specs=pl.BlockSpec((quarter_rows, columns_dev), lambda i: (i, 0)),
        scratch_shapes=[pltpu.VMEM((rows, quarter_rows), BF)],
        compiler_params=PARAMS,
        cost_estimate=cost(2 * rows * width * columns_dev, 8 * width * columns_dev),
    )(grad_columns, *last, total, hbm(key_grad))
    return (mixed, query_grad, key_grad, value_grad, proj_grad)


def solution(mesh):
    placed = (
        P("seq", "head", None),
        P("seq", "head", None),
        P("seq", "head", None),
        P(None, "head", "seq"),
        P("head", None),
        P("seq", "head"),
    )
    return jax.shard_map(
        body,
        mesh=mesh,
        in_specs=placed,
        out_specs=(
            P("seq", "head"),
            P("seq", "head", None),
            P("seq", "head", None),
            P("seq", "head", None),
            P("head", "seq"),
        ),
        check_vma=False,
    )
```

```python
import functools

import jax
import jax.numpy as jnp
from jax import lax
from jax.experimental import pallas as pl
from jax.experimental.pallas import tpu as pltpu
from jax.sharding import PartitionSpec as P

CH = 64
BF = jnp.bfloat16
F32 = jnp.float32
NN = (((1,), (0,)), ((), ()))
NT = (((1,), (1,)), ((), ()))
TN = (((0,), (0,)), ((), ()))
TT = (((0,), (1,)), ((), ()))
VMEM = pl.BlockSpec(memory_space=pltpu.VMEM)
ANY = pl.BlockSpec(memory_space=pl.ANY)
PARAMS = pltpu.CompilerParams(vmem_limit_bytes=14 * 2**20)


def mm(a, b, dims):
    return lax.dot_general(a, b, dims, preferred_element_type=F32)


def cost(flops, moved):
    return pl.CostEstimate(flops=flops, bytes_accessed=moved, transcendentals=0)


def like(shape, dtype):
    return jax.ShapeDtypeStruct(shape, dtype)


def across(block, axis, stride, up_only=False, down_only=False):
    count = lax.axis_size(axis)
    route = []
    for low in range(count):
        high = low | 1 << stride
        if high != low and high < count:
            if not down_only:
                route.append((low, high))
            if not up_only:
                route.append((high, low))
    return lax.ppermute(block, axis, route)


def hbm(array):
    return pltpu.with_memory_space_constraint(array, pltpu.HBM)


def state_kernel(k_hbm, v_hbm, grad_hbm, s_ref, kh_ref, vh_ref, grad_ref, k_ref, v_ref, sems):
    copies = [
        pltpu.make_async_copy(k_hbm, k_ref, sems.at[0]),
        pltpu.make_async_copy(v_hbm, v_ref, sems.at[1]),
        pltpu.make_async_copy(grad_hbm, grad_ref, sems.at[2]),
    ]
    for copy in copies:
        copy.start()
    for copy in copies[:2]:
        copy.wait()
    for h in range(k_ref.shape[1]):
        k = k_ref[:, h, :].astype(BF)
        v = v_ref[:, h, :].astype(BF)
        kh_ref[h] = k
        vh_ref[h] = v
        s_ref[h] = mm(k, v, TN).astype(BF)
    copies[2].wait()


def weight_of(lam_ref, h, rows):
    local_bits = (rows // CH).bit_length() - 1
    s = lax.broadcasted_iota(jnp.int32, (rows, rows), 0)
    t = lax.broadcasted_iota(jnp.int32, (rows, rows), 1)
    differ = (s // CH) ^ (t // CH)
    weight = jnp.broadcast_to(lam_ref[0, h : h + 1, :], (rows, rows))
    for digit in range(local_bits):
        weight = jnp.where(differ >= 1 << digit, lam_ref[1 + digit, h : h + 1, :], weight)
    return jnp.where(s <= t, weight, 0.0)


def upper_weight(lam_ref, b, h, rows):
    local_bits = (rows // CH).bit_length() - 1
    upper = (lax.axis_index("seq") >> b & 1).astype(F32)
    return lam_ref[1 + local_bits + b, h : h + 1, :] * upper


def local_kernel(q_hbm, kh_ref, vh_ref, lam_hbm, w_hbm, after_ref, *refs):
    del after_ref
    pt_ref, att_ref, qh_ref, qw_ref, lam_ref, w_ref, q_ref, lam_rows, sems = refs
    pieces = sems.shape[0] - 2
    share = w_hbm.shape[0] // pieces
    copies = [
        pltpu.make_async_copy(q_hbm, q_ref, sems.at[0]),
        pltpu.make_async_copy(lam_hbm, lam_ref, sems.at[1]),
    ]
    for i in range(pieces):
        piece = pl.ds(i * share, share)
        copies.append(pltpu.make_async_copy(w_hbm.at[piece], w_ref.at[piece], sems.at[2 + i]))
    for copy in copies:
        copy.start()
    for copy in copies[:2]:
        copy.wait()
    rows, heads_dev, _ = q_ref.shape
    bits = qw_ref.shape[0]
    lam_rows[...] = jnp.zeros_like(lam_rows)
    for b in range(bits):
        for h in range(heads_dev):
            at = b * heads_dev + h
            lam_rows[at : at + 1, :] = upper_weight(lam_ref, b, h, rows)
    lam_columns = lam_rows[...].T
    for h in range(heads_dev):
        q32 = q_ref[:, h, :]
        q = q32.astype(BF)
        qh_ref[h] = q
        for b in range(bits):
            at = b * heads_dev + h
            qw_ref[b, h] = (q32 * lam_columns[:, at : at + 1]).astype(BF)
        pt = (mm(kh_ref[h], q, NT) * weight_of(lam_ref, h, rows)).astype(BF)
        pt_ref[h] = pt
        att_ref[h] = mm(pt, vh_ref[h], TN)
    for copy in copies[2:]:
        copy.wait()


def attended_kernel(bits, att_ref, qw_ref, *refs):
    states, out_ref = refs[:bits], refs[-1]
    heads_dev, _, head_dim = att_ref.shape
    for h in range(heads_dev):
        total = att_ref[h]
        for b in range(bits):
            total = total + mm(qw_ref[b, h], states[b][h], NN)
        out_ref[:, h * head_dim : (h + 1) * head_dim] = total.astype(BF)


def cotangent_kernel(blocks, bits, *refs):
    parts, (w_ref, qw_ref, _, gt_ref), sums = (
        refs[:blocks],
        refs[blocks : blocks + 4],
        refs[blocks + 4 :],
    )
    deep = parts[0].shape[1]
    _, heads_dev, _, head_dim = qw_ref.shape
    total = None
    for i in range(blocks):
        column = pl.multiple_of((lax.axis_index("head") ^ i) * deep, deep)
        product = mm(w_ref[:, pl.ds(column, deep)], parts[i][...], NT)
        total = product if total is None else total + product
    for h in range(heads_dev):
        gt = total[h * head_dim : (h + 1) * head_dim].astype(BF)
        gt_ref[h * head_dim : (h + 1) * head_dim, :] = gt
        for b in range(bits):
            sums[b][h] = mm(gt, qw_ref[b, h], NN).astype(BF)


def running_kernel(running_ref, arrived_ref, *refs):
    refs[-1][...] = (running_ref[...].astype(F32) + arrived_ref[...].astype(F32)).astype(BF)


def meet_kernel(top, grad_ref, running_ref, arrived_ref, out_ref):
    upper = (lax.axis_index("seq") >> top & 1) == 1
    running = running_ref[...].astype(F32)
    if arrived_ref is not None:
        running = running + arrived_ref[...].astype(F32)
    out_ref[...] = jnp.where(upper, grad_ref[...], running.astype(BF))


def landed_sum(top, landed):
    upper = (lax.axis_index("seq") >> top & 1) == 1
    total = jnp.where(upper, 0.0, landed[0].astype(F32))
    for block in landed[1:]:
        total = total + block.astype(F32)
    return total


def pending_kernel(top, own_ref, after_ref, *refs):
    del after_ref
    landed, out_ref = [ref[...] for ref in refs[:-1]], refs[-1]
    out_ref[...] = (own_ref[...].astype(F32) + landed_sum(top, landed)).astype(BF)


def turned_group(high, group, bits):
    turned = high >> 1 | (high & 1) << bits - 1
    return turned ^ ((group >> bits - 1 ^ group) & 1) << bits - 1


def turned_high(turned, group, bits):
    turned = turned ^ ((group >> bits - 1 ^ group) & 1) << bits - 1
    return (turned << 1 & (1 << bits) - 1) | turned >> bits - 1


def relay_kernel(block_ref, after_ref, out_ref):
    del after_ref
    out_ref[...] = block_ref[...]


def chunk_kernel(block_ref, *outs):
    columns = outs[0].shape[1]
    low = lax.axis_index("seq") % len(outs)
    for r, out in enumerate(outs):
        out[...] = block_ref[:, pl.ds(pl.multiple_of((low ^ r) * columns, columns), columns)]


def stack_kernel(after_ref, *refs):
    del after_ref
    for r, ref in enumerate(refs[:-1]):
        refs[-1][r] = ref[...]


def columns_kernel(blocks, *refs):
    parts, out_ref = refs[:blocks], refs[blocks]
    per = parts[0].shape[0]
    bits = blocks.bit_length() - 1
    low = lax.axis_index("seq") % per
    for i in range(blocks):
        high = turned_high(lax.axis_index("head") ^ i, lax.axis_index("seq") // per, bits)
        for r in range(per):
            out_ref[high * per + (low ^ r)] = parts[i][r]


def local_grad_kernel(
    bits, gt_ref, qh_ref, kh_ref, vh_ref, pt_ref, lam_ref, after_ref, *refs
):
    del after_ref
    states, (dq_ref, dk_ref, dv_ref) = refs[:bits], refs[bits:]
    heads_dev, rows, head_dim = qh_ref.shape
    for h in range(heads_dev):
        gt = gt_ref[h * head_dim : (h + 1) * head_dim, :]
        g32 = gt.astype(F32)
        dpt = (mm(vh_ref[h], gt, NN) * weight_of(lam_ref, h, rows)).astype(BF)
        dk_ref[h] = mm(dpt, qh_ref[h], NN)
        dv_ref[h] = mm(pt_ref[h], gt, NT)
        dq = mm(dpt, kh_ref[h], TN)
        for b in range(bits):
            gw = (g32 * upper_weight(lam_ref, b, h, rows)).astype(BF)
            dq = dq + mm(gw, states[b][h], TT)
        dq_ref[h] = dq


def query_grad_kernel(top, gt_ref, lam_ref, dql_ref, state_ref, after_ref, dq_ref):
    del after_ref
    heads_dev, rows, head_dim = dql_ref.shape
    for h in range(heads_dev):
        g32 = gt_ref[h * head_dim : (h + 1) * head_dim, :].astype(F32)
        gw = (g32 * upper_weight(lam_ref, top, h, rows)).astype(BF)
        dq_ref[:, h, :] = dql_ref[h] + mm(gw, state_ref[h], TT)


def later_grad_kernel(top, kh_ref, vh_ref, dkl_ref, dvl_ref, after_ref, *refs):
    del after_ref
    landed, (dk_ref, dv_ref) = refs[:-2], refs[-2:]
    for h in range(kh_ref.shape[0]):
        late = landed_sum(top, [ref[h] for ref in landed]).astype(BF)
        dk_ref[:, h, :] = dkl_ref[h] + mm(vh_ref[h], late, NN)
        dv_ref[:, h, :] = dvl_ref[h] + mm(kh_ref[h], late, NT)


def share_kernel(blocks, att_ref, w_ref, *refs):
    send_ref, kept_ref = refs[-2:]
    width = send_ref.shape[2]
    for i in range(blocks):
        out = send_ref if i % 2 else kept_ref
        column = pl.multiple_of((lax.axis_index("head") ^ i) * width, width)
        out[i // 2] = mm(att_ref[...], w_ref[:, pl.ds(column, width)], NN).astype(out.dtype)


def ring_owner(place, offset, devices):
    at = jnp.where(place % 2 == 0, place // 2, devices - 1 - place // 2)
    at = (at + offset + devices) % devices
    return jnp.where(at < devices // 2, 2 * at, 2 * (devices - 1 - at) + 1)


def proj_kernel(offsets, devices, first, cols_ref, *refs):
    total = None if first else refs[len(offsets)][...]
    for i, (offset, low, high) in enumerate(offsets):
        owner = ring_owner(lax.axis_index("seq"), offset, devices)
        product = mm(refs[i][...], cols_ref[owner, low:high, :], TN)
        total = product if total is None else total + product
    refs[-1][...] = total


def last_kernel(
    offset, devices, cols_ref, low_ref, high_ref, total_ref, after_ref, out_ref, held
):
    del after_ref
    half, block = low_ref.shape[0], out_ref.shape[0]
    at = pl.ds(pl.multiple_of(pl.program_id(0) * block, block), block)
    held[:half] = low_ref[:, at]
    held[half:] = high_ref[:, at]
    owner = ring_owner(lax.axis_index("seq"), offset, devices)
    out_ref[...] = total_ref[at, :] + mm(held[...], cols_ref[owner], TN)


def body(queries, keys, values, level_weights, out_proj, out_grad):
    rows, heads_dev, head_dim = queries.shape
    width = heads_dev * head_dim
    devices = lax.axis_size("seq")
    seq_bits = devices.bit_length() - 1
    heads = lax.axis_size("head")
    head_bits = heads.bit_length() - 1
    columns_dev = out_proj.shape[1] // devices

    head_state = like((heads_dev, head_dim, head_dim), BF)
    pinned_state = pltpu.VMEM((heads_dev, head_dim, head_dim), BF)
    per_head = pltpu.VMEM((heads_dev, rows, head_dim), BF)
    per_head_f32 = pltpu.VMEM((heads_dev, rows, head_dim), F32)
    flops_head = 2 * heads_dev * rows * rows * head_dim
    moved_head = 2 * rows * width
    top = seq_bits - 1

    own_state, kh, vh, own_grad = pl.pallas_call(
        state_kernel,
        out_shape=(head_state, per_head, per_head, like(out_grad.shape, BF)),
        in_specs=[ANY] * 3,
        out_specs=(VMEM,) * 4,
        scratch_shapes=[
            pltpu.VMEM(keys.shape, F32),
            pltpu.VMEM(keys.shape, F32),
            pltpu.SemaphoreType.DMA((3,)),
        ],
        compiler_params=PARAMS,
        cost_estimate=cost(flops_head, 7 * moved_head),
    )(hbm(keys), hbm(values), hbm(out_grad))

    def to_group(block, i):
        return lax.ppermute(block, "head", [(at, at ^ i) for at in range(heads)])

    def every_group(block):
        blocks = {0: block}
        for digit in reversed(range(head_bits)):
            for i in sorted(blocks):
                blocks[i ^ 1 << digit] = to_group(blocks[i], 1 << digit)
        return [blocks[i] for i in range(heads)]

    per = devices // heads
    route = [
        (
            (high * per + low) * heads + group_at,
            (group_at * per + low) * heads + turned_group(high, group_at, head_bits),
        )
        for high in range(heads)
        for low in range(per)
        for group_at in range(heads)
    ]
    turned = lax.ppermute(own_grad, ("seq", "head"), route)
    chunks = pl.pallas_call(
        chunk_kernel,
        out_shape=(like((rows, columns_dev), BF),) * per,
        in_specs=[VMEM],
        out_specs=(VMEM,) * per,
        compiler_params=PARAMS,
        cost_estimate=cost(0, 2 * moved_head),
    )(turned)

    def relayed(block):
        return pl.pallas_call(
            relay_kernel,
            out_shape=like(block.shape, block.dtype),
            in_specs=[VMEM, ANY],
            out_specs=VMEM,
            compiler_params=PARAMS,
            cost_estimate=cost(0, 2 * moved_head),
        )(block, chunks[-1])

    grad_blocks = {0: own_grad}
    for digit in reversed(range(head_bits)):
        for i in sorted(grad_blocks):
            block = relayed(grad_blocks[i]) if i else own_grad
            grad_blocks[i ^ 1 << digit] = to_group(block, 1 << digit)
    grad_blocks = [grad_blocks[i] for i in range(heads)]

    partner_states = []
    running, arrived = own_state, None
    for digit in range(top):
        if arrived is not None:
            running = pl.pallas_call(
                running_kernel,
                out_shape=head_state,
                in_specs=[VMEM] * 2,
                out_specs=VMEM,
                compiler_params=PARAMS,
                cost_estimate=cost(0, 3 * moved_head),
            )(running, arrived)
        arrived = across(running, "seq", digit)
        partner_states.append(arrived)

    probs_t, att_local, qh, qw, lam, w = pl.pallas_call(
        local_kernel,
        out_shape=(
            pltpu.VMEM((heads_dev, rows, rows), BF),
            per_head_f32,
            per_head,
            pltpu.VMEM((seq_bits, heads_dev, rows, head_dim), BF),
            pltpu.VMEM(level_weights.shape, F32),
            pltpu.VMEM(out_proj.shape, BF),
        ),
        in_specs=[ANY, VMEM, VMEM, ANY, ANY, ANY],
        out_specs=(VMEM,) * 6,
        scratch_shapes=[
            pltpu.VMEM(queries.shape, F32),
            pltpu.VMEM((rows, rows), F32),
            pltpu.SemaphoreType.DMA((10,)),
        ],
        compiler_params=PARAMS,
        cost_estimate=cost(2 * flops_head, 12 * moved_head),
    )(hbm(queries), kh, vh, hbm(level_weights), hbm(out_proj), running)

    chunks = [chunks[0]] + [
        lax.ppermute(chunks[r], "seq", [(at, at ^ r) for at in range(devices)])
        for r in range(1, per)
    ]
    gt, *grad_sums = pl.pallas_call(
        functools.partial(cotangent_kernel, heads, seq_bits),
        out_shape=(pltpu.VMEM((width, rows), BF),) + (pinned_state,) * seq_bits,
        in_specs=[VMEM] * (heads + 2) + [ANY],
        out_specs=(VMEM,) * (1 + seq_bits),
        compiler_params=PARAMS,
        cost_estimate=cost(2 * rows * width * out_proj.shape[1], 2 * width * out_proj.shape[1]),
    )(*grad_blocks, w, qw, running)

    meeting = pl.pallas_call(
        functools.partial(meet_kernel, top)
        if arrived is not None
        else lambda grad_ref, running_ref, out_ref: meet_kernel(
            top, grad_ref, running_ref, None, out_ref
        ),
        out_shape=head_state,
        in_specs=[VMEM] * (2 if arrived is None else 3),
        out_specs=VMEM,
        compiler_params=PARAMS,
        cost_estimate=cost(0, 4 * moved_head),
    )(grad_sums[top], running, *([] if arrived is None else [arrived]))
    landed = [across(meeting, "seq", top)]
    partner_states.append(landed[0])

    stacked = pl.pallas_call(
        stack_kernel,
        out_shape=like((per, rows, columns_dev), BF),
        in_specs=[ANY] + [VMEM] * per,
        out_specs=VMEM,
        compiler_params=PARAMS,
        cost_estimate=cost(0, 2 * moved_head),
    )(meeting, *chunks)
    column_blocks = [stacked] + [to_group(stacked, i) for i in range(1, heads)]

    grad_columns = pl.pallas_call(
        functools.partial(columns_kernel, heads),
        out_shape=pltpu.VMEM((devices, rows, columns_dev), BF),
        in_specs=[VMEM] * heads,
        out_specs=VMEM,
        compiler_params=PARAMS,
        cost_estimate=cost(0, 8 * moved_head),
    )(*column_blocks)

    query_local, key_local, value_local = pl.pallas_call(
        functools.partial(local_grad_kernel, top),
        out_shape=(per_head_f32,) * 3,
        in_specs=[VMEM] * 6 + [ANY] + [VMEM] * top,
        out_specs=(VMEM,) * 3,
        compiler_params=PARAMS,
        cost_estimate=cost((4 + top) * flops_head, 14 * moved_head),
    )(gt, qh, kh, vh, probs_t, lam, meeting, *partner_states[:top])

    attended = pl.pallas_call(
        functools.partial(attended_kernel, seq_bits),
        out_shape=like((rows, width), BF),
        in_specs=[VMEM] * (2 + seq_bits) + [ANY] * 2,
        out_specs=VMEM,
        compiler_params=PARAMS,
        cost_estimate=cost(seq_bits * flops_head, 8 * moved_head),
    )(att_local, qw, *partner_states, key_local, stacked)

    first_pending = attended
    for digit in reversed(range(top)):
        outgoing = pl.pallas_call(
            functools.partial(pending_kernel, top),
            out_shape=head_state,
            in_specs=[VMEM, ANY] + [VMEM] * len(landed),
            out_specs=VMEM,
            compiler_params=PARAMS,
            cost_estimate=cost(0, 4 * moved_head),
        )(grad_sums[digit], attended, *landed)
        if len(landed) == 1:
            first_pending = outgoing
        landed.append(across(outgoing, "seq", digit))

    query_grad = pl.pallas_call(
        functools.partial(query_grad_kernel, top),
        out_shape=like((rows, heads_dev, head_dim), F32),
        in_specs=[VMEM] * 4 + [ANY],
        out_specs=VMEM,
        compiler_params=PARAMS,
        cost_estimate=cost(flops_head, 6 * moved_head),
    )(gt, lam, query_local, partner_states[top], attended)

    send, kept = pl.pallas_call(
        functools.partial(share_kernel, heads),
        out_shape=(like((heads // 2, rows, width), BF), like((heads // 2, rows, width), F32)),
        in_specs=[VMEM, VMEM, ANY, ANY, ANY],
        out_specs=(VMEM,) * 2,
        compiler_params=PARAMS,
        cost_estimate=cost(2 * rows * width * out_proj.shape[1], 2 * width * out_proj.shape[1]),
    )(attended, w, first_pending, hbm(query_grad), grad_columns)
    for digit in range(head_bits):
        kept = kept + to_group(send, 1 << digit).astype(F32)
        if digit < head_bits - 1:
            send, kept = kept[1::2].astype(BF), kept[0::2]
    mixed = kept[0].astype(BF)

    ring = list(range(0, devices, 2)) + list(range(devices - 1, 0, -2))
    forward = [(ring[i], ring[(i + 1) % devices]) for i in range(devices)]
    backward = [(b, a) for a, b in forward]

    def accumulate(total, blocks, offsets):
        operands = blocks if total is None else blocks + [total]
        return pl.pallas_call(
            functools.partial(proj_kernel, offsets, devices, total is None),
            out_shape=pltpu.VMEM((width, columns_dev), F32),
            in_specs=[VMEM] * (1 + len(operands)),
            out_specs=VMEM,
            compiler_params=PARAMS,
            cost_estimate=cost(
                2 * len(blocks) * rows * width * columns_dev, 4 * width * columns_dev
            ),
        )(grad_columns, *operands)

    blocks, offsets = [attended], [(0, 0, rows)]
    ahead = behind = attended
    half, steps, total = rows // 2, devices // 2, None
    for step in range(1, steps):
        ahead = lax.ppermute(ahead, "seq", forward)
        behind = lax.ppermute(behind, "seq", backward)
        blocks += [ahead, behind]
        offsets += [(-step, 0, rows), (step, 0, rows)]
        if step == steps - 2:
            total = accumulate(None, blocks, offsets)
            blocks, offsets = [], []
    if blocks:
        total = accumulate(total, blocks, offsets)
    last = [
        lax.ppermute(ahead[:half], "seq", forward),
        lax.ppermute(behind[half:], "seq", backward),
    ]
    key_grad, value_grad = pl.pallas_call(
        functools.partial(later_grad_kernel, top),
        out_shape=(like((rows, heads_dev, head_dim), F32),) * 2,
        in_specs=[VMEM] * 4 + [ANY] + [VMEM] * seq_bits,
        out_specs=(VMEM,) * 2,
        compiler_params=PARAMS,
        cost_estimate=cost(2 * flops_head, 11 * moved_head),
    )(kh, vh, key_local, value_local, total, *landed)
    quarter_rows = width // 4
    proj_grad = pl.pallas_call(
        functools.partial(last_kernel, steps, devices),
        out_shape=like((width, columns_dev), F32),
        grid=(4,),
        in_specs=[
            VMEM,
            VMEM,
            VMEM,
            VMEM,
            ANY,
        ],
        out_specs=pl.BlockSpec((quarter_rows, columns_dev), lambda i: (i, 0)),
        scratch_shapes=[pltpu.VMEM((rows, quarter_rows), BF)],
        compiler_params=PARAMS,
        cost_estimate=cost(2 * rows * width * columns_dev, 8 * width * columns_dev),
    )(grad_columns, *last, total, hbm(key_grad))
    return (mixed, query_grad, key_grad, value_grad, proj_grad)


def solution(mesh):
    placed = (
        P("seq", "head", None),
        P("seq", "head", None),
        P("seq", "head", None),
        P(None, "head", "seq"),
        P("head", None),
        P("seq", "head"),
    )
    return jax.shard_map(
        body,
        mesh=mesh,
        in_specs=placed,
        out_specs=(
            P("seq", "head"),
            P("seq", "head", None),
            P("seq", "head", None),
            P("seq", "head", None),
            P("head", "seq"),
        ),
        check_vma=False,
    )
```

```python
import functools

import jax
import jax.numpy as jnp
from jax import lax
from jax.experimental import pallas as pl
from jax.experimental.pallas import tpu as pltpu
from jax.sharding import PartitionSpec as P

CH = 64
BF = jnp.bfloat16
F32 = jnp.float32
NN = (((1,), (0,)), ((), ()))
NT = (((1,), (1,)), ((), ()))
TN = (((0,), (0,)), ((), ()))
TT = (((0,), (1,)), ((), ()))
VMEM = pl.BlockSpec(memory_space=pltpu.VMEM)
ANY = pl.BlockSpec(memory_space=pl.ANY)
PARAMS = pltpu.CompilerParams(vmem_limit_bytes=14 * 2**20)


def mm(a, b, dims):
    return lax.dot_general(a, b, dims, preferred_element_type=F32)


def cost(flops, moved):
    return pl.CostEstimate(flops=flops, bytes_accessed=moved, transcendentals=0)


def like(shape, dtype):
    return jax.ShapeDtypeStruct(shape, dtype)


def across(block, axis, stride, up_only=False, down_only=False):
    count = lax.axis_size(axis)
    route = []
    for low in range(count):
        high = low | 1 << stride
        if high != low and high < count:
            if not down_only:
                route.append((low, high))
            if not up_only:
                route.append((high, low))
    return lax.ppermute(block, axis, route)


def hbm(array):
    return pltpu.with_memory_space_constraint(array, pltpu.HBM)


def state_kernel(k_hbm, v_hbm, grad_hbm, *refs):
    s_ref, kh_ref, vh_ref, grad_ref, low_ref, k_ref, v_ref, sems = refs
    copies = [
        pltpu.make_async_copy(k_hbm, k_ref, sems.at[0]),
        pltpu.make_async_copy(v_hbm, v_ref, sems.at[1]),
        pltpu.make_async_copy(grad_hbm, grad_ref, sems.at[2]),
        pltpu.make_async_copy(grad_hbm.at[pl.ds(0, low_ref.shape[0])], low_ref, sems.at[3]),
    ]
    for copy in copies:
        copy.start()
    for copy in copies[:2]:
        copy.wait()
    for h in range(k_ref.shape[1]):
        k = k_ref[:, h, :].astype(BF)
        v = v_ref[:, h, :].astype(BF)
        kh_ref[h] = k
        vh_ref[h] = v
        s_ref[h] = mm(k, v, TN).astype(BF)
    copies[2].wait()
    copies[3].wait()


def weight_of(lam_ref, h, rows):
    local_bits = (rows // CH).bit_length() - 1
    s = lax.broadcasted_iota(jnp.int32, (rows, rows), 0)
    t = lax.broadcasted_iota(jnp.int32, (rows, rows), 1)
    differ = (s // CH) ^ (t // CH)
    weight = jnp.broadcast_to(lam_ref[0, h : h + 1, :], (rows, rows))
    for digit in range(local_bits):
        weight = jnp.where(differ >= 1 << digit, lam_ref[1 + digit, h : h + 1, :], weight)
    return jnp.where(s <= t, weight, 0.0)


def upper_weight(lam_ref, b, h, rows):
    local_bits = (rows // CH).bit_length() - 1
    upper = (lax.axis_index("seq") >> b & 1).astype(F32)
    return lam_ref[1 + local_bits + b, h : h + 1, :] * upper


def local_kernel(q_hbm, kh_ref, vh_ref, lam_hbm, w_hbm, *refs):
    pt_ref, att_ref, qh_ref, qw_ref, lam_ref, w_ref, q_ref, lam_rows, sems = refs
    pieces = sems.shape[0] - 2
    share = w_hbm.shape[0] // pieces
    copies = [
        pltpu.make_async_copy(q_hbm, q_ref, sems.at[0]),
        pltpu.make_async_copy(lam_hbm, lam_ref, sems.at[1]),
    ]
    for i in range(pieces):
        piece = pl.ds(i * share, share)
        copies.append(pltpu.make_async_copy(w_hbm.at[piece], w_ref.at[piece], sems.at[2 + i]))
    for copy in copies:
        copy.start()
    for copy in copies[:2]:
        copy.wait()
    rows, heads_dev, _ = q_ref.shape
    bits = qw_ref.shape[0]
    lam_rows[...] = jnp.zeros_like(lam_rows)
    for b in range(bits):
        for h in range(heads_dev):
            at = b * heads_dev + h
            lam_rows[at : at + 1, :] = upper_weight(lam_ref, b, h, rows)
    lam_columns = lam_rows[...].T
    for h in range(heads_dev):
        q32 = q_ref[:, h, :]
        q = q32.astype(BF)
        qh_ref[h] = q
        for b in range(bits):
            at = b * heads_dev + h
            qw_ref[b, h] = (q32 * lam_columns[:, at : at + 1]).astype(BF)
        pt = (mm(kh_ref[h], q, NT) * weight_of(lam_ref, h, rows)).astype(BF)
        pt_ref[h] = pt
        att_ref[h] = mm(pt, vh_ref[h], TN)
    for copy in copies[2:]:
        copy.wait()


def attended_kernel(bits, att_ref, qw_ref, *refs):
    states, out_ref = refs[:bits], refs[-1]
    heads_dev, _, head_dim = att_ref.shape
    for h in range(heads_dev):
        total = att_ref[h]
        for b in range(bits):
            total = total + mm(qw_ref[b, h], states[b][h], NN)
        out_ref[:, h * head_dim : (h + 1) * head_dim] = total.astype(BF)


def cotangent_kernel(blocks, bits, *refs):
    parts, (w_ref, qw_ref, _, gt_ref), sums = (
        refs[:blocks],
        refs[blocks : blocks + 4],
        refs[blocks + 4 :],
    )
    deep = parts[0].shape[1]
    _, heads_dev, _, head_dim = qw_ref.shape
    total = None
    for i in range(blocks):
        column = pl.multiple_of((lax.axis_index("head") ^ i) * deep, deep)
        product = mm(w_ref[:, pl.ds(column, deep)], parts[i][...], NT)
        total = product if total is None else total + product
    for h in range(heads_dev):
        gt = total[h * head_dim : (h + 1) * head_dim].astype(BF)
        gt_ref[h * head_dim : (h + 1) * head_dim, :] = gt
        for b in range(bits):
            sums[b][h] = mm(gt, qw_ref[b, h], NN).astype(BF)


def running_kernel(running_ref, arrived_ref, *refs):
    refs[-1][...] = (running_ref[...].astype(F32) + arrived_ref[...].astype(F32)).astype(BF)


def meet_kernel(top, grad_ref, running_ref, arrived_ref, out_ref):
    upper = (lax.axis_index("seq") >> top & 1) == 1
    running = running_ref[...].astype(F32)
    if arrived_ref is not None:
        running = running + arrived_ref[...].astype(F32)
    out_ref[...] = jnp.where(upper, grad_ref[...], running.astype(BF))


def landed_sum(top, landed):
    upper = (lax.axis_index("seq") >> top & 1) == 1
    total = jnp.where(upper, 0.0, landed[0].astype(F32))
    for block in landed[1:]:
        total = total + block.astype(F32)
    return total


def pending_kernel(top, own_ref, after_ref, *refs):
    del after_ref
    landed, out_ref = [ref[...] for ref in refs[:-1]], refs[-1]
    out_ref[...] = (own_ref[...].astype(F32) + landed_sum(top, landed)).astype(BF)


def turned_group(high, group, bits):
    turned = high >> 1 | (high & 1) << bits - 1
    return turned ^ ((group >> bits - 1 ^ group) & 1) << bits - 1


def turned_high(turned, group, bits):
    turned = turned ^ ((group >> bits - 1 ^ group) & 1) << bits - 1
    return (turned << 1 & (1 << bits) - 1) | turned >> bits - 1


def relay_kernel(block_ref, after_ref, out_ref):
    del after_ref
    out_ref[...] = block_ref[...]


def chunk_kernel(low_ref, high_ref, after_ref, *outs):
    del after_ref
    half = low_ref.shape[0]
    columns = outs[0].shape[1]
    low = lax.axis_index("seq") % len(outs)
    for r, out in enumerate(outs):
        at = pl.ds(pl.multiple_of((low ^ r) * columns, columns), columns)
        out[:half] = low_ref[:, at]
        out[half:] = high_ref[:, at]


def stack_kernel(after_ref, *refs):
    del after_ref
    for r, ref in enumerate(refs[:-1]):
        refs[-1][r] = ref[...]


def columns_kernel(blocks, *refs):
    parts, out_ref = refs[:blocks], refs[blocks]
    per = parts[0].shape[0]
    bits = blocks.bit_length() - 1
    low = lax.axis_index("seq") % per
    for i in range(blocks):
        high = turned_high(lax.axis_index("head") ^ i, lax.axis_index("seq") // per, bits)
        for r in range(per):
            out_ref[high * per + (low ^ r)] = parts[i][r]


def local_grad_kernel(
    bits, gt_ref, qh_ref, kh_ref, vh_ref, pt_ref, lam_ref, after_ref, *refs
):
    del after_ref
    states, (dq_ref, dk_ref, dv_ref) = refs[:bits], refs[bits:]
    heads_dev, rows, head_dim = qh_ref.shape
    for h in range(heads_dev):
        gt = gt_ref[h * head_dim : (h + 1) * head_dim, :]
        g32 = gt.astype(F32)
        dpt = (mm(vh_ref[h], gt, NN) * weight_of(lam_ref, h, rows)).astype(BF)
        dk_ref[h] = mm(dpt, qh_ref[h], NN)
        dv_ref[h] = mm(pt_ref[h], gt, NT)
        dq = mm(dpt, kh_ref[h], TN)
        for b in range(bits):
            gw = (g32 * upper_weight(lam_ref, b, h, rows)).astype(BF)
            dq = dq + mm(gw, states[b][h], TT)
        dq_ref[h] = dq


def query_grad_kernel(top, gt_ref, lam_ref, dql_ref, state_ref, after_ref, dq_ref):
    del after_ref
    heads_dev, rows, head_dim = dql_ref.shape
    for h in range(heads_dev):
        g32 = gt_ref[h * head_dim : (h + 1) * head_dim, :].astype(F32)
        gw = (g32 * upper_weight(lam_ref, top, h, rows)).astype(BF)
        dq_ref[:, h, :] = dql_ref[h] + mm(gw, state_ref[h], TT)


def later_grad_kernel(top, kh_ref, vh_ref, dkl_ref, dvl_ref, after_ref, *refs):
    del after_ref
    landed, (dk_ref, dv_ref) = refs[:-2], refs[-2:]
    for h in range(kh_ref.shape[0]):
        late = landed_sum(top, [ref[h] for ref in landed]).astype(BF)
        dk_ref[:, h, :] = dkl_ref[h] + mm(vh_ref[h], late, NN)
        dv_ref[:, h, :] = dvl_ref[h] + mm(kh_ref[h], late, NT)


def share_kernel(blocks, att_ref, w_ref, *refs):
    send_ref, kept_ref = refs[-2:]
    width = send_ref.shape[2]
    for i in range(blocks):
        out = send_ref if i % 2 else kept_ref
        column = pl.multiple_of((lax.axis_index("head") ^ i) * width, width)
        out[i // 2] = mm(att_ref[...], w_ref[:, pl.ds(column, width)], NN).astype(out.dtype)


def ring_owner(place, offset, devices):
    at = jnp.where(place % 2 == 0, place // 2, devices - 1 - place // 2)
    at = (at + offset + devices) % devices
    return jnp.where(at < devices // 2, 2 * at, 2 * (devices - 1 - at) + 1)


def proj_kernel(offsets, devices, first, cols_ref, *refs):
    total = None if first else refs[len(offsets)][...]
    for i, (offset, low, high) in enumerate(offsets):
        owner = ring_owner(lax.axis_index("seq"), offset, devices)
        product = mm(refs[i][...], cols_ref[owner, low:high, :], TN)
        total = product if total is None else total + product
    refs[-1][...] = total


def last_kernel(
    offset, devices, cols_ref, low_ref, high_ref, total_ref, after_ref, out_ref, held
):
    del after_ref
    half, block = low_ref.shape[0], out_ref.shape[0]
    at = pl.ds(pl.multiple_of(pl.program_id(0) * block, block), block)
    held[:half] = low_ref[:, at]
    held[half:] = high_ref[:, at]
    owner = ring_owner(lax.axis_index("seq"), offset, devices)
    out_ref[...] = total_ref[at, :] + mm(held[...], cols_ref[owner], TN)


def body(queries, keys, values, level_weights, out_proj, out_grad):
    rows, heads_dev, head_dim = queries.shape
    width = heads_dev * head_dim
    devices = lax.axis_size("seq")
    seq_bits = devices.bit_length() - 1
    heads = lax.axis_size("head")
    head_bits = heads.bit_length() - 1
    columns_dev = out_proj.shape[1] // devices

    head_state = like((heads_dev, head_dim, head_dim), BF)
    pinned_state = pltpu.VMEM((heads_dev, head_dim, head_dim), BF)
    per_head = pltpu.VMEM((heads_dev, rows, head_dim), BF)
    per_head_f32 = pltpu.VMEM((heads_dev, rows, head_dim), F32)
    flops_head = 2 * heads_dev * rows * rows * head_dim
    moved_head = 2 * rows * width
    top = seq_bits - 1

    half = rows // 2
    own_state, kh, vh, own_grad, own_low = pl.pallas_call(
        state_kernel,
        out_shape=(head_state, per_head, per_head, like(out_grad.shape, BF), like((half, width), BF)),
        in_specs=[ANY] * 3,
        out_specs=(VMEM,) * 5,
        scratch_shapes=[
            pltpu.VMEM(keys.shape, F32),
            pltpu.VMEM(keys.shape, F32),
            pltpu.SemaphoreType.DMA((4,)),
        ],
        compiler_params=PARAMS,
        cost_estimate=cost(flops_head, 7 * moved_head),
    )(hbm(keys), hbm(values), hbm(out_grad))

    def to_group(block, i):
        return lax.ppermute(block, "head", [(at, at ^ i) for at in range(heads)])

    def every_group(block):
        blocks = {0: block}
        for digit in reversed(range(head_bits)):
            for i in sorted(blocks):
                blocks[i ^ 1 << digit] = to_group(blocks[i], 1 << digit)
        return [blocks[i] for i in range(heads)]

    probs_t, att_local, qh, qw, lam, w = pl.pallas_call(
        local_kernel,
        out_shape=(
            pltpu.VMEM((heads_dev, rows, rows), BF),
            per_head_f32,
            per_head,
            pltpu.VMEM((seq_bits, heads_dev, rows, head_dim), BF),
            pltpu.VMEM(level_weights.shape, F32),
            pltpu.VMEM(out_proj.shape, BF),
        ),
        in_specs=[ANY, VMEM, VMEM, ANY, ANY],
        out_specs=(VMEM,) * 6,
        scratch_shapes=[
            pltpu.VMEM(queries.shape, F32),
            pltpu.VMEM((rows, rows), F32),
            pltpu.SemaphoreType.DMA((10,)),
        ],
        compiler_params=PARAMS,
        cost_estimate=cost(2 * flops_head, 12 * moved_head),
    )(hbm(queries), kh, vh, hbm(level_weights), hbm(out_proj))

    def relayed(block):
        return pl.pallas_call(
            relay_kernel,
            out_shape=like(block.shape, block.dtype),
            in_specs=[VMEM, ANY],
            out_specs=VMEM,
            compiler_params=PARAMS,
            cost_estimate=cost(0, 2 * moved_head),
        )(block, qw)

    grad_blocks = {0: own_grad}
    for digit in reversed(range(head_bits)):
        for i in sorted(grad_blocks):
            block = relayed(grad_blocks[i]) if i else own_grad
            grad_blocks[i ^ 1 << digit] = to_group(block, 1 << digit)
    grad_blocks = [grad_blocks[i] for i in range(heads)]

    per = devices // heads
    def turn_route(shift):
        return [
            (
                (high * per + low) * heads + (group_at ^ shift),
                (group_at * per + low) * heads + turned_group(high, group_at, head_bits),
            )
            for high in range(heads)
            for low in range(per)
            for group_at in range(heads)
        ]

    axes, far = ("seq", "head"), heads // 2
    turned = [
        lax.ppermute(own_low, axes, turn_route(0)),
        lax.ppermute(grad_blocks[far][half:], axes, turn_route(far)),
    ]
    partner_states = []
    running, arrived = own_state, None
    for digit in range(top):
        if arrived is not None:
            running = pl.pallas_call(
                running_kernel,
                out_shape=head_state,
                in_specs=[VMEM] * 2 + [ANY],
                out_specs=VMEM,
                compiler_params=PARAMS,
                cost_estimate=cost(0, 3 * moved_head),
            )(running, arrived, qw)
        arrived = across(running, "seq", digit)
        partner_states.append(arrived)

    gt, *grad_sums = pl.pallas_call(
        functools.partial(cotangent_kernel, heads, seq_bits),
        out_shape=(pltpu.VMEM((width, rows), BF),) + (pinned_state,) * seq_bits,
        in_specs=[VMEM] * (heads + 2) + [ANY],
        out_specs=(VMEM,) * (1 + seq_bits),
        compiler_params=PARAMS,
        cost_estimate=cost(2 * rows * width * out_proj.shape[1], 2 * width * out_proj.shape[1]),
    )(*grad_blocks, w, qw, running)

    meeting = pl.pallas_call(
        functools.partial(meet_kernel, top)
        if arrived is not None
        else lambda grad_ref, running_ref, out_ref: meet_kernel(
            top, grad_ref, running_ref, None, out_ref
        ),
        out_shape=head_state,
        in_specs=[VMEM] * (2 if arrived is None else 3),
        out_specs=VMEM,
        compiler_params=PARAMS,
        cost_estimate=cost(0, 4 * moved_head),
    )(grad_sums[top], running, *([] if arrived is None else [arrived]))
    landed = [across(meeting, "seq", top)]
    partner_states.append(landed[0])

    chunks = pl.pallas_call(
        chunk_kernel,
        out_shape=(like((rows, columns_dev), BF),) * per,
        in_specs=[VMEM, VMEM, ANY],
        out_specs=(VMEM,) * per,
        compiler_params=PARAMS,
        cost_estimate=cost(0, 2 * moved_head),
    )(*turned, gt)
    chunks = [chunks[0]] + [
        lax.ppermute(chunks[r], "seq", [(at, at ^ r) for at in range(devices)])
        for r in range(1, per)
    ]
    stacked = pl.pallas_call(
        stack_kernel,
        out_shape=like((per, rows, columns_dev), BF),
        in_specs=[ANY] + [VMEM] * per,
        out_specs=VMEM,
        compiler_params=PARAMS,
        cost_estimate=cost(0, 2 * moved_head),
    )(meeting, *chunks)
    column_blocks = [stacked] + [to_group(stacked, i) for i in range(1, heads)]

    grad_columns = pl.pallas_call(
        functools.partial(columns_kernel, heads),
        out_shape=pltpu.VMEM((devices, rows, columns_dev), BF),
        in_specs=[VMEM] * heads,
        out_specs=VMEM,
        compiler_params=PARAMS,
        cost_estimate=cost(0, 8 * moved_head),
    )(*column_blocks)

    query_local, key_local, value_local = pl.pallas_call(
        functools.partial(local_grad_kernel, top),
        out_shape=(per_head_f32,) * 3,
        in_specs=[VMEM] * 6 + [ANY] + [VMEM] * top,
        out_specs=(VMEM,) * 3,
        compiler_params=PARAMS,
        cost_estimate=cost((4 + top) * flops_head, 14 * moved_head),
    )(gt, qh, kh, vh, probs_t, lam, meeting, *partner_states[:top])

    attended = pl.pallas_call(
        functools.partial(attended_kernel, seq_bits),
        out_shape=like((rows, width), BF),
        in_specs=[VMEM] * (2 + seq_bits) + [ANY] * 2,
        out_specs=VMEM,
        compiler_params=PARAMS,
        cost_estimate=cost(seq_bits * flops_head, 8 * moved_head),
    )(att_local, qw, *partner_states, key_local, stacked)

    first_pending = attended
    for digit in reversed(range(top)):
        outgoing = pl.pallas_call(
            functools.partial(pending_kernel, top),
            out_shape=head_state,
            in_specs=[VMEM, ANY] + [VMEM] * len(landed),
            out_specs=VMEM,
            compiler_params=PARAMS,
            cost_estimate=cost(0, 4 * moved_head),
        )(grad_sums[digit], attended, *landed)
        if len(landed) == 1:
            first_pending = outgoing
        landed.append(across(outgoing, "seq", digit))

    query_grad = pl.pallas_call(
        functools.partial(query_grad_kernel, top),
        out_shape=like((rows, heads_dev, head_dim), F32),
        in_specs=[VMEM] * 4 + [ANY],
        out_specs=VMEM,
        compiler_params=PARAMS,
        cost_estimate=cost(flops_head, 6 * moved_head),
    )(gt, lam, query_local, partner_states[top], attended)

    send, kept = pl.pallas_call(
        functools.partial(share_kernel, heads),
        out_shape=(like((heads // 2, rows, width), BF), like((heads // 2, rows, width), F32)),
        in_specs=[VMEM, VMEM, ANY, ANY, ANY],
        out_specs=(VMEM,) * 2,
        compiler_params=PARAMS,
        cost_estimate=cost(2 * rows * width * out_proj.shape[1], 2 * width * out_proj.shape[1]),
    )(attended, w, first_pending, hbm(query_grad), grad_columns)
    for digit in range(head_bits):
        kept = kept + to_group(send, 1 << digit).astype(F32)
        if digit < head_bits - 1:
            send, kept = kept[1::2].astype(BF), kept[0::2]
    mixed = kept[0].astype(BF)

    ring = list(range(0, devices, 2)) + list(range(devices - 1, 0, -2))
    forward = [(ring[i], ring[(i + 1) % devices]) for i in range(devices)]
    backward = [(b, a) for a, b in forward]

    def accumulate(total, blocks, offsets):
        operands = blocks if total is None else blocks + [total]
        return pl.pallas_call(
            functools.partial(proj_kernel, offsets, devices, total is None),
            out_shape=pltpu.VMEM((width, columns_dev), F32),
            in_specs=[VMEM] * (1 + len(operands)),
            out_specs=VMEM,
            compiler_params=PARAMS,
            cost_estimate=cost(
                2 * len(blocks) * rows * width * columns_dev, 4 * width * columns_dev
            ),
        )(grad_columns, *operands)

    blocks, offsets = [attended], [(0, 0, rows)]
    ahead = behind = attended
    steps, total = devices // 2, None
    for step in range(1, steps):
        ahead = lax.ppermute(ahead, "seq", forward)
        behind = lax.ppermute(behind, "seq", backward)
        blocks += [ahead, behind]
        offsets += [(-step, 0, rows), (step, 0, rows)]
        if step == steps - 2:
            total = accumulate(None, blocks, offsets)
            blocks, offsets = [], []
    if blocks:
        total = accumulate(total, blocks, offsets)
    last = [
        lax.ppermute(ahead[:half], "seq", forward),
        lax.ppermute(behind[half:], "seq", backward),
    ]
    key_grad, value_grad = pl.pallas_call(
        functools.partial(later_grad_kernel, top),
        out_shape=(like((rows, heads_dev, head_dim), F32),) * 2,
        in_specs=[VMEM] * 4 + [ANY] + [VMEM] * seq_bits,
        out_specs=(VMEM,) * 2,
        compiler_params=PARAMS,
        cost_estimate=cost(2 * flops_head, 11 * moved_head),
    )(kh, vh, key_local, value_local, total, *landed)
    quarter_rows = width // 4
    proj_grad = pl.pallas_call(
        functools.partial(last_kernel, steps, devices),
        out_shape=like((width, columns_dev), F32),
        grid=(4,),
        in_specs=[
            VMEM,
            VMEM,
            VMEM,
            VMEM,
            ANY,
        ],
        out_specs=pl.BlockSpec((quarter_rows, columns_dev), lambda i: (i, 0)),
        scratch_shapes=[pltpu.VMEM((rows, quarter_rows), BF)],
        compiler_params=PARAMS,
        cost_estimate=cost(2 * rows * width * columns_dev, 8 * width * columns_dev),
    )(grad_columns, *last, total, hbm(key_grad))
    return (mixed, query_grad, key_grad, value_grad, proj_grad)


def solution(mesh):
    placed = (
        P("seq", "head", None),
        P("seq", "head", None),
        P("seq", "head", None),
        P(None, "head", "seq"),
        P("head", None),
        P("seq", "head"),
    )
    return jax.shard_map(
        body,
        mesh=mesh,
        in_specs=placed,
        out_specs=(
            P("seq", "head"),
            P("seq", "head", None),
            P("seq", "head", None),
            P("seq", "head", None),
            P("head", "seq"),
        ),
        check_vma=False,
    )
```

```python
import functools

import jax
import jax.numpy as jnp
from jax import lax
from jax.experimental import pallas as pl
from jax.experimental.pallas import tpu as pltpu
from jax.sharding import PartitionSpec as P

CH = 64
BF = jnp.bfloat16
F32 = jnp.float32
NN = (((1,), (0,)), ((), ()))
NT = (((1,), (1,)), ((), ()))
TN = (((0,), (0,)), ((), ()))
TT = (((0,), (1,)), ((), ()))
VMEM = pl.BlockSpec(memory_space=pltpu.VMEM)
ANY = pl.BlockSpec(memory_space=pl.ANY)
PARAMS = pltpu.CompilerParams(vmem_limit_bytes=14 * 2**20)


def mm(a, b, dims):
    return lax.dot_general(a, b, dims, preferred_element_type=F32)


def cost(flops, moved):
    return pl.CostEstimate(flops=flops, bytes_accessed=moved, transcendentals=0)


def like(shape, dtype):
    return jax.ShapeDtypeStruct(shape, dtype)


def across(block, axis, stride, up_only=False, down_only=False):
    count = lax.axis_size(axis)
    route = []
    for low in range(count):
        high = low | 1 << stride
        if high != low and high < count:
            if not down_only:
                route.append((low, high))
            if not up_only:
                route.append((high, low))
    return lax.ppermute(block, axis, route)


def hbm(array):
    return pltpu.with_memory_space_constraint(array, pltpu.HBM)


def state_kernel(k_hbm, v_hbm, grad_hbm, *refs):
    s_ref, kh_ref, vh_ref, grad_ref, low_ref, k_ref, v_ref, sems = refs
    copies = [
        pltpu.make_async_copy(k_hbm, k_ref, sems.at[0]),
        pltpu.make_async_copy(v_hbm, v_ref, sems.at[1]),
        pltpu.make_async_copy(grad_hbm, grad_ref, sems.at[2]),
        pltpu.make_async_copy(grad_hbm.at[pl.ds(0, low_ref.shape[0])], low_ref, sems.at[3]),
    ]
    for copy in copies:
        copy.start()
    for copy in copies[:2]:
        copy.wait()
    for h in range(k_ref.shape[1]):
        k = k_ref[:, h, :].astype(BF)
        v = v_ref[:, h, :].astype(BF)
        kh_ref[h] = k
        vh_ref[h] = v
        s_ref[h] = mm(k, v, TN).astype(BF)
    copies[2].wait()
    copies[3].wait()


def weight_of(lam_ref, h, rows):
    local_bits = (rows // CH).bit_length() - 1
    s = lax.broadcasted_iota(jnp.int32, (rows, rows), 0)
    t = lax.broadcasted_iota(jnp.int32, (rows, rows), 1)
    differ = (s // CH) ^ (t // CH)
    weight = jnp.broadcast_to(lam_ref[0, h : h + 1, :], (rows, rows))
    for digit in range(local_bits):
        weight = jnp.where(differ >= 1 << digit, lam_ref[1 + digit, h : h + 1, :], weight)
    return jnp.where(s <= t, weight, 0.0)


def upper_weight(lam_ref, b, h, rows):
    local_bits = (rows // CH).bit_length() - 1
    upper = (lax.axis_index("seq") >> b & 1).astype(F32)
    return lam_ref[1 + local_bits + b, h : h + 1, :] * upper


def local_kernel(q_hbm, kh_ref, vh_ref, lam_hbm, w_hbm, *refs):
    pt_ref, att_ref, qh_ref, qw_ref, lam_ref, w_ref, q_ref, lam_rows, sems = refs
    pieces = sems.shape[0] - 2
    share = w_hbm.shape[0] // pieces
    copies = [
        pltpu.make_async_copy(q_hbm, q_ref, sems.at[0]),
        pltpu.make_async_copy(lam_hbm, lam_ref, sems.at[1]),
    ]
    for i in range(pieces):
        piece = pl.ds(i * share, share)
        copies.append(pltpu.make_async_copy(w_hbm.at[piece], w_ref.at[piece], sems.at[2 + i]))
    for copy in copies:
        copy.start()
    for copy in copies[:2]:
        copy.wait()
    rows, heads_dev, _ = q_ref.shape
    bits = qw_ref.shape[0]
    lam_rows[...] = jnp.zeros_like(lam_rows)
    for b in range(bits):
        for h in range(heads_dev):
            at = b * heads_dev + h
            lam_rows[at : at + 1, :] = upper_weight(lam_ref, b, h, rows)
    lam_columns = lam_rows[...].T
    for h in range(heads_dev):
        q32 = q_ref[:, h, :]
        q = q32.astype(BF)
        qh_ref[h] = q
        for b in range(bits):
            at = b * heads_dev + h
            qw_ref[b, h] = (q32 * lam_columns[:, at : at + 1]).astype(BF)
        pt = (mm(kh_ref[h], q, NT) * weight_of(lam_ref, h, rows)).astype(BF)
        pt_ref[h] = pt
        att_ref[h] = mm(pt, vh_ref[h], TN)
    for copy in copies[2:]:
        copy.wait()


def attended_kernel(bits, att_ref, qw_ref, *refs):
    states, out_ref = refs[:bits], refs[-1]
    heads_dev, _, head_dim = att_ref.shape
    for h in range(heads_dev):
        total = att_ref[h]
        for b in range(bits):
            total = total + mm(qw_ref[b, h], states[b][h], NN)
        out_ref[:, h * head_dim : (h + 1) * head_dim] = total.astype(BF)


def cotangent_kernel(blocks, bits, *refs):
    parts, (w_ref, qw_ref, _, gt_ref), sums = (
        refs[:blocks],
        refs[blocks : blocks + 4],
        refs[blocks + 4 :],
    )
    deep = parts[0].shape[1]
    _, heads_dev, _, head_dim = qw_ref.shape
    total = None
    for i in range(blocks):
        column = pl.multiple_of((lax.axis_index("head") ^ i) * deep, deep)
        product = mm(w_ref[:, pl.ds(column, deep)], parts[i][...], NT)
        total = product if total is None else total + product
    for h in range(heads_dev):
        gt = total[h * head_dim : (h + 1) * head_dim].astype(BF)
        gt_ref[h * head_dim : (h + 1) * head_dim, :] = gt
        for b in range(bits):
            sums[b][h] = mm(gt, qw_ref[b, h], NN).astype(BF)


def running_kernel(running_ref, arrived_ref, *refs):
    refs[-1][...] = (running_ref[...].astype(F32) + arrived_ref[...].astype(F32)).astype(BF)


def meet_kernel(top, grad_ref, running_ref, arrived_ref, out_ref):
    upper = (lax.axis_index("seq") >> top & 1) == 1
    running = running_ref[...].astype(F32)
    if arrived_ref is not None:
        running = running + arrived_ref[...].astype(F32)
    out_ref[...] = jnp.where(upper, grad_ref[...], running.astype(BF))


def landed_sum(top, landed):
    upper = (lax.axis_index("seq") >> top & 1) == 1
    total = jnp.where(upper, 0.0, landed[0].astype(F32))
    for block in landed[1:]:
        total = total + block.astype(F32)
    return total


def pending_kernel(top, own_ref, after_ref, *refs):
    del after_ref
    landed, out_ref = [ref[...] for ref in refs[:-1]], refs[-1]
    out_ref[...] = (own_ref[...].astype(F32) + landed_sum(top, landed)).astype(BF)


def turned_group(high, group, bits):
    turned = high >> 1 | (high & 1) << bits - 1
    return turned ^ ((group >> bits - 1 ^ group) & 1) << bits - 1


def turned_high(turned, group, bits):
    turned = turned ^ ((group >> bits - 1 ^ group) & 1) << bits - 1
    return (turned << 1 & (1 << bits) - 1) | turned >> bits - 1


def relay_kernel(block_ref, after_ref, out_ref):
    del after_ref
    out_ref[...] = block_ref[...]


def chunk_kernel(low_ref, high_ref, after_ref, *outs):
    del after_ref
    half = low_ref.shape[0]
    columns = outs[0].shape[1]
    low = lax.axis_index("seq") % len(outs)
    for r, out in enumerate(outs):
        at = pl.ds(pl.multiple_of((low ^ r) * columns, columns), columns)
        out[:half] = low_ref[:, at]
        out[half:] = high_ref[:, at]


def stack_kernel(after_ref, *refs):
    del after_ref
    for r, ref in enumerate(refs[:-1]):
        refs[-1][r] = ref[...]


def columns_kernel(blocks, *refs):
    parts, out_ref = refs[:blocks], refs[blocks]
    per = parts[0].shape[0]
    bits = blocks.bit_length() - 1
    low = lax.axis_index("seq") % per
    for i in range(blocks):
        high = turned_high(lax.axis_index("head") ^ i, lax.axis_index("seq") // per, bits)
        for r in range(per):
            out_ref[high * per + (low ^ r)] = parts[i][r]


def local_grad_kernel(
    bits, gt_ref, qh_ref, kh_ref, vh_ref, pt_ref, lam_ref, after_ref, *refs
):
    del after_ref
    states, (dq_ref, dk_ref, dv_ref) = refs[:bits], refs[bits:]
    heads_dev, rows, head_dim = qh_ref.shape
    for h in range(heads_dev):
        gt = gt_ref[h * head_dim : (h + 1) * head_dim, :]
        g32 = gt.astype(F32)
        dpt = (mm(vh_ref[h], gt, NN) * weight_of(lam_ref, h, rows)).astype(BF)
        dk_ref[h] = mm(dpt, qh_ref[h], NN)
        dv_ref[h] = mm(pt_ref[h], gt, NT)
        dq = mm(dpt, kh_ref[h], TN)
        for b in range(bits):
            gw = (g32 * upper_weight(lam_ref, b, h, rows)).astype(BF)
            dq = dq + mm(gw, states[b][h], TT)
        dq_ref[h] = dq


def query_grad_kernel(top, gt_ref, lam_ref, dql_ref, state_ref, after_ref, dq_ref):
    del after_ref
    heads_dev, rows, head_dim = dql_ref.shape
    for h in range(heads_dev):
        g32 = gt_ref[h * head_dim : (h + 1) * head_dim, :].astype(F32)
        gw = (g32 * upper_weight(lam_ref, top, h, rows)).astype(BF)
        dq_ref[:, h, :] = dql_ref[h] + mm(gw, state_ref[h], TT)


def later_grad_kernel(top, kh_ref, vh_ref, dkl_ref, dvl_ref, after_ref, *refs):
    del after_ref
    landed, (dk_ref, dv_ref) = refs[:-2], refs[-2:]
    for h in range(kh_ref.shape[0]):
        late = landed_sum(top, [ref[h] for ref in landed]).astype(BF)
        dk_ref[:, h, :] = dkl_ref[h] + mm(vh_ref[h], late, NN)
        dv_ref[:, h, :] = dvl_ref[h] + mm(kh_ref[h], late, NT)


def share_kernel(blocks, att_ref, w_ref, *refs):
    send_ref, kept_ref = refs[-2:]
    width = send_ref.shape[2]
    for i in range(blocks):
        out = send_ref if i % 2 else kept_ref
        column = pl.multiple_of((lax.axis_index("head") ^ i) * width, width)
        out[i // 2] = mm(att_ref[...], w_ref[:, pl.ds(column, width)], NN).astype(out.dtype)


def ring_owner(place, offset, devices):
    at = jnp.where(place % 2 == 0, place // 2, devices - 1 - place // 2)
    at = (at + offset + devices) % devices
    return jnp.where(at < devices // 2, 2 * at, 2 * (devices - 1 - at) + 1)


def proj_kernel(offsets, devices, first, cols_ref, *refs):
    total = None if first else refs[len(offsets)][...]
    for i, (offset, low, high) in enumerate(offsets):
        owner = ring_owner(lax.axis_index("seq"), offset, devices)
        product = mm(refs[i][...], cols_ref[owner, low:high, :], TN)
        total = product if total is None else total + product
    refs[-1][...] = total


def last_kernel(
    offset, devices, cols_ref, low_ref, high_ref, total_ref, after_ref, out_ref, held
):
    del after_ref
    half, block = low_ref.shape[0], out_ref.shape[0]
    at = pl.ds(pl.multiple_of(pl.program_id(0) * block, block), block)
    held[:half] = low_ref[:, at]
    held[half:] = high_ref[:, at]
    owner = ring_owner(lax.axis_index("seq"), offset, devices)
    out_ref[...] = total_ref[at, :] + mm(held[...], cols_ref[owner], TN)


def body(queries, keys, values, level_weights, out_proj, out_grad):
    rows, heads_dev, head_dim = queries.shape
    width = heads_dev * head_dim
    devices = lax.axis_size("seq")
    seq_bits = devices.bit_length() - 1
    heads = lax.axis_size("head")
    head_bits = heads.bit_length() - 1
    columns_dev = out_proj.shape[1] // devices

    head_state = like((heads_dev, head_dim, head_dim), BF)
    pinned_state = pltpu.VMEM((heads_dev, head_dim, head_dim), BF)
    per_head = pltpu.VMEM((heads_dev, rows, head_dim), BF)
    per_head_f32 = pltpu.VMEM((heads_dev, rows, head_dim), F32)
    flops_head = 2 * heads_dev * rows * rows * head_dim
    moved_head = 2 * rows * width
    top = seq_bits - 1

    half = rows // 2
    own_state, kh, vh, own_grad, own_low = pl.pallas_call(
        state_kernel,
        out_shape=(head_state, per_head, per_head, like(out_grad.shape, BF), like((half, width), BF)),
        in_specs=[ANY] * 3,
        out_specs=(VMEM,) * 5,
        scratch_shapes=[
            pltpu.VMEM(keys.shape, F32),
            pltpu.VMEM(keys.shape, F32),
            pltpu.SemaphoreType.DMA((4,)),
        ],
        compiler_params=PARAMS,
        cost_estimate=cost(flops_head, 7 * moved_head),
    )(hbm(keys), hbm(values), hbm(out_grad))

    def to_group(block, i):
        return lax.ppermute(block, "head", [(at, at ^ i) for at in range(heads)])

    def every_group(block):
        blocks = {0: block}
        for digit in reversed(range(head_bits)):
            for i in sorted(blocks):
                blocks[i ^ 1 << digit] = to_group(blocks[i], 1 << digit)
        return [blocks[i] for i in range(heads)]

    probs_t, att_local, qh, qw, lam, w = pl.pallas_call(
        local_kernel,
        out_shape=(
            pltpu.VMEM((heads_dev, rows, rows), BF),
            per_head_f32,
            per_head,
            pltpu.VMEM((seq_bits, heads_dev, rows, head_dim), BF),
            pltpu.VMEM(level_weights.shape, F32),
            pltpu.VMEM(out_proj.shape, BF),
        ),
        in_specs=[ANY, VMEM, VMEM, ANY, ANY],
        out_specs=(VMEM,) * 6,
        scratch_shapes=[
            pltpu.VMEM(queries.shape, F32),
            pltpu.VMEM((rows, rows), F32),
            pltpu.SemaphoreType.DMA((10,)),
        ],
        compiler_params=PARAMS,
        cost_estimate=cost(2 * flops_head, 12 * moved_head),
    )(hbm(queries), kh, vh, hbm(level_weights), hbm(out_proj))

    def relayed(block):
        return pl.pallas_call(
            relay_kernel,
            out_shape=like(block.shape, block.dtype),
            in_specs=[VMEM, ANY],
            out_specs=VMEM,
            compiler_params=PARAMS,
            cost_estimate=cost(0, 2 * moved_head),
        )(block, qw)

    grad_blocks = {0: own_grad}
    for digit in reversed(range(head_bits)):
        for i in sorted(grad_blocks):
            block = relayed(grad_blocks[i]) if i else own_grad
            grad_blocks[i ^ 1 << digit] = to_group(block, 1 << digit)
    grad_blocks = [grad_blocks[i] for i in range(heads)]

    per = devices // heads
    def turn_route(shift):
        return [
            (
                (high * per + low) * heads + (group_at ^ shift),
                (group_at * per + low) * heads + turned_group(high, group_at, head_bits),
            )
            for high in range(heads)
            for low in range(per)
            for group_at in range(heads)
        ]

    axes, far = ("seq", "head"), heads // 2
    turned = [
        lax.ppermute(own_low, axes, turn_route(0)),
        lax.ppermute(grad_blocks[far][half:], axes, turn_route(far)),
    ]
    partner_states = []
    running, arrived = own_state, None
    for digit in range(top):
        if arrived is not None:
            running = pl.pallas_call(
                running_kernel,
                out_shape=head_state,
                in_specs=[VMEM] * 2 + [ANY],
                out_specs=VMEM,
                compiler_params=PARAMS,
                cost_estimate=cost(0, 3 * moved_head),
            )(running, arrived, qw)
        arrived = across(running, "seq", digit)
        partner_states.append(arrived)

    gt, *grad_sums = pl.pallas_call(
        functools.partial(cotangent_kernel, heads, seq_bits),
        out_shape=(pltpu.VMEM((width, rows), BF),) + (pinned_state,) * seq_bits,
        in_specs=[VMEM] * (heads + 2) + [ANY],
        out_specs=(VMEM,) * (1 + seq_bits),
        compiler_params=PARAMS,
        cost_estimate=cost(2 * rows * width * out_proj.shape[1], 2 * width * out_proj.shape[1]),
    )(*grad_blocks, w, qw, running)

    meeting = pl.pallas_call(
        functools.partial(meet_kernel, top)
        if arrived is not None
        else lambda grad_ref, running_ref, out_ref: meet_kernel(
            top, grad_ref, running_ref, None, out_ref
        ),
        out_shape=head_state,
        in_specs=[VMEM] * (2 if arrived is None else 3),
        out_specs=VMEM,
        compiler_params=PARAMS,
        cost_estimate=cost(0, 4 * moved_head),
    )(grad_sums[top], running, *([] if arrived is None else [arrived]))
    landed = [across(meeting, "seq", top)]
    partner_states.append(landed[0])

    chunks = pl.pallas_call(
        chunk_kernel,
        out_shape=(like((rows, columns_dev), BF),) * per,
        in_specs=[VMEM, VMEM, ANY],
        out_specs=(VMEM,) * per,
        compiler_params=PARAMS,
        cost_estimate=cost(0, 2 * moved_head),
    )(*turned, meeting)
    own_chunks = chunks
    chunks = [chunks[0]] + [
        lax.ppermute(chunks[r], "seq", [(at, at ^ r) for at in range(devices)])
        for r in range(1, per)
    ]
    stacked = pl.pallas_call(
        stack_kernel,
        out_shape=like((per, rows, columns_dev), BF),
        in_specs=[ANY] + [VMEM] * per,
        out_specs=VMEM,
        compiler_params=PARAMS,
        cost_estimate=cost(0, 2 * moved_head),
    )(meeting, *chunks)
    column_blocks = [stacked] + [to_group(stacked, i) for i in range(1, heads)]

    grad_columns = pl.pallas_call(
        functools.partial(columns_kernel, heads),
        out_shape=pltpu.VMEM((devices, rows, columns_dev), BF),
        in_specs=[VMEM] * heads,
        out_specs=VMEM,
        compiler_params=PARAMS,
        cost_estimate=cost(0, 8 * moved_head),
    )(*column_blocks)

    query_local, key_local, value_local = pl.pallas_call(
        functools.partial(local_grad_kernel, top),
        out_shape=(per_head_f32,) * 3,
        in_specs=[VMEM] * 6 + [ANY] + [VMEM] * top,
        out_specs=(VMEM,) * 3,
        compiler_params=PARAMS,
        cost_estimate=cost((4 + top) * flops_head, 14 * moved_head),
    )(gt, qh, kh, vh, probs_t, lam, meeting, *partner_states[:top])

    attended = pl.pallas_call(
        functools.partial(attended_kernel, seq_bits),
        out_shape=like((rows, width), BF),
        in_specs=[VMEM] * (2 + seq_bits) + [ANY] * 2,
        out_specs=VMEM,
        compiler_params=PARAMS,
        cost_estimate=cost(seq_bits * flops_head, 8 * moved_head),
    )(att_local, qw, *partner_states, key_local, own_chunks[-1])

    first_pending = attended
    for digit in reversed(range(top)):
        outgoing = pl.pallas_call(
            functools.partial(pending_kernel, top),
            out_shape=head_state,
            in_specs=[VMEM, ANY] + [VMEM] * len(landed),
            out_specs=VMEM,
            compiler_params=PARAMS,
            cost_estimate=cost(0, 4 * moved_head),
        )(grad_sums[digit], attended, *landed)
        if len(landed) == 1:
            first_pending = outgoing
        landed.append(across(outgoing, "seq", digit))

    query_grad = pl.pallas_call(
        functools.partial(query_grad_kernel, top),
        out_shape=like((rows, heads_dev, head_dim), F32),
        in_specs=[VMEM] * 4 + [ANY],
        out_specs=VMEM,
        compiler_params=PARAMS,
        cost_estimate=cost(flops_head, 6 * moved_head),
    )(gt, lam, query_local, partner_states[top], attended)

    send, kept = pl.pallas_call(
        functools.partial(share_kernel, heads),
        out_shape=(like((heads // 2, rows, width), BF), like((heads // 2, rows, width), F32)),
        in_specs=[VMEM] * 2 + [ANY],
        out_specs=(VMEM,) * 2,
        compiler_params=PARAMS,
        cost_estimate=cost(2 * rows * width * out_proj.shape[1], 2 * width * out_proj.shape[1]),
    )(attended, w, stacked)
    for digit in range(head_bits):
        kept = kept + to_group(send, 1 << digit).astype(F32)
        if digit < head_bits - 1:
            send, kept = kept[1::2].astype(BF), kept[0::2]
    mixed = kept[0].astype(BF)

    ring = list(range(0, devices, 2)) + list(range(devices - 1, 0, -2))
    forward = [(ring[i], ring[(i + 1) % devices]) for i in range(devices)]
    backward = [(b, a) for a, b in forward]

    def accumulate(total, blocks, offsets):
        operands = blocks if total is None else blocks + [total]
        return pl.pallas_call(
            functools.partial(proj_kernel, offsets, devices, total is None),
            out_shape=pltpu.VMEM((width, columns_dev), F32),
            in_specs=[VMEM] * (1 + len(operands)),
            out_specs=VMEM,
            compiler_params=PARAMS,
            cost_estimate=cost(
                2 * len(blocks) * rows * width * columns_dev, 4 * width * columns_dev
            ),
        )(grad_columns, *operands)

    blocks, offsets = [attended], [(0, 0, rows)]
    ahead = behind = attended
    steps, total = devices // 2, None
    for step in range(1, steps):
        ahead = lax.ppermute(ahead, "seq", forward)
        behind = lax.ppermute(behind, "seq", backward)
        blocks += [ahead, behind]
        offsets += [(-step, 0, rows), (step, 0, rows)]
        if step == steps - 2:
            total = accumulate(None, blocks, offsets)
            blocks, offsets = [], []
    if blocks:
        total = accumulate(total, blocks, offsets)
    last = [
        lax.ppermute(ahead[:half], "seq", forward),
        lax.ppermute(behind[half:], "seq", backward),
    ]
    key_grad, value_grad = pl.pallas_call(
        functools.partial(later_grad_kernel, top),
        out_shape=(like((rows, heads_dev, head_dim), F32),) * 2,
        in_specs=[VMEM] * 4 + [ANY] + [VMEM] * seq_bits,
        out_specs=(VMEM,) * 2,
        compiler_params=PARAMS,
        cost_estimate=cost(2 * flops_head, 11 * moved_head),
    )(kh, vh, key_local, value_local, total, *landed)
    quarter_rows = width // 4
    proj_grad = pl.pallas_call(
        functools.partial(last_kernel, steps, devices),
        out_shape=like((width, columns_dev), F32),
        grid=(4,),
        in_specs=[
            VMEM,
            VMEM,
            VMEM,
            VMEM,
            ANY,
        ],
        out_specs=pl.BlockSpec((quarter_rows, columns_dev), lambda i: (i, 0)),
        scratch_shapes=[pltpu.VMEM((rows, quarter_rows), BF)],
        compiler_params=PARAMS,
        cost_estimate=cost(2 * rows * width * columns_dev, 8 * width * columns_dev),
    )(grad_columns, *last, total, hbm(key_grad))
    return (mixed, query_grad, key_grad, value_grad, proj_grad)


def solution(mesh):
    placed = (
        P("seq", "head", None),
        P("seq", "head", None),
        P("seq", "head", None),
        P(None, "head", "seq"),
        P("head", None),
        P("seq", "head"),
    )
    return jax.shard_map(
        body,
        mesh=mesh,
        in_specs=placed,
        out_specs=(
            P("seq", "head"),
            P("seq", "head", None),
            P("seq", "head", None),
            P("seq", "head", None),
            P("head", "seq"),
        ),
        check_vma=False,
    )
```

```python
import functools

import jax
import jax.numpy as jnp
from jax import lax
from jax.experimental import pallas as pl
from jax.experimental.pallas import tpu as pltpu
from jax.sharding import PartitionSpec as P

CH = 64
BF = jnp.bfloat16
F32 = jnp.float32
NN = (((1,), (0,)), ((), ()))
NT = (((1,), (1,)), ((), ()))
TN = (((0,), (0,)), ((), ()))
TT = (((0,), (1,)), ((), ()))
VMEM = pl.BlockSpec(memory_space=pltpu.VMEM)
ANY = pl.BlockSpec(memory_space=pl.ANY)
PARAMS = pltpu.CompilerParams(vmem_limit_bytes=14 * 2**20)


def mm(a, b, dims):
    return lax.dot_general(a, b, dims, preferred_element_type=F32)


def cost(flops, moved):
    return pl.CostEstimate(flops=flops, bytes_accessed=moved, transcendentals=0)


def like(shape, dtype):
    return jax.ShapeDtypeStruct(shape, dtype)


def across(block, axis, stride, up_only=False, down_only=False):
    count = lax.axis_size(axis)
    route = []
    for low in range(count):
        high = low | 1 << stride
        if high != low and high < count:
            if not down_only:
                route.append((low, high))
            if not up_only:
                route.append((high, low))
    return lax.ppermute(block, axis, route)


def hbm(array):
    return pltpu.with_memory_space_constraint(array, pltpu.HBM)


def state_kernel(k_hbm, v_hbm, grad_hbm, *refs):
    s_ref, kh_ref, vh_ref, grad_ref, low_ref, k_ref, v_ref, sems = refs
    copies = [
        pltpu.make_async_copy(k_hbm, k_ref, sems.at[0]),
        pltpu.make_async_copy(v_hbm, v_ref, sems.at[1]),
        pltpu.make_async_copy(grad_hbm, grad_ref, sems.at[2]),
        pltpu.make_async_copy(grad_hbm.at[pl.ds(0, low_ref.shape[0])], low_ref, sems.at[3]),
    ]
    for copy in copies:
        copy.start()
    for copy in copies[:2]:
        copy.wait()
    for h in range(k_ref.shape[1]):
        k = k_ref[:, h, :].astype(BF)
        v = v_ref[:, h, :].astype(BF)
        kh_ref[h] = k
        vh_ref[h] = v
        s_ref[h] = mm(k, v, TN).astype(BF)
    copies[2].wait()
    copies[3].wait()


def weight_of(lam_ref, h, rows):
    local_bits = (rows // CH).bit_length() - 1
    s = lax.broadcasted_iota(jnp.int32, (rows, rows), 0)
    t = lax.broadcasted_iota(jnp.int32, (rows, rows), 1)
    differ = (s // CH) ^ (t // CH)
    weight = jnp.broadcast_to(lam_ref[0, h : h + 1, :], (rows, rows))
    for digit in range(local_bits):
        weight = jnp.where(differ >= 1 << digit, lam_ref[1 + digit, h : h + 1, :], weight)
    return jnp.where(s <= t, weight, 0.0)


def upper_weight(lam_ref, b, h, rows):
    local_bits = (rows // CH).bit_length() - 1
    upper = (lax.axis_index("seq") >> b & 1).astype(F32)
    return lam_ref[1 + local_bits + b, h : h + 1, :] * upper


def local_kernel(q_hbm, kh_ref, vh_ref, lam_hbm, w_hbm, *refs):
    pt_ref, att_ref, qh_ref, qw_ref, lam_ref, w_ref, q_ref, lam_rows, sems = refs
    pieces = sems.shape[0] - 2
    share = w_hbm.shape[0] // pieces
    copies = [
        pltpu.make_async_copy(q_hbm, q_ref, sems.at[0]),
        pltpu.make_async_copy(lam_hbm, lam_ref, sems.at[1]),
    ]
    for i in range(pieces):
        piece = pl.ds(i * share, share)
        copies.append(pltpu.make_async_copy(w_hbm.at[piece], w_ref.at[piece], sems.at[2 + i]))
    for copy in copies:
        copy.start()
    for copy in copies[:2]:
        copy.wait()
    rows, heads_dev, _ = q_ref.shape
    bits = qw_ref.shape[0]
    lam_rows[...] = jnp.zeros_like(lam_rows)
    for b in range(bits):
        for h in range(heads_dev):
            at = b * heads_dev + h
            lam_rows[at : at + 1, :] = upper_weight(lam_ref, b, h, rows)
    lam_columns = lam_rows[...].T
    for h in range(heads_dev):
        q32 = q_ref[:, h, :]
        q = q32.astype(BF)
        qh_ref[h] = q
        for b in range(bits):
            at = b * heads_dev + h
            qw_ref[b, h] = (q32 * lam_columns[:, at : at + 1]).astype(BF)
        pt = (mm(kh_ref[h], q, NT) * weight_of(lam_ref, h, rows)).astype(BF)
        pt_ref[h] = pt
        att_ref[h] = mm(pt, vh_ref[h], TN)
    for copy in copies[2:]:
        copy.wait()


def attended_kernel(bits, att_ref, qw_ref, *refs):
    states, out_ref = refs[:bits], refs[-1]
    heads_dev, _, head_dim = att_ref.shape
    for h in range(heads_dev):
        total = att_ref[h]
        for b in range(bits):
            total = total + mm(qw_ref[b, h], states[b][h], NN)
        out_ref[:, h * head_dim : (h + 1) * head_dim] = total.astype(BF)


def cotangent_kernel(blocks, bits, *refs):
    parts, (w_ref, qw_ref, _, gt_ref), sums = (
        refs[:blocks],
        refs[blocks : blocks + 4],
        refs[blocks + 4 :],
    )
    deep = parts[0].shape[1]
    _, heads_dev, _, head_dim = qw_ref.shape
    total = None
    for i in range(blocks):
        column = pl.multiple_of((lax.axis_index("head") ^ i) * deep, deep)
        product = mm(w_ref[:, pl.ds(column, deep)], parts[i][...], NT)
        total = product if total is None else total + product
    for h in range(heads_dev):
        gt = total[h * head_dim : (h + 1) * head_dim].astype(BF)
        gt_ref[h * head_dim : (h + 1) * head_dim, :] = gt
        for b in range(bits):
            sums[b][h] = mm(gt, qw_ref[b, h], NN).astype(BF)


def running_kernel(running_ref, arrived_ref, *refs):
    refs[-1][...] = (running_ref[...].astype(F32) + arrived_ref[...].astype(F32)).astype(BF)


def meet_kernel(top, grad_ref, running_ref, arrived_ref, out_ref):
    upper = (lax.axis_index("seq") >> top & 1) == 1
    running = running_ref[...].astype(F32)
    if arrived_ref is not None:
        running = running + arrived_ref[...].astype(F32)
    out_ref[...] = jnp.where(upper, grad_ref[...], running.astype(BF))


def landed_sum(top, landed):
    upper = (lax.axis_index("seq") >> top & 1) == 1
    total = jnp.where(upper, 0.0, landed[0].astype(F32))
    for block in landed[1:]:
        total = total + block.astype(F32)
    return total


def pending_kernel(top, own_ref, after_ref, *refs):
    del after_ref
    landed, out_ref = [ref[...] for ref in refs[:-1]], refs[-1]
    out_ref[...] = (own_ref[...].astype(F32) + landed_sum(top, landed)).astype(BF)


def turned_group(high, group, bits):
    turned = high >> 1 | (high & 1) << bits - 1
    return turned ^ ((group >> bits - 1 ^ group) & 1) << bits - 1


def turned_high(turned, group, bits):
    turned = turned ^ ((group >> bits - 1 ^ group) & 1) << bits - 1
    return (turned << 1 & (1 << bits) - 1) | turned >> bits - 1


def relay_kernel(block_ref, after_ref, out_ref):
    del after_ref
    out_ref[...] = block_ref[...]


def chunk_kernel(low_ref, high_ref, after_ref, *outs):
    del after_ref
    half = low_ref.shape[0]
    columns = outs[0].shape[1]
    low = lax.axis_index("seq") % len(outs)
    for r, out in enumerate(outs):
        at = pl.ds(pl.multiple_of((low ^ r) * columns, columns), columns)
        out[:half] = low_ref[:, at]
        out[half:] = high_ref[:, at]


def stack_kernel(after_ref, *refs):
    del after_ref
    for r, ref in enumerate(refs[:-1]):
        refs[-1][r] = ref[...]


def columns_kernel(blocks, *refs):
    parts, out_ref = refs[:blocks], refs[blocks]
    per = parts[0].shape[0]
    bits = blocks.bit_length() - 1
    low = lax.axis_index("seq") % per
    for i in range(blocks):
        high = turned_high(lax.axis_index("head") ^ i, lax.axis_index("seq") // per, bits)
        for r in range(per):
            out_ref[high * per + (low ^ r)] = parts[i][r]


def local_grad_kernel(
    bits, gt_ref, qh_ref, kh_ref, vh_ref, pt_ref, lam_ref, after_ref, *refs
):
    del after_ref
    states, (dq_ref, dk_ref, dv_ref) = refs[:bits], refs[bits:]
    heads_dev, rows, head_dim = qh_ref.shape
    for h in range(heads_dev):
        gt = gt_ref[h * head_dim : (h + 1) * head_dim, :]
        g32 = gt.astype(F32)
        dpt = (mm(vh_ref[h], gt, NN) * weight_of(lam_ref, h, rows)).astype(BF)
        dk_ref[h] = mm(dpt, qh_ref[h], NN)
        dv_ref[h] = mm(pt_ref[h], gt, NT)
        dq = mm(dpt, kh_ref[h], TN)
        for b in range(bits):
            gw = (g32 * upper_weight(lam_ref, b, h, rows)).astype(BF)
            dq = dq + mm(gw, states[b][h], TT)
        dq_ref[h] = dq


def query_grad_kernel(top, gt_ref, lam_ref, dql_ref, state_ref, after_ref, dq_ref):
    del after_ref
    heads_dev, rows, head_dim = dql_ref.shape
    for h in range(heads_dev):
        g32 = gt_ref[h * head_dim : (h + 1) * head_dim, :].astype(F32)
        gw = (g32 * upper_weight(lam_ref, top, h, rows)).astype(BF)
        dq_ref[:, h, :] = dql_ref[h] + mm(gw, state_ref[h], TT)


def later_grad_kernel(top, kh_ref, vh_ref, dkl_ref, dvl_ref, after_ref, *refs):
    del after_ref
    landed, (dk_ref, dv_ref) = refs[:-2], refs[-2:]
    for h in range(kh_ref.shape[0]):
        late = landed_sum(top, [ref[h] for ref in landed]).astype(BF)
        dk_ref[:, h, :] = dkl_ref[h] + mm(vh_ref[h], late, NN)
        dv_ref[:, h, :] = dvl_ref[h] + mm(kh_ref[h], late, NT)


def share_kernel(blocks, att_ref, w_ref, *refs):
    send_ref, kept_ref = refs[-2:]
    width = send_ref.shape[2]
    for i in range(blocks):
        out = send_ref if i % 2 else kept_ref
        column = pl.multiple_of((lax.axis_index("head") ^ i) * width, width)
        out[i // 2] = mm(att_ref[...], w_ref[:, pl.ds(column, width)], NN).astype(out.dtype)


def ring_owner(place, offset, devices):
    at = jnp.where(place % 2 == 0, place // 2, devices - 1 - place // 2)
    at = (at + offset + devices) % devices
    return jnp.where(at < devices // 2, 2 * at, 2 * (devices - 1 - at) + 1)


def proj_kernel(offsets, devices, first, cols_ref, *refs):
    total = None if first else refs[len(offsets)][...]
    for i, (offset, low, high) in enumerate(offsets):
        owner = ring_owner(lax.axis_index("seq"), offset, devices)
        product = mm(refs[i][...], cols_ref[owner, low:high, :], TN)
        total = product if total is None else total + product
    refs[-1][...] = total


def last_kernel(
    offset, devices, cols_ref, low_ref, high_ref, total_ref, after_ref, out_ref, held
):
    del after_ref
    half, block = low_ref.shape[0], out_ref.shape[0]
    at = pl.ds(pl.multiple_of(pl.program_id(0) * block, block), block)
    held[:half] = low_ref[:, at]
    held[half:] = high_ref[:, at]
    owner = ring_owner(lax.axis_index("seq"), offset, devices)
    out_ref[...] = total_ref[at, :] + mm(held[...], cols_ref[owner], TN)


def body(queries, keys, values, level_weights, out_proj, out_grad):
    rows, heads_dev, head_dim = queries.shape
    width = heads_dev * head_dim
    devices = lax.axis_size("seq")
    seq_bits = devices.bit_length() - 1
    heads = lax.axis_size("head")
    head_bits = heads.bit_length() - 1
    columns_dev = out_proj.shape[1] // devices

    head_state = like((heads_dev, head_dim, head_dim), BF)
    pinned_state = pltpu.VMEM((heads_dev, head_dim, head_dim), BF)
    per_head = pltpu.VMEM((heads_dev, rows, head_dim), BF)
    per_head_f32 = pltpu.VMEM((heads_dev, rows, head_dim), F32)
    flops_head = 2 * heads_dev * rows * rows * head_dim
    moved_head = 2 * rows * width
    top = seq_bits - 1

    half = rows // 2
    own_state, kh, vh, own_grad, own_low = pl.pallas_call(
        state_kernel,
        out_shape=(head_state, per_head, per_head, like(out_grad.shape, BF), like((half, width), BF)),
        in_specs=[ANY] * 3,
        out_specs=(VMEM,) * 5,
        scratch_shapes=[
            pltpu.VMEM(keys.shape, F32),
            pltpu.VMEM(keys.shape, F32),
            pltpu.SemaphoreType.DMA((4,)),
        ],
        compiler_params=PARAMS,
        cost_estimate=cost(flops_head, 7 * moved_head),
    )(hbm(keys), hbm(values), hbm(out_grad))

    def to_group(block, i):
        return lax.ppermute(block, "head", [(at, at ^ i) for at in range(heads)])

    def every_group(block):
        blocks = {0: block}
        for digit in reversed(range(head_bits)):
            for i in sorted(blocks):
                blocks[i ^ 1 << digit] = to_group(blocks[i], 1 << digit)
        return [blocks[i] for i in range(heads)]

    probs_t, att_local, qh, qw, lam, w = pl.pallas_call(
        local_kernel,
        out_shape=(
            pltpu.VMEM((heads_dev, rows, rows), BF),
            per_head_f32,
            per_head,
            pltpu.VMEM((seq_bits, heads_dev, rows, head_dim), BF),
            pltpu.VMEM(level_weights.shape, F32),
            pltpu.VMEM(out_proj.shape, BF),
        ),
        in_specs=[ANY, VMEM, VMEM, ANY, ANY],
        out_specs=(VMEM,) * 6,
        scratch_shapes=[
            pltpu.VMEM(queries.shape, F32),
            pltpu.VMEM((rows, rows), F32),
            pltpu.SemaphoreType.DMA((10,)),
        ],
        compiler_params=PARAMS,
        cost_estimate=cost(2 * flops_head, 12 * moved_head),
    )(hbm(queries), kh, vh, hbm(level_weights), hbm(out_proj))

    def relayed(block):
        return pl.pallas_call(
            relay_kernel,
            out_shape=like(block.shape, block.dtype),
            in_specs=[VMEM, ANY],
            out_specs=VMEM,
            compiler_params=PARAMS,
            cost_estimate=cost(0, 2 * moved_head),
        )(block, qw)

    grad_blocks = {0: own_grad}
    for digit in reversed(range(head_bits)):
        for i in sorted(grad_blocks):
            block = relayed(grad_blocks[i]) if i else own_grad
            grad_blocks[i ^ 1 << digit] = to_group(block, 1 << digit)
    grad_blocks = [grad_blocks[i] for i in range(heads)]

    per = devices // heads
    def turn_route(shift):
        return [
            (
                (high * per + low) * heads + (group_at ^ shift),
                (group_at * per + low) * heads + turned_group(high, group_at, head_bits),
            )
            for high in range(heads)
            for low in range(per)
            for group_at in range(heads)
        ]

    axes, far = ("seq", "head"), heads // 2
    turned = [
        lax.ppermute(own_low, axes, turn_route(0)),
        lax.ppermute(grad_blocks[far][half:], axes, turn_route(far)),
    ]
    partner_states = []
    running, arrived = own_state, None
    for digit in range(top):
        if arrived is not None:
            running = pl.pallas_call(
                running_kernel,
                out_shape=head_state,
                in_specs=[VMEM] * 2 + [ANY],
                out_specs=VMEM,
                compiler_params=PARAMS,
                cost_estimate=cost(0, 3 * moved_head),
            )(running, arrived, qw)
        arrived = across(running, "seq", digit)
        partner_states.append(arrived)

    gt, *grad_sums = pl.pallas_call(
        functools.partial(cotangent_kernel, heads, seq_bits),
        out_shape=(pltpu.VMEM((width, rows), BF),) + (pinned_state,) * seq_bits,
        in_specs=[VMEM] * (heads + 2) + [ANY],
        out_specs=(VMEM,) * (1 + seq_bits),
        compiler_params=PARAMS,
        cost_estimate=cost(2 * rows * width * out_proj.shape[1], 2 * width * out_proj.shape[1]),
    )(*grad_blocks, w, qw, running)

    meeting = pl.pallas_call(
        functools.partial(meet_kernel, top)
        if arrived is not None
        else lambda grad_ref, running_ref, out_ref: meet_kernel(
            top, grad_ref, running_ref, None, out_ref
        ),
        out_shape=head_state,
        in_specs=[VMEM] * (2 if arrived is None else 3),
        out_specs=VMEM,
        compiler_params=PARAMS,
        cost_estimate=cost(0, 4 * moved_head),
    )(grad_sums[top], running, *([] if arrived is None else [arrived]))
    landed = [across(meeting, "seq", top)]
    partner_states.append(landed[0])

    chunks = pl.pallas_call(
        chunk_kernel,
        out_shape=(like((rows, columns_dev), BF),) * per,
        in_specs=[VMEM, VMEM, ANY],
        out_specs=(VMEM,) * per,
        compiler_params=PARAMS,
        cost_estimate=cost(0, 2 * moved_head),
    )(*turned, meeting)
    own_chunks = chunks
    chunks = [chunks[0]] + [
        lax.ppermute(chunks[r], "seq", [(at, at ^ r) for at in range(devices)])
        for r in range(1, per)
    ]
    stacked = pl.pallas_call(
        stack_kernel,
        out_shape=like((per, rows, columns_dev), BF),
        in_specs=[ANY] + [VMEM] * per,
        out_specs=VMEM,
        compiler_params=PARAMS,
        cost_estimate=cost(0, 2 * moved_head),
    )(meeting, *chunks)
    column_blocks = every_group(stacked)

    grad_columns = pl.pallas_call(
        functools.partial(columns_kernel, heads),
        out_shape=pltpu.VMEM((devices, rows, columns_dev), BF),
        in_specs=[VMEM] * heads,
        out_specs=VMEM,
        compiler_params=PARAMS,
        cost_estimate=cost(0, 8 * moved_head),
    )(*column_blocks)

    query_local, key_local, value_local = pl.pallas_call(
        functools.partial(local_grad_kernel, top),
        out_shape=(per_head_f32,) * 3,
        in_specs=[VMEM] * 6 + [ANY] + [VMEM] * top,
        out_specs=(VMEM,) * 3,
        compiler_params=PARAMS,
        cost_estimate=cost((4 + top) * flops_head, 14 * moved_head),
    )(gt, qh, kh, vh, probs_t, lam, meeting, *partner_states[:top])

    attended = pl.pallas_call(
        functools.partial(attended_kernel, seq_bits),
        out_shape=like((rows, width), BF),
        in_specs=[VMEM] * (2 + seq_bits) + [ANY] * 2,
        out_specs=VMEM,
        compiler_params=PARAMS,
        cost_estimate=cost(seq_bits * flops_head, 8 * moved_head),
    )(att_local, qw, *partner_states, key_local, own_chunks[-1])

    first_pending = attended
    for digit in reversed(range(top)):
        outgoing = pl.pallas_call(
            functools.partial(pending_kernel, top),
            out_shape=head_state,
            in_specs=[VMEM, ANY] + [VMEM] * len(landed),
            out_specs=VMEM,
            compiler_params=PARAMS,
            cost_estimate=cost(0, 4 * moved_head),
        )(grad_sums[digit], attended, *landed)
        if len(landed) == 1:
            first_pending = outgoing
        landed.append(across(outgoing, "seq", digit))

    query_grad = pl.pallas_call(
        functools.partial(query_grad_kernel, top),
        out_shape=like((rows, heads_dev, head_dim), F32),
        in_specs=[VMEM] * 4 + [ANY],
        out_specs=VMEM,
        compiler_params=PARAMS,
        cost_estimate=cost(flops_head, 6 * moved_head),
    )(gt, lam, query_local, partner_states[top], attended)

    send, kept = pl.pallas_call(
        functools.partial(share_kernel, heads),
        out_shape=(like((heads // 2, rows, width), BF), like((heads // 2, rows, width), F32)),
        in_specs=[VMEM] * 2 + [ANY],
        out_specs=(VMEM,) * 2,
        compiler_params=PARAMS,
        cost_estimate=cost(2 * rows * width * out_proj.shape[1], 2 * width * out_proj.shape[1]),
    )(attended, w, stacked)
    for digit in range(head_bits):
        kept = kept + to_group(send, 1 << digit).astype(F32)
        if digit < head_bits - 1:
            send, kept = kept[1::2].astype(BF), kept[0::2]
    mixed = kept[0].astype(BF)

    ring = list(range(0, devices, 2)) + list(range(devices - 1, 0, -2))
    forward = [(ring[i], ring[(i + 1) % devices]) for i in range(devices)]
    backward = [(b, a) for a, b in forward]

    def accumulate(total, blocks, offsets):
        operands = blocks if total is None else blocks + [total]
        return pl.pallas_call(
            functools.partial(proj_kernel, offsets, devices, total is None),
            out_shape=pltpu.VMEM((width, columns_dev), F32),
            in_specs=[VMEM] * (1 + len(operands)),
            out_specs=VMEM,
            compiler_params=PARAMS,
            cost_estimate=cost(
                2 * len(blocks) * rows * width * columns_dev, 4 * width * columns_dev
            ),
        )(grad_columns, *operands)

    blocks, offsets = [attended], [(0, 0, rows)]
    ahead = behind = attended
    steps, total = devices // 2, None
    for step in range(1, steps):
        ahead = lax.ppermute(ahead, "seq", forward)
        behind = lax.ppermute(behind, "seq", backward)
        blocks += [ahead, behind]
        offsets += [(-step, 0, rows), (step, 0, rows)]
        if step == steps - 2:
            total = accumulate(None, blocks, offsets)
            blocks, offsets = [], []
    if blocks:
        total = accumulate(total, blocks, offsets)
    last = [
        lax.ppermute(ahead[:half], "seq", forward),
        lax.ppermute(behind[half:], "seq", backward),
    ]
    key_grad, value_grad = pl.pallas_call(
        functools.partial(later_grad_kernel, top),
        out_shape=(like((rows, heads_dev, head_dim), F32),) * 2,
        in_specs=[VMEM] * 4 + [ANY] + [VMEM] * seq_bits,
        out_specs=(VMEM,) * 2,
        compiler_params=PARAMS,
        cost_estimate=cost(2 * flops_head, 11 * moved_head),
    )(kh, vh, key_local, value_local, total, *landed)
    quarter_rows = width // 4
    proj_grad = pl.pallas_call(
        functools.partial(last_kernel, steps, devices),
        out_shape=like((width, columns_dev), F32),
        grid=(4,),
        in_specs=[
            VMEM,
            VMEM,
            VMEM,
            VMEM,
            ANY,
        ],
        out_specs=pl.BlockSpec((quarter_rows, columns_dev), lambda i: (i, 0)),
        scratch_shapes=[pltpu.VMEM((rows, quarter_rows), BF)],
        compiler_params=PARAMS,
        cost_estimate=cost(2 * rows * width * columns_dev, 8 * width * columns_dev),
    )(grad_columns, *last, total, hbm(key_grad))
    return (mixed, query_grad, key_grad, value_grad, proj_grad)


def solution(mesh):
    placed = (
        P("seq", "head", None),
        P("seq", "head", None),
        P("seq", "head", None),
        P(None, "head", "seq"),
        P("head", None),
        P("seq", "head"),
    )
    return jax.shard_map(
        body,
        mesh=mesh,
        in_specs=placed,
        out_specs=(
            P("seq", "head"),
            P("seq", "head", None),
            P("seq", "head", None),
            P("seq", "head", None),
            P("head", "seq"),
        ),
        check_vma=False,
    )
```

```python
import functools

import jax
import jax.numpy as jnp
from jax import lax
from jax.experimental import pallas as pl
from jax.experimental.pallas import tpu as pltpu
from jax.sharding import PartitionSpec as P

CH = 64
BF = jnp.bfloat16
F32 = jnp.float32
NN = (((1,), (0,)), ((), ()))
NT = (((1,), (1,)), ((), ()))
TN = (((0,), (0,)), ((), ()))
TT = (((0,), (1,)), ((), ()))
VMEM = pl.BlockSpec(memory_space=pltpu.VMEM)
ANY = pl.BlockSpec(memory_space=pl.ANY)
PARAMS = pltpu.CompilerParams(vmem_limit_bytes=14 * 2**20)


def mm(a, b, dims):
    return lax.dot_general(a, b, dims, preferred_element_type=F32)


def cost(flops, moved):
    return pl.CostEstimate(flops=flops, bytes_accessed=moved, transcendentals=0)


def like(shape, dtype):
    return jax.ShapeDtypeStruct(shape, dtype)


def across(block, axis, stride, up_only=False, down_only=False):
    count = lax.axis_size(axis)
    route = []
    for low in range(count):
        high = low | 1 << stride
        if high != low and high < count:
            if not down_only:
                route.append((low, high))
            if not up_only:
                route.append((high, low))
    return lax.ppermute(block, axis, route)


def hbm(array):
    return pltpu.with_memory_space_constraint(array, pltpu.HBM)


def state_kernel(k_hbm, v_hbm, grad_hbm, *refs):
    s_ref, kh_ref, vh_ref, grad_ref, low_ref, k_ref, v_ref, sems = refs
    copies = [
        pltpu.make_async_copy(k_hbm, k_ref, sems.at[0]),
        pltpu.make_async_copy(v_hbm, v_ref, sems.at[1]),
        pltpu.make_async_copy(grad_hbm, grad_ref, sems.at[2]),
        pltpu.make_async_copy(grad_hbm.at[pl.ds(0, low_ref.shape[0])], low_ref, sems.at[3]),
    ]
    for copy in copies:
        copy.start()
    for copy in copies[:2]:
        copy.wait()
    for h in range(k_ref.shape[1]):
        k = k_ref[:, h, :].astype(BF)
        v = v_ref[:, h, :].astype(BF)
        kh_ref[h] = k
        vh_ref[h] = v
        s_ref[h] = mm(k, v, TN).astype(BF)
    copies[2].wait()
    copies[3].wait()


def weight_of(lam_ref, h, rows):
    local_bits = (rows // CH).bit_length() - 1
    s = lax.broadcasted_iota(jnp.int32, (rows, rows), 0)
    t = lax.broadcasted_iota(jnp.int32, (rows, rows), 1)
    differ = (s // CH) ^ (t // CH)
    weight = jnp.broadcast_to(lam_ref[0, h : h + 1, :], (rows, rows))
    for digit in range(local_bits):
        weight = jnp.where(differ >= 1 << digit, lam_ref[1 + digit, h : h + 1, :], weight)
    return jnp.where(s <= t, weight, 0.0)


def upper_weight(lam_ref, b, h, rows):
    local_bits = (rows // CH).bit_length() - 1
    upper = (lax.axis_index("seq") >> b & 1).astype(F32)
    return lam_ref[1 + local_bits + b, h : h + 1, :] * upper


def local_kernel(q_hbm, kh_ref, vh_ref, lam_hbm, w_hbm, *refs):
    pt_ref, att_ref, qh_ref, qw_ref, lam_ref, w_ref, q_ref, lam_rows, sems = refs
    pieces = sems.shape[0] - 2
    share = w_hbm.shape[0] // pieces
    copies = [
        pltpu.make_async_copy(q_hbm, q_ref, sems.at[0]),
        pltpu.make_async_copy(lam_hbm, lam_ref, sems.at[1]),
    ]
    for i in range(pieces):
        piece = pl.ds(i * share, share)
        copies.append(pltpu.make_async_copy(w_hbm.at[piece], w_ref.at[piece], sems.at[2 + i]))
    for copy in copies:
        copy.start()
    for copy in copies[:2]:
        copy.wait()
    rows, heads_dev, _ = q_ref.shape
    bits = qw_ref.shape[0]
    lam_rows[...] = jnp.zeros_like(lam_rows)
    for b in range(bits):
        for h in range(heads_dev):
            at = b * heads_dev + h
            lam_rows[at : at + 1, :] = upper_weight(lam_ref, b, h, rows)
    lam_columns = lam_rows[...].T
    for h in range(heads_dev):
        q32 = q_ref[:, h, :]
        q = q32.astype(BF)
        qh_ref[h] = q
        for b in range(bits):
            at = b * heads_dev + h
            qw_ref[b, h] = (q32 * lam_columns[:, at : at + 1]).astype(BF)
        pt = (mm(kh_ref[h], q, NT) * weight_of(lam_ref, h, rows)).astype(BF)
        pt_ref[h] = pt
        att_ref[h] = mm(pt, vh_ref[h], TN)
    for copy in copies[2:]:
        copy.wait()


def attended_kernel(bits, att_ref, qw_ref, *refs):
    states, out_ref = refs[:bits], refs[-1]
    heads_dev, _, head_dim = att_ref.shape
    for h in range(heads_dev):
        total = att_ref[h]
        for b in range(bits):
            total = total + mm(qw_ref[b, h], states[b][h], NN)
        out_ref[:, h * head_dim : (h + 1) * head_dim] = total.astype(BF)


def cotangent_kernel(blocks, bits, *refs):
    parts, (w_ref, qw_ref, _, gt_ref), sums = (
        refs[:blocks],
        refs[blocks : blocks + 4],
        refs[blocks + 4 :],
    )
    deep = parts[0].shape[1]
    _, heads_dev, _, head_dim = qw_ref.shape
    total = None
    for i in range(blocks):
        column = pl.multiple_of((lax.axis_index("head") ^ i) * deep, deep)
        product = mm(w_ref[:, pl.ds(column, deep)], parts[i][...], NT)
        total = product if total is None else total + product
    for h in range(heads_dev):
        gt = total[h * head_dim : (h + 1) * head_dim].astype(BF)
        gt_ref[h * head_dim : (h + 1) * head_dim, :] = gt
        for b in range(bits):
            sums[b][h] = mm(gt, qw_ref[b, h], NN).astype(BF)


def running_kernel(running_ref, arrived_ref, *refs):
    refs[-1][...] = (running_ref[...].astype(F32) + arrived_ref[...].astype(F32)).astype(BF)


def meet_kernel(top, grad_ref, running_ref, arrived_ref, out_ref):
    upper = (lax.axis_index("seq") >> top & 1) == 1
    running = running_ref[...].astype(F32)
    if arrived_ref is not None:
        running = running + arrived_ref[...].astype(F32)
    out_ref[...] = jnp.where(upper, grad_ref[...], running.astype(BF))


def landed_sum(top, landed):
    upper = (lax.axis_index("seq") >> top & 1) == 1
    total = jnp.where(upper, 0.0, landed[0].astype(F32))
    for block in landed[1:]:
        total = total + block.astype(F32)
    return total


def pending_kernel(top, own_ref, after_ref, *refs):
    del after_ref
    landed, out_ref = [ref[...] for ref in refs[:-1]], refs[-1]
    out_ref[...] = (own_ref[...].astype(F32) + landed_sum(top, landed)).astype(BF)


def turned_group(high, group, bits):
    turned = high >> 1 | (high & 1) << bits - 1
    return turned ^ ((group >> bits - 1 ^ group) & 1) << bits - 1


def turned_high(turned, group, bits):
    turned = turned ^ ((group >> bits - 1 ^ group) & 1) << bits - 1
    return (turned << 1 & (1 << bits) - 1) | turned >> bits - 1


def relay_kernel(block_ref, after_ref, out_ref):
    del after_ref
    out_ref[...] = block_ref[...]


def chunk_kernel(low_ref, high_ref, after_ref, *outs):
    del after_ref
    half = low_ref.shape[0]
    columns = outs[0].shape[1]
    low = lax.axis_index("seq") % len(outs)
    for r, out in enumerate(outs):
        at = pl.ds(pl.multiple_of((low ^ r) * columns, columns), columns)
        out[:half] = low_ref[:, at]
        out[half:] = high_ref[:, at]


def stack_kernel(after_ref, *refs):
    del after_ref
    for r, ref in enumerate(refs[:-1]):
        refs[-1][r] = ref[...]


def columns_kernel(blocks, *refs):
    parts, out_ref = refs[:blocks], refs[blocks]
    per = parts[0].shape[0]
    bits = blocks.bit_length() - 1
    low = lax.axis_index("seq") % per
    for i in range(blocks):
        high = turned_high(lax.axis_index("head") ^ i, lax.axis_index("seq") // per, bits)
        for r in range(per):
            out_ref[high * per + (low ^ r)] = parts[i][r]


def local_grad_kernel(
    bits, gt_ref, qh_ref, kh_ref, vh_ref, pt_ref, lam_ref, after_ref, *refs
):
    del after_ref
    states, (dq_ref, dk_ref, dv_ref) = refs[:bits], refs[bits:]
    heads_dev, rows, head_dim = qh_ref.shape
    for h in range(heads_dev):
        gt = gt_ref[h * head_dim : (h + 1) * head_dim, :]
        g32 = gt.astype(F32)
        dpt = (mm(vh_ref[h], gt, NN) * weight_of(lam_ref, h, rows)).astype(BF)
        dk_ref[h] = mm(dpt, qh_ref[h], NN)
        dv_ref[h] = mm(pt_ref[h], gt, NT)
        dq = mm(dpt, kh_ref[h], TN)
        for b in range(bits):
            gw = (g32 * upper_weight(lam_ref, b, h, rows)).astype(BF)
            dq = dq + mm(gw, states[b][h], TT)
        dq_ref[h] = dq


def query_grad_kernel(top, gt_ref, lam_ref, dql_ref, state_ref, after_ref, dq_ref):
    del after_ref
    heads_dev, rows, head_dim = dql_ref.shape
    for h in range(heads_dev):
        g32 = gt_ref[h * head_dim : (h + 1) * head_dim, :].astype(F32)
        gw = (g32 * upper_weight(lam_ref, top, h, rows)).astype(BF)
        dq_ref[:, h, :] = dql_ref[h] + mm(gw, state_ref[h], TT)


def later_grad_kernel(top, kh_ref, vh_ref, dkl_ref, dvl_ref, after_ref, *refs):
    del after_ref
    landed, (dk_ref, dv_ref) = refs[:-2], refs[-2:]
    for h in range(kh_ref.shape[0]):
        late = landed_sum(top, [ref[h] for ref in landed]).astype(BF)
        dk_ref[:, h, :] = dkl_ref[h] + mm(vh_ref[h], late, NN)
        dv_ref[:, h, :] = dvl_ref[h] + mm(kh_ref[h], late, NT)


def share_kernel(offsets, att_ref, w_ref, after_ref, out_ref):
    del after_ref
    width = out_ref.shape[2]
    for n, i in enumerate(offsets):
        column = pl.multiple_of((lax.axis_index("head") ^ i) * width, width)
        out_ref[n] = mm(att_ref[...], w_ref[:, pl.ds(column, width)], NN).astype(out_ref.dtype)


def ring_owner(place, offset, devices):
    at = jnp.where(place % 2 == 0, place // 2, devices - 1 - place // 2)
    at = (at + offset + devices) % devices
    return jnp.where(at < devices // 2, 2 * at, 2 * (devices - 1 - at) + 1)


def proj_kernel(offsets, devices, first, cols_ref, *refs):
    total = None if first else refs[len(offsets)][...]
    for i, (offset, low, high) in enumerate(offsets):
        owner = ring_owner(lax.axis_index("seq"), offset, devices)
        product = mm(refs[i][...], cols_ref[owner, low:high, :], TN)
        total = product if total is None else total + product
    refs[-1][...] = total


def last_kernel(
    offset, devices, cols_ref, low_ref, high_ref, total_ref, after_ref, out_ref, held
):
    del after_ref
    half, block = low_ref.shape[0], out_ref.shape[0]
    at = pl.ds(pl.multiple_of(pl.program_id(0) * block, block), block)
    held[:half] = low_ref[:, at]
    held[half:] = high_ref[:, at]
    owner = ring_owner(lax.axis_index("seq"), offset, devices)
    out_ref[...] = total_ref[at, :] + mm(held[...], cols_ref[owner], TN)


def body(queries, keys, values, level_weights, out_proj, out_grad):
    rows, heads_dev, head_dim = queries.shape
    width = heads_dev * head_dim
    devices = lax.axis_size("seq")
    seq_bits = devices.bit_length() - 1
    heads = lax.axis_size("head")
    head_bits = heads.bit_length() - 1
    columns_dev = out_proj.shape[1] // devices

    head_state = like((heads_dev, head_dim, head_dim), BF)
    pinned_state = pltpu.VMEM((heads_dev, head_dim, head_dim), BF)
    per_head = pltpu.VMEM((heads_dev, rows, head_dim), BF)
    per_head_f32 = pltpu.VMEM((heads_dev, rows, head_dim), F32)
    flops_head = 2 * heads_dev * rows * rows * head_dim
    moved_head = 2 * rows * width
    top = seq_bits - 1

    half = rows // 2
    own_state, kh, vh, own_grad, own_low = pl.pallas_call(
        state_kernel,
        out_shape=(head_state, per_head, per_head, like(out_grad.shape, BF), like((half, width), BF)),
        in_specs=[ANY] * 3,
        out_specs=(VMEM,) * 5,
        scratch_shapes=[
            pltpu.VMEM(keys.shape, F32),
            pltpu.VMEM(keys.shape, F32),
            pltpu.SemaphoreType.DMA((4,)),
        ],
        compiler_params=PARAMS,
        cost_estimate=cost(flops_head, 7 * moved_head),
    )(hbm(keys), hbm(values), hbm(out_grad))

    def to_group(block, i):
        return lax.ppermute(block, "head", [(at, at ^ i) for at in range(heads)])

    def every_group(block):
        blocks = {0: block}
        for digit in reversed(range(head_bits)):
            for i in sorted(blocks):
                blocks[i ^ 1 << digit] = to_group(blocks[i], 1 << digit)
        return [blocks[i] for i in range(heads)]

    probs_t, att_local, qh, qw, lam, w = pl.pallas_call(
        local_kernel,
        out_shape=(
            pltpu.VMEM((heads_dev, rows, rows), BF),
            per_head_f32,
            per_head,
            pltpu.VMEM((seq_bits, heads_dev, rows, head_dim), BF),
            pltpu.VMEM(level_weights.shape, F32),
            pltpu.VMEM(out_proj.shape, BF),
        ),
        in_specs=[ANY, VMEM, VMEM, ANY, ANY],
        out_specs=(VMEM,) * 6,
        scratch_shapes=[
            pltpu.VMEM(queries.shape, F32),
            pltpu.VMEM((rows, rows), F32),
            pltpu.SemaphoreType.DMA((10,)),
        ],
        compiler_params=PARAMS,
        cost_estimate=cost(2 * flops_head, 12 * moved_head),
    )(hbm(queries), kh, vh, hbm(level_weights), hbm(out_proj))

    def relayed(block):
        return pl.pallas_call(
            relay_kernel,
            out_shape=like(block.shape, block.dtype),
            in_specs=[VMEM, ANY],
            out_specs=VMEM,
            compiler_params=PARAMS,
            cost_estimate=cost(0, 2 * moved_head),
        )(block, qw)

    grad_blocks = {0: own_grad}
    for digit in reversed(range(head_bits)):
        for i in sorted(grad_blocks):
            block = relayed(grad_blocks[i]) if i else own_grad
            grad_blocks[i ^ 1 << digit] = to_group(block, 1 << digit)
    grad_blocks = [grad_blocks[i] for i in range(heads)]

    per = devices // heads
    def turn_route(shift):
        return [
            (
                (high * per + low) * heads + (group_at ^ shift),
                (group_at * per + low) * heads + turned_group(high, group_at, head_bits),
            )
            for high in range(heads)
            for low in range(per)
            for group_at in range(heads)
        ]

    axes, far = ("seq", "head"), heads // 2
    turned = [
        lax.ppermute(own_low, axes, turn_route(0)),
        lax.ppermute(grad_blocks[far][half:], axes, turn_route(far)),
    ]
    partner_states = []
    running, arrived = own_state, None
    for digit in range(top):
        if arrived is not None:
            running = pl.pallas_call(
                running_kernel,
                out_shape=head_state,
                in_specs=[VMEM] * 2 + [ANY],
                out_specs=VMEM,
                compiler_params=PARAMS,
                cost_estimate=cost(0, 3 * moved_head),
            )(running, arrived, qw)
        arrived = across(running, "seq", digit)
        partner_states.append(arrived)

    gt, *grad_sums = pl.pallas_call(
        functools.partial(cotangent_kernel, heads, seq_bits),
        out_shape=(pltpu.VMEM((width, rows), BF),) + (pinned_state,) * seq_bits,
        in_specs=[VMEM] * (heads + 2) + [ANY],
        out_specs=(VMEM,) * (1 + seq_bits),
        compiler_params=PARAMS,
        cost_estimate=cost(2 * rows * width * out_proj.shape[1], 2 * width * out_proj.shape[1]),
    )(*grad_blocks, w, qw, running)

    meeting = pl.pallas_call(
        functools.partial(meet_kernel, top)
        if arrived is not None
        else lambda grad_ref, running_ref, out_ref: meet_kernel(
            top, grad_ref, running_ref, None, out_ref
        ),
        out_shape=head_state,
        in_specs=[VMEM] * (2 if arrived is None else 3),
        out_specs=VMEM,
        compiler_params=PARAMS,
        cost_estimate=cost(0, 4 * moved_head),
    )(grad_sums[top], running, *([] if arrived is None else [arrived]))
    landed = [across(meeting, "seq", top)]
    partner_states.append(landed[0])

    chunks = pl.pallas_call(
        chunk_kernel,
        out_shape=(like((rows, columns_dev), BF),) * per,
        in_specs=[VMEM, VMEM, ANY],
        out_specs=(VMEM,) * per,
        compiler_params=PARAMS,
        cost_estimate=cost(0, 2 * moved_head),
    )(*turned, meeting)
    own_chunks = chunks
    chunks = [chunks[0]] + [
        lax.ppermute(chunks[r], "seq", [(at, at ^ r) for at in range(devices)])
        for r in range(1, per)
    ]
    stacked = pl.pallas_call(
        stack_kernel,
        out_shape=like((per, rows, columns_dev), BF),
        in_specs=[ANY] + [VMEM] * per,
        out_specs=VMEM,
        compiler_params=PARAMS,
        cost_estimate=cost(0, 2 * moved_head),
    )(meeting, *chunks)
    column_blocks = every_group(stacked)

    grad_columns = pl.pallas_call(
        functools.partial(columns_kernel, heads),
        out_shape=pltpu.VMEM((devices, rows, columns_dev), BF),
        in_specs=[VMEM] * heads,
        out_specs=VMEM,
        compiler_params=PARAMS,
        cost_estimate=cost(0, 8 * moved_head),
    )(*column_blocks)

    query_local, key_local, value_local = pl.pallas_call(
        functools.partial(local_grad_kernel, top),
        out_shape=(per_head_f32,) * 3,
        in_specs=[VMEM] * 6 + [ANY] + [VMEM] * top,
        out_specs=(VMEM,) * 3,
        compiler_params=PARAMS,
        cost_estimate=cost((4 + top) * flops_head, 14 * moved_head),
    )(gt, qh, kh, vh, probs_t, lam, meeting, *partner_states[:top])

    attended = pl.pallas_call(
        functools.partial(attended_kernel, seq_bits),
        out_shape=like((rows, width), BF),
        in_specs=[VMEM] * (2 + seq_bits) + [ANY] * 2,
        out_specs=VMEM,
        compiler_params=PARAMS,
        cost_estimate=cost(seq_bits * flops_head, 8 * moved_head),
    )(att_local, qw, *partner_states, key_local, own_chunks[-1])

    first_pending = attended
    for digit in reversed(range(top)):
        outgoing = pl.pallas_call(
            functools.partial(pending_kernel, top),
            out_shape=head_state,
            in_specs=[VMEM, ANY] + [VMEM] * len(landed),
            out_specs=VMEM,
            compiler_params=PARAMS,
            cost_estimate=cost(0, 4 * moved_head),
        )(grad_sums[digit], attended, *landed)
        if len(landed) == 1:
            first_pending = outgoing
        landed.append(across(outgoing, "seq", digit))

    query_grad = pl.pallas_call(
        functools.partial(query_grad_kernel, top),
        out_shape=like((rows, heads_dev, head_dim), F32),
        in_specs=[VMEM] * 4 + [ANY],
        out_specs=VMEM,
        compiler_params=PARAMS,
        cost_estimate=cost(flops_head, 6 * moved_head),
    )(gt, lam, query_local, partner_states[top], attended)

    def share(offsets, kind, after):
        return pl.pallas_call(
            functools.partial(share_kernel, offsets),
            out_shape=like((len(offsets), rows, width), kind),
            in_specs=[VMEM, VMEM, ANY],
            out_specs=VMEM,
            compiler_params=PARAMS,
            cost_estimate=cost(
                2 * rows * width * len(offsets) * width, 2 * width * len(offsets) * width
            ),
        )(attended, w, after)

    send = share(range(1, heads, 2), BF, stacked)
    kept = share(range(0, heads, 2), F32, first_pending)
    for digit in range(head_bits):
        kept = kept + to_group(send, 1 << digit).astype(F32)
        if digit < head_bits - 1:
            send, kept = kept[1::2].astype(BF), kept[0::2]
    mixed = kept[0].astype(BF)

    ring = list(range(0, devices, 2)) + list(range(devices - 1, 0, -2))
    forward = [(ring[i], ring[(i + 1) % devices]) for i in range(devices)]
    backward = [(b, a) for a, b in forward]

    def accumulate(total, blocks, offsets):
        operands = blocks if total is None else blocks + [total]
        return pl.pallas_call(
            functools.partial(proj_kernel, offsets, devices, total is None),
            out_shape=pltpu.VMEM((width, columns_dev), F32),
            in_specs=[VMEM] * (1 + len(operands)),
            out_specs=VMEM,
            compiler_params=PARAMS,
            cost_estimate=cost(
                2 * len(blocks) * rows * width * columns_dev, 4 * width * columns_dev
            ),
        )(grad_columns, *operands)

    blocks, offsets = [attended], [(0, 0, rows)]
    ahead = behind = attended
    steps, total = devices // 2, None
    for step in range(1, steps):
        ahead = lax.ppermute(ahead, "seq", forward)
        behind = lax.ppermute(behind, "seq", backward)
        blocks += [ahead, behind]
        offsets += [(-step, 0, rows), (step, 0, rows)]
        if step == steps - 2:
            total = accumulate(None, blocks, offsets)
            blocks, offsets = [], []
    if blocks:
        total = accumulate(total, blocks, offsets)
    last = [
        lax.ppermute(ahead[:half], "seq", forward),
        lax.ppermute(behind[half:], "seq", backward),
    ]
    key_grad, value_grad = pl.pallas_call(
        functools.partial(later_grad_kernel, top),
        out_shape=(like((rows, heads_dev, head_dim), F32),) * 2,
        in_specs=[VMEM] * 4 + [ANY] + [VMEM] * seq_bits,
        out_specs=(VMEM,) * 2,
        compiler_params=PARAMS,
        cost_estimate=cost(2 * flops_head, 11 * moved_head),
    )(kh, vh, key_local, value_local, total, *landed)
    quarter_rows = width // 4
    proj_grad = pl.pallas_call(
        functools.partial(last_kernel, steps, devices),
        out_shape=like((width, columns_dev), F32),
        grid=(4,),
        in_specs=[
            VMEM,
            VMEM,
            VMEM,
            VMEM,
            ANY,
        ],
        out_specs=pl.BlockSpec((quarter_rows, columns_dev), lambda i: (i, 0)),
        scratch_shapes=[pltpu.VMEM((rows, quarter_rows), BF)],
        compiler_params=PARAMS,
        cost_estimate=cost(2 * rows * width * columns_dev, 8 * width * columns_dev),
    )(grad_columns, *last, total, hbm(key_grad))
    return (mixed, query_grad, key_grad, value_grad, proj_grad)


def solution(mesh):
    placed = (
        P("seq", "head", None),
        P("seq", "head", None),
        P("seq", "head", None),
        P(None, "head", "seq"),
        P("head", None),
        P("seq", "head"),
    )
    return jax.shard_map(
        body,
        mesh=mesh,
        in_specs=placed,
        out_specs=(
            P("seq", "head"),
            P("seq", "head", None),
            P("seq", "head", None),
            P("seq", "head", None),
            P("head", "seq"),
        ),
        check_vma=False,
    )
```

```python
import functools

import jax
import jax.numpy as jnp
from jax import lax
from jax.experimental import pallas as pl
from jax.experimental.pallas import tpu as pltpu
from jax.sharding import PartitionSpec as P

CH = 64
BF = jnp.bfloat16
F32 = jnp.float32
NN = (((1,), (0,)), ((), ()))
NT = (((1,), (1,)), ((), ()))
TN = (((0,), (0,)), ((), ()))
TT = (((0,), (1,)), ((), ()))
VMEM = pl.BlockSpec(memory_space=pltpu.VMEM)
ANY = pl.BlockSpec(memory_space=pl.ANY)
PARAMS = pltpu.CompilerParams(vmem_limit_bytes=14 * 2**20)


def mm(a, b, dims):
    return lax.dot_general(a, b, dims, preferred_element_type=F32)


def cost(flops, moved):
    return pl.CostEstimate(flops=flops, bytes_accessed=moved, transcendentals=0)


def like(shape, dtype):
    return jax.ShapeDtypeStruct(shape, dtype)


def across(block, axis, stride, up_only=False, down_only=False):
    count = lax.axis_size(axis)
    route = []
    for low in range(count):
        high = low | 1 << stride
        if high != low and high < count:
            if not down_only:
                route.append((low, high))
            if not up_only:
                route.append((high, low))
    return lax.ppermute(block, axis, route)


def hbm(array):
    return pltpu.with_memory_space_constraint(array, pltpu.HBM)


def state_kernel(k_hbm, v_hbm, grad_hbm, *refs):
    s_ref, kh_ref, vh_ref, grad_ref, low_ref, k_ref, v_ref, sems = refs
    copies = [
        pltpu.make_async_copy(k_hbm, k_ref, sems.at[0]),
        pltpu.make_async_copy(v_hbm, v_ref, sems.at[1]),
        pltpu.make_async_copy(grad_hbm, grad_ref, sems.at[2]),
        pltpu.make_async_copy(grad_hbm.at[pl.ds(0, low_ref.shape[0])], low_ref, sems.at[3]),
    ]
    for copy in copies:
        copy.start()
    for copy in copies[:2]:
        copy.wait()
    for h in range(k_ref.shape[1]):
        k = k_ref[:, h, :].astype(BF)
        v = v_ref[:, h, :].astype(BF)
        kh_ref[h] = k
        vh_ref[h] = v
        s_ref[h] = mm(k, v, TN).astype(BF)
    copies[2].wait()
    copies[3].wait()


def weight_of(lam_ref, h, rows):
    local_bits = (rows // CH).bit_length() - 1
    s = lax.broadcasted_iota(jnp.int32, (rows, rows), 0)
    t = lax.broadcasted_iota(jnp.int32, (rows, rows), 1)
    differ = (s // CH) ^ (t // CH)
    weight = jnp.broadcast_to(lam_ref[0, h : h + 1, :], (rows, rows))
    for digit in range(local_bits):
        weight = jnp.where(differ >= 1 << digit, lam_ref[1 + digit, h : h + 1, :], weight)
    return jnp.where(s <= t, weight, 0.0)


def upper_weight(lam_ref, b, h, rows):
    local_bits = (rows // CH).bit_length() - 1
    upper = (lax.axis_index("seq") >> b & 1).astype(F32)
    return lam_ref[1 + local_bits + b, h : h + 1, :] * upper


def local_kernel(q_hbm, kh_ref, vh_ref, lam_hbm, w_hbm, *refs):
    pt_ref, att_ref, qh_ref, qw_ref, lam_ref, w_ref, q_ref, lam_rows, sems = refs
    pieces = sems.shape[0] - 2
    share = w_hbm.shape[0] // pieces
    copies = [
        pltpu.make_async_copy(q_hbm, q_ref, sems.at[0]),
        pltpu.make_async_copy(lam_hbm, lam_ref, sems.at[1]),
    ]
    for i in range(pieces):
        piece = pl.ds(i * share, share)
        copies.append(pltpu.make_async_copy(w_hbm.at[piece], w_ref.at[piece], sems.at[2 + i]))
    for copy in copies:
        copy.start()
    for copy in copies[:2]:
        copy.wait()
    rows, heads_dev, _ = q_ref.shape
    bits = qw_ref.shape[0]
    lam_rows[...] = jnp.zeros_like(lam_rows)
    for b in range(bits):
        for h in range(heads_dev):
            at = b * heads_dev + h
            lam_rows[at : at + 1, :] = upper_weight(lam_ref, b, h, rows)
    lam_columns = lam_rows[...].T
    for h in range(heads_dev):
        q32 = q_ref[:, h, :]
        q = q32.astype(BF)
        qh_ref[h] = q
        for b in range(bits):
            at = b * heads_dev + h
            qw_ref[b, h] = (q32 * lam_columns[:, at : at + 1]).astype(BF)
        pt = (mm(kh_ref[h], q, NT) * weight_of(lam_ref, h, rows)).astype(BF)
        pt_ref[h] = pt
        att_ref[h] = mm(pt, vh_ref[h], TN)
    for copy in copies[2:]:
        copy.wait()


def attended_kernel(bits, att_ref, qw_ref, *refs):
    states, out_ref = refs[:bits], refs[-1]
    heads_dev, _, head_dim = att_ref.shape
    for h in range(heads_dev):
        total = att_ref[h]
        for b in range(bits):
            total = total + mm(qw_ref[b, h], states[b][h], NN)
        out_ref[:, h * head_dim : (h + 1) * head_dim] = total.astype(BF)


def cotangent_kernel(blocks, bits, *refs):
    parts, (w_ref, qw_ref, _, gt_ref), sums = (
        refs[:blocks],
        refs[blocks : blocks + 4],
        refs[blocks + 4 :],
    )
    deep = parts[0].shape[1]
    _, heads_dev, _, head_dim = qw_ref.shape
    total = None
    for i in range(blocks):
        column = pl.multiple_of((lax.axis_index("head") ^ i) * deep, deep)
        product = mm(w_ref[:, pl.ds(column, deep)], parts[i][...], NT)
        total = product if total is None else total + product
    for h in range(heads_dev):
        gt = total[h * head_dim : (h + 1) * head_dim].astype(BF)
        gt_ref[h * head_dim : (h + 1) * head_dim, :] = gt
        for b in range(bits):
            sums[b][h] = mm(gt, qw_ref[b, h], NN).astype(BF)


def running_kernel(running_ref, arrived_ref, *refs):
    refs[-1][...] = (running_ref[...].astype(F32) + arrived_ref[...].astype(F32)).astype(BF)


def meet_kernel(top, grad_ref, running_ref, arrived_ref, out_ref):
    upper = (lax.axis_index("seq") >> top & 1) == 1
    running = running_ref[...].astype(F32)
    if arrived_ref is not None:
        running = running + arrived_ref[...].astype(F32)
    out_ref[...] = jnp.where(upper, grad_ref[...], running.astype(BF))


def landed_sum(top, landed):
    upper = (lax.axis_index("seq") >> top & 1) == 1
    total = jnp.where(upper, 0.0, landed[0].astype(F32))
    for block in landed[1:]:
        total = total + block.astype(F32)
    return total


def pending_kernel(top, own_ref, after_ref, *refs):
    del after_ref
    landed, out_ref = [ref[...] for ref in refs[:-1]], refs[-1]
    out_ref[...] = (own_ref[...].astype(F32) + landed_sum(top, landed)).astype(BF)


def turned_group(high, group, bits):
    turned = high >> 1 | (high & 1) << bits - 1
    return turned ^ ((group >> bits - 1 ^ group) & 1) << bits - 1


def turned_high(turned, group, bits):
    turned = turned ^ ((group >> bits - 1 ^ group) & 1) << bits - 1
    return (turned << 1 & (1 << bits) - 1) | turned >> bits - 1


def relay_kernel(block_ref, after_ref, out_ref):
    del after_ref
    out_ref[...] = block_ref[...]


def chunk_kernel(low_ref, high_ref, after_ref, *outs):
    del after_ref
    half = low_ref.shape[0]
    columns = outs[0].shape[1]
    low = lax.axis_index("seq") % len(outs)
    for r, out in enumerate(outs):
        at = pl.ds(pl.multiple_of((low ^ r) * columns, columns), columns)
        out[:half] = low_ref[:, at]
        out[half:] = high_ref[:, at]


def stack_kernel(after_ref, *refs):
    del after_ref
    for r, ref in enumerate(refs[:-1]):
        refs[-1][r] = ref[...]


def columns_kernel(blocks, *refs):
    parts, out_ref = refs[:blocks], refs[blocks]
    per = parts[0].shape[0]
    bits = blocks.bit_length() - 1
    low = lax.axis_index("seq") % per
    for i in range(blocks):
        high = turned_high(lax.axis_index("head") ^ i, lax.axis_index("seq") // per, bits)
        for r in range(per):
            out_ref[high * per + (low ^ r)] = parts[i][r]


def local_grad_kernel(
    bits, gt_ref, qh_ref, kh_ref, vh_ref, pt_ref, lam_ref, after_ref, *refs
):
    del after_ref
    states, (dq_ref, dk_ref, dv_ref) = refs[:bits], refs[bits:]
    heads_dev, rows, head_dim = qh_ref.shape
    for h in range(heads_dev):
        gt = gt_ref[h * head_dim : (h + 1) * head_dim, :]
        g32 = gt.astype(F32)
        dpt = (mm(vh_ref[h], gt, NN) * weight_of(lam_ref, h, rows)).astype(BF)
        dk_ref[h] = mm(dpt, qh_ref[h], NN)
        dv_ref[h] = mm(pt_ref[h], gt, NT)
        dq = mm(dpt, kh_ref[h], TN)
        for b in range(bits):
            gw = (g32 * upper_weight(lam_ref, b, h, rows)).astype(BF)
            dq = dq + mm(gw, states[b][h], TT)
        dq_ref[h] = dq


def query_grad_kernel(top, gt_ref, lam_ref, dql_ref, state_ref, after_ref, dq_ref):
    del after_ref
    heads_dev, rows, head_dim = dql_ref.shape
    for h in range(heads_dev):
        g32 = gt_ref[h * head_dim : (h + 1) * head_dim, :].astype(F32)
        gw = (g32 * upper_weight(lam_ref, top, h, rows)).astype(BF)
        dq_ref[:, h, :] = dql_ref[h] + mm(gw, state_ref[h], TT)


def later_grad_kernel(top, kh_ref, vh_ref, dkl_ref, dvl_ref, after_ref, *refs):
    del after_ref
    landed, (dk_ref, dv_ref) = refs[:-2], refs[-2:]
    for h in range(kh_ref.shape[0]):
        late = landed_sum(top, [ref[h] for ref in landed]).astype(BF)
        dk_ref[:, h, :] = dkl_ref[h] + mm(vh_ref[h], late, NN)
        dv_ref[:, h, :] = dvl_ref[h] + mm(kh_ref[h], late, NT)


def share_kernel(offsets, att_ref, w_ref, after_ref, out_ref):
    del after_ref
    width = out_ref.shape[2]
    for n, i in enumerate(offsets):
        column = pl.multiple_of((lax.axis_index("head") ^ i) * width, width)
        out_ref[n] = mm(att_ref[...], w_ref[:, pl.ds(column, width)], NN).astype(out_ref.dtype)


def ring_owner(place, offset, devices):
    at = jnp.where(place % 2 == 0, place // 2, devices - 1 - place // 2)
    at = (at + offset + devices) % devices
    return jnp.where(at < devices // 2, 2 * at, 2 * (devices - 1 - at) + 1)


def proj_kernel(offsets, devices, first, cols_ref, *refs):
    total = None if first else refs[len(offsets)][...]
    for i, (offset, low, high) in enumerate(offsets):
        owner = ring_owner(lax.axis_index("seq"), offset, devices)
        product = mm(refs[i][...], cols_ref[owner, low:high, :], TN)
        total = product if total is None else total + product
    refs[-1][...] = total


def last_kernel(offset, devices, cols_ref, low_ref, high_ref, total_ref, after_ref, out_hbm, *refs):
    del after_ref
    held, result, sems = refs
    half = low_ref.shape[0]
    held[:half] = low_ref[...]
    held[half:] = high_ref[...]
    cols = cols_ref[ring_owner(lax.axis_index("seq"), offset, devices)]
    pieces = sems.shape[0]
    block = held.shape[1] // pieces
    copies = []
    for i in range(pieces):
        at = pl.ds(i * block, block)
        result[at, :] = total_ref[at, :] + mm(held[:, at], cols, TN)
        copies.append(pltpu.make_async_copy(result.at[at], out_hbm.at[at], sems.at[i]))
        copies[-1].start()
    for copy in copies:
        copy.wait()


def body(queries, keys, values, level_weights, out_proj, out_grad):
    rows, heads_dev, head_dim = queries.shape
    width = heads_dev * head_dim
    devices = lax.axis_size("seq")
    seq_bits = devices.bit_length() - 1
    heads = lax.axis_size("head")
    head_bits = heads.bit_length() - 1
    columns_dev = out_proj.shape[1] // devices

    head_state = like((heads_dev, head_dim, head_dim), BF)
    pinned_state = pltpu.VMEM((heads_dev, head_dim, head_dim), BF)
    per_head = pltpu.VMEM((heads_dev, rows, head_dim), BF)
    per_head_f32 = pltpu.VMEM((heads_dev, rows, head_dim), F32)
    flops_head = 2 * heads_dev * rows * rows * head_dim
    moved_head = 2 * rows * width
    top = seq_bits - 1

    half = rows // 2
    own_state, kh, vh, own_grad, own_low = pl.pallas_call(
        state_kernel,
        out_shape=(head_state, per_head, per_head, like(out_grad.shape, BF), like((half, width), BF)),
        in_specs=[ANY] * 3,
        out_specs=(VMEM,) * 5,
        scratch_shapes=[
            pltpu.VMEM(keys.shape, F32),
            pltpu.VMEM(keys.shape, F32),
            pltpu.SemaphoreType.DMA((4,)),
        ],
        compiler_params=PARAMS,
        cost_estimate=cost(flops_head, 7 * moved_head),
    )(hbm(keys), hbm(values), hbm(out_grad))

    def to_group(block, i):
        return lax.ppermute(block, "head", [(at, at ^ i) for at in range(heads)])

    def every_group(block):
        blocks = {0: block}
        for digit in reversed(range(head_bits)):
            for i in sorted(blocks):
                blocks[i ^ 1 << digit] = to_group(blocks[i], 1 << digit)
        return [blocks[i] for i in range(heads)]

    probs_t, att_local, qh, qw, lam, w = pl.pallas_call(
        local_kernel,
        out_shape=(
            pltpu.VMEM((heads_dev, rows, rows), BF),
            per_head_f32,
            per_head,
            pltpu.VMEM((seq_bits, heads_dev, rows, head_dim), BF),
            pltpu.VMEM(level_weights.shape, F32),
            pltpu.VMEM(out_proj.shape, BF),
        ),
        in_specs=[ANY, VMEM, VMEM, ANY, ANY],
        out_specs=(VMEM,) * 6,
        scratch_shapes=[
            pltpu.VMEM(queries.shape, F32),
            pltpu.VMEM((rows, rows), F32),
            pltpu.SemaphoreType.DMA((10,)),
        ],
        compiler_params=PARAMS,
        cost_estimate=cost(2 * flops_head, 12 * moved_head),
    )(hbm(queries), kh, vh, hbm(level_weights), hbm(out_proj))

    def relayed(block):
        return pl.pallas_call(
            relay_kernel,
            out_shape=like(block.shape, block.dtype),
            in_specs=[VMEM, ANY],
            out_specs=VMEM,
            compiler_params=PARAMS,
            cost_estimate=cost(0, 2 * moved_head),
        )(block, qw)

    grad_blocks = {0: own_grad}
    for digit in reversed(range(head_bits)):
        for i in sorted(grad_blocks):
            block = relayed(grad_blocks[i]) if i else own_grad
            grad_blocks[i ^ 1 << digit] = to_group(block, 1 << digit)
    grad_blocks = [grad_blocks[i] for i in range(heads)]

    per = devices // heads
    def turn_route(shift):
        return [
            (
                (high * per + low) * heads + (group_at ^ shift),
                (group_at * per + low) * heads + turned_group(high, group_at, head_bits),
            )
            for high in range(heads)
            for low in range(per)
            for group_at in range(heads)
        ]

    axes, far = ("seq", "head"), heads // 2
    turned = [
        lax.ppermute(own_low, axes, turn_route(0)),
        lax.ppermute(grad_blocks[far][half:], axes, turn_route(far)),
    ]
    partner_states = []
    running, arrived = own_state, None
    for digit in range(top):
        if arrived is not None:
            running = pl.pallas_call(
                running_kernel,
                out_shape=head_state,
                in_specs=[VMEM] * 2 + [ANY],
                out_specs=VMEM,
                compiler_params=PARAMS,
                cost_estimate=cost(0, 3 * moved_head),
            )(running, arrived, qw)
        arrived = across(running, "seq", digit)
        partner_states.append(arrived)

    gt, *grad_sums = pl.pallas_call(
        functools.partial(cotangent_kernel, heads, seq_bits),
        out_shape=(pltpu.VMEM((width, rows), BF),) + (pinned_state,) * seq_bits,
        in_specs=[VMEM] * (heads + 2) + [ANY],
        out_specs=(VMEM,) * (1 + seq_bits),
        compiler_params=PARAMS,
        cost_estimate=cost(2 * rows * width * out_proj.shape[1], 2 * width * out_proj.shape[1]),
    )(*grad_blocks, w, qw, running)

    meeting = pl.pallas_call(
        functools.partial(meet_kernel, top)
        if arrived is not None
        else lambda grad_ref, running_ref, out_ref: meet_kernel(
            top, grad_ref, running_ref, None, out_ref
        ),
        out_shape=head_state,
        in_specs=[VMEM] * (2 if arrived is None else 3),
        out_specs=VMEM,
        compiler_params=PARAMS,
        cost_estimate=cost(0, 4 * moved_head),
    )(grad_sums[top], running, *([] if arrived is None else [arrived]))
    landed = [across(meeting, "seq", top)]
    partner_states.append(landed[0])

    chunks = pl.pallas_call(
        chunk_kernel,
        out_shape=(like((rows, columns_dev), BF),) * per,
        in_specs=[VMEM, VMEM, ANY],
        out_specs=(VMEM,) * per,
        compiler_params=PARAMS,
        cost_estimate=cost(0, 2 * moved_head),
    )(*turned, meeting)
    own_chunks = chunks
    chunks = [chunks[0]] + [
        lax.ppermute(chunks[r], "seq", [(at, at ^ r) for at in range(devices)])
        for r in range(1, per)
    ]
    stacked = pl.pallas_call(
        stack_kernel,
        out_shape=like((per, rows, columns_dev), BF),
        in_specs=[ANY] + [VMEM] * per,
        out_specs=VMEM,
        compiler_params=PARAMS,
        cost_estimate=cost(0, 2 * moved_head),
    )(meeting, *chunks)
    column_blocks = every_group(stacked)

    grad_columns = pl.pallas_call(
        functools.partial(columns_kernel, heads),
        out_shape=pltpu.VMEM((devices, rows, columns_dev), BF),
        in_specs=[VMEM] * heads,
        out_specs=VMEM,
        compiler_params=PARAMS,
        cost_estimate=cost(0, 8 * moved_head),
    )(*column_blocks)

    query_local, key_local, value_local = pl.pallas_call(
        functools.partial(local_grad_kernel, top),
        out_shape=(per_head_f32,) * 3,
        in_specs=[VMEM] * 6 + [ANY] + [VMEM] * top,
        out_specs=(VMEM,) * 3,
        compiler_params=PARAMS,
        cost_estimate=cost((4 + top) * flops_head, 14 * moved_head),
    )(gt, qh, kh, vh, probs_t, lam, meeting, *partner_states[:top])

    attended = pl.pallas_call(
        functools.partial(attended_kernel, seq_bits),
        out_shape=like((rows, width), BF),
        in_specs=[VMEM] * (2 + seq_bits) + [ANY] * 2,
        out_specs=VMEM,
        compiler_params=PARAMS,
        cost_estimate=cost(seq_bits * flops_head, 8 * moved_head),
    )(att_local, qw, *partner_states, key_local, own_chunks[-1])

    first_pending = attended
    for digit in reversed(range(top)):
        outgoing = pl.pallas_call(
            functools.partial(pending_kernel, top),
            out_shape=head_state,
            in_specs=[VMEM, ANY] + [VMEM] * len(landed),
            out_specs=VMEM,
            compiler_params=PARAMS,
            cost_estimate=cost(0, 4 * moved_head),
        )(grad_sums[digit], attended, *landed)
        if len(landed) == 1:
            first_pending = outgoing
        landed.append(across(outgoing, "seq", digit))

    query_grad = pl.pallas_call(
        functools.partial(query_grad_kernel, top),
        out_shape=like((rows, heads_dev, head_dim), F32),
        in_specs=[VMEM] * 4 + [ANY],
        out_specs=VMEM,
        compiler_params=PARAMS,
        cost_estimate=cost(flops_head, 6 * moved_head),
    )(gt, lam, query_local, partner_states[top], attended)

    def share(offsets, kind, after):
        return pl.pallas_call(
            functools.partial(share_kernel, offsets),
            out_shape=like((len(offsets), rows, width), kind),
            in_specs=[VMEM, VMEM, ANY],
            out_specs=VMEM,
            compiler_params=PARAMS,
            cost_estimate=cost(
                2 * rows * width * len(offsets) * width, 2 * width * len(offsets) * width
            ),
        )(attended, w, after)

    send = share(range(1, heads, 2), BF, stacked)
    kept = share(range(0, heads, 2), F32, first_pending)
    for digit in range(head_bits):
        kept = kept + to_group(send, 1 << digit).astype(F32)
        if digit < head_bits - 1:
            send, kept = kept[1::2].astype(BF), kept[0::2]
    mixed = kept[0].astype(BF)

    ring = list(range(0, devices, 2)) + list(range(devices - 1, 0, -2))
    forward = [(ring[i], ring[(i + 1) % devices]) for i in range(devices)]
    backward = [(b, a) for a, b in forward]

    def accumulate(total, blocks, offsets):
        operands = blocks if total is None else blocks + [total]
        return pl.pallas_call(
            functools.partial(proj_kernel, offsets, devices, total is None),
            out_shape=pltpu.VMEM((width, columns_dev), F32),
            in_specs=[VMEM] * (1 + len(operands)),
            out_specs=VMEM,
            compiler_params=PARAMS,
            cost_estimate=cost(
                2 * len(blocks) * rows * width * columns_dev, 4 * width * columns_dev
            ),
        )(grad_columns, *operands)

    blocks, offsets = [attended], [(0, 0, rows)]
    ahead = behind = attended
    steps, total = devices // 2, None
    for step in range(1, steps):
        ahead = lax.ppermute(ahead, "seq", forward)
        behind = lax.ppermute(behind, "seq", backward)
        blocks += [ahead, behind]
        offsets += [(-step, 0, rows), (step, 0, rows)]
        if step == steps - 2:
            total = accumulate(None, blocks, offsets)
            blocks, offsets = [], []
    if blocks:
        total = accumulate(total, blocks, offsets)
    last = [
        lax.ppermute(ahead[:half], "seq", forward),
        lax.ppermute(behind[half:], "seq", backward),
    ]
    key_grad, value_grad = pl.pallas_call(
        functools.partial(later_grad_kernel, top),
        out_shape=(like((rows, heads_dev, head_dim), F32),) * 2,
        in_specs=[VMEM] * 4 + [ANY] + [VMEM] * seq_bits,
        out_specs=(VMEM,) * 2,
        compiler_params=PARAMS,
        cost_estimate=cost(2 * flops_head, 11 * moved_head),
    )(kh, vh, key_local, value_local, total, *landed)
    proj_grad = pl.pallas_call(
        functools.partial(last_kernel, steps, devices),
        out_shape=like((width, columns_dev), F32),
        in_specs=[VMEM] * 4 + [ANY],
        out_specs=ANY,
        scratch_shapes=[
            pltpu.VMEM((rows, width), BF),
            pltpu.VMEM((width, columns_dev), F32),
            pltpu.SemaphoreType.DMA((4,)),
        ],
        compiler_params=PARAMS,
        cost_estimate=cost(2 * rows * width * columns_dev, 8 * width * columns_dev),
    )(grad_columns, *last, total, hbm(key_grad))
    return (mixed, query_grad, key_grad, value_grad, proj_grad)


def solution(mesh):
    placed = (
        P("seq", "head", None),
        P("seq", "head", None),
        P("seq", "head", None),
        P(None, "head", "seq"),
        P("head", None),
        P("seq", "head"),
    )
    return jax.shard_map(
        body,
        mesh=mesh,
        in_specs=placed,
        out_specs=(
            P("seq", "head"),
            P("seq", "head", None),
            P("seq", "head", None),
            P("seq", "head", None),
            P("head", "seq"),
        ),
        check_vma=False,
    )
```

```python
import functools

import jax
import jax.numpy as jnp
from jax import lax
from jax.experimental import pallas as pl
from jax.experimental.pallas import tpu as pltpu
from jax.sharding import PartitionSpec as P

CH = 64
BF = jnp.bfloat16
F32 = jnp.float32
NN = (((1,), (0,)), ((), ()))
NT = (((1,), (1,)), ((), ()))
TN = (((0,), (0,)), ((), ()))
TT = (((0,), (1,)), ((), ()))
VMEM = pl.BlockSpec(memory_space=pltpu.VMEM)
ANY = pl.BlockSpec(memory_space=pl.ANY)
PARAMS = pltpu.CompilerParams(vmem_limit_bytes=14 * 2**20)


def mm(a, b, dims):
    return lax.dot_general(a, b, dims, preferred_element_type=F32)


def cost(flops, moved):
    return pl.CostEstimate(flops=flops, bytes_accessed=moved, transcendentals=0)


def like(shape, dtype):
    return jax.ShapeDtypeStruct(shape, dtype)


def across(block, axis, stride, up_only=False, down_only=False):
    count = lax.axis_size(axis)
    route = []
    for low in range(count):
        high = low | 1 << stride
        if high != low and high < count:
            if not down_only:
                route.append((low, high))
            if not up_only:
                route.append((high, low))
    return lax.ppermute(block, axis, route)


def hbm(array):
    return pltpu.with_memory_space_constraint(array, pltpu.HBM)


def state_kernel(k_hbm, v_hbm, grad_hbm, *refs):
    s_ref, kh_ref, vh_ref, grad_ref, low_ref, k_ref, v_ref, sems = refs
    copies = [
        pltpu.make_async_copy(k_hbm, k_ref, sems.at[0]),
        pltpu.make_async_copy(v_hbm, v_ref, sems.at[1]),
        pltpu.make_async_copy(grad_hbm, grad_ref, sems.at[2]),
        pltpu.make_async_copy(grad_hbm.at[pl.ds(0, low_ref.shape[0])], low_ref, sems.at[3]),
    ]
    for copy in copies:
        copy.start()
    for copy in copies[:2]:
        copy.wait()
    for h in range(k_ref.shape[1]):
        k = k_ref[:, h, :].astype(BF)
        v = v_ref[:, h, :].astype(BF)
        kh_ref[h] = k
        vh_ref[h] = v
        s_ref[h] = mm(k, v, TN).astype(BF)
    copies[2].wait()
    copies[3].wait()


def weight_of(lam_ref, h, rows):
    local_bits = (rows // CH).bit_length() - 1
    s = lax.broadcasted_iota(jnp.int32, (rows, rows), 0)
    t = lax.broadcasted_iota(jnp.int32, (rows, rows), 1)
    differ = (s // CH) ^ (t // CH)
    weight = jnp.broadcast_to(lam_ref[0, h : h + 1, :], (rows, rows))
    for digit in range(local_bits):
        weight = jnp.where(differ >= 1 << digit, lam_ref[1 + digit, h : h + 1, :], weight)
    return jnp.where(s <= t, weight, 0.0)


def upper_weight(lam_ref, b, h, rows):
    local_bits = (rows // CH).bit_length() - 1
    upper = (lax.axis_index("seq") >> b & 1).astype(F32)
    return lam_ref[1 + local_bits + b, h : h + 1, :] * upper


def local_kernel(q_hbm, kh_ref, vh_ref, lam_hbm, w_hbm, *refs):
    pt_ref, att_ref, qh_ref, qw_ref, lam_ref, w_ref, q_ref, lam_rows, sems = refs
    pieces = sems.shape[0] - 2
    share = w_hbm.shape[0] // pieces
    copies = [
        pltpu.make_async_copy(q_hbm, q_ref, sems.at[0]),
        pltpu.make_async_copy(lam_hbm, lam_ref, sems.at[1]),
    ]
    for i in range(pieces):
        piece = pl.ds(i * share, share)
        copies.append(pltpu.make_async_copy(w_hbm.at[piece], w_ref.at[piece], sems.at[2 + i]))
    for copy in copies:
        copy.start()
    for copy in copies[:2]:
        copy.wait()
    rows, heads_dev, _ = q_ref.shape
    bits = qw_ref.shape[0]
    lam_rows[...] = jnp.zeros_like(lam_rows)
    for b in range(bits):
        for h in range(heads_dev):
            at = b * heads_dev + h
            lam_rows[at : at + 1, :] = upper_weight(lam_ref, b, h, rows)
    lam_columns = lam_rows[...].T
    for h in range(heads_dev):
        q32 = q_ref[:, h, :]
        q = q32.astype(BF)
        qh_ref[h] = q
        for b in range(bits):
            at = b * heads_dev + h
            qw_ref[b, h] = (q32 * lam_columns[:, at : at + 1]).astype(BF)
        pt = (mm(kh_ref[h], q, NT) * weight_of(lam_ref, h, rows)).astype(BF)
        pt_ref[h] = pt
        att_ref[h] = mm(pt, vh_ref[h], TN)
    for copy in copies[2:]:
        copy.wait()


def attended_kernel(bits, att_ref, qw_ref, *refs):
    states, out_ref = refs[:bits], refs[-1]
    heads_dev, _, head_dim = att_ref.shape
    for h in range(heads_dev):
        total = att_ref[h]
        for b in range(bits):
            total = total + mm(qw_ref[b, h], states[b][h], NN)
        out_ref[:, h * head_dim : (h + 1) * head_dim] = total.astype(BF)


def cotangent_kernel(blocks, bits, *refs):
    parts, (w_ref, qw_ref, _, gt_ref), sums = (
        refs[:blocks],
        refs[blocks : blocks + 4],
        refs[blocks + 4 :],
    )
    deep = parts[0].shape[1]
    _, heads_dev, _, head_dim = qw_ref.shape
    total = None
    for i in range(blocks):
        column = pl.multiple_of((lax.axis_index("head") ^ i) * deep, deep)
        product = mm(w_ref[:, pl.ds(column, deep)], parts[i][...], NT)
        total = product if total is None else total + product
    for h in range(heads_dev):
        gt = total[h * head_dim : (h + 1) * head_dim].astype(BF)
        gt_ref[h * head_dim : (h + 1) * head_dim, :] = gt
        for b in range(bits):
            sums[b][h] = mm(gt, qw_ref[b, h], NN).astype(BF)


def running_kernel(running_ref, arrived_ref, *refs):
    refs[-1][...] = (running_ref[...].astype(F32) + arrived_ref[...].astype(F32)).astype(BF)


def meet_kernel(top, grad_ref, running_ref, arrived_ref, out_ref):
    upper = (lax.axis_index("seq") >> top & 1) == 1
    running = running_ref[...].astype(F32)
    if arrived_ref is not None:
        running = running + arrived_ref[...].astype(F32)
    out_ref[...] = jnp.where(upper, grad_ref[...], running.astype(BF))


def landed_sum(top, landed):
    upper = (lax.axis_index("seq") >> top & 1) == 1
    total = jnp.where(upper, 0.0, landed[0].astype(F32))
    for block in landed[1:]:
        total = total + block.astype(F32)
    return total


def pending_kernel(top, own_ref, after_ref, *refs):
    del after_ref
    landed, out_ref = [ref[...] for ref in refs[:-1]], refs[-1]
    out_ref[...] = (own_ref[...].astype(F32) + landed_sum(top, landed)).astype(BF)


def turned_group(high, group, bits):
    turned = high >> 1 | (high & 1) << bits - 1
    return turned ^ ((group >> bits - 1 ^ group) & 1) << bits - 1


def turned_high(turned, group, bits):
    turned = turned ^ ((group >> bits - 1 ^ group) & 1) << bits - 1
    return (turned << 1 & (1 << bits) - 1) | turned >> bits - 1


def relay_kernel(block_ref, after_ref, out_ref):
    del after_ref
    out_ref[...] = block_ref[...]


def chunk_kernel(low_ref, high_ref, after_ref, *outs):
    del after_ref
    half = low_ref.shape[0]
    columns = outs[0].shape[1]
    low = lax.axis_index("seq") % len(outs)
    for r, out in enumerate(outs):
        at = pl.ds(pl.multiple_of((low ^ r) * columns, columns), columns)
        out[:half] = low_ref[:, at]
        out[half:] = high_ref[:, at]


def stack_kernel(after_ref, *refs):
    del after_ref
    for r, ref in enumerate(refs[:-1]):
        refs[-1][r] = ref[...]


def columns_kernel(blocks, *refs):
    parts, out_ref = refs[:blocks], refs[blocks]
    per = parts[0].shape[0]
    bits = blocks.bit_length() - 1
    low = lax.axis_index("seq") % per
    for i in range(blocks):
        high = turned_high(lax.axis_index("head") ^ i, lax.axis_index("seq") // per, bits)
        for r in range(per):
            out_ref[high * per + (low ^ r)] = parts[i][r]


def local_grad_kernel(
    bits, gt_ref, qh_ref, kh_ref, vh_ref, pt_ref, lam_ref, after_ref, *refs
):
    del after_ref
    states, (dq_ref, dk_ref, dv_ref) = refs[:bits], refs[bits:]
    heads_dev, rows, head_dim = qh_ref.shape
    for h in range(heads_dev):
        gt = gt_ref[h * head_dim : (h + 1) * head_dim, :]
        g32 = gt.astype(F32)
        dpt = (mm(vh_ref[h], gt, NN) * weight_of(lam_ref, h, rows)).astype(BF)
        dk_ref[h] = mm(dpt, qh_ref[h], NN)
        dv_ref[h] = mm(pt_ref[h], gt, NT)
        dq = mm(dpt, kh_ref[h], TN)
        for b in range(bits):
            gw = (g32 * upper_weight(lam_ref, b, h, rows)).astype(BF)
            dq = dq + mm(gw, states[b][h], TT)
        dq_ref[h] = dq


def query_grad_kernel(top, gt_ref, lam_ref, dql_ref, state_ref, after_ref, dq_ref):
    del after_ref
    heads_dev, rows, head_dim = dql_ref.shape
    for h in range(heads_dev):
        g32 = gt_ref[h * head_dim : (h + 1) * head_dim, :].astype(F32)
        gw = (g32 * upper_weight(lam_ref, top, h, rows)).astype(BF)
        dq_ref[:, h, :] = dql_ref[h] + mm(gw, state_ref[h], TT)


def later_grad_kernel(top, kh_ref, vh_ref, dkl_ref, dvl_ref, after_ref, *refs):
    del after_ref
    landed, (dk_ref, dv_ref) = refs[:-2], refs[-2:]
    for h in range(kh_ref.shape[0]):
        late = landed_sum(top, [ref[h] for ref in landed]).astype(BF)
        dk_ref[:, h, :] = dkl_ref[h] + mm(vh_ref[h], late, NN)
        dv_ref[:, h, :] = dvl_ref[h] + mm(kh_ref[h], late, NT)


def share_kernel(offsets, att_ref, w_ref, after_ref, out_ref):
    del after_ref
    width = out_ref.shape[2]
    for n, i in enumerate(offsets):
        column = pl.multiple_of((lax.axis_index("head") ^ i) * width, width)
        out_ref[n] = mm(att_ref[...], w_ref[:, pl.ds(column, width)], NN).astype(out_ref.dtype)


def ring_owner(place, offset, devices):
    at = jnp.where(place % 2 == 0, place // 2, devices - 1 - place // 2)
    at = (at + offset + devices) % devices
    return jnp.where(at < devices // 2, 2 * at, 2 * (devices - 1 - at) + 1)


def proj_kernel(offsets, devices, first, cols_ref, after_ref, *refs):
    del after_ref
    total = None if first else refs[len(offsets)][...]
    for i, (offset, low, high) in enumerate(offsets):
        owner = ring_owner(lax.axis_index("seq"), offset, devices)
        product = mm(refs[i][...], cols_ref[owner, low:high, :], TN)
        total = product if total is None else total + product
    refs[-1][...] = total


def last_kernel(offset, devices, cols_ref, low_ref, high_ref, total_ref, after_ref, out_hbm, *refs):
    del after_ref
    held, result, sems = refs
    half = low_ref.shape[0]
    held[:half] = low_ref[...]
    held[half:] = high_ref[...]
    cols = cols_ref[ring_owner(lax.axis_index("seq"), offset, devices)]
    pieces = sems.shape[0]
    block = held.shape[1] // pieces
    copies = []
    for i in range(pieces):
        at = pl.ds(i * block, block)
        result[at, :] = total_ref[at, :] + mm(held[:, at], cols, TN)
        copies.append(pltpu.make_async_copy(result.at[at], out_hbm.at[at], sems.at[i]))
        copies[-1].start()
    for copy in copies:
        copy.wait()


def body(queries, keys, values, level_weights, out_proj, out_grad):
    rows, heads_dev, head_dim = queries.shape
    width = heads_dev * head_dim
    devices = lax.axis_size("seq")
    seq_bits = devices.bit_length() - 1
    heads = lax.axis_size("head")
    head_bits = heads.bit_length() - 1
    columns_dev = out_proj.shape[1] // devices

    head_state = like((heads_dev, head_dim, head_dim), BF)
    pinned_state = pltpu.VMEM((heads_dev, head_dim, head_dim), BF)
    per_head = pltpu.VMEM((heads_dev, rows, head_dim), BF)
    per_head_f32 = pltpu.VMEM((heads_dev, rows, head_dim), F32)
    flops_head = 2 * heads_dev * rows * rows * head_dim
    moved_head = 2 * rows * width
    top = seq_bits - 1

    half = rows // 2
    own_state, kh, vh, own_grad, own_low = pl.pallas_call(
        state_kernel,
        out_shape=(head_state, per_head, per_head, like(out_grad.shape, BF), like((half, width), BF)),
        in_specs=[ANY] * 3,
        out_specs=(VMEM,) * 5,
        scratch_shapes=[
            pltpu.VMEM(keys.shape, F32),
            pltpu.VMEM(keys.shape, F32),
            pltpu.SemaphoreType.DMA((4,)),
        ],
        compiler_params=PARAMS,
        cost_estimate=cost(flops_head, 7 * moved_head),
    )(hbm(keys), hbm(values), hbm(out_grad))

    def to_group(block, i):
        return lax.ppermute(block, "head", [(at, at ^ i) for at in range(heads)])

    def every_group(block):
        blocks = {0: block}
        for digit in reversed(range(head_bits)):
            for i in sorted(blocks):
                blocks[i ^ 1 << digit] = to_group(blocks[i], 1 << digit)
        return [blocks[i] for i in range(heads)]

    probs_t, att_local, qh, qw, lam, w = pl.pallas_call(
        local_kernel,
        out_shape=(
            pltpu.VMEM((heads_dev, rows, rows), BF),
            per_head_f32,
            per_head,
            pltpu.VMEM((seq_bits, heads_dev, rows, head_dim), BF),
            pltpu.VMEM(level_weights.shape, F32),
            pltpu.VMEM(out_proj.shape, BF),
        ),
        in_specs=[ANY, VMEM, VMEM, ANY, ANY],
        out_specs=(VMEM,) * 6,
        scratch_shapes=[
            pltpu.VMEM(queries.shape, F32),
            pltpu.VMEM((rows, rows), F32),
            pltpu.SemaphoreType.DMA((10,)),
        ],
        compiler_params=PARAMS,
        cost_estimate=cost(2 * flops_head, 12 * moved_head),
    )(hbm(queries), kh, vh, hbm(level_weights), hbm(out_proj))

    def relayed(block):
        return pl.pallas_call(
            relay_kernel,
            out_shape=like(block.shape, block.dtype),
            in_specs=[VMEM, ANY],
            out_specs=VMEM,
            compiler_params=PARAMS,
            cost_estimate=cost(0, 2 * moved_head),
        )(block, qw)

    grad_blocks = {0: own_grad}
    for digit in reversed(range(head_bits)):
        for i in sorted(grad_blocks):
            block = relayed(grad_blocks[i]) if i else own_grad
            grad_blocks[i ^ 1 << digit] = to_group(block, 1 << digit)
    grad_blocks = [grad_blocks[i] for i in range(heads)]

    per = devices // heads
    def turn_route(shift):
        return [
            (
                (high * per + low) * heads + (group_at ^ shift),
                (group_at * per + low) * heads + turned_group(high, group_at, head_bits),
            )
            for high in range(heads)
            for low in range(per)
            for group_at in range(heads)
        ]

    axes, far = ("seq", "head"), heads // 2
    turned = [
        lax.ppermute(own_low, axes, turn_route(0)),
        lax.ppermute(grad_blocks[far][half:], axes, turn_route(far)),
    ]
    partner_states = []
    running, arrived = own_state, None
    for digit in range(top):
        if arrived is not None:
            running = pl.pallas_call(
                running_kernel,
                out_shape=head_state,
                in_specs=[VMEM] * 2 + [ANY],
                out_specs=VMEM,
                compiler_params=PARAMS,
                cost_estimate=cost(0, 3 * moved_head),
            )(running, arrived, qw)
        arrived = across(running, "seq", digit)
        partner_states.append(arrived)

    gt, *grad_sums = pl.pallas_call(
        functools.partial(cotangent_kernel, heads, seq_bits),
        out_shape=(pltpu.VMEM((width, rows), BF),) + (pinned_state,) * seq_bits,
        in_specs=[VMEM] * (heads + 2) + [ANY],
        out_specs=(VMEM,) * (1 + seq_bits),
        compiler_params=PARAMS,
        cost_estimate=cost(2 * rows * width * out_proj.shape[1], 2 * width * out_proj.shape[1]),
    )(*grad_blocks, w, qw, running)

    meeting = pl.pallas_call(
        functools.partial(meet_kernel, top)
        if arrived is not None
        else lambda grad_ref, running_ref, out_ref: meet_kernel(
            top, grad_ref, running_ref, None, out_ref
        ),
        out_shape=head_state,
        in_specs=[VMEM] * (2 if arrived is None else 3),
        out_specs=VMEM,
        compiler_params=PARAMS,
        cost_estimate=cost(0, 4 * moved_head),
    )(grad_sums[top], running, *([] if arrived is None else [arrived]))
    landed = [across(meeting, "seq", top)]
    partner_states.append(landed[0])

    chunks = pl.pallas_call(
        chunk_kernel,
        out_shape=(like((rows, columns_dev), BF),) * per,
        in_specs=[VMEM, VMEM, ANY],
        out_specs=(VMEM,) * per,
        compiler_params=PARAMS,
        cost_estimate=cost(0, 2 * moved_head),
    )(*turned, meeting)
    own_chunks = chunks
    chunks = [chunks[0]] + [
        lax.ppermute(chunks[r], "seq", [(at, at ^ r) for at in range(devices)])
        for r in range(1, per)
    ]
    stacked = pl.pallas_call(
        stack_kernel,
        out_shape=like((per, rows, columns_dev), BF),
        in_specs=[ANY] + [VMEM] * per,
        out_specs=VMEM,
        compiler_params=PARAMS,
        cost_estimate=cost(0, 2 * moved_head),
    )(meeting, *chunks)
    column_blocks = every_group(stacked)

    grad_columns = pl.pallas_call(
        functools.partial(columns_kernel, heads),
        out_shape=pltpu.VMEM((devices, rows, columns_dev), BF),
        in_specs=[VMEM] * heads,
        out_specs=VMEM,
        compiler_params=PARAMS,
        cost_estimate=cost(0, 8 * moved_head),
    )(*column_blocks)

    query_local, key_local, value_local = pl.pallas_call(
        functools.partial(local_grad_kernel, top),
        out_shape=(per_head_f32,) * 3,
        in_specs=[VMEM] * 6 + [ANY] + [VMEM] * top,
        out_specs=(VMEM,) * 3,
        compiler_params=PARAMS,
        cost_estimate=cost((4 + top) * flops_head, 14 * moved_head),
    )(gt, qh, kh, vh, probs_t, lam, meeting, *partner_states[:top])

    attended = pl.pallas_call(
        functools.partial(attended_kernel, seq_bits),
        out_shape=like((rows, width), BF),
        in_specs=[VMEM] * (2 + seq_bits) + [ANY] * 2,
        out_specs=VMEM,
        compiler_params=PARAMS,
        cost_estimate=cost(seq_bits * flops_head, 8 * moved_head),
    )(att_local, qw, *partner_states, key_local, own_chunks[-1])

    first_pending = attended
    for digit in reversed(range(top)):
        outgoing = pl.pallas_call(
            functools.partial(pending_kernel, top),
            out_shape=head_state,
            in_specs=[VMEM, ANY] + [VMEM] * len(landed),
            out_specs=VMEM,
            compiler_params=PARAMS,
            cost_estimate=cost(0, 4 * moved_head),
        )(grad_sums[digit], attended, *landed)
        if len(landed) == 1:
            first_pending = outgoing
        landed.append(across(outgoing, "seq", digit))

    query_grad = pl.pallas_call(
        functools.partial(query_grad_kernel, top),
        out_shape=like((rows, heads_dev, head_dim), F32),
        in_specs=[VMEM] * 4 + [ANY],
        out_specs=VMEM,
        compiler_params=PARAMS,
        cost_estimate=cost(flops_head, 6 * moved_head),
    )(gt, lam, query_local, partner_states[top], attended)

    def share(offsets, kind, after):
        return pl.pallas_call(
            functools.partial(share_kernel, offsets),
            out_shape=like((len(offsets), rows, width), kind),
            in_specs=[VMEM, VMEM, ANY],
            out_specs=VMEM,
            compiler_params=PARAMS,
            cost_estimate=cost(
                2 * rows * width * len(offsets) * width, 2 * width * len(offsets) * width
            ),
        )(attended, w, after)

    send = share(range(1, heads, 2), BF, stacked)
    kept = share(range(0, heads, 2), F32, first_pending)
    for digit in range(head_bits):
        kept = kept + to_group(send, 1 << digit).astype(F32)
        if digit < head_bits - 1:
            send, kept = kept[1::2].astype(BF), kept[0::2]
    mixed = kept[0].astype(BF)

    key_grad, value_grad = pl.pallas_call(
        functools.partial(later_grad_kernel, top),
        out_shape=(like((rows, heads_dev, head_dim), F32),) * 2,
        in_specs=[VMEM] * 4 + [ANY] + [VMEM] * seq_bits,
        out_specs=(VMEM,) * 2,
        compiler_params=PARAMS,
        cost_estimate=cost(2 * flops_head, 11 * moved_head),
    )(kh, vh, key_local, value_local, attended, *landed)

    ring = list(range(0, devices, 2)) + list(range(devices - 1, 0, -2))
    forward = [(ring[i], ring[(i + 1) % devices]) for i in range(devices)]
    backward = [(b, a) for a, b in forward]

    def accumulate(total, blocks, offsets):
        operands = blocks if total is None else blocks + [total]
        return pl.pallas_call(
            functools.partial(proj_kernel, offsets, devices, total is None),
            out_shape=pltpu.VMEM((width, columns_dev), F32),
            in_specs=[VMEM, ANY] + [VMEM] * len(operands),
            out_specs=VMEM,
            compiler_params=PARAMS,
            cost_estimate=cost(
                2 * len(blocks) * rows * width * columns_dev, 4 * width * columns_dev
            ),
        )(grad_columns, hbm(key_grad), *operands)

    blocks, offsets = [attended], [(0, 0, rows)]
    ahead = behind = attended
    steps, total = devices // 2, None
    for step in range(1, steps):
        ahead = lax.ppermute(ahead, "seq", forward)
        behind = lax.ppermute(behind, "seq", backward)
        blocks += [ahead, behind]
        offsets += [(-step, 0, rows), (step, 0, rows)]
        if step == steps - 2:
            total = accumulate(None, blocks, offsets)
            blocks, offsets = [], []
    if blocks:
        total = accumulate(total, blocks, offsets)
    last = [
        lax.ppermute(ahead[:half], "seq", forward),
        lax.ppermute(behind[half:], "seq", backward),
    ]
    proj_grad = pl.pallas_call(
        functools.partial(last_kernel, steps, devices),
        out_shape=like((width, columns_dev), F32),
        in_specs=[VMEM] * 4 + [ANY],
        out_specs=ANY,
        scratch_shapes=[
            pltpu.VMEM((rows, width), BF),
            pltpu.VMEM((width, columns_dev), F32),
            pltpu.SemaphoreType.DMA((4,)),
        ],
        compiler_params=PARAMS,
        cost_estimate=cost(2 * rows * width * columns_dev, 8 * width * columns_dev),
    )(grad_columns, *last, total, hbm(key_grad))
    return (mixed, query_grad, key_grad, value_grad, proj_grad)


def solution(mesh):
    placed = (
        P("seq", "head", None),
        P("seq", "head", None),
        P("seq", "head", None),
        P(None, "head", "seq"),
        P("head", None),
        P("seq", "head"),
    )
    return jax.shard_map(
        body,
        mesh=mesh,
        in_specs=placed,
        out_specs=(
            P("seq", "head"),
            P("seq", "head", None),
            P("seq", "head", None),
            P("seq", "head", None),
            P("head", "seq"),
        ),
        check_vma=False,
    )
```

```python
import functools

import jax
import jax.numpy as jnp
from jax import lax
from jax.experimental import pallas as pl
from jax.experimental.pallas import tpu as pltpu
from jax.sharding import PartitionSpec as P

CH = 64
BF = jnp.bfloat16
F32 = jnp.float32
NN = (((1,), (0,)), ((), ()))
NT = (((1,), (1,)), ((), ()))
TN = (((0,), (0,)), ((), ()))
TT = (((0,), (1,)), ((), ()))
VMEM = pl.BlockSpec(memory_space=pltpu.VMEM)
ANY = pl.BlockSpec(memory_space=pl.ANY)
PARAMS = pltpu.CompilerParams(vmem_limit_bytes=14 * 2**20)


def mm(a, b, dims):
    return lax.dot_general(a, b, dims, preferred_element_type=F32)


def cost(flops, moved):
    return pl.CostEstimate(flops=flops, bytes_accessed=moved, transcendentals=0)


def like(shape, dtype):
    return jax.ShapeDtypeStruct(shape, dtype)


def across(block, axis, stride, up_only=False, down_only=False):
    count = lax.axis_size(axis)
    route = []
    for low in range(count):
        high = low | 1 << stride
        if high != low and high < count:
            if not down_only:
                route.append((low, high))
            if not up_only:
                route.append((high, low))
    return lax.ppermute(block, axis, route)


def hbm(array):
    return pltpu.with_memory_space_constraint(array, pltpu.HBM)


def state_kernel(k_hbm, v_hbm, grad_hbm, *refs):
    s_ref, kh_ref, vh_ref, grad_ref, low_ref, k_ref, v_ref, sems = refs
    copies = [
        pltpu.make_async_copy(k_hbm, k_ref, sems.at[0]),
        pltpu.make_async_copy(v_hbm, v_ref, sems.at[1]),
        pltpu.make_async_copy(grad_hbm, grad_ref, sems.at[2]),
        pltpu.make_async_copy(grad_hbm.at[pl.ds(0, low_ref.shape[0])], low_ref, sems.at[3]),
    ]
    for copy in copies:
        copy.start()
    for copy in copies[:2]:
        copy.wait()
    for h in range(k_ref.shape[1]):
        k = k_ref[:, h, :].astype(BF)
        v = v_ref[:, h, :].astype(BF)
        kh_ref[h] = k
        vh_ref[h] = v
        s_ref[h] = mm(k, v, TN).astype(BF)
    copies[2].wait()
    copies[3].wait()


def weight_of(lam_ref, h, rows):
    local_bits = (rows // CH).bit_length() - 1
    s = lax.broadcasted_iota(jnp.int32, (rows, rows), 0)
    t = lax.broadcasted_iota(jnp.int32, (rows, rows), 1)
    differ = (s // CH) ^ (t // CH)
    weight = jnp.broadcast_to(lam_ref[0, h : h + 1, :], (rows, rows))
    for digit in range(local_bits):
        weight = jnp.where(differ >= 1 << digit, lam_ref[1 + digit, h : h + 1, :], weight)
    return jnp.where(s <= t, weight, 0.0)


def upper_weight(lam_ref, b, h, rows):
    local_bits = (rows // CH).bit_length() - 1
    upper = (lax.axis_index("seq") >> b & 1).astype(F32)
    return lam_ref[1 + local_bits + b, h : h + 1, :] * upper


def local_kernel(q_hbm, kh_ref, vh_ref, lam_hbm, w_hbm, *refs):
    pt_ref, att_ref, qh_ref, qw_ref, lam_ref, w_ref, q_ref, lam_rows, sems = refs
    pieces = sems.shape[0] - 2
    share = w_hbm.shape[0] // pieces
    copies = [
        pltpu.make_async_copy(q_hbm, q_ref, sems.at[0]),
        pltpu.make_async_copy(lam_hbm, lam_ref, sems.at[1]),
    ]
    for i in range(pieces):
        piece = pl.ds(i * share, share)
        copies.append(pltpu.make_async_copy(w_hbm.at[piece], w_ref.at[piece], sems.at[2 + i]))
    for copy in copies:
        copy.start()
    for copy in copies[:2]:
        copy.wait()
    rows, heads_dev, _ = q_ref.shape
    bits = qw_ref.shape[0]
    lam_rows[...] = jnp.zeros_like(lam_rows)
    for b in range(bits):
        for h in range(heads_dev):
            at = b * heads_dev + h
            lam_rows[at : at + 1, :] = upper_weight(lam_ref, b, h, rows)
    lam_columns = lam_rows[...].T
    for h in range(heads_dev):
        q32 = q_ref[:, h, :]
        q = q32.astype(BF)
        qh_ref[h] = q
        for b in range(bits):
            at = b * heads_dev + h
            qw_ref[b, h] = (q32 * lam_columns[:, at : at + 1]).astype(BF)
        pt = (mm(kh_ref[h], q, NT) * weight_of(lam_ref, h, rows)).astype(BF)
        pt_ref[h] = pt
        att_ref[h] = mm(pt, vh_ref[h], TN)
    for copy in copies[2:]:
        copy.wait()


def attended_kernel(bits, att_ref, qw_ref, *refs):
    states, out_ref = refs[:bits], refs[-1]
    heads_dev, _, head_dim = att_ref.shape
    for h in range(heads_dev):
        total = att_ref[h]
        for b in range(bits):
            total = total + mm(qw_ref[b, h], states[b][h], NN)
        out_ref[:, h * head_dim : (h + 1) * head_dim] = total.astype(BF)


def cotangent_kernel(blocks, bits, *refs):
    parts, (w_ref, qw_ref, _, gt_ref), sums = (
        refs[:blocks],
        refs[blocks : blocks + 4],
        refs[blocks + 4 :],
    )
    deep = parts[0].shape[1]
    _, heads_dev, _, head_dim = qw_ref.shape
    total = None
    for i in range(blocks):
        column = pl.multiple_of((lax.axis_index("head") ^ i) * deep, deep)
        product = mm(w_ref[:, pl.ds(column, deep)], parts[i][...], NT)
        total = product if total is None else total + product
    for h in range(heads_dev):
        gt = total[h * head_dim : (h + 1) * head_dim].astype(BF)
        gt_ref[h * head_dim : (h + 1) * head_dim, :] = gt
        for b in range(bits):
            sums[b][h] = mm(gt, qw_ref[b, h], NN).astype(BF)


def running_kernel(running_ref, arrived_ref, *refs):
    refs[-1][...] = (running_ref[...].astype(F32) + arrived_ref[...].astype(F32)).astype(BF)


def meet_kernel(top, grad_ref, running_ref, arrived_ref, out_ref):
    upper = (lax.axis_index("seq") >> top & 1) == 1
    running = running_ref[...].astype(F32)
    if arrived_ref is not None:
        running = running + arrived_ref[...].astype(F32)
    out_ref[...] = jnp.where(upper, grad_ref[...], running.astype(BF))


def landed_sum(top, landed):
    upper = (lax.axis_index("seq") >> top & 1) == 1
    total = jnp.where(upper, 0.0, landed[0].astype(F32))
    for block in landed[1:]:
        total = total + block.astype(F32)
    return total


def pending_kernel(top, own_ref, after_ref, *refs):
    del after_ref
    landed, out_ref = [ref[...] for ref in refs[:-1]], refs[-1]
    out_ref[...] = (own_ref[...].astype(F32) + landed_sum(top, landed)).astype(BF)


def turned_group(high, group, bits):
    turned = high >> 1 | (high & 1) << bits - 1
    return turned ^ ((group >> bits - 1 ^ group) & 1) << bits - 1


def turned_high(turned, group, bits):
    turned = turned ^ ((group >> bits - 1 ^ group) & 1) << bits - 1
    return (turned << 1 & (1 << bits) - 1) | turned >> bits - 1


def feed_kernel(own_ref, far_ref, after_ref, low_ref, high_ref):
    del after_ref
    half = low_ref.shape[0]
    low_ref[...] = own_ref[:half]
    high_ref[...] = far_ref[half:]


def relay_kernel(block_ref, after_ref, out_ref):
    del after_ref
    out_ref[...] = block_ref[...]


def chunk_kernel(low_ref, high_ref, after_ref, *outs):
    del after_ref
    half = low_ref.shape[0]
    columns = outs[0].shape[1]
    low = lax.axis_index("seq") % len(outs)
    for r, out in enumerate(outs):
        at = pl.ds(pl.multiple_of((low ^ r) * columns, columns), columns)
        out[:half] = low_ref[:, at]
        out[half:] = high_ref[:, at]


def stack_kernel(after_ref, *refs):
    del after_ref
    for r, ref in enumerate(refs[:-1]):
        refs[-1][r] = ref[...]


def columns_kernel(blocks, *refs):
    parts, out_ref = refs[:blocks], refs[blocks]
    per = parts[0].shape[0]
    bits = blocks.bit_length() - 1
    low = lax.axis_index("seq") % per
    for i in range(blocks):
        high = turned_high(lax.axis_index("head") ^ i, lax.axis_index("seq") // per, bits)
        for r in range(per):
            out_ref[high * per + (low ^ r)] = parts[i][r]


def local_grad_kernel(
    bits, gt_ref, qh_ref, kh_ref, vh_ref, pt_ref, lam_ref, after_ref, *refs
):
    del after_ref
    states, (dq_ref, dk_ref, dv_ref) = refs[:bits], refs[bits:]
    heads_dev, rows, head_dim = qh_ref.shape
    for h in range(heads_dev):
        gt = gt_ref[h * head_dim : (h + 1) * head_dim, :]
        g32 = gt.astype(F32)
        dpt = (mm(vh_ref[h], gt, NN) * weight_of(lam_ref, h, rows)).astype(BF)
        dk_ref[h] = mm(dpt, qh_ref[h], NN)
        dv_ref[h] = mm(pt_ref[h], gt, NT)
        dq = mm(dpt, kh_ref[h], TN)
        for b in range(bits):
            gw = (g32 * upper_weight(lam_ref, b, h, rows)).astype(BF)
            dq = dq + mm(gw, states[b][h], TT)
        dq_ref[h] = dq


def query_grad_kernel(top, gt_ref, lam_ref, dql_ref, state_ref, after_ref, dq_ref):
    del after_ref
    heads_dev, rows, head_dim = dql_ref.shape
    for h in range(heads_dev):
        g32 = gt_ref[h * head_dim : (h + 1) * head_dim, :].astype(F32)
        gw = (g32 * upper_weight(lam_ref, top, h, rows)).astype(BF)
        dq_ref[:, h, :] = dql_ref[h] + mm(gw, state_ref[h], TT)


def later_grad_kernel(top, kh_ref, vh_ref, dkl_ref, dvl_ref, after_ref, *refs):
    del after_ref
    landed, (dk_ref, dv_ref) = refs[:-2], refs[-2:]
    for h in range(kh_ref.shape[0]):
        late = landed_sum(top, [ref[h] for ref in landed]).astype(BF)
        dk_ref[:, h, :] = dkl_ref[h] + mm(vh_ref[h], late, NN)
        dv_ref[:, h, :] = dvl_ref[h] + mm(kh_ref[h], late, NT)


def share_kernel(offsets, att_ref, w_ref, after_ref, out_ref):
    del after_ref
    width = out_ref.shape[2]
    for n, i in enumerate(offsets):
        column = pl.multiple_of((lax.axis_index("head") ^ i) * width, width)
        out_ref[n] = mm(att_ref[...], w_ref[:, pl.ds(column, width)], NN).astype(out_ref.dtype)


def ring_owner(place, offset, devices):
    at = jnp.where(place % 2 == 0, place // 2, devices - 1 - place // 2)
    at = (at + offset + devices) % devices
    return jnp.where(at < devices // 2, 2 * at, 2 * (devices - 1 - at) + 1)


def proj_kernel(offsets, devices, first, cols_ref, after_ref, *refs):
    del after_ref
    total = None if first else refs[len(offsets)][...]
    for i, (offset, low, high) in enumerate(offsets):
        owner = ring_owner(lax.axis_index("seq"), offset, devices)
        product = mm(refs[i][...], cols_ref[owner, low:high, :], TN)
        total = product if total is None else total + product
    refs[-1][...] = total


def last_kernel(offset, devices, cols_ref, low_ref, high_ref, total_ref, after_ref, out_hbm, *refs):
    del after_ref
    held, result, sems = refs
    half = low_ref.shape[0]
    held[:half] = low_ref[...]
    held[half:] = high_ref[...]
    cols = cols_ref[ring_owner(lax.axis_index("seq"), offset, devices)]
    pieces = sems.shape[0]
    block = held.shape[1] // pieces
    copies = []
    for i in range(pieces):
        at = pl.ds(i * block, block)
        result[at, :] = total_ref[at, :] + mm(held[:, at], cols, TN)
        copies.append(pltpu.make_async_copy(result.at[at], out_hbm.at[at], sems.at[i]))
        copies[-1].start()
    for copy in copies:
        copy.wait()


def body(queries, keys, values, level_weights, out_proj, out_grad):
    rows, heads_dev, head_dim = queries.shape
    width = heads_dev * head_dim
    devices = lax.axis_size("seq")
    seq_bits = devices.bit_length() - 1
    heads = lax.axis_size("head")
    head_bits = heads.bit_length() - 1
    columns_dev = out_proj.shape[1] // devices

    head_state = like((heads_dev, head_dim, head_dim), BF)
    pinned_state = pltpu.VMEM((heads_dev, head_dim, head_dim), BF)
    per_head = pltpu.VMEM((heads_dev, rows, head_dim), BF)
    per_head_f32 = pltpu.VMEM((heads_dev, rows, head_dim), F32)
    flops_head = 2 * heads_dev * rows * rows * head_dim
    moved_head = 2 * rows * width
    top = seq_bits - 1

    half = rows // 2
    own_state, kh, vh, own_grad, own_low = pl.pallas_call(
        state_kernel,
        out_shape=(head_state, per_head, per_head, like(out_grad.shape, BF), like((half, width), BF)),
        in_specs=[ANY] * 3,
        out_specs=(VMEM,) * 5,
        scratch_shapes=[
            pltpu.VMEM(keys.shape, F32),
            pltpu.VMEM(keys.shape, F32),
            pltpu.SemaphoreType.DMA((4,)),
        ],
        compiler_params=PARAMS,
        cost_estimate=cost(flops_head, 7 * moved_head),
    )(hbm(keys), hbm(values), hbm(out_grad))

    def to_group(block, i):
        return lax.ppermute(block, "head", [(at, at ^ i) for at in range(heads)])

    def every_group(block):
        blocks = {0: block}
        for digit in reversed(range(head_bits)):
            for i in sorted(blocks):
                blocks[i ^ 1 << digit] = to_group(blocks[i], 1 << digit)
        return [blocks[i] for i in range(heads)]

    probs_t, att_local, qh, qw, lam, w = pl.pallas_call(
        local_kernel,
        out_shape=(
            pltpu.VMEM((heads_dev, rows, rows), BF),
            per_head_f32,
            per_head,
            pltpu.VMEM((seq_bits, heads_dev, rows, head_dim), BF),
            pltpu.VMEM(level_weights.shape, F32),
            pltpu.VMEM(out_proj.shape, BF),
        ),
        in_specs=[ANY, VMEM, VMEM, ANY, ANY],
        out_specs=(VMEM,) * 6,
        scratch_shapes=[
            pltpu.VMEM(queries.shape, F32),
            pltpu.VMEM((rows, rows), F32),
            pltpu.SemaphoreType.DMA((10,)),
        ],
        compiler_params=PARAMS,
        cost_estimate=cost(2 * flops_head, 12 * moved_head),
    )(hbm(queries), kh, vh, hbm(level_weights), hbm(out_proj))

    def relayed(block):
        return pl.pallas_call(
            relay_kernel,
            out_shape=like(block.shape, block.dtype),
            in_specs=[VMEM, ANY],
            out_specs=VMEM,
            compiler_params=PARAMS,
            cost_estimate=cost(0, 2 * moved_head),
        )(block, qw)

    grad_blocks = {0: own_grad}
    for digit in reversed(range(head_bits)):
        for i in sorted(grad_blocks):
            block = relayed(grad_blocks[i]) if i else own_grad
            grad_blocks[i ^ 1 << digit] = to_group(block, 1 << digit)
    grad_blocks = [grad_blocks[i] for i in range(heads)]

    partner_states = []
    running, arrived = own_state, None
    for digit in range(top):
        if arrived is not None:
            running = pl.pallas_call(
                running_kernel,
                out_shape=head_state,
                in_specs=[VMEM] * 2 + [ANY],
                out_specs=VMEM,
                compiler_params=PARAMS,
                cost_estimate=cost(0, 3 * moved_head),
            )(running, arrived, qw)
        arrived = across(running, "seq", digit)
        partner_states.append(arrived)

    gt, *grad_sums = pl.pallas_call(
        functools.partial(cotangent_kernel, heads, seq_bits),
        out_shape=(pltpu.VMEM((width, rows), BF),) + (pinned_state,) * seq_bits,
        in_specs=[VMEM] * (heads + 2) + [ANY],
        out_specs=(VMEM,) * (1 + seq_bits),
        compiler_params=PARAMS,
        cost_estimate=cost(2 * rows * width * out_proj.shape[1], 2 * width * out_proj.shape[1]),
    )(*grad_blocks, w, qw, running)

    per = devices // heads
    def turn_route(shift):
        return [
            (
                (high * per + low) * heads + (group_at ^ shift),
                (group_at * per + low) * heads + turned_group(high, group_at, head_bits),
            )
            for high in range(heads)
            for low in range(per)
            for group_at in range(heads)
        ]

    axes, far = ("seq", "head"), heads // 2
    low_rows, high_rows = pl.pallas_call(
        feed_kernel,
        out_shape=(like((half, width), BF),) * 2,
        in_specs=[VMEM, VMEM, ANY],
        out_specs=(VMEM,) * 2,
        compiler_params=PARAMS,
        cost_estimate=cost(0, 2 * moved_head),
    )(own_grad, grad_blocks[far], gt)
    turned = [
        lax.ppermute(low_rows, axes, turn_route(0)),
        lax.ppermute(high_rows, axes, turn_route(far)),
    ]
    meeting = pl.pallas_call(
        functools.partial(meet_kernel, top)
        if arrived is not None
        else lambda grad_ref, running_ref, out_ref: meet_kernel(
            top, grad_ref, running_ref, None, out_ref
        ),
        out_shape=head_state,
        in_specs=[VMEM] * (2 if arrived is None else 3),
        out_specs=VMEM,
        compiler_params=PARAMS,
        cost_estimate=cost(0, 4 * moved_head),
    )(grad_sums[top], running, *([] if arrived is None else [arrived]))
    landed = [across(meeting, "seq", top)]
    partner_states.append(landed[0])

    chunks = pl.pallas_call(
        chunk_kernel,
        out_shape=(like((rows, columns_dev), BF),) * per,
        in_specs=[VMEM, VMEM, ANY],
        out_specs=(VMEM,) * per,
        compiler_params=PARAMS,
        cost_estimate=cost(0, 2 * moved_head),
    )(*turned, meeting)
    own_chunks = chunks
    chunks = [chunks[0]] + [
        lax.ppermute(chunks[r], "seq", [(at, at ^ r) for at in range(devices)])
        for r in range(1, per)
    ]
    stacked = pl.pallas_call(
        stack_kernel,
        out_shape=like((per, rows, columns_dev), BF),
        in_specs=[ANY] + [VMEM] * per,
        out_specs=VMEM,
        compiler_params=PARAMS,
        cost_estimate=cost(0, 2 * moved_head),
    )(meeting, *chunks)
    column_blocks = every_group(stacked)

    grad_columns = pl.pallas_call(
        functools.partial(columns_kernel, heads),
        out_shape=pltpu.VMEM((devices, rows, columns_dev), BF),
        in_specs=[VMEM] * heads,
        out_specs=VMEM,
        compiler_params=PARAMS,
        cost_estimate=cost(0, 8 * moved_head),
    )(*column_blocks)

    query_local, key_local, value_local = pl.pallas_call(
        functools.partial(local_grad_kernel, top),
        out_shape=(per_head_f32,) * 3,
        in_specs=[VMEM] * 6 + [ANY] + [VMEM] * top,
        out_specs=(VMEM,) * 3,
        compiler_params=PARAMS,
        cost_estimate=cost((4 + top) * flops_head, 14 * moved_head),
    )(gt, qh, kh, vh, probs_t, lam, meeting, *partner_states[:top])

    attended = pl.pallas_call(
        functools.partial(attended_kernel, seq_bits),
        out_shape=like((rows, width), BF),
        in_specs=[VMEM] * (2 + seq_bits) + [ANY] * 2,
        out_specs=VMEM,
        compiler_params=PARAMS,
        cost_estimate=cost(seq_bits * flops_head, 8 * moved_head),
    )(att_local, qw, *partner_states, key_local, own_chunks[-1])

    first_pending = attended
    for digit in reversed(range(top)):
        outgoing = pl.pallas_call(
            functools.partial(pending_kernel, top),
            out_shape=head_state,
            in_specs=[VMEM, ANY] + [VMEM] * len(landed),
            out_specs=VMEM,
            compiler_params=PARAMS,
            cost_estimate=cost(0, 4 * moved_head),
        )(grad_sums[digit], attended, *landed)
        if len(landed) == 1:
            first_pending = outgoing
        landed.append(across(outgoing, "seq", digit))

    query_grad = pl.pallas_call(
        functools.partial(query_grad_kernel, top),
        out_shape=like((rows, heads_dev, head_dim), F32),
        in_specs=[VMEM] * 4 + [ANY],
        out_specs=VMEM,
        compiler_params=PARAMS,
        cost_estimate=cost(flops_head, 6 * moved_head),
    )(gt, lam, query_local, partner_states[top], attended)

    def share(offsets, kind, after):
        return pl.pallas_call(
            functools.partial(share_kernel, offsets),
            out_shape=like((len(offsets), rows, width), kind),
            in_specs=[VMEM, VMEM, ANY],
            out_specs=VMEM,
            compiler_params=PARAMS,
            cost_estimate=cost(
                2 * rows * width * len(offsets) * width, 2 * width * len(offsets) * width
            ),
        )(attended, w, after)

    send = share(range(1, heads, 2), BF, stacked)
    kept = share(range(0, heads, 2), F32, first_pending)
    for digit in range(head_bits):
        kept = kept + to_group(send, 1 << digit).astype(F32)
        if digit < head_bits - 1:
            send, kept = kept[1::2].astype(BF), kept[0::2]
    mixed = kept[0].astype(BF)

    key_grad, value_grad = pl.pallas_call(
        functools.partial(later_grad_kernel, top),
        out_shape=(like((rows, heads_dev, head_dim), F32),) * 2,
        in_specs=[VMEM] * 4 + [ANY] + [VMEM] * seq_bits,
        out_specs=(VMEM,) * 2,
        compiler_params=PARAMS,
        cost_estimate=cost(2 * flops_head, 11 * moved_head),
    )(kh, vh, key_local, value_local, attended, *landed)

    ring = list(range(0, devices, 2)) + list(range(devices - 1, 0, -2))
    forward = [(ring[i], ring[(i + 1) % devices]) for i in range(devices)]
    backward = [(b, a) for a, b in forward]

    def accumulate(total, blocks, offsets):
        operands = blocks if total is None else blocks + [total]
        return pl.pallas_call(
            functools.partial(proj_kernel, offsets, devices, total is None),
            out_shape=pltpu.VMEM((width, columns_dev), F32),
            in_specs=[VMEM, ANY] + [VMEM] * len(operands),
            out_specs=VMEM,
            compiler_params=PARAMS,
            cost_estimate=cost(
                2 * len(blocks) * rows * width * columns_dev, 4 * width * columns_dev
            ),
        )(grad_columns, hbm(key_grad), *operands)

    blocks, offsets = [attended], [(0, 0, rows)]
    ahead = behind = attended
    steps, total = devices // 2, None
    for step in range(1, steps):
        ahead = lax.ppermute(ahead, "seq", forward)
        behind = lax.ppermute(behind, "seq", backward)
        blocks += [ahead, behind]
        offsets += [(-step, 0, rows), (step, 0, rows)]
        if step == steps - 2:
            total = accumulate(None, blocks, offsets)
            blocks, offsets = [], []
    if blocks:
        total = accumulate(total, blocks, offsets)
    last = [
        lax.ppermute(ahead[:half], "seq", forward),
        lax.ppermute(behind[half:], "seq", backward),
    ]
    proj_grad = pl.pallas_call(
        functools.partial(last_kernel, steps, devices),
        out_shape=like((width, columns_dev), F32),
        in_specs=[VMEM] * 4 + [ANY],
        out_specs=ANY,
        scratch_shapes=[
            pltpu.VMEM((rows, width), BF),
            pltpu.VMEM((width, columns_dev), F32),
            pltpu.SemaphoreType.DMA((4,)),
        ],
        compiler_params=PARAMS,
        cost_estimate=cost(2 * rows * width * columns_dev, 8 * width * columns_dev),
    )(grad_columns, *last, total, hbm(key_grad))
    return (mixed, query_grad, key_grad, value_grad, proj_grad)


def solution(mesh):
    placed = (
        P("seq", "head", None),
        P("seq", "head", None),
        P("seq", "head", None),
        P(None, "head", "seq"),
        P("head", None),
        P("seq", "head"),
    )
    return jax.shard_map(
        body,
        mesh=mesh,
        in_specs=placed,
        out_specs=(
            P("seq", "head"),
            P("seq", "head", None),
            P("seq", "head", None),
            P("seq", "head", None),
            P("head", "seq"),
        ),
        check_vma=False,
    )
```

```python
import functools

import jax
import jax.numpy as jnp
from jax import lax
from jax.experimental import pallas as pl
from jax.experimental.pallas import tpu as pltpu
from jax.sharding import PartitionSpec as P

CH = 64
BF = jnp.bfloat16
F32 = jnp.float32
NN = (((1,), (0,)), ((), ()))
NT = (((1,), (1,)), ((), ()))
TN = (((0,), (0,)), ((), ()))
TT = (((0,), (1,)), ((), ()))
VMEM = pl.BlockSpec(memory_space=pltpu.VMEM)
ANY = pl.BlockSpec(memory_space=pl.ANY)
PARAMS = pltpu.CompilerParams(vmem_limit_bytes=14 * 2**20)


def mm(a, b, dims):
    return lax.dot_general(a, b, dims, preferred_element_type=F32)


def cost(flops, moved):
    return pl.CostEstimate(flops=flops, bytes_accessed=moved, transcendentals=0)


def like(shape, dtype):
    return jax.ShapeDtypeStruct(shape, dtype)


def across(block, axis, stride, up_only=False, down_only=False):
    count = lax.axis_size(axis)
    route = []
    for low in range(count):
        high = low | 1 << stride
        if high != low and high < count:
            if not down_only:
                route.append((low, high))
            if not up_only:
                route.append((high, low))
    return lax.ppermute(block, axis, route)


def hbm(array):
    return pltpu.with_memory_space_constraint(array, pltpu.HBM)


def state_kernel(k_hbm, v_hbm, grad_hbm, *refs):
    s_ref, kh_ref, vh_ref, grad_ref, low_ref, k_ref, v_ref, sems = refs
    copies = [
        pltpu.make_async_copy(k_hbm, k_ref, sems.at[0]),
        pltpu.make_async_copy(v_hbm, v_ref, sems.at[1]),
        pltpu.make_async_copy(grad_hbm, grad_ref, sems.at[2]),
        pltpu.make_async_copy(grad_hbm.at[pl.ds(0, low_ref.shape[0])], low_ref, sems.at[3]),
    ]
    for copy in copies:
        copy.start()
    for copy in copies[:2]:
        copy.wait()
    for h in range(k_ref.shape[1]):
        k = k_ref[:, h, :].astype(BF)
        v = v_ref[:, h, :].astype(BF)
        kh_ref[h] = k
        vh_ref[h] = v
        s_ref[h] = mm(k, v, TN).astype(BF)
    copies[2].wait()
    copies[3].wait()


def weight_of(lam_ref, h, rows):
    local_bits = (rows // CH).bit_length() - 1
    s = lax.broadcasted_iota(jnp.int32, (rows, rows), 0)
    t = lax.broadcasted_iota(jnp.int32, (rows, rows), 1)
    differ = (s // CH) ^ (t // CH)
    weight = jnp.broadcast_to(lam_ref[0, h : h + 1, :], (rows, rows))
    for digit in range(local_bits):
        weight = jnp.where(differ >= 1 << digit, lam_ref[1 + digit, h : h + 1, :], weight)
    return jnp.where(s <= t, weight, 0.0)


def upper_weight(lam_ref, b, h, rows):
    local_bits = (rows // CH).bit_length() - 1
    upper = (lax.axis_index("seq") >> b & 1).astype(F32)
    return lam_ref[1 + local_bits + b, h : h + 1, :] * upper


def local_kernel(q_hbm, kh_ref, vh_ref, lam_hbm, w_hbm, *refs):
    pt_ref, att_ref, qh_ref, qw_ref, lam_ref, w_ref, q_ref, lam_rows, sems = refs
    pieces = sems.shape[0] - 2
    share = w_hbm.shape[0] // pieces
    copies = [
        pltpu.make_async_copy(q_hbm, q_ref, sems.at[0]),
        pltpu.make_async_copy(lam_hbm, lam_ref, sems.at[1]),
    ]
    for i in range(pieces):
        piece = pl.ds(i * share, share)
        copies.append(pltpu.make_async_copy(w_hbm.at[piece], w_ref.at[piece], sems.at[2 + i]))
    for copy in copies:
        copy.start()
    for copy in copies[:2]:
        copy.wait()
    rows, heads_dev, _ = q_ref.shape
    bits = qw_ref.shape[0]
    lam_rows[...] = jnp.zeros_like(lam_rows)
    for b in range(bits):
        for h in range(heads_dev):
            at = b * heads_dev + h
            lam_rows[at : at + 1, :] = upper_weight(lam_ref, b, h, rows)
    lam_columns = lam_rows[...].T
    for h in range(heads_dev):
        q32 = q_ref[:, h, :]
        q = q32.astype(BF)
        qh_ref[h] = q
        for b in range(bits):
            at = b * heads_dev + h
            qw_ref[b, h] = (q32 * lam_columns[:, at : at + 1]).astype(BF)
        pt = (mm(kh_ref[h], q, NT) * weight_of(lam_ref, h, rows)).astype(BF)
        pt_ref[h] = pt
        att_ref[h] = mm(pt, vh_ref[h], TN)
    for copy in copies[2:]:
        copy.wait()


def attended_kernel(bits, att_ref, qw_ref, *refs):
    states, out_ref = refs[:bits], refs[-1]
    heads_dev, _, head_dim = att_ref.shape
    for h in range(heads_dev):
        total = att_ref[h]
        for b in range(bits):
            total = total + mm(qw_ref[b, h], states[b][h], NN)
        out_ref[:, h * head_dim : (h + 1) * head_dim] = total.astype(BF)


def cotangent_kernel(blocks, bits, *refs):
    parts, (w_ref, qw_ref, _, gt_ref), sums = (
        refs[:blocks],
        refs[blocks : blocks + 4],
        refs[blocks + 4 :],
    )
    deep = parts[0].shape[1]
    _, heads_dev, _, head_dim = qw_ref.shape
    total = None
    for i in range(blocks):
        column = pl.multiple_of((lax.axis_index("head") ^ i) * deep, deep)
        product = mm(w_ref[:, pl.ds(column, deep)], parts[i][...], NT)
        total = product if total is None else total + product
    for h in range(heads_dev):
        gt = total[h * head_dim : (h + 1) * head_dim].astype(BF)
        gt_ref[h * head_dim : (h + 1) * head_dim, :] = gt
        for b in range(bits):
            sums[b][h] = mm(gt, qw_ref[b, h], NN).astype(BF)


def running_kernel(running_ref, arrived_ref, *refs):
    refs[-1][...] = (running_ref[...].astype(F32) + arrived_ref[...].astype(F32)).astype(BF)


def meet_kernel(top, grad_ref, running_ref, arrived_ref, out_ref):
    upper = (lax.axis_index("seq") >> top & 1) == 1
    running = running_ref[...].astype(F32)
    if arrived_ref is not None:
        running = running + arrived_ref[...].astype(F32)
    out_ref[...] = jnp.where(upper, grad_ref[...], running.astype(BF))


def landed_sum(top, landed):
    upper = (lax.axis_index("seq") >> top & 1) == 1
    total = jnp.where(upper, 0.0, landed[0].astype(F32))
    for block in landed[1:]:
        total = total + block.astype(F32)
    return total


def pending_kernel(top, own_ref, after_ref, *refs):
    del after_ref
    landed, out_ref = [ref[...] for ref in refs[:-1]], refs[-1]
    out_ref[...] = (own_ref[...].astype(F32) + landed_sum(top, landed)).astype(BF)


def turned_group(high, group, bits):
    turned = high >> 1 | (high & 1) << bits - 1
    return turned ^ ((group >> bits - 1 ^ group) & 1) << bits - 1


def turned_high(turned, group, bits):
    turned = turned ^ ((group >> bits - 1 ^ group) & 1) << bits - 1
    return (turned << 1 & (1 << bits) - 1) | turned >> bits - 1


def relay_kernel(block_ref, after_ref, out_ref):
    del after_ref
    out_ref[...] = block_ref[...]


def chunk_kernel(low_ref, high_ref, after_ref, *outs):
    del after_ref
    half = low_ref.shape[0]
    columns = outs[0].shape[1]
    low = lax.axis_index("seq") % len(outs)
    for r, out in enumerate(outs):
        at = pl.ds(pl.multiple_of((low ^ r) * columns, columns), columns)
        out[:half] = low_ref[:, at]
        out[half:] = high_ref[:, at]


def stack_kernel(after_ref, *refs):
    del after_ref
    for r, ref in enumerate(refs[:-1]):
        refs[-1][r] = ref[...]


def columns_kernel(blocks, *refs):
    parts, out_ref = refs[:blocks], refs[blocks]
    per = parts[0].shape[0]
    bits = blocks.bit_length() - 1
    low = lax.axis_index("seq") % per
    for i in range(blocks):
        high = turned_high(lax.axis_index("head") ^ i, lax.axis_index("seq") // per, bits)
        for r in range(per):
            out_ref[high * per + (low ^ r)] = parts[i][r]


def local_grad_kernel(
    bits, gt_ref, qh_ref, kh_ref, vh_ref, pt_ref, lam_ref, after_ref, *refs
):
    del after_ref
    states, (dq_ref, dk_ref, dv_ref) = refs[:bits], refs[bits:]
    heads_dev, rows, head_dim = qh_ref.shape
    for h in range(heads_dev):
        gt = gt_ref[h * head_dim : (h + 1) * head_dim, :]
        g32 = gt.astype(F32)
        dpt = (mm(vh_ref[h], gt, NN) * weight_of(lam_ref, h, rows)).astype(BF)
        dk_ref[h] = mm(dpt, qh_ref[h], NN)
        dv_ref[h] = mm(pt_ref[h], gt, NT)
        dq = mm(dpt, kh_ref[h], TN)
        for b in range(bits):
            gw = (g32 * upper_weight(lam_ref, b, h, rows)).astype(BF)
            dq = dq + mm(gw, states[b][h], TT)
        dq_ref[h] = dq


def query_grad_kernel(top, gt_ref, lam_ref, dql_ref, state_ref, after_ref, dq_ref):
    del after_ref
    heads_dev, rows, head_dim = dql_ref.shape
    for h in range(heads_dev):
        g32 = gt_ref[h * head_dim : (h + 1) * head_dim, :].astype(F32)
        gw = (g32 * upper_weight(lam_ref, top, h, rows)).astype(BF)
        dq_ref[:, h, :] = dql_ref[h] + mm(gw, state_ref[h], TT)


def later_grad_kernel(top, kh_ref, vh_ref, dkl_ref, dvl_ref, after_ref, *refs):
    del after_ref
    landed, (dk_ref, dv_ref) = refs[:-2], refs[-2:]
    for h in range(kh_ref.shape[0]):
        late = landed_sum(top, [ref[h] for ref in landed]).astype(BF)
        dk_ref[:, h, :] = dkl_ref[h] + mm(vh_ref[h], late, NN)
        dv_ref[:, h, :] = dvl_ref[h] + mm(kh_ref[h], late, NT)


def share_kernel(offsets, att_ref, w_ref, *refs):
    out_ref = refs[-1]
    width = out_ref.shape[2]
    for n, i in enumerate(offsets):
        column = pl.multiple_of((lax.axis_index("head") ^ i) * width, width)
        out_ref[n] = mm(att_ref[...], w_ref[:, pl.ds(column, width)], NN).astype(out_ref.dtype)


def ring_owner(place, offset, devices):
    at = jnp.where(place % 2 == 0, place // 2, devices - 1 - place // 2)
    at = (at + offset + devices) % devices
    return jnp.where(at < devices // 2, 2 * at, 2 * (devices - 1 - at) + 1)


def proj_kernel(offsets, devices, first, cols_ref, after_ref, *refs):
    del after_ref
    total = None if first else refs[len(offsets)][...]
    for i, (offset, low, high) in enumerate(offsets):
        owner = ring_owner(lax.axis_index("seq"), offset, devices)
        product = mm(refs[i][...], cols_ref[owner, low:high, :], TN)
        total = product if total is None else total + product
    refs[-1][...] = total


def last_kernel(offset, devices, cols_ref, low_ref, high_ref, total_ref, after_ref, out_hbm, *refs):
    del after_ref
    held, result, sems = refs
    half = low_ref.shape[0]
    held[:half] = low_ref[...]
    held[half:] = high_ref[...]
    cols = cols_ref[ring_owner(lax.axis_index("seq"), offset, devices)]
    pieces = sems.shape[0]
    block = held.shape[1] // pieces
    copies = []
    for i in range(pieces):
        at = pl.ds(i * block, block)
        result[at, :] = total_ref[at, :] + mm(held[:, at], cols, TN)
        copies.append(pltpu.make_async_copy(result.at[at], out_hbm.at[at], sems.at[i]))
        copies[-1].start()
    for copy in copies:
        copy.wait()


def body(queries, keys, values, level_weights, out_proj, out_grad):
    rows, heads_dev, head_dim = queries.shape
    width = heads_dev * head_dim
    devices = lax.axis_size("seq")
    seq_bits = devices.bit_length() - 1
    heads = lax.axis_size("head")
    head_bits = heads.bit_length() - 1
    columns_dev = out_proj.shape[1] // devices

    head_state = like((heads_dev, head_dim, head_dim), BF)
    pinned_state = pltpu.VMEM((heads_dev, head_dim, head_dim), BF)
    per_head = pltpu.VMEM((heads_dev, rows, head_dim), BF)
    per_head_f32 = pltpu.VMEM((heads_dev, rows, head_dim), F32)
    flops_head = 2 * heads_dev * rows * rows * head_dim
    moved_head = 2 * rows * width
    top = seq_bits - 1

    half = rows // 2
    own_state, kh, vh, own_grad, own_low = pl.pallas_call(
        state_kernel,
        out_shape=(head_state, per_head, per_head, like(out_grad.shape, BF), like((half, width), BF)),
        in_specs=[ANY] * 3,
        out_specs=(VMEM,) * 5,
        scratch_shapes=[
            pltpu.VMEM(keys.shape, F32),
            pltpu.VMEM(keys.shape, F32),
            pltpu.SemaphoreType.DMA((4,)),
        ],
        compiler_params=PARAMS,
        cost_estimate=cost(flops_head, 7 * moved_head),
    )(hbm(keys), hbm(values), hbm(out_grad))

    def to_group(block, i):
        return lax.ppermute(block, "head", [(at, at ^ i) for at in range(heads)])

    def every_group(block):
        blocks = {0: block}
        for digit in reversed(range(head_bits)):
            for i in sorted(blocks):
                blocks[i ^ 1 << digit] = to_group(blocks[i], 1 << digit)
        return [blocks[i] for i in range(heads)]

    probs_t, att_local, qh, qw, lam, w = pl.pallas_call(
        local_kernel,
        out_shape=(
            pltpu.VMEM((heads_dev, rows, rows), BF),
            per_head_f32,
            per_head,
            pltpu.VMEM((seq_bits, heads_dev, rows, head_dim), BF),
            pltpu.VMEM(level_weights.shape, F32),
            pltpu.VMEM(out_proj.shape, BF),
        ),
        in_specs=[ANY, VMEM, VMEM, ANY, ANY],
        out_specs=(VMEM,) * 6,
        scratch_shapes=[
            pltpu.VMEM(queries.shape, F32),
            pltpu.VMEM((rows, rows), F32),
            pltpu.SemaphoreType.DMA((10,)),
        ],
        compiler_params=PARAMS,
        cost_estimate=cost(2 * flops_head, 12 * moved_head),
    )(hbm(queries), kh, vh, hbm(level_weights), hbm(out_proj))

    def relayed(block):
        return pl.pallas_call(
            relay_kernel,
            out_shape=like(block.shape, block.dtype),
            in_specs=[VMEM, ANY],
            out_specs=VMEM,
            compiler_params=PARAMS,
            cost_estimate=cost(0, 2 * moved_head),
        )(block, qw)

    grad_blocks = {0: own_grad}
    for digit in reversed(range(head_bits)):
        for i in sorted(grad_blocks):
            block = relayed(grad_blocks[i]) if i else own_grad
            grad_blocks[i ^ 1 << digit] = to_group(block, 1 << digit)
    grad_blocks = [grad_blocks[i] for i in range(heads)]

    per = devices // heads
    def turn_route(shift):
        return [
            (
                (high * per + low) * heads + (group_at ^ shift),
                (group_at * per + low) * heads + turned_group(high, group_at, head_bits),
            )
            for high in range(heads)
            for low in range(per)
            for group_at in range(heads)
        ]

    axes, far = ("seq", "head"), heads // 2
    turned = [
        lax.ppermute(own_low, axes, turn_route(0)),
        lax.ppermute(grad_blocks[far][half:], axes, turn_route(far)),
    ]
    partner_states = []
    running, arrived = own_state, None
    for digit in range(top):
        if arrived is not None:
            running = pl.pallas_call(
                running_kernel,
                out_shape=head_state,
                in_specs=[VMEM] * 2 + [ANY],
                out_specs=VMEM,
                compiler_params=PARAMS,
                cost_estimate=cost(0, 3 * moved_head),
            )(running, arrived, qw)
        arrived = across(running, "seq", digit)
        partner_states.append(arrived)

    gt, *grad_sums = pl.pallas_call(
        functools.partial(cotangent_kernel, heads, seq_bits),
        out_shape=(pltpu.VMEM((width, rows), BF),) + (pinned_state,) * seq_bits,
        in_specs=[VMEM] * (heads + 2) + [ANY],
        out_specs=(VMEM,) * (1 + seq_bits),
        compiler_params=PARAMS,
        cost_estimate=cost(2 * rows * width * out_proj.shape[1], 2 * width * out_proj.shape[1]),
    )(*grad_blocks, w, qw, running)

    meeting = pl.pallas_call(
        functools.partial(meet_kernel, top)
        if arrived is not None
        else lambda grad_ref, running_ref, out_ref: meet_kernel(
            top, grad_ref, running_ref, None, out_ref
        ),
        out_shape=head_state,
        in_specs=[VMEM] * (2 if arrived is None else 3),
        out_specs=VMEM,
        compiler_params=PARAMS,
        cost_estimate=cost(0, 4 * moved_head),
    )(grad_sums[top], running, *([] if arrived is None else [arrived]))
    landed = [across(meeting, "seq", top)]
    partner_states.append(landed[0])

    chunks = pl.pallas_call(
        chunk_kernel,
        out_shape=(like((rows, columns_dev), BF),) * per,
        in_specs=[VMEM, VMEM, ANY],
        out_specs=(VMEM,) * per,
        compiler_params=PARAMS,
        cost_estimate=cost(0, 2 * moved_head),
    )(*turned, meeting)
    own_chunks = chunks
    chunks = [chunks[0]] + [
        lax.ppermute(chunks[r], "seq", [(at, at ^ r) for at in range(devices)])
        for r in range(1, per)
    ]
    stacked = pl.pallas_call(
        stack_kernel,
        out_shape=like((per, rows, columns_dev), BF),
        in_specs=[ANY] + [VMEM] * per,
        out_specs=VMEM,
        compiler_params=PARAMS,
        cost_estimate=cost(0, 2 * moved_head),
    )(meeting, *chunks)
    column_blocks = every_group(stacked)

    grad_columns = pl.pallas_call(
        functools.partial(columns_kernel, heads),
        out_shape=pltpu.VMEM((devices, rows, columns_dev), BF),
        in_specs=[VMEM] * heads,
        out_specs=VMEM,
        compiler_params=PARAMS,
        cost_estimate=cost(0, 8 * moved_head),
    )(*column_blocks)

    query_local, key_local, value_local = pl.pallas_call(
        functools.partial(local_grad_kernel, top),
        out_shape=(per_head_f32,) * 3,
        in_specs=[VMEM] * 6 + [ANY] + [VMEM] * top,
        out_specs=(VMEM,) * 3,
        compiler_params=PARAMS,
        cost_estimate=cost((4 + top) * flops_head, 14 * moved_head),
    )(gt, qh, kh, vh, probs_t, lam, meeting, *partner_states[:top])

    attended = pl.pallas_call(
        functools.partial(attended_kernel, seq_bits),
        out_shape=like((rows, width), BF),
        in_specs=[VMEM] * (2 + seq_bits) + [ANY] * 2,
        out_specs=VMEM,
        compiler_params=PARAMS,
        cost_estimate=cost(seq_bits * flops_head, 8 * moved_head),
    )(att_local, qw, *partner_states, key_local, own_chunks[-1])

    first_pending = attended
    for digit in reversed(range(top)):
        outgoing = pl.pallas_call(
            functools.partial(pending_kernel, top),
            out_shape=head_state,
            in_specs=[VMEM, ANY] + [VMEM] * len(landed),
            out_specs=VMEM,
            compiler_params=PARAMS,
            cost_estimate=cost(0, 4 * moved_head),
        )(grad_sums[digit], attended, *landed)
        if len(landed) == 1:
            first_pending = outgoing
        landed.append(across(outgoing, "seq", digit))

    query_grad = pl.pallas_call(
        functools.partial(query_grad_kernel, top),
        out_shape=like((rows, heads_dev, head_dim), F32),
        in_specs=[VMEM] * 4 + [ANY],
        out_specs=VMEM,
        compiler_params=PARAMS,
        cost_estimate=cost(flops_head, 6 * moved_head),
    )(gt, lam, query_local, partner_states[top], attended)

    def share(offsets, kind, *after):
        return pl.pallas_call(
            functools.partial(share_kernel, offsets),
            out_shape=like((len(offsets), rows, width), kind),
            in_specs=[VMEM] * 2 + [ANY] * len(after),
            out_specs=VMEM,
            compiler_params=PARAMS,
            cost_estimate=cost(
                2 * rows * width * len(offsets) * width, 2 * width * len(offsets) * width
            ),
        )(attended, w, *after)

    send = share(range(1, heads, 2), BF, stacked)
    kept = share(range(0, heads, 2), F32, first_pending, hbm(query_grad))
    for digit in range(head_bits):
        kept = kept + to_group(send, 1 << digit).astype(F32)
        if digit < head_bits - 1:
            send, kept = kept[1::2].astype(BF), kept[0::2]
    mixed = kept[0].astype(BF)

    key_grad, value_grad = pl.pallas_call(
        functools.partial(later_grad_kernel, top),
        out_shape=(like((rows, heads_dev, head_dim), F32),) * 2,
        in_specs=[VMEM] * 4 + [ANY] + [VMEM] * seq_bits,
        out_specs=(VMEM,) * 2,
        compiler_params=PARAMS,
        cost_estimate=cost(2 * flops_head, 11 * moved_head),
    )(kh, vh, key_local, value_local, attended, *landed)

    ring = list(range(0, devices, 2)) + list(range(devices - 1, 0, -2))
    forward = [(ring[i], ring[(i + 1) % devices]) for i in range(devices)]
    backward = [(b, a) for a, b in forward]

    def accumulate(total, blocks, offsets):
        operands = blocks if total is None else blocks + [total]
        return pl.pallas_call(
            functools.partial(proj_kernel, offsets, devices, total is None),
            out_shape=pltpu.VMEM((width, columns_dev), F32),
            in_specs=[VMEM, ANY] + [VMEM] * len(operands),
            out_specs=VMEM,
            compiler_params=PARAMS,
            cost_estimate=cost(
                2 * len(blocks) * rows * width * columns_dev, 4 * width * columns_dev
            ),
        )(grad_columns, hbm(key_grad), *operands)

    blocks, offsets = [attended], [(0, 0, rows)]
    ahead = behind = attended
    steps, total = devices // 2, None
    for step in range(1, steps):
        ahead = lax.ppermute(ahead, "seq", forward)
        behind = lax.ppermute(behind, "seq", backward)
        blocks += [ahead, behind]
        offsets += [(-step, 0, rows), (step, 0, rows)]
        if step == steps - 2:
            total = accumulate(None, blocks, offsets)
            blocks, offsets = [], []
    if blocks:
        total = accumulate(total, blocks, offsets)
    last = [
        lax.ppermute(ahead[:half], "seq", forward),
        lax.ppermute(behind[half:], "seq", backward),
    ]
    proj_grad = pl.pallas_call(
        functools.partial(last_kernel, steps, devices),
        out_shape=like((width, columns_dev), F32),
        in_specs=[VMEM] * 4 + [ANY],
        out_specs=ANY,
        scratch_shapes=[
            pltpu.VMEM((rows, width), BF),
            pltpu.VMEM((width, columns_dev), F32),
            pltpu.SemaphoreType.DMA((4,)),
        ],
        compiler_params=PARAMS,
        cost_estimate=cost(2 * rows * width * columns_dev, 8 * width * columns_dev),
    )(grad_columns, *last, total, hbm(key_grad))
    return (mixed, query_grad, key_grad, value_grad, proj_grad)


def solution(mesh):
    placed = (
        P("seq", "head", None),
        P("seq", "head", None),
        P("seq", "head", None),
        P(None, "head", "seq"),
        P("head", None),
        P("seq", "head"),
    )
    return jax.shard_map(
        body,
        mesh=mesh,
        in_specs=placed,
        out_specs=(
            P("seq", "head"),
            P("seq", "head", None),
            P("seq", "head", None),
            P("seq", "head", None),
            P("head", "seq"),
        ),
        check_vma=False,
    )
```

```python
import functools

import jax
import jax.numpy as jnp
from jax import lax
from jax.experimental import pallas as pl
from jax.experimental.pallas import tpu as pltpu
from jax.sharding import PartitionSpec as P

CH = 64
BF = jnp.bfloat16
F32 = jnp.float32
NN = (((1,), (0,)), ((), ()))
NT = (((1,), (1,)), ((), ()))
TN = (((0,), (0,)), ((), ()))
TT = (((0,), (1,)), ((), ()))
VMEM = pl.BlockSpec(memory_space=pltpu.VMEM)
ANY = pl.BlockSpec(memory_space=pl.ANY)
PARAMS = pltpu.CompilerParams(vmem_limit_bytes=14 * 2**20)


def mm(a, b, dims):
    return lax.dot_general(a, b, dims, preferred_element_type=F32)


def cost(flops, moved):
    return pl.CostEstimate(flops=flops, bytes_accessed=moved, transcendentals=0)


def like(shape, dtype):
    return jax.ShapeDtypeStruct(shape, dtype)


def across(block, axis, stride, up_only=False, down_only=False):
    count = lax.axis_size(axis)
    route = []
    for low in range(count):
        high = low | 1 << stride
        if high != low and high < count:
            if not down_only:
                route.append((low, high))
            if not up_only:
                route.append((high, low))
    return lax.ppermute(block, axis, route)


def hbm(array):
    return pltpu.with_memory_space_constraint(array, pltpu.HBM)


def state_kernel(k_hbm, v_hbm, grad_hbm, *refs):
    s_ref, kh_ref, vh_ref, grad_ref, low_ref, k_ref, v_ref, sems = refs
    pieces = (sems.shape[0] - 2) // 2
    share = k_ref.shape[0] // pieces
    copies = []
    for i in range(pieces):
        at = pl.ds(i * share, share)
        copies.append(pltpu.make_async_copy(k_hbm.at[at], k_ref.at[at], sems.at[2 + 2 * i]))
        copies.append(pltpu.make_async_copy(v_hbm.at[at], v_ref.at[at], sems.at[3 + 2 * i]))
    later = [
        pltpu.make_async_copy(grad_hbm, grad_ref, sems.at[0]),
        pltpu.make_async_copy(grad_hbm.at[pl.ds(0, low_ref.shape[0])], low_ref, sems.at[1]),
    ]
    for copy in copies + later:
        copy.start()
    for copy in copies:
        copy.wait()
    for h in range(k_ref.shape[1]):
        k = k_ref[:, h, :].astype(BF)
        v = v_ref[:, h, :].astype(BF)
        kh_ref[h] = k
        vh_ref[h] = v
        s_ref[h] = mm(k, v, TN).astype(BF)
    for copy in later:
        copy.wait()


def weight_of(lam_ref, h, rows):
    local_bits = (rows // CH).bit_length() - 1
    s = lax.broadcasted_iota(jnp.int32, (rows, rows), 0)
    t = lax.broadcasted_iota(jnp.int32, (rows, rows), 1)
    differ = (s // CH) ^ (t // CH)
    weight = jnp.broadcast_to(lam_ref[0, h : h + 1, :], (rows, rows))
    for digit in range(local_bits):
        weight = jnp.where(differ >= 1 << digit, lam_ref[1 + digit, h : h + 1, :], weight)
    return jnp.where(s <= t, weight, 0.0)


def upper_weight(lam_ref, b, h, rows):
    local_bits = (rows // CH).bit_length() - 1
    upper = (lax.axis_index("seq") >> b & 1).astype(F32)
    return lam_ref[1 + local_bits + b, h : h + 1, :] * upper


def local_kernel(q_hbm, kh_ref, vh_ref, lam_hbm, w_hbm, *refs):
    pt_ref, att_ref, qh_ref, qw_ref, lam_ref, w_ref, q_ref, lam_rows, sems = refs
    pieces = sems.shape[0] - 2
    share = w_hbm.shape[0] // pieces
    copies = [
        pltpu.make_async_copy(q_hbm, q_ref, sems.at[0]),
        pltpu.make_async_copy(lam_hbm, lam_ref, sems.at[1]),
    ]
    for i in range(pieces):
        piece = pl.ds(i * share, share)
        copies.append(pltpu.make_async_copy(w_hbm.at[piece], w_ref.at[piece], sems.at[2 + i]))
    for copy in copies:
        copy.start()
    for copy in copies[:2]:
        copy.wait()
    rows, heads_dev, _ = q_ref.shape
    bits = qw_ref.shape[0]
    lam_rows[...] = jnp.zeros_like(lam_rows)
    for b in range(bits):
        for h in range(heads_dev):
            at = b * heads_dev + h
            lam_rows[at : at + 1, :] = upper_weight(lam_ref, b, h, rows)
    lam_columns = lam_rows[...].T
    for h in range(heads_dev):
        q32 = q_ref[:, h, :]
        q = q32.astype(BF)
        qh_ref[h] = q
        for b in range(bits):
            at = b * heads_dev + h
            qw_ref[b, h] = (q32 * lam_columns[:, at : at + 1]).astype(BF)
        pt = (mm(kh_ref[h], q, NT) * weight_of(lam_ref, h, rows)).astype(BF)
        pt_ref[h] = pt
        att_ref[h] = mm(pt, vh_ref[h], TN)
    for copy in copies[2:]:
        copy.wait()


def attended_kernel(bits, att_ref, qw_ref, *refs):
    states, out_ref = refs[:bits], refs[-1]
    heads_dev, _, head_dim = att_ref.shape
    for h in range(heads_dev):
        total = att_ref[h]
        for b in range(bits):
            total = total + mm(qw_ref[b, h], states[b][h], NN)
        out_ref[:, h * head_dim : (h + 1) * head_dim] = total.astype(BF)


def cotangent_kernel(blocks, bits, *refs):
    parts, (w_ref, qw_ref, _, gt_ref), sums = (
        refs[:blocks],
        refs[blocks : blocks + 4],
        refs[blocks + 4 :],
    )
    deep = parts[0].shape[1]
    _, heads_dev, _, head_dim = qw_ref.shape
    total = None
    for i in range(blocks):
        column = pl.multiple_of((lax.axis_index("head") ^ i) * deep, deep)
        product = mm(w_ref[:, pl.ds(column, deep)], parts[i][...], NT)
        total = product if total is None else total + product
    for h in range(heads_dev):
        gt = total[h * head_dim : (h + 1) * head_dim].astype(BF)
        gt_ref[h * head_dim : (h + 1) * head_dim, :] = gt
        for b in range(bits):
            sums[b][h] = mm(gt, qw_ref[b, h], NN).astype(BF)


def running_kernel(running_ref, arrived_ref, *refs):
    refs[-1][...] = (running_ref[...].astype(F32) + arrived_ref[...].astype(F32)).astype(BF)


def meet_kernel(top, grad_ref, running_ref, arrived_ref, out_ref):
    upper = (lax.axis_index("seq") >> top & 1) == 1
    running = running_ref[...].astype(F32)
    if arrived_ref is not None:
        running = running + arrived_ref[...].astype(F32)
    out_ref[...] = jnp.where(upper, grad_ref[...], running.astype(BF))


def landed_sum(top, landed):
    upper = (lax.axis_index("seq") >> top & 1) == 1
    total = jnp.where(upper, 0.0, landed[0].astype(F32))
    for block in landed[1:]:
        total = total + block.astype(F32)
    return total


def pending_kernel(top, own_ref, after_ref, *refs):
    del after_ref
    landed, out_ref = [ref[...] for ref in refs[:-1]], refs[-1]
    out_ref[...] = (own_ref[...].astype(F32) + landed_sum(top, landed)).astype(BF)


def turned_group(high, group, bits):
    turned = high >> 1 | (high & 1) << bits - 1
    return turned ^ ((group >> bits - 1 ^ group) & 1) << bits - 1


def turned_high(turned, group, bits):
    turned = turned ^ ((group >> bits - 1 ^ group) & 1) << bits - 1
    return (turned << 1 & (1 << bits) - 1) | turned >> bits - 1


def relay_kernel(block_ref, after_ref, out_ref):
    del after_ref
    out_ref[...] = block_ref[...]


def chunk_kernel(low_ref, high_ref, after_ref, *outs):
    del after_ref
    half = low_ref.shape[0]
    columns = outs[0].shape[1]
    low = lax.axis_index("seq") % len(outs)
    for r, out in enumerate(outs):
        at = pl.ds(pl.multiple_of((low ^ r) * columns, columns), columns)
        out[:half] = low_ref[:, at]
        out[half:] = high_ref[:, at]


def stack_kernel(after_ref, *refs):
    del after_ref
    for r, ref in enumerate(refs[:-1]):
        refs[-1][r] = ref[...]


def columns_kernel(blocks, *refs):
    parts, out_ref = refs[:blocks], refs[blocks]
    per = parts[0].shape[0]
    bits = blocks.bit_length() - 1
    low = lax.axis_index("seq") % per
    for i in range(blocks):
        high = turned_high(lax.axis_index("head") ^ i, lax.axis_index("seq") // per, bits)
        for r in range(per):
            out_ref[high * per + (low ^ r)] = parts[i][r]


def local_grad_kernel(
    bits, gt_ref, qh_ref, kh_ref, vh_ref, pt_ref, lam_ref, after_ref, *refs
):
    del after_ref
    states, (dq_ref, dk_ref, dv_ref) = refs[:bits], refs[bits:]
    heads_dev, rows, head_dim = qh_ref.shape
    for h in range(heads_dev):
        gt = gt_ref[h * head_dim : (h + 1) * head_dim, :]
        g32 = gt.astype(F32)
        dpt = (mm(vh_ref[h], gt, NN) * weight_of(lam_ref, h, rows)).astype(BF)
        dk_ref[h] = mm(dpt, qh_ref[h], NN)
        dv_ref[h] = mm(pt_ref[h], gt, NT)
        dq = mm(dpt, kh_ref[h], TN)
        for b in range(bits):
            gw = (g32 * upper_weight(lam_ref, b, h, rows)).astype(BF)
            dq = dq + mm(gw, states[b][h], TT)
        dq_ref[h] = dq


def query_grad_kernel(top, gt_ref, lam_ref, dql_ref, state_ref, after_ref, dq_ref):
    del after_ref
    heads_dev, rows, head_dim = dql_ref.shape
    for h in range(heads_dev):
        g32 = gt_ref[h * head_dim : (h + 1) * head_dim, :].astype(F32)
        gw = (g32 * upper_weight(lam_ref, top, h, rows)).astype(BF)
        dq_ref[:, h, :] = dql_ref[h] + mm(gw, state_ref[h], TT)


def later_grad_kernel(top, kh_ref, vh_ref, dkl_ref, dvl_ref, after_ref, *refs):
    del after_ref
    landed, (dk_ref, dv_ref) = refs[:-2], refs[-2:]
    for h in range(kh_ref.shape[0]):
        late = landed_sum(top, [ref[h] for ref in landed]).astype(BF)
        dk_ref[:, h, :] = dkl_ref[h] + mm(vh_ref[h], late, NN)
        dv_ref[:, h, :] = dvl_ref[h] + mm(kh_ref[h], late, NT)


def share_kernel(offsets, att_ref, w_ref, after_ref, out_ref):
    del after_ref
    width = out_ref.shape[2]
    for n, i in enumerate(offsets):
        column = pl.multiple_of((lax.axis_index("head") ^ i) * width, width)
        out_ref[n] = mm(att_ref[...], w_ref[:, pl.ds(column, width)], NN).astype(out_ref.dtype)


def ring_owner(place, offset, devices):
    at = jnp.where(place % 2 == 0, place // 2, devices - 1 - place // 2)
    at = (at + offset + devices) % devices
    return jnp.where(at < devices // 2, 2 * at, 2 * (devices - 1 - at) + 1)


def proj_kernel(offsets, devices, first, cols_ref, after_ref, *refs):
    del after_ref
    total = None if first else refs[len(offsets)][...]
    for i, (offset, low, high) in enumerate(offsets):
        owner = ring_owner(lax.axis_index("seq"), offset, devices)
        product = mm(refs[i][...], cols_ref[owner, low:high, :], TN)
        total = product if total is None else total + product
    refs[-1][...] = total


def last_kernel(offset, devices, cols_ref, low_ref, high_ref, total_ref, after_ref, out_hbm, *refs):
    del after_ref
    held, result, sems = refs
    half = low_ref.shape[0]
    held[:half] = low_ref[...]
    held[half:] = high_ref[...]
    cols = cols_ref[ring_owner(lax.axis_index("seq"), offset, devices)]
    pieces = sems.shape[0]
    block = held.shape[1] // pieces
    copies = []
    for i in range(pieces):
        at = pl.ds(i * block, block)
        result[at, :] = total_ref[at, :] + mm(held[:, at], cols, TN)
        copies.append(pltpu.make_async_copy(result.at[at], out_hbm.at[at], sems.at[i]))
        copies[-1].start()
    for copy in copies:
        copy.wait()


def body(queries, keys, values, level_weights, out_proj, out_grad):
    rows, heads_dev, head_dim = queries.shape
    width = heads_dev * head_dim
    devices = lax.axis_size("seq")
    seq_bits = devices.bit_length() - 1
    heads = lax.axis_size("head")
    head_bits = heads.bit_length() - 1
    columns_dev = out_proj.shape[1] // devices

    head_state = like((heads_dev, head_dim, head_dim), BF)
    pinned_state = pltpu.VMEM((heads_dev, head_dim, head_dim), BF)
    per_head = pltpu.VMEM((heads_dev, rows, head_dim), BF)
    per_head_f32 = pltpu.VMEM((heads_dev, rows, head_dim), F32)
    flops_head = 2 * heads_dev * rows * rows * head_dim
    moved_head = 2 * rows * width
    top = seq_bits - 1

    half = rows // 2
    own_state, kh, vh, own_grad, own_low = pl.pallas_call(
        state_kernel,
        out_shape=(head_state, per_head, per_head, like(out_grad.shape, BF), like((half, width), BF)),
        in_specs=[ANY] * 3,
        out_specs=(VMEM,) * 5,
        scratch_shapes=[
            pltpu.VMEM(keys.shape, F32),
            pltpu.VMEM(keys.shape, F32),
            pltpu.SemaphoreType.DMA((10,)),
        ],
        compiler_params=PARAMS,
        cost_estimate=cost(flops_head, 7 * moved_head),
    )(hbm(keys), hbm(values), hbm(out_grad))

    def to_group(block, i):
        return lax.ppermute(block, "head", [(at, at ^ i) for at in range(heads)])

    def every_group(block):
        blocks = {0: block}
        for digit in reversed(range(head_bits)):
            for i in sorted(blocks):
                blocks[i ^ 1 << digit] = to_group(blocks[i], 1 << digit)
        return [blocks[i] for i in range(heads)]

    probs_t, att_local, qh, qw, lam, w = pl.pallas_call(
        local_kernel,
        out_shape=(
            pltpu.VMEM((heads_dev, rows, rows), BF),
            per_head_f32,
            per_head,
            pltpu.VMEM((seq_bits, heads_dev, rows, head_dim), BF),
            pltpu.VMEM(level_weights.shape, F32),
            pltpu.VMEM(out_proj.shape, BF),
        ),
        in_specs=[ANY, VMEM, VMEM, ANY, ANY],
        out_specs=(VMEM,) * 6,
        scratch_shapes=[
            pltpu.VMEM(queries.shape, F32),
            pltpu.VMEM((rows, rows), F32),
            pltpu.SemaphoreType.DMA((10,)),
        ],
        compiler_params=PARAMS,
        cost_estimate=cost(2 * flops_head, 12 * moved_head),
    )(hbm(queries), kh, vh, hbm(level_weights), hbm(out_proj))

    def relayed(block):
        return pl.pallas_call(
            relay_kernel,
            out_shape=like(block.shape, block.dtype),
            in_specs=[VMEM, ANY],
            out_specs=VMEM,
            compiler_params=PARAMS,
            cost_estimate=cost(0, 2 * moved_head),
        )(block, qw)

    grad_blocks = {0: own_grad}
    for digit in reversed(range(head_bits)):
        for i in sorted(grad_blocks):
            block = relayed(grad_blocks[i]) if i else own_grad
            grad_blocks[i ^ 1 << digit] = to_group(block, 1 << digit)
    grad_blocks = [grad_blocks[i] for i in range(heads)]

    per = devices // heads
    def turn_route(shift):
        return [
            (
                (high * per + low) * heads + (group_at ^ shift),
                (group_at * per + low) * heads + turned_group(high, group_at, head_bits),
            )
            for high in range(heads)
            for low in range(per)
            for group_at in range(heads)
        ]

    axes, far = ("seq", "head"), heads // 2
    turned = [
        lax.ppermute(own_low, axes, turn_route(0)),
        lax.ppermute(grad_blocks[far][half:], axes, turn_route(far)),
    ]
    partner_states = []
    running, arrived = own_state, None
    for digit in range(top):
        if arrived is not None:
            running = pl.pallas_call(
                running_kernel,
                out_shape=head_state,
                in_specs=[VMEM] * 2 + [ANY],
                out_specs=VMEM,
                compiler_params=PARAMS,
                cost_estimate=cost(0, 3 * moved_head),
            )(running, arrived, qw)
        arrived = across(running, "seq", digit)
        partner_states.append(arrived)

    gt, *grad_sums = pl.pallas_call(
        functools.partial(cotangent_kernel, heads, seq_bits),
        out_shape=(pltpu.VMEM((width, rows), BF),) + (pinned_state,) * seq_bits,
        in_specs=[VMEM] * (heads + 2) + [ANY],
        out_specs=(VMEM,) * (1 + seq_bits),
        compiler_params=PARAMS,
        cost_estimate=cost(2 * rows * width * out_proj.shape[1], 2 * width * out_proj.shape[1]),
    )(*grad_blocks, w, qw, running)

    meeting = pl.pallas_call(
        functools.partial(meet_kernel, top)
        if arrived is not None
        else lambda grad_ref, running_ref, out_ref: meet_kernel(
            top, grad_ref, running_ref, None, out_ref
        ),
        out_shape=head_state,
        in_specs=[VMEM] * (2 if arrived is None else 3),
        out_specs=VMEM,
        compiler_params=PARAMS,
        cost_estimate=cost(0, 4 * moved_head),
    )(grad_sums[top], running, *([] if arrived is None else [arrived]))
    landed = [across(meeting, "seq", top)]
    partner_states.append(landed[0])

    chunks = pl.pallas_call(
        chunk_kernel,
        out_shape=(like((rows, columns_dev), BF),) * per,
        in_specs=[VMEM, VMEM, ANY],
        out_specs=(VMEM,) * per,
        compiler_params=PARAMS,
        cost_estimate=cost(0, 2 * moved_head),
    )(*turned, meeting)
    own_chunks = chunks
    chunks = [chunks[0]] + [
        lax.ppermute(chunks[r], "seq", [(at, at ^ r) for at in range(devices)])
        for r in range(1, per)
    ]
    stacked = pl.pallas_call(
        stack_kernel,
        out_shape=like((per, rows, columns_dev), BF),
        in_specs=[ANY] + [VMEM] * per,
        out_specs=VMEM,
        compiler_params=PARAMS,
        cost_estimate=cost(0, 2 * moved_head),
    )(meeting, *chunks)
    column_blocks = every_group(stacked)

    grad_columns = pl.pallas_call(
        functools.partial(columns_kernel, heads),
        out_shape=pltpu.VMEM((devices, rows, columns_dev), BF),
        in_specs=[VMEM] * heads,
        out_specs=VMEM,
        compiler_params=PARAMS,
        cost_estimate=cost(0, 8 * moved_head),
    )(*column_blocks)

    query_local, key_local, value_local = pl.pallas_call(
        functools.partial(local_grad_kernel, top),
        out_shape=(per_head_f32,) * 3,
        in_specs=[VMEM] * 6 + [ANY] + [VMEM] * top,
        out_specs=(VMEM,) * 3,
        compiler_params=PARAMS,
        cost_estimate=cost((4 + top) * flops_head, 14 * moved_head),
    )(gt, qh, kh, vh, probs_t, lam, meeting, *partner_states[:top])

    attended = pl.pallas_call(
        functools.partial(attended_kernel, seq_bits),
        out_shape=like((rows, width), BF),
        in_specs=[VMEM] * (2 + seq_bits) + [ANY] * 2,
        out_specs=VMEM,
        compiler_params=PARAMS,
        cost_estimate=cost(seq_bits * flops_head, 8 * moved_head),
    )(att_local, qw, *partner_states, key_local, own_chunks[-1])

    first_pending = attended
    for digit in reversed(range(top)):
        outgoing = pl.pallas_call(
            functools.partial(pending_kernel, top),
            out_shape=head_state,
            in_specs=[VMEM, ANY] + [VMEM] * len(landed),
            out_specs=VMEM,
            compiler_params=PARAMS,
            cost_estimate=cost(0, 4 * moved_head),
        )(grad_sums[digit], attended, *landed)
        if len(landed) == 1:
            first_pending = outgoing
        landed.append(across(outgoing, "seq", digit))

    query_grad = pl.pallas_call(
        functools.partial(query_grad_kernel, top),
        out_shape=like((rows, heads_dev, head_dim), F32),
        in_specs=[VMEM] * 4 + [ANY],
        out_specs=VMEM,
        compiler_params=PARAMS,
        cost_estimate=cost(flops_head, 6 * moved_head),
    )(gt, lam, query_local, partner_states[top], attended)

    def share(offsets, kind, after):
        return pl.pallas_call(
            functools.partial(share_kernel, offsets),
            out_shape=like((len(offsets), rows, width), kind),
            in_specs=[VMEM, VMEM, ANY],
            out_specs=VMEM,
            compiler_params=PARAMS,
            cost_estimate=cost(
                2 * rows * width * len(offsets) * width, 2 * width * len(offsets) * width
            ),
        )(attended, w, after)

    send = share(range(1, heads, 2), BF, stacked)
    kept = share(range(0, heads, 2), F32, first_pending)
    for digit in range(head_bits):
        kept = kept + to_group(send, 1 << digit).astype(F32)
        if digit < head_bits - 1:
            send, kept = kept[1::2].astype(BF), kept[0::2]
    mixed = kept[0].astype(BF)

    key_grad, value_grad = pl.pallas_call(
        functools.partial(later_grad_kernel, top),
        out_shape=(like((rows, heads_dev, head_dim), F32),) * 2,
        in_specs=[VMEM] * 4 + [ANY] + [VMEM] * seq_bits,
        out_specs=(VMEM,) * 2,
        compiler_params=PARAMS,
        cost_estimate=cost(2 * flops_head, 11 * moved_head),
    )(kh, vh, key_local, value_local, attended, *landed)

    ring = list(range(0, devices, 2)) + list(range(devices - 1, 0, -2))
    forward = [(ring[i], ring[(i + 1) % devices]) for i in range(devices)]
    backward = [(b, a) for a, b in forward]

    def accumulate(total, blocks, offsets):
        operands = blocks if total is None else blocks + [total]
        return pl.pallas_call(
            functools.partial(proj_kernel, offsets, devices, total is None),
            out_shape=pltpu.VMEM((width, columns_dev), F32),
            in_specs=[VMEM, ANY] + [VMEM] * len(operands),
            out_specs=VMEM,
            compiler_params=PARAMS,
            cost_estimate=cost(
                2 * len(blocks) * rows * width * columns_dev, 4 * width * columns_dev
            ),
        )(grad_columns, hbm(key_grad), *operands)

    blocks, offsets = [attended], [(0, 0, rows)]
    ahead = behind = attended
    steps, total = devices // 2, None
    for step in range(1, steps):
        ahead = lax.ppermute(ahead, "seq", forward)
        behind = lax.ppermute(behind, "seq", backward)
        blocks += [ahead, behind]
        offsets += [(-step, 0, rows), (step, 0, rows)]
        if step == steps - 2:
            total = accumulate(None, blocks, offsets)
            blocks, offsets = [], []
    if blocks:
        total = accumulate(total, blocks, offsets)
    last = [
        lax.ppermute(ahead[:half], "seq", forward),
        lax.ppermute(behind[half:], "seq", backward),
    ]
    proj_grad = pl.pallas_call(
        functools.partial(last_kernel, steps, devices),
        out_shape=like((width, columns_dev), F32),
        in_specs=[VMEM] * 4 + [ANY],
        out_specs=ANY,
        scratch_shapes=[
            pltpu.VMEM((rows, width), BF),
            pltpu.VMEM((width, columns_dev), F32),
            pltpu.SemaphoreType.DMA((4,)),
        ],
        compiler_params=PARAMS,
        cost_estimate=cost(2 * rows * width * columns_dev, 8 * width * columns_dev),
    )(grad_columns, *last, total, hbm(key_grad))
    return (mixed, query_grad, key_grad, value_grad, proj_grad)


def solution(mesh):
    placed = (
        P("seq", "head", None),
        P("seq", "head", None),
        P("seq", "head", None),
        P(None, "head", "seq"),
        P("head", None),
        P("seq", "head"),
    )
    return jax.shard_map(
        body,
        mesh=mesh,
        in_specs=placed,
        out_specs=(
            P("seq", "head"),
            P("seq", "head", None),
            P("seq", "head", None),
            P("seq", "head", None),
            P("head", "seq"),
        ),
        check_vma=False,
    )
```

```python
import functools

import jax
import jax.numpy as jnp
from jax import lax
from jax.experimental import pallas as pl
from jax.experimental.pallas import tpu as pltpu
from jax.sharding import PartitionSpec as P

CH = 64
BF = jnp.bfloat16
F32 = jnp.float32
NN = (((1,), (0,)), ((), ()))
NT = (((1,), (1,)), ((), ()))
TN = (((0,), (0,)), ((), ()))
TT = (((0,), (1,)), ((), ()))
VMEM = pl.BlockSpec(memory_space=pltpu.VMEM)
ANY = pl.BlockSpec(memory_space=pl.ANY)
PARAMS = pltpu.CompilerParams(vmem_limit_bytes=14 * 2**20)


def mm(a, b, dims):
    return lax.dot_general(a, b, dims, preferred_element_type=F32)


def cost(flops, moved):
    return pl.CostEstimate(flops=flops, bytes_accessed=moved, transcendentals=0)


def like(shape, dtype):
    return jax.ShapeDtypeStruct(shape, dtype)


def across(block, axis, stride, up_only=False, down_only=False):
    count = lax.axis_size(axis)
    route = []
    for low in range(count):
        high = low | 1 << stride
        if high != low and high < count:
            if not down_only:
                route.append((low, high))
            if not up_only:
                route.append((high, low))
    return lax.ppermute(block, axis, route)


def hbm(array):
    return pltpu.with_memory_space_constraint(array, pltpu.HBM)


def state_kernel(k_hbm, v_hbm, grad_hbm, *refs):
    s_ref, kh_ref, vh_ref, grad_ref, low_ref, k_ref, v_ref, sems = refs
    copies = [
        pltpu.make_async_copy(k_hbm, k_ref, sems.at[0]),
        pltpu.make_async_copy(v_hbm, v_ref, sems.at[1]),
        pltpu.make_async_copy(grad_hbm, grad_ref, sems.at[2]),
        pltpu.make_async_copy(grad_hbm.at[pl.ds(0, low_ref.shape[0])], low_ref, sems.at[3]),
    ]
    for copy in copies:
        copy.start()
    for copy in copies[:2]:
        copy.wait()
    for h in range(k_ref.shape[1]):
        k = k_ref[:, h, :].astype(BF)
        v = v_ref[:, h, :].astype(BF)
        kh_ref[h] = k
        vh_ref[h] = v
        s_ref[h] = mm(k, v, TN).astype(BF)
    copies[2].wait()
    copies[3].wait()


def weight_of(lam_ref, h, rows):
    local_bits = (rows // CH).bit_length() - 1
    s = lax.broadcasted_iota(jnp.int32, (rows, rows), 0)
    t = lax.broadcasted_iota(jnp.int32, (rows, rows), 1)
    differ = (s // CH) ^ (t // CH)
    weight = jnp.broadcast_to(lam_ref[0, h : h + 1, :], (rows, rows))
    for digit in range(local_bits):
        weight = jnp.where(differ >= 1 << digit, lam_ref[1 + digit, h : h + 1, :], weight)
    return jnp.where(s <= t, weight, 0.0)


def upper_weight(lam_ref, b, h, rows):
    local_bits = (rows // CH).bit_length() - 1
    upper = (lax.axis_index("seq") >> b & 1).astype(F32)
    return lam_ref[1 + local_bits + b, h : h + 1, :] * upper


def local_kernel(q_hbm, kh_ref, vh_ref, lam_hbm, w_hbm, *refs):
    pt_ref, att_ref, qh_ref, qw_ref, lam_ref, w_ref, q_ref, lam_rows, sems = refs
    pieces = sems.shape[0] - 2
    share = w_hbm.shape[0] // pieces
    copies = [
        pltpu.make_async_copy(q_hbm, q_ref, sems.at[0]),
        pltpu.make_async_copy(lam_hbm, lam_ref, sems.at[1]),
    ]
    for i in range(pieces):
        piece = pl.ds(i * share, share)
        copies.append(pltpu.make_async_copy(w_hbm.at[piece], w_ref.at[piece], sems.at[2 + i]))
    for copy in copies:
        copy.start()
    for copy in copies[:2]:
        copy.wait()
    rows, heads_dev, _ = q_ref.shape
    bits = qw_ref.shape[0]
    lam_rows[...] = jnp.zeros_like(lam_rows)
    for b in range(bits):
        for h in range(heads_dev):
            at = b * heads_dev + h
            lam_rows[at : at + 1, :] = upper_weight(lam_ref, b, h, rows)
    lam_columns = lam_rows[...].T
    for h in range(heads_dev):
        q32 = q_ref[:, h, :]
        q = q32.astype(BF)
        qh_ref[h] = q
        for b in range(bits):
            at = b * heads_dev + h
            qw_ref[b, h] = (q32 * lam_columns[:, at : at + 1]).astype(BF)
        pt = (mm(kh_ref[h], q, NT) * weight_of(lam_ref, h, rows)).astype(BF)
        pt_ref[h] = pt
        att_ref[h] = mm(pt, vh_ref[h], TN)
    for copy in copies[2:]:
        copy.wait()


def attended_kernel(bits, att_ref, qw_ref, *refs):
    states, out_ref = refs[:bits], refs[-1]
    heads_dev, _, head_dim = att_ref.shape
    for h in range(heads_dev):
        total = att_ref[h]
        for b in range(bits):
            total = total + mm(qw_ref[b, h], states[b][h], NN)
        out_ref[:, h * head_dim : (h + 1) * head_dim] = total.astype(BF)


def cotangent_kernel(blocks, bits, *refs):
    parts, (w_ref, qw_ref, _, gt_ref), sums = (
        refs[:blocks],
        refs[blocks : blocks + 4],
        refs[blocks + 4 :],
    )
    deep = parts[0].shape[1]
    _, heads_dev, _, head_dim = qw_ref.shape
    total = None
    for i in range(blocks):
        column = pl.multiple_of((lax.axis_index("head") ^ i) * deep, deep)
        product = mm(w_ref[:, pl.ds(column, deep)], parts[i][...], NT)
        total = product if total is None else total + product
    for h in range(heads_dev):
        gt = total[h * head_dim : (h + 1) * head_dim].astype(BF)
        gt_ref[h * head_dim : (h + 1) * head_dim, :] = gt
        for b in range(bits):
            sums[b][h] = mm(gt, qw_ref[b, h], NN).astype(BF)


def running_kernel(running_ref, arrived_ref, *refs):
    refs[-1][...] = (running_ref[...].astype(F32) + arrived_ref[...].astype(F32)).astype(BF)


def meet_kernel(top, grad_ref, running_ref, arrived_ref, out_ref):
    upper = (lax.axis_index("seq") >> top & 1) == 1
    running = running_ref[...].astype(F32)
    if arrived_ref is not None:
        running = running + arrived_ref[...].astype(F32)
    out_ref[...] = jnp.where(upper, grad_ref[...], running.astype(BF))


def landed_sum(top, landed):
    upper = (lax.axis_index("seq") >> top & 1) == 1
    total = jnp.where(upper, 0.0, landed[0].astype(F32))
    for block in landed[1:]:
        total = total + block.astype(F32)
    return total


def pending_kernel(top, own_ref, after_ref, *refs):
    del after_ref
    landed, out_ref = [ref[...] for ref in refs[:-1]], refs[-1]
    out_ref[...] = (own_ref[...].astype(F32) + landed_sum(top, landed)).astype(BF)


def turned_group(high, group, bits):
    turned = high >> 1 | (high & 1) << bits - 1
    return turned ^ ((group >> bits - 1 ^ group) & 1) << bits - 1


def turned_high(turned, group, bits):
    turned = turned ^ ((group >> bits - 1 ^ group) & 1) << bits - 1
    return (turned << 1 & (1 << bits) - 1) | turned >> bits - 1


def relay_kernel(block_ref, after_ref, out_ref):
    del after_ref
    out_ref[...] = block_ref[...]


def chunk_kernel(low_ref, high_ref, after_ref, *outs):
    del after_ref
    half = low_ref.shape[0]
    columns = outs[0].shape[1]
    low = lax.axis_index("seq") % len(outs)
    for r, out in enumerate(outs):
        at = pl.ds(pl.multiple_of((low ^ r) * columns, columns), columns)
        out[:half] = low_ref[:, at]
        out[half:] = high_ref[:, at]


def stack_kernel(after_ref, *refs):
    del after_ref
    for r, ref in enumerate(refs[:-1]):
        refs[-1][r] = ref[...]


def columns_kernel(blocks, *refs):
    parts, out_ref = refs[:blocks], refs[blocks]
    per = parts[0].shape[0]
    bits = blocks.bit_length() - 1
    low = lax.axis_index("seq") % per
    for i in range(blocks):
        high = turned_high(lax.axis_index("head") ^ i, lax.axis_index("seq") // per, bits)
        for r in range(per):
            out_ref[high * per + (low ^ r)] = parts[i][r]


def local_grad_kernel(
    bits, gt_ref, qh_ref, kh_ref, vh_ref, pt_ref, lam_ref, after_ref, *refs
):
    del after_ref
    states, (dq_ref, dk_ref, dv_ref) = refs[:bits], refs[bits:]
    heads_dev, rows, head_dim = qh_ref.shape
    for h in range(heads_dev):
        gt = gt_ref[h * head_dim : (h + 1) * head_dim, :]
        g32 = gt.astype(F32)
        dpt = (mm(vh_ref[h], gt, NN) * weight_of(lam_ref, h, rows)).astype(BF)
        dk_ref[h] = mm(dpt, qh_ref[h], NN)
        dv_ref[h] = mm(pt_ref[h], gt, NT)
        dq = mm(dpt, kh_ref[h], TN)
        for b in range(bits):
            gw = (g32 * upper_weight(lam_ref, b, h, rows)).astype(BF)
            dq = dq + mm(gw, states[b][h], TT)
        dq_ref[h] = dq


def query_grad_kernel(top, gt_ref, lam_ref, dql_ref, state_ref, after_ref, dq_ref):
    del after_ref
    heads_dev, rows, head_dim = dql_ref.shape
    for h in range(heads_dev):
        g32 = gt_ref[h * head_dim : (h + 1) * head_dim, :].astype(F32)
        gw = (g32 * upper_weight(lam_ref, top, h, rows)).astype(BF)
        dq_ref[:, h, :] = dql_ref[h] + mm(gw, state_ref[h], TT)


def later_grad_kernel(top, kh_ref, vh_ref, dkl_ref, dvl_ref, after_ref, *refs):
    del after_ref
    landed, (dk_ref, dv_ref) = refs[:-2], refs[-2:]
    for h in range(kh_ref.shape[0]):
        late = landed_sum(top, [ref[h] for ref in landed]).astype(BF)
        dk_ref[:, h, :] = dkl_ref[h] + mm(vh_ref[h], late, NN)
        dv_ref[:, h, :] = dvl_ref[h] + mm(kh_ref[h], late, NT)


def share_kernel(offsets, att_ref, w_ref, after_ref, out_ref):
    del after_ref
    width = out_ref.shape[2]
    for n, i in enumerate(offsets):
        column = pl.multiple_of((lax.axis_index("head") ^ i) * width, width)
        out_ref[n] = mm(att_ref[...], w_ref[:, pl.ds(column, width)], NN).astype(out_ref.dtype)


def ring_owner(place, offset, devices):
    at = jnp.where(place % 2 == 0, place // 2, devices - 1 - place // 2)
    at = (at + offset + devices) % devices
    return jnp.where(at < devices // 2, 2 * at, 2 * (devices - 1 - at) + 1)


def proj_kernel(offsets, devices, first, cols_ref, after_ref, *refs):
    del after_ref
    total = None if first else refs[len(offsets)][...]
    for i, (offset, low, high) in enumerate(offsets):
        owner = ring_owner(lax.axis_index("seq"), offset, devices)
        product = mm(refs[i][...], cols_ref[owner, low:high, :], TN)
        total = product if total is None else total + product
    refs[-1][...] = total


def last_kernel(offset, devices, cols_ref, low_ref, high_ref, total_ref, after_ref, out_hbm, *refs):
    del after_ref
    held, result, sems = refs
    half = low_ref.shape[0]
    held[:half] = low_ref[...]
    held[half:] = high_ref[...]
    cols = cols_ref[ring_owner(lax.axis_index("seq"), offset, devices)]
    pieces = sems.shape[0]
    block = held.shape[1] // pieces
    copies = []
    for i in range(pieces):
        at = pl.ds(i * block, block)
        result[at, :] = total_ref[at, :] + mm(held[:, at], cols, TN)
        copies.append(pltpu.make_async_copy(result.at[at], out_hbm.at[at], sems.at[i]))
        copies[-1].start()
    for copy in copies:
        copy.wait()


def body(queries, keys, values, level_weights, out_proj, out_grad):
    rows, heads_dev, head_dim = queries.shape
    width = heads_dev * head_dim
    devices = lax.axis_size("seq")
    seq_bits = devices.bit_length() - 1
    heads = lax.axis_size("head")
    head_bits = heads.bit_length() - 1
    columns_dev = out_proj.shape[1] // devices

    head_state = like((heads_dev, head_dim, head_dim), BF)
    pinned_state = pltpu.VMEM((heads_dev, head_dim, head_dim), BF)
    per_head = pltpu.VMEM((heads_dev, rows, head_dim), BF)
    per_head_f32 = pltpu.VMEM((heads_dev, rows, head_dim), F32)
    flops_head = 2 * heads_dev * rows * rows * head_dim
    moved_head = 2 * rows * width
    top = seq_bits - 1

    half = rows // 2
    own_state, kh, vh, own_grad, own_low = pl.pallas_call(
        state_kernel,
        out_shape=(head_state, per_head, per_head, like(out_grad.shape, BF), like((half, width), BF)),
        in_specs=[ANY] * 3,
        out_specs=(VMEM,) * 5,
        scratch_shapes=[
            pltpu.VMEM(keys.shape, F32),
            pltpu.VMEM(keys.shape, F32),
            pltpu.SemaphoreType.DMA((4,)),
        ],
        compiler_params=PARAMS,
        cost_estimate=cost(flops_head, 7 * moved_head),
    )(hbm(keys), hbm(values), hbm(out_grad))

    def to_group(block, i):
        return lax.ppermute(block, "head", [(at, at ^ i) for at in range(heads)])

    def every_group(block):
        blocks = {0: block}
        for digit in reversed(range(head_bits)):
            for i in sorted(blocks):
                blocks[i ^ 1 << digit] = to_group(blocks[i], 1 << digit)
        return [blocks[i] for i in range(heads)]

    probs_t, att_local, qh, qw, lam, w = pl.pallas_call(
        local_kernel,
        out_shape=(
            pltpu.VMEM((heads_dev, rows, rows), BF),
            per_head_f32,
            per_head,
            pltpu.VMEM((seq_bits, heads_dev, rows, head_dim), BF),
            pltpu.VMEM(level_weights.shape, F32),
            pltpu.VMEM(out_proj.shape, BF),
        ),
        in_specs=[ANY, VMEM, VMEM, ANY, ANY],
        out_specs=(VMEM,) * 6,
        scratch_shapes=[
            pltpu.VMEM(queries.shape, F32),
            pltpu.VMEM((rows, rows), F32),
            pltpu.SemaphoreType.DMA((10,)),
        ],
        compiler_params=PARAMS,
        cost_estimate=cost(2 * flops_head, 12 * moved_head),
    )(hbm(queries), kh, vh, hbm(level_weights), hbm(out_proj))

    def relayed(block):
        return pl.pallas_call(
            relay_kernel,
            out_shape=like(block.shape, block.dtype),
            in_specs=[VMEM, ANY],
            out_specs=VMEM,
            compiler_params=PARAMS,
            cost_estimate=cost(0, 2 * moved_head),
        )(block, qw)

    grad_blocks = {0: own_grad}
    for digit in reversed(range(head_bits)):
        for i in sorted(grad_blocks):
            block = relayed(grad_blocks[i]) if i else own_grad
            grad_blocks[i ^ 1 << digit] = to_group(block, 1 << digit)
    grad_blocks = [grad_blocks[i] for i in range(heads)]

    per = devices // heads
    def turn_route(shift):
        return [
            (
                (high * per + low) * heads + (group_at ^ shift),
                (group_at * per + low) * heads + turned_group(high, group_at, head_bits),
            )
            for high in range(heads)
            for low in range(per)
            for group_at in range(heads)
        ]

    axes, far = ("seq", "head"), heads // 2
    turned = [
        lax.ppermute(own_low, axes, turn_route(0)),
        lax.ppermute(grad_blocks[far][half:], axes, turn_route(far)),
    ]
    partner_states = []
    running, arrived = own_state, None
    for digit in range(top):
        if arrived is not None:
            running = pl.pallas_call(
                running_kernel,
                out_shape=head_state,
                in_specs=[VMEM] * 2 + [ANY],
                out_specs=VMEM,
                compiler_params=PARAMS,
                cost_estimate=cost(0, 3 * moved_head),
            )(running, arrived, qw)
        arrived = across(running, "seq", digit)
        partner_states.append(arrived)

    gt, *grad_sums = pl.pallas_call(
        functools.partial(cotangent_kernel, heads, seq_bits),
        out_shape=(pltpu.VMEM((width, rows), BF),) + (pinned_state,) * seq_bits,
        in_specs=[VMEM] * (heads + 2) + [ANY],
        out_specs=(VMEM,) * (1 + seq_bits),
        compiler_params=PARAMS,
        cost_estimate=cost(2 * rows * width * out_proj.shape[1], 2 * width * out_proj.shape[1]),
    )(*grad_blocks, w, qw, running)

    meeting = pl.pallas_call(
        functools.partial(meet_kernel, top)
        if arrived is not None
        else lambda grad_ref, running_ref, out_ref: meet_kernel(
            top, grad_ref, running_ref, None, out_ref
        ),
        out_shape=head_state,
        in_specs=[VMEM] * (2 if arrived is None else 3),
        out_specs=VMEM,
        compiler_params=PARAMS,
        cost_estimate=cost(0, 4 * moved_head),
    )(grad_sums[top], running, *([] if arrived is None else [arrived]))
    landed = [across(meeting, "seq", top)]
    partner_states.append(landed[0])

    chunks = pl.pallas_call(
        chunk_kernel,
        out_shape=(like((rows, columns_dev), BF),) * per,
        in_specs=[VMEM, VMEM, ANY],
        out_specs=(VMEM,) * per,
        compiler_params=PARAMS,
        cost_estimate=cost(0, 2 * moved_head),
    )(*turned, meeting)
    own_chunks = chunks
    chunks = [chunks[0]] + [
        lax.ppermute(chunks[r], "seq", [(at, at ^ r) for at in range(devices)])
        for r in range(1, per)
    ]
    stacked = pl.pallas_call(
        stack_kernel,
        out_shape=like((per, rows, columns_dev), BF),
        in_specs=[ANY] + [VMEM] * per,
        out_specs=VMEM,
        compiler_params=PARAMS,
        cost_estimate=cost(0, 2 * moved_head),
    )(meeting, *chunks)
    column_blocks = every_group(stacked)

    grad_columns = pl.pallas_call(
        functools.partial(columns_kernel, heads),
        out_shape=pltpu.VMEM((devices, rows, columns_dev), BF),
        in_specs=[VMEM] * heads,
        out_specs=VMEM,
        compiler_params=PARAMS,
        cost_estimate=cost(0, 8 * moved_head),
    )(*column_blocks)

    query_local, key_local, value_local = pl.pallas_call(
        functools.partial(local_grad_kernel, top),
        out_shape=(per_head_f32,) * 3,
        in_specs=[VMEM] * 6 + [ANY] + [VMEM] * top,
        out_specs=(VMEM,) * 3,
        compiler_params=PARAMS,
        cost_estimate=cost((4 + top) * flops_head, 14 * moved_head),
    )(gt, qh, kh, vh, probs_t, lam, meeting, *partner_states[:top])

    attended = pl.pallas_call(
        functools.partial(attended_kernel, seq_bits),
        out_shape=like((rows, width), BF),
        in_specs=[VMEM] * (2 + seq_bits) + [ANY],
        out_specs=VMEM,
        compiler_params=PARAMS,
        cost_estimate=cost(seq_bits * flops_head, 8 * moved_head),
    )(att_local, qw, *partner_states, key_local)

    first_pending = attended
    for digit in reversed(range(top)):
        outgoing = pl.pallas_call(
            functools.partial(pending_kernel, top),
            out_shape=head_state,
            in_specs=[VMEM, ANY] + [VMEM] * len(landed),
            out_specs=VMEM,
            compiler_params=PARAMS,
            cost_estimate=cost(0, 4 * moved_head),
        )(grad_sums[digit], attended, *landed)
        if len(landed) == 1:
            first_pending = outgoing
        landed.append(across(outgoing, "seq", digit))

    query_grad = pl.pallas_call(
        functools.partial(query_grad_kernel, top),
        out_shape=like((rows, heads_dev, head_dim), F32),
        in_specs=[VMEM] * 4 + [ANY],
        out_specs=VMEM,
        compiler_params=PARAMS,
        cost_estimate=cost(flops_head, 6 * moved_head),
    )(gt, lam, query_local, partner_states[top], attended)

    def share(offsets, kind, after):
        return pl.pallas_call(
            functools.partial(share_kernel, offsets),
            out_shape=like((len(offsets), rows, width), kind),
            in_specs=[VMEM, VMEM, ANY],
            out_specs=VMEM,
            compiler_params=PARAMS,
            cost_estimate=cost(
                2 * rows * width * len(offsets) * width, 2 * width * len(offsets) * width
            ),
        )(attended, w, after)

    send = share(range(1, heads, 2), BF, stacked)
    kept = share(range(0, heads, 2), F32, first_pending)
    for digit in range(head_bits):
        kept = kept + to_group(send, 1 << digit).astype(F32)
        if digit < head_bits - 1:
            send, kept = kept[1::2].astype(BF), kept[0::2]
    mixed = kept[0].astype(BF)

    key_grad, value_grad = pl.pallas_call(
        functools.partial(later_grad_kernel, top),
        out_shape=(like((rows, heads_dev, head_dim), F32),) * 2,
        in_specs=[VMEM] * 4 + [ANY] + [VMEM] * seq_bits,
        out_specs=(VMEM,) * 2,
        compiler_params=PARAMS,
        cost_estimate=cost(2 * flops_head, 11 * moved_head),
    )(kh, vh, key_local, value_local, attended, *landed)

    ring = list(range(0, devices, 2)) + list(range(devices - 1, 0, -2))
    forward = [(ring[i], ring[(i + 1) % devices]) for i in range(devices)]
    backward = [(b, a) for a, b in forward]

    def accumulate(total, blocks, offsets):
        operands = blocks if total is None else blocks + [total]
        return pl.pallas_call(
            functools.partial(proj_kernel, offsets, devices, total is None),
            out_shape=pltpu.VMEM((width, columns_dev), F32),
            in_specs=[VMEM, ANY] + [VMEM] * len(operands),
            out_specs=VMEM,
            compiler_params=PARAMS,
            cost_estimate=cost(
                2 * len(blocks) * rows * width * columns_dev, 4 * width * columns_dev
            ),
        )(grad_columns, hbm(key_grad), *operands)

    blocks, offsets = [attended], [(0, 0, rows)]
    ahead = behind = attended
    steps, total = devices // 2, None
    for step in range(1, steps):
        ahead = lax.ppermute(ahead, "seq", forward)
        behind = lax.ppermute(behind, "seq", backward)
        blocks += [ahead, behind]
        offsets += [(-step, 0, rows), (step, 0, rows)]
        if step == steps - 2:
            total = accumulate(None, blocks, offsets)
            blocks, offsets = [], []
    if blocks:
        total = accumulate(total, blocks, offsets)
    last = [
        lax.ppermute(ahead[:half], "seq", forward),
        lax.ppermute(behind[half:], "seq", backward),
    ]
    proj_grad = pl.pallas_call(
        functools.partial(last_kernel, steps, devices),
        out_shape=like((width, columns_dev), F32),
        in_specs=[VMEM] * 4 + [ANY],
        out_specs=ANY,
        scratch_shapes=[
            pltpu.VMEM((rows, width), BF),
            pltpu.VMEM((width, columns_dev), F32),
            pltpu.SemaphoreType.DMA((4,)),
        ],
        compiler_params=PARAMS,
        cost_estimate=cost(2 * rows * width * columns_dev, 8 * width * columns_dev),
    )(grad_columns, *last, total, hbm(key_grad))
    return (mixed, query_grad, key_grad, value_grad, proj_grad)


def solution(mesh):
    placed = (
        P("seq", "head", None),
        P("seq", "head", None),
        P("seq", "head", None),
        P(None, "head", "seq"),
        P("head", None),
        P("seq", "head"),
    )
    return jax.shard_map(
        body,
        mesh=mesh,
        in_specs=placed,
        out_specs=(
            P("seq", "head"),
            P("seq", "head", None),
            P("seq", "head", None),
            P("seq", "head", None),
            P("head", "seq"),
        ),
        check_vma=False,
    )
```
